32 devices in a mesh: dp: 2 (over y), mp: 16 (over z, x, core).
Axes of the slice: x: 2, y: 2, z: 4, core: 2. Of those that a mesh axis runs over, the one named last changes fastest.
Arguments:
- state_action: bfloat16 [16384, 23], P(('dp', 'mp')), may hold values from -6 to 6
- next_state: bfloat16 [16384, 17], P(('dp', 'mp')), may hold values from -6 to 6
- reward: float32 [16384], P(('dp', 'mp')), may hold values from -6 to 6
- done_flags: int32 [16384], P(('dp', 'mp')), may hold values from 0 to 2, as said below
- noise_index: int32 [16384], P(('dp', 'mp')), may hold values from 0 to 255
- noise_table: float32 [256, 6], replicated, may hold values from -4 to 4
- subsets: int32 [16384, 2], P(('dp', 'mp')), may hold values from 0 to 9, all different within a row
- policy_in: bfloat16 [17, 256], replicated, may hold values from -1.5 to 1.5
- policy_mid: bfloat16 [256, 256], replicated, may hold values from -0.375 to 0.375
- policy_out: bfloat16 [256, 12], replicated, may hold values from -0.375 to 0.375
- critic_in: float32 [23, 10240], P(None, ('dp', 'mp')), may hold values from -1.25 to 1.25
- in_first: float32 [23, 10240], P(None, ('dp', 'mp')), may hold values from -0.0009765625 to 0.0009765625
- in_second: float32 [23, 10240], P(None, ('dp', 'mp')), may hold values from 3.90625e-10 to 1.5625e-09
- critic_norms: float32 [4, 10240], P(None, ('dp', 'mp')), as said below
- norm_first: float32 [4, 10240], P(None, ('dp', 'mp')), may hold values from -0.0009765625 to 0.0009765625
- norm_second: float32 [4, 10240], P(None, ('dp', 'mp')), may hold values from 3.90625e-10 to 1.5625e-09
- critic_head: float32 [10240], P(('dp', 'mp')), may hold values from -0.1875 to 0.1875
- head_first: float32 [10240], P(('dp', 'mp')), may hold values from -0.03125 to 0.03125
- head_second: float32 [10240], P(('dp', 'mp')), may hold values from 3.90625e-07 to 1.5625e-06
- critic_hidden: float32 [10, 1024, 1024], P(None, 'mp', 'dp'), may hold values from -0.1875 to 0.1875
- hidden_moment: float32 [10, 1024, 1024], P(None, 'mp', 'dp'), may hold values from -0.009765625 to 0.009765625
- left_stats: float32 [10, 1024, 1024], P(None, 'mp', 'dp'), as said below
- right_stats: float32 [10, 1024, 1024], P(None, 'mp', 'dp'), as said below
- target_in: float32 [23, 10240], P(None, ('dp', 'mp')), may hold values from -1.25 to 1.25
- target_norms: float32 [4, 10240], P(None, ('dp', 'mp')), as said below
- target_head: float32 [10240], P(('dp', 'mp')), may hold values from -0.1875 to 0.1875
- target_hidden: float32 [10, 1024, 1024], P(None, 'mp', 'dp'), may hold values from -0.1875 to 0.1875
Outputs:
- loss_total: float32 [], replicated
- valid_total: float32 [], replicated
- in_moment: float32 [23, 10240], P(None, ('dp', 'mp'))
- in_square: float32 [23, 10240], P(None, ('dp', 'mp'))
- in_updated: float32 [23, 10240], P(None, ('dp', 'mp'))
- norm_moment: float32 [4, 10240], P(None, ('dp', 'mp'))
- norm_square: float32 [4, 10240], P(None, ('dp', 'mp'))
- norm_updated: float32 [4, 10240], P(None, ('dp', 'mp'))
- head_moment: float32 [10240], P(('dp', 'mp'))
- head_square: float32 [10240], P(('dp', 'mp'))
- head_updated: float32 [10240], P(('dp', 'mp'))
- hidden_momentum: float32 [10, 1024, 1024], P(None, 'mp', 'dp')
- left_renewed: float32 [10, 1024, 1024], P(None, 'mp', 'dp')
- right_renewed: float32 [10, 1024, 1024], P(None, 'mp', 'dp')
- hidden_updated: float32 [10, 1024, 1024], P(None, 'mp', 'dp')
The draws below stay inside these ranges and needn't reach their ends.
Inputs may be any that keep to these rules, and one draw needn't show every extreme that they name: `done_flags`: the first row of each block of 512 rows is never 2. `critic_norms`: rows 0 and 2 are gains, rows 1 and 3 shifts. `target_norms`: rows 0 and 2 are gains, rows 1 and 3 shifts. `left_stats`: zero except the diagonal of each 32 x 32 block, which is positive. `right_stats`: zero except the diagonal of each 32 x 32 block, which is positive.
All inputs are finite; a program needn't handle non-finite values.
Results may differ from the reference program's by a relative error of at most 0.0051.
Values may be sent and summed in bfloat16 or wider, within the bound.
A program may use at most 320 MiB of HBM per device.

```python
import math
import jax
import jax.numpy as jnp
from jax import lax

OBS = 17
ACT = 6
IN = 23
H = 1024
CRIT = 10
PH = 256
NOISE = 256
BLK = 32
NEWTON = 5
STEP = 10
ROWS_DEV = 512
ROWS = 16384
N_DP = 2
N_MP = 16
DEVICES = 32


def draw_done_flags(key, part):
    key = jax.random.fold_in(key, 3)
    keep_key, rate_key, end_key = jax.random.split(key, 3)
    row_ids = jnp.arange(ROWS)
    device = row_ids // ROWS_DEV
    row_group = device // N_MP
    column_group = device % N_MP
    keep_milli = 150 + 350 * row_group // max(N_DP - 1, 1) + 350 * column_group // max(N_MP - 1, 1)
    keep_rolls = jax.random.randint(keep_key, (ROWS,), 0, 1000)
    end_rates = jax.random.randint(rate_key, (DEVICES,), 20, 300)
    end_rolls = jax.random.randint(end_key, (ROWS,), 0, 1000)
    flag_values = jnp.where(end_rolls < end_rates[device], 1, 0)
    flag_values = jnp.where(keep_rolls >= keep_milli, 2, flag_values)
    flag_values = jnp.where(row_ids % ROWS_DEV == 0, 0, flag_values)
    return flag_values.astype(jnp.int32)


def gain_shift_draw(key):
    gain_key, shift_key = jax.random.split(key)
    gains = jax.random.uniform(gain_key, (2, CRIT * H), jnp.float32, 0.6, 1.4)
    shifts = 0.3 * jax.random.normal(shift_key, (2, CRIT * H), jnp.float32)
    return jnp.stack([gains[0], shifts[0], gains[1], shifts[1]])


def draw_critic_norms(key, part):
    key = jax.random.fold_in(key, 5)
    return gain_shift_draw(key)


def draw_target_norms(key, part):
    key = jax.random.fold_in(key, 7)
    return gain_shift_draw(key)


def diagonal_stats(key, log_range):
    row_place = jnp.arange(H)[:, None] % BLK
    col_place = jnp.arange(H)[None, :] % BLK
    on_diagonal = (row_place == col_place).astype(jnp.float32)
    spread = jnp.exp(jax.random.uniform(key, (CRIT, H, H), jnp.float32, 0.0, log_range))
    return on_diagonal[None] * spread * (0.0068 * BLK / ROWS)


def draw_left_stats(key, part):
    key = jax.random.fold_in(key, 11)
    return diagonal_stats(key, math.log(4.0))


def draw_right_stats(key, part):
    key = jax.random.fold_in(key, 13)
    return diagonal_stats(key, math.log(4.0))


def with_ends(drawn, own_key, smallest, top_value):
    place = [jax.random.randint(jax.random.fold_in(own_key, axis), (), 0, length) for axis, length in enumerate(drawn.shape)]
    widest = drawn.shape.index(max(drawn.shape))
    next_to = place[:widest] + [(place[widest] + 1) % drawn.shape[widest]] + place[widest + 1:]
    return drawn.at[tuple(place)].set(smallest).at[tuple(next_to)].set(top_value)


def steps_of(own_key, shape, cuts, low, high):
    def one(dim, blocks):
        heights = jax.random.uniform(jax.random.fold_in(jax.random.fold_in(own_key, 6), dim), (blocks,), jnp.float32, low / len(cuts), high / len(cuts))
        return jnp.repeat(jnp.exp(heights), shape[dim] // blocks).reshape((-1,) + (1,) * (len(shape) - dim - 1))

    loudness = one(*cuts[0])
    for cut in cuts[1:]:
        loudness = loudness * one(*cut)
    return loudness


def distinct(stream_key, rows, count, top, lift):
    sequence = jax.random.permutation(jax.random.fold_in(stream_key, 1), count)
    favour = sequence
    for power in range(3):
        favour = favour * favour // count
    favour = favour * lift // count
    tickets = jax.random.randint(jax.random.fold_in(stream_key, 2), (rows, count), 0, 4096) + favour
    fixed_rows = jax.random.permutation(jax.random.fold_in(stream_key, 3), rows)[jnp.arange(count) % rows]
    tickets = jnp.where(jnp.arange(rows)[:, None] == fixed_rows[None, :], 1 << 14, tickets)
    score = tickets * count + jnp.arange(count)
    return lax.top_k(score.astype(jnp.int32), top)[1].astype(jnp.int32)


def noise(key, extent, scale, most, cuts=(), held_as=jnp.bfloat16):
    values = jax.random.normal(key, extent, jnp.float32) * scale
    if len(cuts) > 0:
        values = steps_of(key, extent, cuts, -0.22, 0.18) * values
    return jnp.clip(values, min=-most, max=most).astype(held_as)


def setup_inputs(seed: int = 0) -> dict:
    key_list = jax.random.split(jax.random.key(seed), 28)
    state_action = noise(key_list[0], (ROWS, IN), 1.0, 6.0, ((0, 32),))
    next_state = noise(key_list[1], (ROWS, OBS), 1.0, 6.0, ((0, 32),))
    reward = noise(key_list[2], (ROWS,), 1.0, 6.0, ((0, 32),), jnp.float32)
    done_flags = draw_done_flags(jax.random.fold_in(key_list[27], 71), 0)
    noise_index = with_ends(jax.random.randint(key_list[4], (ROWS,), 0, NOISE), jax.random.fold_in(key_list[4], 1), 0, NOISE - 1).astype(jnp.int32)
    noise_table = noise(key_list[5], (NOISE, ACT), 1.0, 4.0, (), jnp.float32)
    subsets = distinct(key_list[6], ROWS, CRIT, 2, 0)
    policy_in = noise(key_list[7], (OBS, PH), OBS ** -0.5, 1.5)
    policy_mid = noise(key_list[8], (PH, PH), PH ** -0.5, 0.375)
    policy_out = noise(key_list[9], (PH, 2 * ACT), PH ** -0.5, 0.375)
    critic_in = noise(key_list[10], (IN, CRIT * H), IN ** -0.5, 1.25, ((1, 32),), jnp.float32)
    in_first = noise(key_list[11], (IN, CRIT * H), (0.11 * (0.0064 / ROWS) ** 0.5), 0.0009765625, ((1, 32),), jnp.float32)
    in_second = jnp.clip(jnp.exp(math.log(1.5625000182595272e-09) - 1.3862944 * jax.random.uniform(key_list[12], (IN, CRIT * H), jnp.float32) ** steps_of(key_list[12], (IN, CRIT * H), ((1, 32),), -0.2, 0.2)), 3.906250045648818e-10, 1.5625000182595272e-09)
    critic_norms = draw_critic_norms(jax.random.fold_in(key_list[27], 71), 0)
    norm_first = noise(key_list[14], (4, CRIT * H), (0.11 * (0.0064 / ROWS) ** 0.5), 0.0009765625, ((1, 32),), jnp.float32)
    norm_second = jnp.clip(jnp.exp(math.log(1.5625000182595272e-09) - 1.3862944 * jax.random.uniform(key_list[15], (4, CRIT * H), jnp.float32) ** steps_of(key_list[15], (4, CRIT * H), ((1, 32),), -0.2, 0.2)), 3.906250045648818e-10, 1.5625000182595272e-09)
    critic_head = noise(key_list[16], (CRIT * H,), H ** -0.5, 0.1875, ((0, 32),), jnp.float32)
    head_first = noise(key_list[17], (CRIT * H,), (0.11 * (6.4 / ROWS) ** 0.5), 0.03125, ((0, 32),), jnp.float32)
    head_second = jnp.clip(jnp.exp(math.log(1.56249996052793e-06) - 1.3862944 * jax.random.uniform(key_list[18], (CRIT * H,), jnp.float32) ** steps_of(key_list[18], (CRIT * H,), ((0, 32),), -0.2, 0.2)), 3.906249901319825e-07, 1.56249996052793e-06)
    critic_hidden = noise(key_list[19], (CRIT, H, H), H ** -0.5, 0.1875, ((1, 16), (2, 2)), jnp.float32)
    hidden_moment = noise(key_list[20], (CRIT, H, H), ((0.0065 / ROWS) ** 0.5), 0.009765625, ((1, 16), (2, 2)), jnp.float32)
    left_stats = draw_left_stats(jax.random.fold_in(key_list[27], 71), 0)
    right_stats = draw_right_stats(jax.random.fold_in(key_list[27], 71), 0)
    target_in = noise(key_list[23], (IN, CRIT * H), IN ** -0.5, 1.25, ((1, 32),), jnp.float32)
    target_norms = draw_target_norms(jax.random.fold_in(key_list[27], 71), 0)
    target_head = noise(key_list[25], (CRIT * H,), H ** -0.5, 0.1875, ((0, 32),), jnp.float32)
    target_hidden = noise(key_list[26], (CRIT, H, H), H ** -0.5, 0.1875, ((1, 16), (2, 2)), jnp.float32)
    return dict(state_action=state_action, next_state=next_state, reward=reward, done_flags=done_flags, noise_index=noise_index, noise_table=noise_table, subsets=subsets, policy_in=policy_in, policy_mid=policy_mid, policy_out=policy_out, critic_in=critic_in, in_first=in_first, in_second=in_second, critic_norms=critic_norms, norm_first=norm_first, norm_second=norm_second, critic_head=critic_head, head_first=head_first, head_second=head_second, critic_hidden=critic_hidden, hidden_moment=hidden_moment, left_stats=left_stats, right_stats=right_stats, target_in=target_in, target_norms=target_norms, target_head=target_head, target_hidden=target_hidden)


@jax.custom_vjp
def low(v):
    return lax.optimization_barrier(v.astype(jnp.bfloat16)).astype(jnp.float32)

@jax.custom_vjp
def low_back(v):
    return v

def low_keep(v):
    return (low(v), None)

def low_pass(kept, grad):
    return (grad,)

def back_keep(v):
    return (v, None)

def back_low(kept, grad):
    return (low(grad),)
low.defvjp(low_keep, low_pass)
low_back.defvjp(back_keep, back_low)
HIGHEST = lax.Precision.HIGHEST
REWARD_DISCOUNT = 0.99
ENTROPY_TEMP = 0.2
FIRST_DECAY = 0.9
SECOND_DECAY = 0.999
WEIGHT_DECAY = 0.01
RATE_INPUT = 0.1
RATE_NORMS = 0.3
RATE_HEAD = 0.03
RATE_HIDDEN = 0.01
MOMENTUM = 0.9
STAT_DECAY = 0.95

def swish(values):
    return values * jax.nn.sigmoid(values)

def normed_swish(preact, gain, shift):
    centered = preact - lax.optimization_barrier(jnp.mean(preact, -1, keepdims=True))
    scaled = centered * lax.rsqrt(lax.optimization_barrier(jnp.mean(centered * centered, -1, keepdims=True)) + 1e-05)
    return swish(scaled * gain + shift)

def keep_same(values):
    return values

def critic(inputs, weight_in, weight_hidden, gains, head_row, rounding):
    count_rows = inputs.shape[0]
    norm_rows = gains.reshape(4, CRIT, H)
    first_pre = rounding(jnp.dot(inputs, low(weight_in), precision=HIGHEST).reshape(count_rows, CRIT, H))
    first_act = low(normed_swish(first_pre, norm_rows[0], norm_rows[1]))
    second_pre = rounding(jnp.einsum('rck,ckn->rcn', first_act, low(weight_hidden), precision=HIGHEST))
    second_act = normed_swish(second_pre, norm_rows[2], norm_rows[3])
    return lax.optimization_barrier(jnp.sum(second_act * head_row.reshape(CRIT, H), -1))

def policy_sample(next_state, noise_rows, policy_in, policy_mid, policy_out):
    layer_one = low(swish(jnp.dot(next_state, policy_in, precision=HIGHEST)))
    layer_two = low(swish(jnp.dot(layer_one, policy_mid, precision=HIGHEST)))
    output = jnp.dot(layer_two, policy_out, precision=HIGHEST)
    means = output[:, :ACT]
    log_std = -5.0 + 3.5 * (jnp.tanh(output[:, ACT:]) + 1.0)
    squashed = means + jnp.exp(log_std) * noise_rows
    action = jnp.tanh(squashed)
    correction = 2.0 * (math.log(2.0) - squashed - jax.nn.softplus(-2.0 * squashed))
    action_log_density = lax.optimization_barrier(jnp.sum(-0.5 * noise_rows * noise_rows - log_std - 0.5 * math.log(2.0 * math.pi) - correction, -1))
    return (low(action), action_log_density)

def td_target(next_state, reward, done_flags, noise_index, noise_table, subsets, policy_all, targets_all):
    noise_rows = noise_table[noise_index]
    action, action_log_density = policy_sample(next_state, noise_rows, policy_all[0], policy_all[1], policy_all[2])
    inputs = jnp.concatenate([next_state, action], 1)
    q_target = critic(inputs, targets_all[0], targets_all[1], targets_all[2], targets_all[3], keep_same)
    picks = jnp.arange(CRIT)[None, :]
    first_critic_choice = lax.optimization_barrier(jnp.sum(jnp.where(picks == subsets[:, 0:1], q_target, 0.0), -1))
    second_critic_choice = lax.optimization_barrier(jnp.sum(jnp.where(picks == subsets[:, 1:2], q_target, 0.0), -1))
    bootstrap_value = (done_flags == 0).astype(jnp.float32)
    return reward + REWARD_DISCOUNT * bootstrap_value * (jnp.minimum(first_critic_choice, second_critic_choice) - ENTROPY_TEMP * action_log_density)

def adamw(grad, moment, square, weight, rate):
    moment_new = FIRST_DECAY * moment + (1.0 - FIRST_DECAY) * grad
    square_new = SECOND_DECAY * square + (1.0 - SECOND_DECAY) * grad * grad
    moment_hat = moment_new / (1.0 - FIRST_DECAY ** STEP)
    square_hat = square_new / (1.0 - SECOND_DECAY ** STEP)
    weight_new = weight - rate * (moment_hat / (jnp.sqrt(square_hat) + 1e-08) + WEIGHT_DECAY * weight)
    return (moment_new, square_new, weight_new)

def to_blocks(matrix):
    depth, rows_all, cols_all = matrix.shape
    shaped = matrix.reshape(depth, rows_all // BLK, BLK, cols_all // BLK, BLK)
    return shaped.transpose(0, 1, 3, 2, 4)

def from_blocks(blocks):
    depth, row_blocks, col_blocks, side, other = blocks.shape
    return blocks.transpose(0, 1, 3, 2, 4).reshape(depth, row_blocks * side, col_blocks * other)

def matmul(left, right):
    return jnp.einsum('...ij,...jk->...ik', left, right, precision=HIGHEST)

def inverse_root(stat):
    identity = jnp.eye(stat.shape[-1], dtype=jnp.float32)
    scale = jnp.sqrt(lax.optimization_barrier(jnp.sum(stat * stat, axis=(-2, -1), keepdims=True)))
    root = identity * lax.rsqrt(jnp.sqrt(scale))
    scaled = stat / scale
    for sweep in range(NEWTON):
        factor = (5.0 * identity - scaled) * 0.25
        root = matmul(root, factor)
        square_factor = matmul(factor, factor)
        scaled = matmul(matmul(square_factor, square_factor), scaled)
    return root

def shampoo(grad, moment, left, right, weight):
    grad_blocks = to_blocks(grad)
    moment_new = MOMENTUM * to_blocks(moment) + grad_blocks
    left_new = STAT_DECAY * to_blocks(left) + (1.0 - STAT_DECAY) * jnp.einsum('...ij,...kj->...ik', grad_blocks, grad_blocks, precision=HIGHEST)
    right_new = STAT_DECAY * to_blocks(right) + (1.0 - STAT_DECAY) * jnp.einsum('...ji,...jk->...ik', grad_blocks, grad_blocks, precision=HIGHEST)
    update_direction = matmul(matmul(inverse_root(left_new), moment_new), inverse_root(right_new))
    update_direction = update_direction * lax.rsqrt(lax.optimization_barrier(jnp.mean(update_direction * update_direction, axis=(-2, -1), keepdims=True)) + 1e-06)
    weight_new = weight - RATE_HIDDEN * (from_blocks(update_direction) + WEIGHT_DECAY * weight)
    return (from_blocks(moment_new), from_blocks(left_new), from_blocks(right_new), weight_new)

def reference(state_action, next_state, reward, done_flags, noise_index, noise_table, subsets, policy_in, policy_mid, policy_out, critic_in, in_first, in_second, critic_norms, norm_first, norm_second, critic_head, head_first, head_second, critic_hidden, hidden_moment, left_stats, right_stats, target_in, target_norms, target_head, target_hidden):
    weights = (critic_in, critic_hidden, critic_norms, critic_head)
    targets_all = (target_in, target_hidden, target_norms, target_head)
    policy_all = (policy_in.astype(jnp.float32), policy_mid.astype(jnp.float32), policy_out.astype(jnp.float32))
    validity = (done_flags != 2).astype(jnp.float32)
    valid_total = jnp.sum(validity)
    block_rows = ROWS_DEV * 4

    def one_block(carry, index):
        start = (index * block_rows).astype(jnp.int32)

        def cut(array):
            return lax.dynamic_slice_in_dim(array, start, block_rows, 0)
        goal = td_target(cut(next_state).astype(jnp.float32), cut(reward), cut(done_flags), cut(noise_index), noise_table, cut(subsets), policy_all, targets_all)
        inputs = cut(state_action).astype(jnp.float32)
        mask_rows = cut(validity)

        def block_loss(params):
            q_values = critic(inputs, params[0], params[1], params[2], params[3], low_back)
            errors = q_values - goal[:, None]
            return jnp.sum(mask_rows[:, None] * errors * errors)
        total, pullback = jax.vjp(jax.checkpoint(block_loss), weights)
        grads = pullback(jnp.ones((), jnp.float32) / valid_total)[0]
        summed = jax.tree.map(jnp.add, carry[1], grads)
        return ((carry[0] + total, summed), None)
    zeros = jax.tree.map(jnp.zeros_like, weights)
    (loss_total, grads), unused = lax.scan(one_block, (jnp.zeros((), jnp.float32), zeros), jnp.arange(ROWS // block_rows).astype(jnp.int32))
    in_moment, in_square, in_updated = adamw(grads[0], in_first, in_second, critic_in, RATE_INPUT)
    norm_moment, norm_square, norm_updated = adamw(grads[2], norm_first, norm_second, critic_norms, RATE_NORMS)
    head_moment, head_square, head_updated = adamw(grads[3], head_first, head_second, critic_head, RATE_HEAD)
    hidden_momentum, left_renewed, right_renewed, hidden_updated = shampoo(grads[1], hidden_moment, left_stats, right_stats, critic_hidden)
    return (loss_total, valid_total, in_moment, in_square, in_updated, norm_moment, norm_square, norm_updated, head_moment, head_square, head_updated, hidden_momentum, left_renewed, right_renewed, hidden_updated)
```

```python
import functools
import math

import jax
import jax.numpy as jnp
from jax import lax
from jax.experimental import pallas as pl
from jax.experimental.pallas import tpu as pltpu
from jax.sharding import PartitionSpec as P

ACT = 6
OBS = 17
IN = 23
H = 1024
CRIT = 10
BLK = 32
NEWTON = 5
STEP = 10
REWARD_DISCOUNT = 0.99
ENTROPY_TEMP = 0.2
FIRST_DECAY = 0.9
SECOND_DECAY = 0.999
WEIGHT_DECAY = 0.01
RATE_INPUT = 0.1
RATE_NORMS = 0.3
RATE_HEAD = 0.03
RATE_HIDDEN = 0.01
MOMENTUM = 0.9
STAT_DECAY = 0.95

F32, BF16, I32 = jnp.float32, jnp.bfloat16, jnp.int32
MESH = pl.DeviceIdType.MESH
LANES = 128
HALF = 64
TILE = 256
L_TGT = 23
L_BASE = 46
L_BOOT = 49
L_S0 = 50
L_S1 = 51
L_VALID = 52
L_CNT = 53
VMEM_LIMIT = 60 * 1024 * 1024


def nn(a, b):
    return jnp.dot(a, b, preferred_element_type=F32)


def nt(a, b):
    return lax.dot_general(a, b, (((1,), (1,)), ((), ())), preferred_element_type=F32)


def tn(a, b):
    return lax.dot_general(a, b, (((0,), (0,)), ((), ())), preferred_element_type=F32)


def iota(shape, dim):
    return lax.broadcasted_iota(I32, shape, dim)


def split2(x):
    high = x.astype(BF16)
    return high, (x - high.astype(F32)).astype(BF16)


def split3(x):
    high = x.astype(BF16)
    rest = x - high.astype(F32)
    mid = rest.astype(BF16)
    return high, mid, (rest - mid.astype(F32)).astype(BF16)


def swish(values):
    return values * jax.nn.sigmoid(values)


class Plan:
    def __init__(self, mesh):
        self.n_dp, self.n_mp = mesh.shape["dp"], mesh.shape["mp"]
        self.n = self.n_dp * self.n_mp
        self.groups = self.n // CRIT
        self.workers = self.groups * CRIT
        self.turns = -(-self.n // self.groups)

    def rank(self, dp, mp):
        size = 4 * self.n_dp
        layer = mp // 4
        inner = dp * 4 + (mp % 4 + 2 * (dp % 2)) % 4
        return layer * size + inner + (layer % 2) * (size - 1 - 2 * inner)

    def place(self, k):
        size = 4 * self.n_dp
        layer, inner = k // size, k % size
        inner = inner + (layer % 2) * (size - 1 - 2 * inner)
        dp = inner // 4
        return dp, layer * 4 + (inner % 4 + 2 * (dp % 2)) % 4

    def device(self, s):
        return s // self.n_mp, s % self.n_mp

    def pairs(self, rows):
        per = -(-rows // self.groups)
        return -(-per // 32) * 16

    def cap(self, rows):
        return -(-(self.n * -(-rows // self.groups)) // TILE) * TILE


def chunks_of(columns):
    width = math.gcd(math.gcd(columns, H), HALF)
    return width, columns // width, H // width


def assemble(chunks_ref, width, shift):
    groups = []
    lane = iota((32, LANES), 1)
    for g in range(H // LANES):
        block = jnp.zeros((32, LANES), F32)
        for i in range(LANES // width):
            chunk = chunks_ref[g * (LANES // width) + i]
            turn = (i * width - shift) % LANES
            moved = pltpu.roll(chunk, turn, 1) if turn else chunk
            block = jnp.where(lane // width == i, moved, block)
        groups.append(block)
    return jnp.concatenate(groups, 1)


def all_barrier(plan, dp, mp):
    barrier = pltpu.get_barrier_semaphore()

    def tell(s, _):
        sdp, smp = s // plan.n_mp, s % plan.n_mp

        @pl.when(jnp.logical_or(sdp != dp, smp != mp))
        def _():
            pl.semaphore_signal(barrier, inc=1, device_id=(sdp, smp), device_id_type=MESH)

        return 0

    lax.fori_loop(0, plan.n, tell, 0)
    pl.semaphore_wait(barrier, plan.n - 1)


def dispatch_kernel(
    plan,
    crit_ref,
    targ_ref,
    crit_small,
    targ_small,
    sa_ref,
    ns_ref,
    rows_ref,
    subs_ref,
    table_ref,
    pin_ref,
    pmid_ref,
    pout_ref,
    wt_ref,
    wc_ref,
    x_ref,
    p_ref,
    low,
    msg,
    wide,
    chunk,
    send_w,
    recv_w,
    pass_w,
    send_x,
    recv_x,
    send_p,
    recv_p,
):
    dp, mp = lax.axis_index("dp"), lax.axis_index("mp")
    me = plan.rank(dp, mp)
    index = dp * plan.n_mp + mp
    groups, workers = plan.groups, plan.workers
    critic, group = me // groups, me % groups
    rw, cw = crit_ref.shape[1], crit_ref.shape[2]
    rows = sa_ref.shape[0]
    columns = crit_small[0].shape[1]
    width, mine, per = chunks_of(columns)
    nets = (wt_ref, wc_ref)

    def to_low(c, _):
        low[0, c] = targ_ref[c].astype(BF16)
        low[1, c] = crit_ref[c].astype(BF16)
        return 0

    lax.fori_loop(0, CRIT, to_low, 0)
    all_barrier(plan, dp, mp)

    def w_slot(t, s):
        sdp, smp = plan.device(s)
        return nets[t].at[pl.ds(pl.multiple_of(smp * rw, rw), rw), pl.ds(pl.multiple_of(sdp * cw, cw), cw)]

    def to_worker(src, dst, send, recv, k):
        return pltpu.make_async_remote_copy(
            src_ref=src, dst_ref=dst, send_sem=send, recv_sem=recv, device_id=plan.place(k), device_id_type=MESH
        )

    def first_hop(t, c):
        k = c * groups + index % groups
        return k, to_worker(low.at[t, c], w_slot(t, index), send_w.at[t, c], recv_w.at[t, index], k)

    def send_weights(t):
        def one(i, _):
            c = (critic + i) % CRIT
            k, copy = first_hop(t, c)

            @pl.when(k == me)
            def _():
                pltpu.make_async_copy(low.at[t, c], w_slot(t, index), recv_w.at[t, index]).start()

            @pl.when(k != me)
            def _():
                copy.start()

            return 0

        lax.fori_loop(0, CRIT, one, 0)

    send_weights(0)
    send_weights(1)

    wide[...] = jnp.zeros_like(wide)
    for t, parts in enumerate((targ_small, crit_small)):
        wide[t, 0:IN, 0:columns] = parts[0][...]
        wide[t, IN : IN + 4, 0:columns] = parts[1][...]
        wide[t, IN + 4 : IN + 5, 0:columns] = parts[2][...]
    for j in range(mine):
        start, offset = j * width // LANES * LANES, j * width % LANES
        both = [wide[t, :, start : start + LANES] for t in range(2)]
        turned = [pltpu.roll(v, turn, 1) if turn else v for v, turn in zip(both, ((-offset) % LANES, (HALF - offset) % LANES))]
        chunk[j] = jnp.where(iota((32, LANES), 1) < HALF, turned[0], turned[1])

    def small_hop(j, r):
        g = index * mine + j
        k = (g // per) * groups + r
        return k, to_worker(chunk.at[j], p_ref.at[g % per], send_p.at[j, r], recv_p.at[g % per], k)

    def send_small(i, _):
        j, r = i // groups, i % groups
        k, copy = small_hop(j, r)

        @pl.when(k == me)
        def _():
            slot = (index * mine + j) % per
            pltpu.make_async_copy(chunk.at[j], p_ref.at[slot], recv_p.at[slot]).start()

        @pl.when(k != me)
        def _():
            copy.start()

        return 0

    lax.fori_loop(0, mine * groups, send_small, 0)

    lane = iota((rows, LANES), 1)
    place = lambda height, offset: (iota((height, LANES), 1) == iota((height, LANES), 0) + offset).astype(F32).astype(BF16)
    hidden = swish(nn(ns_ref[...], pin_ref[...])).astype(BF16)
    hidden = swish(nn(hidden, pmid_ref[...])).astype(BF16)
    pout = pout_ref[...]
    spread = lambda offset: nn(
        pout, (iota((2 * ACT, LANES), 0) == iota((2 * ACT, LANES), 1) + offset).astype(F32).astype(BF16)
    ).astype(BF16)
    keep = lane < ACT
    means = nn(hidden, spread(0))
    raw = nn(hidden, spread(ACT))
    facts = rows_ref[...]
    across = jnp.transpose(facts)
    picked = (iota((rows, table_ref.shape[0]), 1) == across[:, 2:3].astype(I32)).astype(F32).astype(BF16)
    noise = jnp.zeros((rows, LANES), F32)
    for part in split3(table_ref[...]):
        noise = noise + nn(picked, nn(part, place(ACT, 0)).astype(BF16))
    log_std = -5.0 + 3.5 * (jnp.tanh(raw) + 1.0)
    squashed = means + jnp.exp(log_std) * noise
    action = jnp.tanh(squashed).astype(BF16)
    twice = -2.0 * squashed
    softplus = jnp.maximum(twice, 0.0) + jnp.log(1.0 + jnp.exp(-jnp.abs(twice)))
    correction = 2.0 * (math.log(2.0) - squashed - softplus)
    density = jnp.sum(
        jnp.where(keep, -0.5 * noise * noise - log_std - 0.5 * math.log(2.0 * math.pi) - correction, 0.0), -1, keepdims=True
    )
    done = across[:, 1:2]
    boot = (done == 0.0).astype(F32)
    base = across[:, 0:1] - (REWARD_DISCOUNT * ENTROPY_TEMP) * boot * density
    high, mid, rest = split3(base)
    subs = subs_ref[...].astype(F32)
    on = lambda k, value: jnp.where(lane == k, value, 0.0)
    features = (
        nn(sa_ref[...], place(IN, 0))
        + nn(ns_ref[...], place(OBS, L_TGT))
        + nn(jnp.where(keep, action.astype(F32), 0.0).astype(BF16), place(LANES, L_TGT + OBS))
        + on(L_BASE, high.astype(F32))
        + on(L_BASE + 1, mid.astype(F32))
        + on(L_BASE + 2, rest.astype(F32))
        + on(L_BOOT, boot)
        + on(L_S0, subs[:, 0:1])
        + on(L_S1, subs[:, 1:2])
        + on(L_VALID, 1.0)
    ).astype(BF16)

    pairs = msg.shape[1]
    valid = (facts[1:2, :] != 2.0).astype(F32)
    before = (iota((rows, rows), 0) < iota((rows, rows), 1)).astype(F32).astype(BF16)
    order = nn(jnp.broadcast_to(valid, (8, rows)).astype(BF16), before)[0:1, :]
    order = jnp.where(valid > 0.0, order, -1.0)
    count = jnp.sum(valid, -1, keepdims=True)
    count_half = jnp.floor(count * 0.5)
    mlane = iota((pairs, LANES), 1)
    tail = jnp.where(mlane == L_CNT, count_half, 0.0) + jnp.where(mlane == L_CNT + 1, count - 2.0 * count_half, 0.0)

    def deal(r, _):
        slot = iota((pairs, rows), 0) * (2 * groups) + r
        halves = []
        for h in range(2):
            hot = (order == (slot + h * groups).astype(F32)).astype(F32).astype(BF16)
            halves.append(nn(hot, features))
        msg[r] = (halves[0] + pltpu.roll(halves[1], HALF, 1) + tail).astype(BF16)
        return 0

    lax.fori_loop(0, groups, deal, 0)

    def row_hop(k):
        return to_worker(msg.at[k % groups], x_ref.at[index], send_x.at[k], recv_x.at[index], k)

    def send_rows(i, _):
        k = (me + i) % workers

        @pl.when(k == me)
        def _():
            pltpu.make_async_copy(msg.at[group], x_ref.at[index], recv_x.at[index]).start()

        @pl.when(k != me)
        def _():
            row_hop(k).start()

        return 0

    lax.fori_loop(0, workers, send_rows, 0)

    def pass_on(t, turn, i):
        s = group + groups * turn
        k = critic * groups + (group + 1 + i) % groups
        return to_worker(w_slot(t, s), w_slot(t, s), pass_w.at[t, turn, i], recv_w.at[t, s], k)

    def arrived_w(t, s):
        pltpu.make_async_copy(low.at[t, 0], w_slot(t, s), recv_w.at[t, s]).wait()

    turns = (plan.n - group + groups - 1) // groups

    @pl.when(me < workers)
    def _():
        for t in range(2):

            def relay(turn, _):
                arrived_w(t, group + groups * turn)

                def one(i, _):
                    pass_on(t, turn, i).start()
                    return 0

                lax.fori_loop(0, groups - 1, one, 0)
                return 0

            lax.fori_loop(0, turns, relay, 0)

        def arrived(s, _):
            @pl.when(s % groups != group)
            def _():
                arrived_w(0, s)
                arrived_w(1, s)

            pltpu.make_async_copy(msg.at[0], x_ref.at[s], recv_x.at[s]).wait()
            return 0

        lax.fori_loop(0, plan.n, arrived, 0)

        def arrived_small(j, _):
            pltpu.make_async_copy(chunk.at[0], p_ref.at[j], recv_p.at[j]).wait()
            return 0

        lax.fori_loop(0, per, arrived_small, 0)
        for t in range(2):

            def passed(turn, _):
                def one(i, _):
                    pass_on(t, turn, i).wait_send()
                    return 0

                lax.fori_loop(0, groups - 1, one, 0)
                return 0

            lax.fori_loop(0, turns, passed, 0)

    def sent_weights(c, _):
        for t in range(2):
            k, copy = first_hop(t, c)

            @pl.when(k != me)
            def _():
                copy.wait_send()

        return 0

    lax.fori_loop(0, CRIT, sent_weights, 0)

    def sent_small(i, _):
        k, copy = small_hop(i // groups, i % groups)

        @pl.when(k != me)
        def _():
            copy.wait_send()

        return 0

    lax.fori_loop(0, mine * groups, sent_small, 0)

    def sent_rows(k, _):
        @pl.when(k != me)
        def _():
            row_hop(k).wait_send()

        return 0

    lax.fori_loop(0, workers, sent_rows, 0)


def dispatch(plan, critic_hidden, target_hidden, critic_small, target_small, rows_args, policy):
    rows = rows_args[0].shape[0]
    pairs = plan.pairs(rows)
    columns = critic_small[0].shape[1]
    _width, mine, per = chunks_of(columns)
    vmem = pl.BlockSpec(memory_space=pltpu.VMEM)
    anywhere = pl.BlockSpec(memory_space=pl.ANY)
    dma = pltpu.SemaphoreType.DMA
    return pl.pallas_call(
        functools.partial(dispatch_kernel, plan),
        out_shape=(
            jax.ShapeDtypeStruct((H, H), BF16),
            jax.ShapeDtypeStruct((H, H), BF16),
            jax.ShapeDtypeStruct((plan.n, pairs, LANES), BF16),
            jax.ShapeDtypeStruct((per, 32, LANES), F32),
        ),
        in_specs=[vmem, vmem, (vmem,) * 3, (vmem,) * 3] + [vmem] * 8,
        out_specs=(anywhere,) * 4,
        scratch_shapes=[
            pltpu.VMEM((2,) + critic_hidden.shape, BF16),
            pltpu.VMEM((plan.groups, pairs, LANES), BF16),
            pltpu.VMEM((2, 32, -(-columns // LANES) * LANES), F32),
            pltpu.VMEM((mine, 32, LANES), F32),
            dma((2, CRIT)),
            dma((2, plan.n)),
            dma((2, plan.turns, plan.groups - 1)),
            dma((plan.workers,)),
            dma((plan.n,)),
            dma((mine, plan.groups)),
            dma((per,)),
        ],
        compiler_params=pltpu.CompilerParams(collective_id=0, has_side_effects=True, vmem_limit_bytes=VMEM_LIMIT),
        name="dispatch",
    )(critic_hidden, target_hidden, critic_small, target_small, *rows_args, *policy)


def norm_parts(pre):
    centered = pre - jnp.sum(pre, -1, keepdims=True) * (1.0 / H)
    inv = lax.rsqrt(jnp.sum(centered * centered, -1, keepdims=True) * (1.0 / H) + 1e-05)
    return centered * inv, inv


def swish_parts(half):
    t = jnp.tanh(half)
    product = half * t
    return half + product, (1.0 + t) * (1.0 + (half - product))


def low_input(params):
    return jnp.where(iota((32, H), 0) < IN, params, 0.0).astype(BF16)


def tile_span(t):
    return pl.ds(pl.multiple_of(t * TILE, TILE), TILE)


def target_kernel(
    plan, width, role_ref, x_ref, w_ref, p_ref, xc_ref, q_ref, info_ref, rows_f, picked, value, hot, win, par, cnt_v, cnt_s, base_s, sem
):
    critic, group, active = role_ref[0], role_ref[1], role_ref[2]
    groups, n = plan.groups, plan.n
    pairs = x_ref.shape[1]
    first = x_ref[:, 0, :].astype(F32)
    lane = iota(first.shape, 1)
    counts = 2.0 * jnp.sum(jnp.where(lane == L_CNT, first, 0.0), -1, keepdims=True) + jnp.sum(
        jnp.where(lane == L_CNT + 1, first, 0.0), -1, keepdims=True
    )
    counts = jnp.where(active > 0, jnp.broadcast_to(counts, first.shape), 0.0)
    mine = jnp.floor((counts + (groups - 1 - group).astype(F32)) * (1.0 / groups) + 0.5 / groups)
    earlier = (iota((n, n), 1) < iota((n, n), 0)).astype(F32).astype(BF16)
    starts = nn(earlier, mine.astype(BF16))
    total = jnp.sum(counts, 0, keepdims=True)
    cnt_v[0:n, :] = mine.astype(I32)
    cnt_v[n : 2 * n, :] = starts.astype(I32)
    cnt_v[2 * n : 2 * n + 8, :] = jnp.broadcast_to(total, (8, LANES)).astype(I32)
    copy = pltpu.make_async_copy(cnt_v, cnt_s, sem)
    copy.start()
    par[...] = assemble(p_ref, width, 0)
    win[...] = jnp.zeros_like(win)
    win[0:32, :] = low_input(par[...])
    copy.wait()
    number = cnt_s[n - 1, 0] + cnt_s[2 * n - 1, 0]
    tiles = (number + TILE - 1) // TILE
    info_ref[0] = number
    info_ref[1] = cnt_s[2 * n, 0]

    def compact(s, _):
        block = x_ref[s].astype(F32)
        have, start = cnt_s[s, 0], cnt_s[n + s, 0]
        rows_f[pl.ds(start, pairs), :] = block
        rows_f[pl.ds(start + (have + 1) // 2, pairs), :] = pltpu.roll(block, HALF, 1)
        return 0

    @pl.when(active > 0)
    def _():
        lax.fori_loop(0, n, compact, 0)

    rows_f[pl.ds(number, TILE), :] = jnp.zeros((TILE, LANES), F32)

    until = (iota((TILE, TILE), 1) < iota((TILE, TILE), 0)).astype(F32).astype(BF16)
    place = iota((TILE, TILE), 1).astype(F32)
    this = critic.astype(F32)

    def choose(t, base):
        wide = rows_f[tile_span(t), :]
        x = wide.astype(BF16)
        xc_ref[tile_span(t), :] = x
        wanted = jnp.logical_or(wide[:, L_S0 : L_S0 + 1] == this, wide[:, L_S1 : L_S1 + 1] == this)
        wanted = jnp.where(jnp.logical_and(wanted, wide[:, L_BOOT : L_BOOT + 1] > 0.0), 1.0, 0.0)
        order = nn(until, jnp.broadcast_to(wanted, (TILE, LANES)).astype(BF16))[:, 0:1]
        chosen = (jnp.where(wanted > 0.0, order, -1.0) == place).astype(F32).astype(BF16)
        hot[t] = chosen
        picked[pl.ds(base, TILE), :] = tn(chosen, x)
        base_s[t] = base
        return base + jnp.sum(wanted).astype(I32)

    chosen_rows = lax.fori_loop(0, tiles, choose, 0)
    picked[pl.ds(chosen_rows, TILE), :] = jnp.zeros((TILE, LANES), F32)
    chosen_tiles = (chosen_rows + TILE - 1) // TILE
    half = jnp.where(iota((32, 1), 0) < IN + 4, 0.5, 1.0)
    par[...] = par[...] * half
    gain1, shift1, gain2, shift2, head = (par[IN + k : IN + k + 1, :] for k in range(5))

    def tile(t, _):
        x = pltpu.roll(picked[tile_span(t), :], LANES - L_TGT, 1).astype(BF16)
        z, _unused = norm_parts(nn(x, win[...]))
        y = z * gain1 + shift1
        act = (y + y * jnp.tanh(y)).astype(BF16)
        z, _unused = norm_parts(nn(act, w_ref[...]))
        y = z * gain2 + shift2
        q = jnp.sum((y + y * jnp.tanh(y)) * head, -1, keepdims=True)
        value[tile_span(t), :] = jnp.broadcast_to(q, (TILE, LANES))
        return 0

    lax.fori_loop(0, chosen_tiles, tile, 0)
    value[tile_span(chosen_tiles), :] = jnp.zeros((TILE, LANES), F32)

    def spread(t, _):
        lane = iota((TILE, LANES), 1)
        high, mid, rest = (v.astype(F32) for v in split3(value[pl.ds(base_s[t], TILE), :]))
        parts = jnp.where(lane == 0, high, jnp.where(lane == 1, mid, jnp.where(lane == 2, rest, 0.0)))
        q = jnp.broadcast_to(jnp.sum(nn(hot[t], parts.astype(BF16)), -1, keepdims=True), (TILE, LANES))
        for h in range(TILE // LANES):
            flat = jnp.transpose(q[h * LANES : (h + 1) * LANES, :])
            q_ref[pl.ds(t * (TILE // LANES) + h, 1), :] = flat[0:1, :]
        return 0

    lax.fori_loop(0, tiles, spread, 0)


def target_values(plan, rows, width, role, x, weights, params):
    capacity = plan.cap(rows)
    vmem = pl.BlockSpec(memory_space=pltpu.VMEM)
    smem = pl.BlockSpec(memory_space=pltpu.SMEM)
    return pl.pallas_call(
        functools.partial(target_kernel, plan, width),
        out_shape=(
            jax.ShapeDtypeStruct((capacity, LANES), BF16),
            jax.ShapeDtypeStruct((capacity // LANES, LANES), F32),
            jax.ShapeDtypeStruct((2,), I32),
        ),
        in_specs=[smem, vmem, vmem, vmem],
        out_specs=(vmem, vmem, smem),
        scratch_shapes=[
            pltpu.VMEM((capacity + TILE + x.shape[1], LANES), F32),
            pltpu.VMEM((capacity + TILE, LANES), F32),
            pltpu.VMEM((capacity + TILE, LANES), F32),
            pltpu.VMEM((capacity // TILE, TILE, TILE), BF16),
            pltpu.VMEM((LANES, H), BF16),
            pltpu.VMEM((32, H), F32),
            pltpu.VMEM((2 * plan.n + 8, LANES), I32),
            pltpu.SMEM((2 * plan.n + 8, LANES), I32),
            pltpu.SMEM((capacity // TILE,), I32),
            pltpu.SemaphoreType.DMA,
        ],
        compiler_params=pltpu.CompilerParams(vmem_limit_bytes=VMEM_LIMIT),
        name="target_values",
    )(role, x, weights, params)


def share_kernel(plan, q_ref, all_ref, send, recv):
    dp, mp = lax.axis_index("dp"), lax.axis_index("mp")
    me = plan.rank(dp, mp)
    groups = plan.groups
    critic, group = me // groups, me % groups
    barrier = pltpu.get_barrier_semaphore()

    @pl.when(me < plan.workers)
    def _():
        def peer(i):
            other = (critic + i) % CRIT
            return other, plan.place(other * groups + group)

        def tell(i, _):
            pl.semaphore_signal(barrier, inc=1, device_id=peer(i)[1], device_id_type=MESH)
            return 0

        lax.fori_loop(1, CRIT, tell, 0)
        pl.semaphore_wait(barrier, CRIT - 1)
        all_ref[critic] = q_ref[...]

        def copy(i):
            other, device = peer(i)
            return pltpu.make_async_remote_copy(
                src_ref=q_ref,
                dst_ref=all_ref.at[critic],
                send_sem=send.at[other],
                recv_sem=recv.at[critic],
                device_id=device,
                device_id_type=MESH,
            )

        def start(i, _):
            copy(i).start()
            return 0

        lax.fori_loop(1, CRIT, start, 0)

        def finish(i, _):
            copy(i).wait_send()
            other = peer(i)[0]
            pltpu.make_async_copy(q_ref, all_ref.at[other], recv.at[other]).wait()
            return 0

        lax.fori_loop(1, CRIT, finish, 0)


def share_values(plan, q):
    vmem = pl.BlockSpec(memory_space=pltpu.VMEM)
    return pl.pallas_call(
        functools.partial(share_kernel, plan),
        out_shape=jax.ShapeDtypeStruct((CRIT,) + q.shape, F32),
        in_specs=[vmem],
        out_specs=vmem,
        scratch_shapes=[pltpu.SemaphoreType.DMA((CRIT,)), pltpu.SemaphoreType.DMA((CRIT,))],
        compiler_params=pltpu.CompilerParams(collective_id=1, has_side_effects=True, vmem_limit_bytes=VMEM_LIMIT),
        name="share_values",
    )(q)


def critic_kernel(
    plan, width, info_ref, xc_ref, q_ref, w_ref, p_ref, grad_ref, small_ref, sums_ref, z_one, slope, act, low, fact, par, win, picks, acc
):
    number = info_ref[0]
    scale = 2.0 / jnp.maximum(info_ref[1], 1).astype(F32)
    tiles = (number + TILE - 1) // TILE
    par[...] = assemble(p_ref, width, HALF)
    win[...] = jnp.zeros_like(win)
    win[0:32, :] = low_input(par[...])
    grad_ref[...] = jnp.zeros_like(grad_ref)
    acc[...] = jnp.zeros_like(acc)
    picks[...] = jnp.zeros_like(picks)
    sums_ref[...] = jnp.zeros_like(sums_ref)
    gain1, shift1, gain2, shift2, head = (par[IN + k : IN + k + 1, :] for k in range(5))

    def fold(k, value):
        acc[32 + k * 8 : 40 + k * 8, :] += jnp.sum(value.reshape(TILE // 8, 8, H), 0)

    def tile(t, _):
        x = xc_ref[tile_span(t), :]
        wide = x.astype(F32)
        for h in range(TILE // LANES):
            picks[0:CRIT, :] = q_ref[:, pl.ds(t * (TILE // LANES) + h, 1), :].reshape(CRIT, LANES)
            table = jnp.transpose(picks[...])
            part = wide[h * LANES : (h + 1) * LANES, :]
            critic = iota(table.shape, 1).astype(F32)
            one = jnp.sum(jnp.where(critic == part[:, L_S0 : L_S0 + 1], table, 0.0), -1, keepdims=True)
            two = jnp.sum(jnp.where(critic == part[:, L_S1 : L_S1 + 1], table, 0.0), -1, keepdims=True)
            base = part[:, L_BASE : L_BASE + 1] + part[:, L_BASE + 1 : L_BASE + 2] + part[:, L_BASE + 2 : L_BASE + 3]
            goal = base + jnp.where(part[:, L_BOOT : L_BOOT + 1] > 0.0, REWARD_DISCOUNT * jnp.minimum(one, two), 0.0)
            fact[h * LANES : (h + 1) * LANES, 0:1] = goal
        z, inv_one = norm_parts(nn(x, win[...]))
        z_one[...] = z
        value, twice = swish_parts(z * (0.5 * gain1) + 0.5 * shift1)
        slope[...] = 0.5 * twice
        act[...] = value.astype(BF16)
        z, inv = norm_parts(nn(act[...], w_ref[...]))
        value, twice = swish_parts(z * (0.5 * gain2) + 0.5 * shift2)
        q = jnp.sum(value * head, -1, keepdims=True)
        error = (q - fact[:, 0:1]) * wide[:, L_VALID : L_VALID + 1]
        sums_ref[0:1, :] += jnp.broadcast_to(jnp.sum(error * error, 0, keepdims=True), (1, LANES))
        dq = error * scale
        fold(4, dq * value)
        dy = dq * (twice * (0.5 * head))
        fold(3, dy)
        fold(2, dy * z)
        dz = dy * gain2
        mean = jnp.sum(dz, -1, keepdims=True) * (1.0 / H)
        along = jnp.sum(dz * z, -1, keepdims=True) * (1.0 / H)
        low[...] = (inv * (dz - mean - z * along)).astype(BF16)
        down = nt(low[...], w_ref[...])
        grad_ref[...] += tn(act[...], low[...])
        z = z_one[...]
        dy = down * slope[...]
        fold(1, dy)
        fold(0, dy * z)
        dz = dy * gain1
        mean = jnp.sum(dz, -1, keepdims=True) * (1.0 / H)
        along = jnp.sum(dz * z, -1, keepdims=True) * (1.0 / H)
        acc[0:32, :] += tn(x[:, 0:32], (inv_one * (dz - mean - z * along)).astype(BF16))
        return 0

    lax.fori_loop(0, tiles, tile, 0)
    sums_ref[1:2, :] = jnp.broadcast_to(info_ref[1].astype(F32), (1, LANES))
    for k in range(5):
        acc[IN + k : IN + k + 1, :] = jnp.sum(acc[32 + k * 8 : 40 + k * 8, :], 0, keepdims=True)
    for i in range(H // width):
        start, offset = i * width // LANES * LANES, i * width % LANES
        block = acc[0:32, start : start + LANES]
        small_ref[i] = pltpu.roll(block, LANES - offset, 1) if offset else block


def critic_step(plan, width, info, xc, q_all, weights, params):
    vmem = pl.BlockSpec(memory_space=pltpu.VMEM)
    smem = pl.BlockSpec(memory_space=pltpu.SMEM)
    return pl.pallas_call(
        functools.partial(critic_kernel, plan, width),
        out_shape=(
            jax.ShapeDtypeStruct((H, H), F32),
            jax.ShapeDtypeStruct((H // width, 32, LANES), F32),
            jax.ShapeDtypeStruct((8, LANES), F32),
        ),
        in_specs=[smem] + [vmem] * 4,
        out_specs=(vmem,) * 3,
        scratch_shapes=[
            pltpu.VMEM((TILE, H), F32),
            pltpu.VMEM((TILE, H), F32),
            pltpu.VMEM((TILE, H), BF16),
            pltpu.VMEM((TILE, H), BF16),
            pltpu.VMEM((TILE, LANES), F32),
            pltpu.VMEM((32, H), F32),
            pltpu.VMEM((LANES, H), BF16),
            pltpu.VMEM((16, LANES), F32),
            pltpu.VMEM((72, H), F32),
        ],
        compiler_params=pltpu.CompilerParams(vmem_limit_bytes=VMEM_LIMIT),
        name="critic_step",
    )(info, xc, q_all, weights, params)


PRECISE = 2


LAG = 2


def shampoo_kernel(
    plan,
    g_ref,
    small_ref,
    sums_ref,
    mom_ref,
    left_ref,
    right_ref,
    w_ref,
    mo_ref,
    lo_ref,
    ro_ref,
    wo_ref,
    own_ref,
    out_ref,
    parts,
    pieces,
    given,
    shares,
    totals,
    send_one,
    recv_one,
    send_two,
    recv_two,
    send_s,
    recv_s,
    send_t,
    recv_t,
):
    dp, mp = lax.axis_index("dp"), lax.axis_index("mp")
    me = plan.rank(dp, mp)
    index = dp * plan.n_mp + mp
    groups, workers, n, turns = plan.groups, plan.workers, plan.n, plan.turns
    critic, group = me // groups, me % groups
    rw, cw = mom_ref.shape[1], mom_ref.shape[2]
    mine, per = shares.shape[1], small_ref.shape[0]
    columns = own_ref.shape[1]
    chunk_width = H // per
    all_barrier(plan, dp, mp)

    def to_device(src, dst, send, recv, device):
        return pltpu.make_async_remote_copy(
            src_ref=src, dst_ref=dst, send_sem=send, recv_sem=recv, device_id=device, device_id_type=MESH
        )

    def block(s):
        sdp, smp = plan.device(s)
        return pl.ds(pl.multiple_of(smp * rw, rw), rw), pl.ds(pl.multiple_of(sdp * cw, cw), cw)

    def turn_of(step):
        return (step + critic) % turns

    def first_hop(step, i):
        other = (group + 1 + i) % groups
        turn = turn_of(step)
        s = other + groups * turn
        copy = to_device(
            g_ref.at[block(s)],
            parts.at[groups - 2 - i, turn],
            send_one.at[step, i],
            recv_one.at[groups - 2 - i, turn],
            plan.place(critic * groups + other),
        )
        return s, copy

    def second_hop(turn):
        s = group + groups * turn
        return s, to_device(pieces.at[turn], given.at[critic], send_two.at[turn], recv_two.at[critic], plan.device(s))

    def small_hop(q):
        g = critic * per + q
        s = g // mine
        return s, to_device(
            small_ref.at[q], shares.at[group, g % mine], send_s.at[q], recv_s.at[group, g % mine], plan.device(s)
        )

    def total_hop(s):
        return to_device(sums_ref, totals.at[me], send_t.at[s], recv_t.at[me], plan.device(s))

    @pl.when(me < workers)
    def _():
        def start(step, _):
            def one(i, _):
                s, copy = first_hop(step, i)

                @pl.when(s < n)
                def _():
                    copy.start()

                return 0

            lax.fori_loop(0, groups - 1, one, 0)
            return 0

        lax.fori_loop(0, turns, start, 0)

        def start_small(q, _):
            s, copy = small_hop(q)

            @pl.when(s == index)
            def _():
                slot = (critic * per + q) % mine
                pltpu.make_async_copy(small_ref.at[q], shares.at[group, slot], recv_s.at[group, slot]).start()

            @pl.when(s != index)
            def _():
                copy.start()

            return 0

        lax.fori_loop(0, per, start_small, 0)
        totals[me] = sums_ref[...]

        def start_total(i, _):
            total_hop((index + i) % n).start()
            return 0

        lax.fori_loop(1, n, start_total, 0)

    def add_up(step):
        turn = turn_of(step)
        s, copy = second_hop(turn)

        @pl.when(s < n)
        def _():
            for i in range(groups - 1):
                pltpu.make_async_copy(pieces.at[0], parts.at[i, turn], recv_one.at[i, turn]).wait()
            value = g_ref[block(s)]
            for i in range(groups - 1):
                value = value + parts[i, turn]
            pieces[turn] = value

            @pl.when(s == index)
            def _():
                pltpu.make_async_copy(pieces.at[turn], given.at[critic], recv_two.at[critic]).start()

            @pl.when(s != index)
            def _():
                copy.start()

    width = min(256, cw)
    many = width // BLK
    nr, nc = rw // BLK, cw // width
    subs = [(i, j) for i in range(nr) for j in range(nc)]
    mask = (iota((width, width), 0) // BLK == iota((width, width), 1) // BLK).astype(F32).astype(BF16)
    eye = (iota((BLK, width), 0) == iota((BLK, width), 1) % BLK).astype(F32)
    eye_low = eye.astype(BF16)

    def diag(x):
        return jnp.concatenate([x] * many, 0) * mask

    def precise(a, b):
        ah, al = split2(a)
        bh, bl = split2(b)
        both = nn(jnp.concatenate([ah, al], 0), diag(bh))
        return both[:BLK] + both[BLK:] + nn(ah, diag(bl))

    def block_sums(s):
        high, rest = split2(s)
        return nn(high, mask) + nn(rest, mask)

    def place(c, i, j):
        return (c, slice(i * BLK, (i + 1) * BLK), slice(j * width, (j + 1) * width))

    def blocked(i):
        c = (index // groups + 2 * CRIT - i) % CRIT
        pltpu.make_async_copy(pieces.at[0], given.at[c], recv_two.at[c]).wait()
        sums = []
        for i, j in subs:
            at = place(c, i, j)
            grad = given[at]
            mo_ref[at] = MOMENTUM * mom_ref[at] + grad
            low = grad.astype(BF16)
            wide = diag(low)
            left = STAT_DECAY * left_ref[at] + (1.0 - STAT_DECAY) * nt(low, wide)
            flip = nt(eye_low, wide).astype(BF16)
            right = STAT_DECAY * right_ref[at] + (1.0 - STAT_DECAY) * nn(flip, wide)
            lo_ref[at] = left
            ro_ref[at] = right
            for stat in (left, right):
                sums.append(jnp.sum((stat * stat).reshape(BLK // 8, 8, width), 0))
        total = block_sums(jnp.concatenate(sums, 0))
        chains = []
        for k, (i, j) in enumerate(subs):
            for side, ref in enumerate((lo_ref, ro_ref)):
                spot = (2 * k + side) * 8
                inv = lax.rsqrt(jnp.sum(total[spot : spot + 8], 0, keepdims=True))
                rest = (eye - ref[place(c, i, j)] * inv) * 0.25
                chains.append([rest, eye + rest, jnp.sqrt(jnp.sqrt(inv))])
        for it in range(NEWTON - 1):
            full = it < PRECISE
            work = []
            for ch in chains:
                high, rest = split2(ch[0])
                wide = diag(high)
                wide_rest = diag(rest) if full else None
                lhs = [high] + ([rest] if full else []) + ([ch[1].astype(BF16)] if it > 0 else [])
                out = nn(jnp.concatenate(lhs, 0), wide)
                power = out[:BLK]
                if full:
                    power = power + out[BLK : 2 * BLK] + nn(high, wide_rest)
                if it > 0:
                    ch[1] = ch[1] + out[-BLK:]
                work.append([wide, wide_rest, power])
            for factor in (3.75, 5.0, 2.5):
                for ch, wk in zip(chains, work):
                    high, rest = split2(factor * ch[0] + wk[2])
                    if full:
                        out = nn(jnp.concatenate([high, rest], 0), wk[0])
                        wk[2] = out[:BLK] + out[BLK:] + nn(high, wk[1])
                    else:
                        wk[2] = nn(high, wk[0])
            for ch, wk in zip(chains, work):
                ch[0] = wk[2]
        for ch in chains:
            ch[1] = ch[1] + nn(ch[1].astype(BF16), diag(ch[0].astype(BF16)))
        for k, (i, j) in enumerate(subs):
            at = place(c, i, j)
            lc, rc = chains[2 * k], chains[2 * k + 1]
            step = precise(precise(lc[1], mo_ref[at]), rc[1]) * (lc[2] * rc[2])
            squares = block_sums(jnp.sum((step * step).reshape(BLK // 8, 8, width), 0))
            square = jnp.sum(squares, 0, keepdims=True) * (1.0 / (BLK * BLK))
            old = w_ref[at]
            wo_ref[at] = old - RATE_HIDDEN * (step * lax.rsqrt(square + 1e-06) + WEIGHT_DECAY * old)

    def round_(i, _):
        @pl.when(jnp.logical_and(me < workers, i < turns))
        def _():
            add_up(i)

        @pl.when(jnp.logical_and(i >= LAG, i < CRIT + LAG))
        def _():
            blocked(i - LAG)

        return 0

    lax.fori_loop(0, max(turns, CRIT + LAG), round_, 0)

    def arrived_small(i, _):
        pltpu.make_async_copy(small_ref.at[0], shares.at[i // mine, i % mine], recv_s.at[i // mine, i % mine]).wait()
        return 0

    lax.fori_loop(0, groups * mine, arrived_small, 0)
    for g in range(columns // LANES):
        part = jnp.zeros((32, LANES), F32)
        for j in range(mine):
            if j * chunk_width // LANES == g:
                value = shares[0, j]
                for r in range(1, groups):
                    value = value + shares[r, j]
                turn = j * chunk_width % LANES
                moved = pltpu.roll(value, turn, 1) if turn else value
                part = jnp.where(iota((32, LANES), 1) // chunk_width == turn // chunk_width, moved, part)
        own_ref[:, g * LANES : (g + 1) * LANES] = part

    def arrived_total(k, _):
        @pl.when(k != me)
        def _():
            pltpu.make_async_copy(sums_ref, totals.at[k], recv_t.at[k]).wait()

        return 0

    lax.fori_loop(0, workers, arrived_total, 0)
    out_ref[0:1, :] = jnp.sum(totals[:, 0, :], 0, keepdims=True)
    out_ref[1:2, :] = totals[0, 1:2, :]
    out_ref[2:8, :] = jnp.zeros((6, LANES), F32)

    @pl.when(me < workers)
    def _():
        def finish(step, _):
            def one(i, _):
                s, copy = first_hop(step, i)

                @pl.when(s < n)
                def _():
                    copy.wait_send()

                return 0

            lax.fori_loop(0, groups - 1, one, 0)
            s, copy = second_hop(step)

            @pl.when(jnp.logical_and(s < n, s != index))
            def _():
                copy.wait_send()

            return 0

        lax.fori_loop(0, turns, finish, 0)

        def finish_small(q, _):
            s, copy = small_hop(q)

            @pl.when(s != index)
            def _():
                copy.wait_send()

            return 0

        lax.fori_loop(0, per, finish_small, 0)

        def finish_total(i, _):
            total_hop((index + i) % n).wait_send()
            return 0

        lax.fori_loop(1, n, finish_total, 0)


def shampoo(plan, columns, grad, small, sums, moment, left, right, weight):
    vmem = pl.BlockSpec(memory_space=pltpu.VMEM)
    shape = jax.ShapeDtypeStruct(moment.shape, F32)
    _width, mine, per = chunks_of(columns)
    piece = moment.shape[1:]
    dma = pltpu.SemaphoreType.DMA
    return pl.pallas_call(
        functools.partial(shampoo_kernel, plan),
        out_shape=(shape,) * 4
        + (jax.ShapeDtypeStruct((32, -(-columns // LANES) * LANES), F32), jax.ShapeDtypeStruct((8, LANES), F32)),
        in_specs=[vmem] * 7,
        out_specs=(vmem,) * 6,
        scratch_shapes=[
            pltpu.VMEM((plan.groups - 1, plan.turns) + piece, F32),
            pltpu.VMEM((plan.turns,) + piece, F32),
            pltpu.VMEM((CRIT,) + piece, F32),
            pltpu.VMEM((plan.groups, mine, 32, LANES), F32),
            pltpu.VMEM((plan.workers, 8, LANES), F32),
            dma((plan.turns, plan.groups - 1)),
            dma((plan.groups - 1, plan.turns)),
            dma((plan.turns,)),
            dma((CRIT,)),
            dma((per,)),
            dma((plan.groups, mine)),
            dma((plan.n,)),
            dma((plan.workers,)),
        ],
        compiler_params=pltpu.CompilerParams(collective_id=2, has_side_effects=True, vmem_limit_bytes=VMEM_LIMIT),
        name="shampoo",
    )(grad, small, sums, moment, left, right, weight)


def adamw(grad, moment, square, weight, rate):
    moment_new = FIRST_DECAY * moment + (1.0 - FIRST_DECAY) * grad
    square_new = SECOND_DECAY * square + (1.0 - SECOND_DECAY) * grad * grad
    moment_hat = moment_new / (1.0 - FIRST_DECAY**STEP)
    square_hat = square_new / (1.0 - SECOND_DECAY**STEP)
    weight_new = weight - rate * (moment_hat / (jnp.sqrt(square_hat) + 1e-08) + WEIGHT_DECAY * weight)
    return (moment_new, square_new, weight_new)


def local(
    plan,
    state_action,
    next_state,
    reward,
    done_flags,
    noise_index,
    noise_table,
    subsets,
    policy_in,
    policy_mid,
    policy_out,
    critic_in,
    in_first,
    in_second,
    critic_norms,
    norm_first,
    norm_second,
    critic_head,
    head_first,
    head_second,
    critic_hidden,
    hidden_moment,
    left_stats,
    right_stats,
    target_in,
    target_norms,
    target_head,
    target_hidden,
):
    me = plan.rank(lax.axis_index("dp"), lax.axis_index("mp"))
    critic, group = me // plan.groups, me % plan.groups
    role = jnp.stack([critic, group, (me < plan.workers).astype(I32)])
    rows, columns = state_action.shape[0], critic_in.shape[1]
    width = chunks_of(columns)[0]
    facts = jnp.stack([reward, done_flags.astype(F32), noise_index.astype(F32)])
    facts = jnp.pad(facts, ((0, 5), (0, 0)))
    w_target, w_critic, x, params = dispatch(
        plan,
        critic_hidden,
        target_hidden,
        (critic_in, critic_norms, critic_head[None]),
        (target_in, target_norms, target_head[None]),
        (state_action, next_state, facts, subsets),
        (noise_table, policy_in, policy_mid, policy_out),
    )
    xc, q, info = target_values(plan, rows, width, role, x, w_target, params)
    q_all = share_values(plan, q)
    grad_hidden, grad_small, sums = critic_step(plan, width, info, xc, q_all, w_critic, params)
    hidden_momentum, left_renewed, right_renewed, hidden_updated, own, totals = shampoo(
        plan, columns, grad_hidden, grad_small, sums, hidden_moment, left_stats, right_stats, critic_hidden
    )
    own = own[:, :columns]
    loss_total, counted = totals[0, 0], totals[1, 0]
    in_moment, in_square, in_updated = adamw(own[:IN], in_first, in_second, critic_in, RATE_INPUT)
    norm_moment, norm_square, norm_updated = adamw(own[IN : IN + 4], norm_first, norm_second, critic_norms, RATE_NORMS)
    head_moment, head_square, head_updated = adamw(own[IN + 4], head_first, head_second, critic_head, RATE_HEAD)
    return (
        loss_total,
        counted,
        in_moment,
        in_square,
        in_updated,
        norm_moment,
        norm_square,
        norm_updated,
        head_moment,
        head_square,
        head_updated,
        hidden_momentum,
        left_renewed,
        right_renewed,
        hidden_updated,
    )


def solution(mesh):
    both = ("dp", "mp")
    rows, columns, flat, hidden = P(both, None), P(None, both), P(both), P(None, "mp", "dp")
    return jax.shard_map(
        functools.partial(local, Plan(mesh)),
        mesh=mesh,
        in_specs=(
            (rows, rows, flat, flat, flat, P(), rows, P(), P(), P())
            + (columns,) * 6
            + (flat,) * 3
            + (hidden,) * 4
            + (columns, columns, flat, hidden)
        ),
        out_specs=(P(), P()) + (columns,) * 6 + (flat,) * 3 + (hidden,) * 4,
        check_vma=False,
    )
```

```python
import functools
import math

import jax
import jax.numpy as jnp
from jax import lax
from jax.experimental import pallas as pl
from jax.experimental.pallas import tpu as pltpu
from jax.sharding import PartitionSpec as P

ACT = 6
OBS = 17
IN = 23
H = 1024
CRIT = 10
BLK = 32
NEWTON = 5
STEP = 10
REWARD_DISCOUNT = 0.99
ENTROPY_TEMP = 0.2
FIRST_DECAY = 0.9
SECOND_DECAY = 0.999
WEIGHT_DECAY = 0.01
RATE_INPUT = 0.1
RATE_NORMS = 0.3
RATE_HEAD = 0.03
RATE_HIDDEN = 0.01
MOMENTUM = 0.9
STAT_DECAY = 0.95

F32, BF16, I32 = jnp.float32, jnp.bfloat16, jnp.int32
MESH = pl.DeviceIdType.MESH
LANES = 128
HALF = 64
TILE = 256
L_TGT = 23
L_BASE = 46
L_BOOT = 49
L_S0 = 50
L_S1 = 51
L_VALID = 52
L_CNT = 53
VMEM_LIMIT = 60 * 1024 * 1024


def nn(a, b):
    return jnp.dot(a, b, preferred_element_type=F32)


def nt(a, b):
    return lax.dot_general(a, b, (((1,), (1,)), ((), ())), preferred_element_type=F32)


def tn(a, b):
    return lax.dot_general(a, b, (((0,), (0,)), ((), ())), preferred_element_type=F32)


def iota(shape, dim):
    return lax.broadcasted_iota(I32, shape, dim)


def split2(x):
    high = x.astype(BF16)
    return high, (x - high.astype(F32)).astype(BF16)


def split3(x):
    high = x.astype(BF16)
    rest = x - high.astype(F32)
    mid = rest.astype(BF16)
    return high, mid, (rest - mid.astype(F32)).astype(BF16)


def swish(values):
    return values * jax.nn.sigmoid(values)


class Plan:
    def __init__(self, mesh):
        self.n_dp, self.n_mp = mesh.shape["dp"], mesh.shape["mp"]
        self.n = self.n_dp * self.n_mp
        self.groups = self.n // CRIT
        self.workers = self.groups * CRIT
        self.turns = -(-self.n // self.groups)

    def rank(self, dp, mp):
        size = 4 * self.n_dp
        layer = mp // 4
        inner = dp * 4 + (mp % 4 + 2 * (dp % 2)) % 4
        if self.n != 32:
            return layer * size + inner
        far, near = layer // 2, jnp.logical_or(layer == 1, layer == 2)
        six = 24 + 3 * far + jnp.where(near, 2, 0)
        seven = jnp.where(near, 30 + far, 25 + 3 * far)
        return jnp.where(inner < 6, 6 * layer + inner, jnp.where(inner == 6, six, seven))

    def place(self, k):
        size = 4 * self.n_dp
        if self.n != 32:
            layer, inner = k // size, k % size
        else:
            extra = jnp.maximum(k - 24, 0)
            which, j = extra // 3, extra % 3
            layer = jnp.where(which == 0, j // 2, jnp.where(which == 1, 3 - j // 2, 1 + j))
            inner = jnp.where(which == 2, 7, 6 + j % 2)
            layer = jnp.where(k < 24, k // 6, layer)
            inner = jnp.where(k < 24, k % 6, inner)
        dp = inner // 4
        return dp, layer * 4 + (inner % 4 + 2 * (dp % 2)) % 4

    def device(self, s):
        return s // self.n_mp, s % self.n_mp

    def pairs(self, rows):
        per = -(-rows // self.groups)
        return -(-per // 32) * 16

    def cap(self, rows):
        return -(-(self.n * -(-rows // self.groups)) // TILE) * TILE


def chunks_of(columns):
    width = math.gcd(math.gcd(columns, H), HALF)
    return width, columns // width, H // width


def assemble(chunks_ref, width, shift):
    groups = []
    lane = iota((32, LANES), 1)
    for g in range(H // LANES):
        block = jnp.zeros((32, LANES), F32)
        for i in range(LANES // width):
            chunk = chunks_ref[g * (LANES // width) + i]
            turn = (i * width - shift) % LANES
            moved = pltpu.roll(chunk, turn, 1) if turn else chunk
            block = jnp.where(lane // width == i, moved, block)
        groups.append(block)
    return jnp.concatenate(groups, 1)


def all_barrier(plan, dp, mp):
    barrier = pltpu.get_barrier_semaphore()

    def tell(s, _):
        sdp, smp = s // plan.n_mp, s % plan.n_mp

        @pl.when(jnp.logical_or(sdp != dp, smp != mp))
        def _():
            pl.semaphore_signal(barrier, inc=1, device_id=(sdp, smp), device_id_type=MESH)

        return 0

    lax.fori_loop(0, plan.n, tell, 0)
    pl.semaphore_wait(barrier, plan.n - 1)


def dispatch_kernel(
    plan,
    crit_ref,
    targ_ref,
    crit_small,
    targ_small,
    head_ref,
    sa_ref,
    ns_ref,
    rows_ref,
    table_ref,
    pin_ref,
    pmid_ref,
    pout_ref,
    wt_ref,
    wc_ref,
    x_ref,
    p_ref,
    low,
    msg,
    wide,
    chunk,
    send_w,
    recv_w,
    pass_w,
    send_x,
    recv_x,
    send_p,
    recv_p,
):
    dp, mp = lax.axis_index("dp"), lax.axis_index("mp")
    me = plan.rank(dp, mp)
    index = dp * plan.n_mp + mp
    groups, workers = plan.groups, plan.workers
    critic, group = me // groups, me % groups
    rw, cw = crit_ref.shape[1], crit_ref.shape[2]
    rows = sa_ref.shape[1]
    columns = crit_small[0].shape[1]
    width, mine, per = chunks_of(columns)
    nets = (wt_ref, wc_ref)

    def to_low(c, _):
        low[0, c] = targ_ref[c].astype(BF16)
        low[1, c] = crit_ref[c].astype(BF16)
        return 0

    lax.fori_loop(0, CRIT, to_low, 0)
    all_barrier(plan, dp, mp)

    def w_slot(t, s):
        sdp, smp = plan.device(s)
        return nets[t].at[pl.ds(pl.multiple_of(smp * rw, rw), rw), pl.ds(pl.multiple_of(sdp * cw, cw), cw)]

    def to_worker(src, dst, send, recv, k):
        return pltpu.make_async_remote_copy(
            src_ref=src, dst_ref=dst, send_sem=send, recv_sem=recv, device_id=plan.place(k), device_id_type=MESH
        )

    def first_hop(t, c):
        k = c * groups + index % groups
        return k, to_worker(low.at[t, c], w_slot(t, index), send_w.at[t, c], recv_w.at[t, index], k)

    def send_weights(t):
        def one(i, _):
            c = (critic + i) % CRIT
            k, copy = first_hop(t, c)

            @pl.when(k == me)
            def _():
                pltpu.make_async_copy(low.at[t, c], w_slot(t, index), recv_w.at[t, index]).start()

            @pl.when(k != me)
            def _():
                copy.start()

            return 0

        lax.fori_loop(0, CRIT, one, 0)

    send_weights(0)
    send_weights(1)

    wide[...] = jnp.zeros_like(wide)
    for t, parts in enumerate((targ_small, crit_small)):
        wide[t, 0:IN, 0:columns] = parts[0][...]
        wide[t, IN : IN + 4, 0:columns] = parts[1][...]
        wide[t, IN + 4 : IN + 5, 0:columns] = head_ref[t : t + 1, :]
    for j in range(mine):
        start, offset = j * width // LANES * LANES, j * width % LANES
        both = [wide[t, :, start : start + LANES] for t in range(2)]
        turned = [pltpu.roll(v, turn, 1) if turn else v for v, turn in zip(both, ((-offset) % LANES, (HALF - offset) % LANES))]
        chunk[j] = jnp.where(iota((32, LANES), 1) < HALF, turned[0], turned[1])

    def small_hop(j, r):
        g = index * mine + j
        k = (g // per) * groups + r
        return k, to_worker(chunk.at[j], p_ref.at[g % per], send_p.at[j, r], recv_p.at[g % per], k)

    def send_small(i, _):
        j, r = i // groups, i % groups
        k, copy = small_hop(j, r)

        @pl.when(k == me)
        def _():
            slot = (index * mine + j) % per
            pltpu.make_async_copy(chunk.at[j], p_ref.at[slot], recv_p.at[slot]).start()

        @pl.when(k != me)
        def _():
            copy.start()

        return 0

    lax.fori_loop(0, mine * groups, send_small, 0)

    lane = iota((rows, LANES), 1)
    place = lambda height, offset: (iota((height, LANES), 1) == iota((height, LANES), 0) + offset).astype(F32).astype(BF16)
    hidden = swish(tn(ns_ref[...], pin_ref[...])).astype(BF16)
    hidden = swish(nn(hidden, pmid_ref[...])).astype(BF16)
    pout = pout_ref[...]
    spread = lambda offset: tn(
        pout, (iota((2 * ACT, LANES), 0) == iota((2 * ACT, LANES), 1) + offset).astype(F32).astype(BF16)
    ).astype(BF16)
    keep = lane < ACT
    means = nn(hidden, spread(0))
    raw = nn(hidden, spread(ACT))
    facts = rows_ref[...]
    across = jnp.transpose(facts)
    picked = (iota((rows, table_ref.shape[1]), 1) == across[:, 2:3].astype(I32)).astype(F32).astype(BF16)
    noise = jnp.zeros((rows, LANES), F32)
    for part in split3(table_ref[...]):
        noise = noise + nn(picked, tn(part, place(ACT, 0)).astype(BF16))
    log_std = -5.0 + 3.5 * (jnp.tanh(raw) + 1.0)
    squashed = means + jnp.exp(log_std) * noise
    action = jnp.tanh(squashed).astype(BF16)
    twice = -2.0 * squashed
    softplus = jnp.maximum(twice, 0.0) + jnp.log(1.0 + jnp.exp(-jnp.abs(twice)))
    correction = 2.0 * (math.log(2.0) - squashed - softplus)
    density = jnp.sum(
        jnp.where(keep, -0.5 * noise * noise - log_std - 0.5 * math.log(2.0 * math.pi) - correction, 0.0), -1, keepdims=True
    )
    done = across[:, 1:2]
    boot = (done == 0.0).astype(F32)
    base = across[:, 0:1] - (REWARD_DISCOUNT * ENTROPY_TEMP) * boot * density
    high, mid, rest = split3(base)
    on = lambda k, value: jnp.where(lane == k, value, 0.0)
    features = (
        tn(sa_ref[...], place(IN, 0))
        + tn(ns_ref[...], place(OBS, L_TGT))
        + nn(jnp.where(keep, action.astype(F32), 0.0).astype(BF16), place(LANES, L_TGT + OBS))
        + on(L_BASE, high.astype(F32))
        + on(L_BASE + 1, mid.astype(F32))
        + on(L_BASE + 2, rest.astype(F32))
        + on(L_BOOT, boot)
        + on(L_S0, across[:, 3:4])
        + on(L_S1, across[:, 4:5])
        + on(L_VALID, 1.0)
    ).astype(BF16)

    pairs = msg.shape[1]
    valid = (facts[1:2, :] != 2.0).astype(F32)
    before = (iota((rows, rows), 0) < iota((rows, rows), 1)).astype(F32).astype(BF16)
    order = nn(jnp.broadcast_to(valid, (8, rows)).astype(BF16), before)[0:1, :]
    order = jnp.where(valid > 0.0, order, -1.0)
    count = jnp.sum(valid, -1, keepdims=True)
    count_half = jnp.floor(count * 0.5)
    mlane = iota((pairs, LANES), 1)
    tail = jnp.where(mlane == L_CNT, count_half, 0.0) + jnp.where(mlane == L_CNT + 1, count - 2.0 * count_half, 0.0)

    def deal(r, _):
        slot = iota((pairs, rows), 0) * (2 * groups) + r
        halves = []
        for h in range(2):
            hot = (order == (slot + h * groups).astype(F32)).astype(F32).astype(BF16)
            halves.append(nn(hot, features))
        msg[r] = (halves[0] + pltpu.roll(halves[1], HALF, 1) + tail).astype(BF16)
        return 0

    lax.fori_loop(0, groups, deal, 0)

    def row_hop(k):
        return to_worker(msg.at[k % groups], x_ref.at[index], send_x.at[k], recv_x.at[index], k)

    def send_rows(i, _):
        k = (me + i) % workers

        @pl.when(k == me)
        def _():
            pltpu.make_async_copy(msg.at[group], x_ref.at[index], recv_x.at[index]).start()

        @pl.when(k != me)
        def _():
            row_hop(k).start()

        return 0

    lax.fori_loop(0, workers, send_rows, 0)

    def pass_on(t, turn, i):
        s = group + groups * turn
        k = critic * groups + (group + 1 + i) % groups
        return to_worker(w_slot(t, s), w_slot(t, s), pass_w.at[t, turn, i], recv_w.at[t, s], k)

    def arrived_w(t, s):
        pltpu.make_async_copy(low.at[t, 0], w_slot(t, s), recv_w.at[t, s]).wait()

    turns = (plan.n - group + groups - 1) // groups

    @pl.when(me < workers)
    def _():
        for t in range(2):

            def relay(turn, _):
                arrived_w(t, group + groups * turn)

                def one(i, _):
                    pass_on(t, turn, i).start()
                    return 0

                lax.fori_loop(0, groups - 1, one, 0)
                return 0

            lax.fori_loop(0, turns, relay, 0)

        def arrived(s, _):
            @pl.when(s % groups != group)
            def _():
                arrived_w(0, s)
                arrived_w(1, s)

            pltpu.make_async_copy(msg.at[0], x_ref.at[s], recv_x.at[s]).wait()
            return 0

        lax.fori_loop(0, plan.n, arrived, 0)

        def arrived_small(j, _):
            pltpu.make_async_copy(chunk.at[0], p_ref.at[j], recv_p.at[j]).wait()
            return 0

        lax.fori_loop(0, per, arrived_small, 0)
        for t in range(2):

            def passed(turn, _):
                def one(i, _):
                    pass_on(t, turn, i).wait_send()
                    return 0

                lax.fori_loop(0, groups - 1, one, 0)
                return 0

            lax.fori_loop(0, turns, passed, 0)

    def sent_weights(c, _):
        for t in range(2):
            k, copy = first_hop(t, c)

            @pl.when(k != me)
            def _():
                copy.wait_send()

        return 0

    lax.fori_loop(0, CRIT, sent_weights, 0)

    def sent_small(i, _):
        k, copy = small_hop(i // groups, i % groups)

        @pl.when(k != me)
        def _():
            copy.wait_send()

        return 0

    lax.fori_loop(0, mine * groups, sent_small, 0)

    def sent_rows(k, _):
        @pl.when(k != me)
        def _():
            row_hop(k).wait_send()

        return 0

    lax.fori_loop(0, workers, sent_rows, 0)


def dispatch(plan, critic_hidden, target_hidden, critic_small, target_small, heads, rows_args, policy):
    rows = rows_args[0].shape[1]
    pairs = plan.pairs(rows)
    columns = critic_small[0].shape[1]
    _width, mine, per = chunks_of(columns)
    vmem = pl.BlockSpec(memory_space=pltpu.VMEM)
    anywhere = pl.BlockSpec(memory_space=pl.ANY)
    dma = pltpu.SemaphoreType.DMA
    return pl.pallas_call(
        functools.partial(dispatch_kernel, plan),
        out_shape=(
            jax.ShapeDtypeStruct((H, H), BF16),
            jax.ShapeDtypeStruct((H, H), BF16),
            jax.ShapeDtypeStruct((plan.n, pairs, LANES), BF16),
            jax.ShapeDtypeStruct((per, 32, LANES), F32),
        ),
        in_specs=[vmem, vmem, (vmem,) * 2, (vmem,) * 2] + [vmem] * 8,
        out_specs=(anywhere,) * 4,
        scratch_shapes=[
            pltpu.VMEM((2,) + critic_hidden.shape, BF16),
            pltpu.VMEM((plan.groups, pairs, LANES), BF16),
            pltpu.VMEM((2, 32, -(-columns // LANES) * LANES), F32),
            pltpu.VMEM((mine, 32, LANES), F32),
            dma((2, CRIT)),
            dma((2, plan.n)),
            dma((2, plan.turns, plan.groups - 1)),
            dma((plan.workers,)),
            dma((plan.n,)),
            dma((mine, plan.groups)),
            dma((per,)),
        ],
        compiler_params=pltpu.CompilerParams(collective_id=0, has_side_effects=True, vmem_limit_bytes=VMEM_LIMIT),
        name="dispatch",
    )(critic_hidden, target_hidden, critic_small, target_small, heads, *rows_args, *policy)


def norm_parts(pre):
    centered = pre - jnp.sum(pre, -1, keepdims=True) * (1.0 / H)
    inv = lax.rsqrt(jnp.sum(centered * centered, -1, keepdims=True) * (1.0 / H) + 1e-05)
    return centered * inv, inv


def swish_parts(half):
    t = jnp.tanh(half)
    product = half * t
    return half + product, (1.0 + t) * (1.0 + (half - product))


def low_input(params):
    return jnp.where(iota((32, H), 0) < IN, params, 0.0).astype(BF16)


def tile_span(t):
    return pl.ds(pl.multiple_of(t * TILE, TILE), TILE)


def target_kernel(
    plan, width, role_ref, x_ref, w_ref, p_ref, xc_ref, q_ref, info_ref, rows_f, picked, value, hot, win, par, cnt_v, cnt_s, base_s, sem
):
    critic, group, active = role_ref[0], role_ref[1], role_ref[2]
    groups, n = plan.groups, plan.n
    pairs = x_ref.shape[1]
    first = x_ref[:, 0, :].astype(F32)
    lane = iota(first.shape, 1)
    counts = 2.0 * jnp.sum(jnp.where(lane == L_CNT, first, 0.0), -1, keepdims=True) + jnp.sum(
        jnp.where(lane == L_CNT + 1, first, 0.0), -1, keepdims=True
    )
    counts = jnp.where(active > 0, jnp.broadcast_to(counts, first.shape), 0.0)
    mine = jnp.floor((counts + (groups - 1 - group).astype(F32)) * (1.0 / groups) + 0.5 / groups)
    earlier = (iota((n, n), 1) < iota((n, n), 0)).astype(F32).astype(BF16)
    starts = nn(earlier, mine.astype(BF16))
    total = jnp.sum(counts, 0, keepdims=True)
    cnt_v[0:n, :] = mine.astype(I32)
    cnt_v[n : 2 * n, :] = starts.astype(I32)
    cnt_v[2 * n : 2 * n + 8, :] = jnp.broadcast_to(total, (8, LANES)).astype(I32)
    copy = pltpu.make_async_copy(cnt_v, cnt_s, sem)
    copy.start()
    par[...] = assemble(p_ref, width, 0)
    win[...] = jnp.zeros_like(win)
    win[0:32, :] = low_input(par[...])
    copy.wait()
    number = cnt_s[n - 1, 0] + cnt_s[2 * n - 1, 0]
    tiles = (number + TILE - 1) // TILE
    info_ref[0] = number
    info_ref[1] = cnt_s[2 * n, 0]

    def compact(s, _):
        block = x_ref[s].astype(F32)
        have, start = cnt_s[s, 0], cnt_s[n + s, 0]
        rows_f[pl.ds(start, pairs), :] = block
        rows_f[pl.ds(start + (have + 1) // 2, pairs), :] = pltpu.roll(block, HALF, 1)
        return 0

    @pl.when(active > 0)
    def _():
        lax.fori_loop(0, n, compact, 0)

    rows_f[pl.ds(number, TILE), :] = jnp.zeros((TILE, LANES), F32)

    until = (iota((TILE, TILE), 1) < iota((TILE, TILE), 0)).astype(F32).astype(BF16)
    place = iota((TILE, TILE), 1).astype(F32)
    this = critic.astype(F32)

    def choose(t, base):
        wide = rows_f[tile_span(t), :]
        x = wide.astype(BF16)
        xc_ref[tile_span(t), :] = x
        wanted = jnp.logical_or(wide[:, L_S0 : L_S0 + 1] == this, wide[:, L_S1 : L_S1 + 1] == this)
        wanted = jnp.where(jnp.logical_and(wanted, wide[:, L_BOOT : L_BOOT + 1] > 0.0), 1.0, 0.0)
        order = nn(until, jnp.broadcast_to(wanted, (TILE, LANES)).astype(BF16))[:, 0:1]
        chosen = (jnp.where(wanted > 0.0, order, -1.0) == place).astype(F32).astype(BF16)
        hot[t] = chosen
        picked[pl.ds(base, TILE), :] = tn(chosen, x)
        base_s[t] = base
        return base + jnp.sum(wanted).astype(I32)

    chosen_rows = lax.fori_loop(0, tiles, choose, 0)
    picked[pl.ds(chosen_rows, TILE), :] = jnp.zeros((TILE, LANES), F32)
    chosen_tiles = (chosen_rows + TILE - 1) // TILE
    half = jnp.where(iota((32, 1), 0) < IN + 4, 0.5, 1.0)
    par[...] = par[...] * half
    gain1, shift1, gain2, shift2, head = (par[IN + k : IN + k + 1, :] for k in range(5))

    def tile(t, _):
        x = pltpu.roll(picked[tile_span(t), :], LANES - L_TGT, 1).astype(BF16)
        z, _unused = norm_parts(nn(x, win[...]))
        y = z * gain1 + shift1
        act = (y + y * jnp.tanh(y)).astype(BF16)
        z, _unused = norm_parts(nn(act, w_ref[...]))
        y = z * gain2 + shift2
        q = jnp.sum((y + y * jnp.tanh(y)) * head, -1, keepdims=True)
        value[tile_span(t), :] = jnp.broadcast_to(q, (TILE, LANES))
        return 0

    lax.fori_loop(0, chosen_tiles, tile, 0)
    value[tile_span(chosen_tiles), :] = jnp.zeros((TILE, LANES), F32)

    def spread(t, _):
        lane = iota((TILE, LANES), 1)
        high, mid, rest = (v.astype(F32) for v in split3(value[pl.ds(base_s[t], TILE), :]))
        parts = jnp.where(lane == 0, high, jnp.where(lane == 1, mid, jnp.where(lane == 2, rest, 0.0)))
        q = jnp.broadcast_to(jnp.sum(nn(hot[t], parts.astype(BF16)), -1, keepdims=True), (TILE, LANES))
        for h in range(TILE // LANES):
            flat = jnp.transpose(q[h * LANES : (h + 1) * LANES, :])
            q_ref[pl.ds(t * (TILE // LANES) + h, 1), :] = flat[0:1, :]
        return 0

    lax.fori_loop(0, tiles, spread, 0)


def target_values(plan, rows, width, role, x, weights, params):
    capacity = plan.cap(rows)
    vmem = pl.BlockSpec(memory_space=pltpu.VMEM)
    smem = pl.BlockSpec(memory_space=pltpu.SMEM)
    return pl.pallas_call(
        functools.partial(target_kernel, plan, width),
        out_shape=(
            jax.ShapeDtypeStruct((capacity, LANES), BF16),
            jax.ShapeDtypeStruct((capacity // LANES, LANES), F32),
            jax.ShapeDtypeStruct((2,), I32),
        ),
        in_specs=[smem, vmem, vmem, vmem],
        out_specs=(vmem, vmem, smem),
        scratch_shapes=[
            pltpu.VMEM((capacity + TILE + x.shape[1], LANES), F32),
            pltpu.VMEM((capacity + TILE, LANES), F32),
            pltpu.VMEM((capacity + TILE, LANES), F32),
            pltpu.VMEM((capacity // TILE, TILE, TILE), BF16),
            pltpu.VMEM((LANES, H), BF16),
            pltpu.VMEM((32, H), F32),
            pltpu.VMEM((2 * plan.n + 8, LANES), I32),
            pltpu.SMEM((2 * plan.n + 8, LANES), I32),
            pltpu.SMEM((capacity // TILE,), I32),
            pltpu.SemaphoreType.DMA,
        ],
        compiler_params=pltpu.CompilerParams(vmem_limit_bytes=VMEM_LIMIT),
        name="target_values",
    )(role, x, weights, params)


def share_kernel(plan, q_ref, all_ref, send, recv):
    dp, mp = lax.axis_index("dp"), lax.axis_index("mp")
    me = plan.rank(dp, mp)
    groups = plan.groups
    critic, group = me // groups, me % groups
    barrier = pltpu.get_barrier_semaphore()

    @pl.when(me < plan.workers)
    def _():
        def peer(i):
            other = (critic + i) % CRIT
            return other, plan.place(other * groups + group)

        def tell(i, _):
            pl.semaphore_signal(barrier, inc=1, device_id=peer(i)[1], device_id_type=MESH)
            return 0

        lax.fori_loop(1, CRIT, tell, 0)
        pl.semaphore_wait(barrier, CRIT - 1)
        all_ref[critic] = q_ref[...]

        def copy(i):
            other, device = peer(i)
            return pltpu.make_async_remote_copy(
                src_ref=q_ref,
                dst_ref=all_ref.at[critic],
                send_sem=send.at[other],
                recv_sem=recv.at[critic],
                device_id=device,
                device_id_type=MESH,
            )

        def start(i, _):
            copy(i).start()
            return 0

        lax.fori_loop(1, CRIT, start, 0)

        def finish(i, _):
            copy(i).wait_send()
            other = peer(i)[0]
            pltpu.make_async_copy(q_ref, all_ref.at[other], recv.at[other]).wait()
            return 0

        lax.fori_loop(1, CRIT, finish, 0)


def share_values(plan, q):
    vmem = pl.BlockSpec(memory_space=pltpu.VMEM)
    return pl.pallas_call(
        functools.partial(share_kernel, plan),
        out_shape=jax.ShapeDtypeStruct((CRIT,) + q.shape, F32),
        in_specs=[vmem],
        out_specs=vmem,
        scratch_shapes=[pltpu.SemaphoreType.DMA((CRIT,)), pltpu.SemaphoreType.DMA((CRIT,))],
        compiler_params=pltpu.CompilerParams(collective_id=1, has_side_effects=True, vmem_limit_bytes=VMEM_LIMIT),
        name="share_values",
    )(q)


def critic_kernel(
    plan, width, info_ref, xc_ref, q_ref, w_ref, p_ref, grad_ref, small_ref, sums_ref, z_one, slope, act, low, fact, par, win, picks, acc
):
    number = info_ref[0]
    scale = 2.0 / jnp.maximum(info_ref[1], 1).astype(F32)
    tiles = (number + TILE - 1) // TILE
    par[...] = assemble(p_ref, width, HALF)
    win[...] = jnp.zeros_like(win)
    win[0:32, :] = low_input(par[...])
    grad_ref[...] = jnp.zeros_like(grad_ref)
    acc[...] = jnp.zeros_like(acc)
    picks[...] = jnp.zeros_like(picks)
    sums_ref[...] = jnp.zeros_like(sums_ref)
    gain1, shift1, gain2, shift2, head = (par[IN + k : IN + k + 1, :] for k in range(5))

    def fold(k, value):
        acc[32 + k * 8 : 40 + k * 8, :] += jnp.sum(value.reshape(TILE // 8, 8, H), 0)

    def tile(t, _):
        x = xc_ref[tile_span(t), :]
        wide = x.astype(F32)
        for h in range(TILE // LANES):
            picks[0:CRIT, :] = q_ref[:, pl.ds(t * (TILE // LANES) + h, 1), :].reshape(CRIT, LANES)
            table = jnp.transpose(picks[...])
            part = wide[h * LANES : (h + 1) * LANES, :]
            critic = iota(table.shape, 1).astype(F32)
            one = jnp.sum(jnp.where(critic == part[:, L_S0 : L_S0 + 1], table, 0.0), -1, keepdims=True)
            two = jnp.sum(jnp.where(critic == part[:, L_S1 : L_S1 + 1], table, 0.0), -1, keepdims=True)
            base = part[:, L_BASE : L_BASE + 1] + part[:, L_BASE + 1 : L_BASE + 2] + part[:, L_BASE + 2 : L_BASE + 3]
            goal = base + jnp.where(part[:, L_BOOT : L_BOOT + 1] > 0.0, REWARD_DISCOUNT * jnp.minimum(one, two), 0.0)
            fact[h * LANES : (h + 1) * LANES, 0:1] = goal
        z, inv_one = norm_parts(nn(x, win[...]))
        z_one[...] = z
        value, twice = swish_parts(z * (0.5 * gain1) + 0.5 * shift1)
        slope[...] = 0.5 * twice
        act[...] = value.astype(BF16)
        z, inv = norm_parts(nn(act[...], w_ref[...]))
        value, twice = swish_parts(z * (0.5 * gain2) + 0.5 * shift2)
        q = jnp.sum(value * head, -1, keepdims=True)
        error = (q - fact[:, 0:1]) * wide[:, L_VALID : L_VALID + 1]
        sums_ref[0:1, :] += jnp.broadcast_to(jnp.sum(error * error, 0, keepdims=True), (1, LANES))
        dq = error * scale
        fold(4, dq * value)
        dy = dq * (twice * (0.5 * head))
        fold(3, dy)
        fold(2, dy * z)
        dz = dy * gain2
        mean = jnp.sum(dz, -1, keepdims=True) * (1.0 / H)
        along = jnp.sum(dz * z, -1, keepdims=True) * (1.0 / H)
        low[...] = (inv * (dz - mean - z * along)).astype(BF16)
        down = nt(low[...], w_ref[...])
        grad_ref[...] += tn(act[...], low[...])
        z = z_one[...]
        dy = down * slope[...]
        fold(1, dy)
        fold(0, dy * z)
        dz = dy * gain1
        mean = jnp.sum(dz, -1, keepdims=True) * (1.0 / H)
        along = jnp.sum(dz * z, -1, keepdims=True) * (1.0 / H)
        acc[0:32, :] += tn(x[:, 0:32], (inv_one * (dz - mean - z * along)).astype(BF16))
        return 0

    lax.fori_loop(0, tiles, tile, 0)
    sums_ref[1:2, :] = jnp.broadcast_to(info_ref[1].astype(F32), (1, LANES))
    for k in range(5):
        acc[IN + k : IN + k + 1, :] = jnp.sum(acc[32 + k * 8 : 40 + k * 8, :], 0, keepdims=True)
    for i in range(H // width):
        start, offset = i * width // LANES * LANES, i * width % LANES
        block = acc[0:32, start : start + LANES]
        small_ref[i] = pltpu.roll(block, LANES - offset, 1) if offset else block


def critic_step(plan, width, info, xc, q_all, weights, params):
    vmem = pl.BlockSpec(memory_space=pltpu.VMEM)
    smem = pl.BlockSpec(memory_space=pltpu.SMEM)
    return pl.pallas_call(
        functools.partial(critic_kernel, plan, width),
        out_shape=(
            jax.ShapeDtypeStruct((H, H), F32),
            jax.ShapeDtypeStruct((H // width, 32, LANES), F32),
            jax.ShapeDtypeStruct((8, LANES), F32),
        ),
        in_specs=[smem] + [vmem] * 4,
        out_specs=(vmem,) * 3,
        scratch_shapes=[
            pltpu.VMEM((TILE, H), F32),
            pltpu.VMEM((TILE, H), F32),
            pltpu.VMEM((TILE, H), BF16),
            pltpu.VMEM((TILE, H), BF16),
            pltpu.VMEM((TILE, LANES), F32),
            pltpu.VMEM((32, H), F32),
            pltpu.VMEM((LANES, H), BF16),
            pltpu.VMEM((16, LANES), F32),
            pltpu.VMEM((72, H), F32),
        ],
        compiler_params=pltpu.CompilerParams(vmem_limit_bytes=VMEM_LIMIT),
        name="critic_step",
    )(info, xc, q_all, weights, params)


PRECISE = 2


LAG = 2
AHEAD = 3


def shampoo_kernel(
    plan,
    g_ref,
    small_ref,
    sums_ref,
    mom_ref,
    left_ref,
    right_ref,
    w_ref,
    mo_ref,
    lo_ref,
    ro_ref,
    wo_ref,
    own_ref,
    out_ref,
    parts,
    pieces,
    given,
    shares,
    totals,
    send_one,
    recv_one,
    send_two,
    recv_two,
    send_s,
    recv_s,
    send_t,
    recv_t,
):
    dp, mp = lax.axis_index("dp"), lax.axis_index("mp")
    me = plan.rank(dp, mp)
    index = dp * plan.n_mp + mp
    groups, workers, n, turns = plan.groups, plan.workers, plan.n, plan.turns
    critic, group = me // groups, me % groups
    rw, cw = mom_ref.shape[1], mom_ref.shape[2]
    mine, per = shares.shape[1], small_ref.shape[0]
    columns = own_ref.shape[1]
    chunk_width = H // per
    all_barrier(plan, dp, mp)

    def to_device(src, dst, send, recv, device):
        return pltpu.make_async_remote_copy(
            src_ref=src, dst_ref=dst, send_sem=send, recv_sem=recv, device_id=device, device_id_type=MESH
        )

    def block(s):
        sdp, smp = plan.device(s)
        return pl.ds(pl.multiple_of(smp * rw, rw), rw), pl.ds(pl.multiple_of(sdp * cw, cw), cw)

    def turn_of(step):
        return (step + critic) % turns

    def first_hop(step, i):
        other = (group + 1 + i) % groups
        turn = turn_of(step)
        s = other + groups * turn
        copy = to_device(
            g_ref.at[block(s)],
            parts.at[groups - 2 - i, turn],
            send_one.at[step, i],
            recv_one.at[groups - 2 - i, turn],
            plan.place(critic * groups + other),
        )
        return s, copy

    def second_hop(turn):
        s = group + groups * turn
        return s, to_device(pieces.at[turn], given.at[critic], send_two.at[turn], recv_two.at[critic], plan.device(s))

    def small_hop(q):
        g = critic * per + q
        s = g // mine
        return s, to_device(
            small_ref.at[q], shares.at[group, g % mine], send_s.at[q], recv_s.at[group, g % mine], plan.device(s)
        )

    def total_hop(s):
        return to_device(sums_ref, totals.at[me], send_t.at[s], recv_t.at[me], plan.device(s))

    def start_first(step):
        def one(i, _):
            s, copy = first_hop(step, i)

            @pl.when(s < n)
            def _():
                copy.start()

            return 0

        lax.fori_loop(0, groups - 1, one, 0)

    def start_rest():
        def start_small(q, _):
            s, copy = small_hop(q)

            @pl.when(s == index)
            def _():
                slot = (critic * per + q) % mine
                pltpu.make_async_copy(small_ref.at[q], shares.at[group, slot], recv_s.at[group, slot]).start()

            @pl.when(s != index)
            def _():
                copy.start()

            return 0

        lax.fori_loop(0, per, start_small, 0)
        totals[me] = sums_ref[...]

        def start_total(i, _):
            total_hop((index + i) % n).start()
            return 0

        lax.fori_loop(1, n, start_total, 0)

    @pl.when(me < workers)
    def _():
        for step in range(AHEAD):
            start_first(step)

    def add_up(step):
        turn = turn_of(step)
        s, copy = second_hop(turn)

        @pl.when(s < n)
        def _():
            for i in range(groups - 1):
                pltpu.make_async_copy(pieces.at[0], parts.at[i, turn], recv_one.at[i, turn]).wait()
            value = g_ref[block(s)]
            for i in range(groups - 1):
                value = value + parts[i, turn]
            pieces[turn] = value

            @pl.when(s == index)
            def _():
                pltpu.make_async_copy(pieces.at[turn], given.at[critic], recv_two.at[critic]).start()

            @pl.when(s != index)
            def _():
                copy.start()

    width = min(256, cw)
    many = width // BLK
    nr, nc = rw // BLK, cw // width
    subs = [(i, j) for i in range(nr) for j in range(nc)]
    mask = (iota((width, width), 0) // BLK == iota((width, width), 1) // BLK).astype(F32).astype(BF16)
    eye = (iota((BLK, width), 0) == iota((BLK, width), 1) % BLK).astype(F32)
    eye_low = eye.astype(BF16)

    def diag(x):
        return jnp.concatenate([x] * many, 0) * mask

    def precise(a, b):
        ah, al = split2(a)
        bh, bl = split2(b)
        both = nn(jnp.concatenate([ah, al], 0), diag(bh))
        return both[:BLK] + both[BLK:] + nn(ah, diag(bl))

    def block_sums(s):
        high, rest = split2(s)
        return nn(high, mask) + nn(rest, mask)

    def place(c, i, j):
        return (c, slice(i * BLK, (i + 1) * BLK), slice(j * width, (j + 1) * width))

    def blocked(c):
        pltpu.make_async_copy(pieces.at[0], given.at[c], recv_two.at[c]).wait()
        sums = []
        for i, j in subs:
            at = place(c, i, j)
            grad = given[at]
            mo_ref[at] = MOMENTUM * mom_ref[at] + grad
            low = grad.astype(BF16)
            wide = diag(low)
            left = STAT_DECAY * left_ref[at] + (1.0 - STAT_DECAY) * nt(low, wide)
            flip = nt(eye_low, wide).astype(BF16)
            right = STAT_DECAY * right_ref[at] + (1.0 - STAT_DECAY) * nn(flip, wide)
            lo_ref[at] = left
            ro_ref[at] = right
            for stat in (left, right):
                sums.append(jnp.sum((stat * stat).reshape(BLK // 8, 8, width), 0))
        total = block_sums(jnp.concatenate(sums, 0))
        chains = []
        for k, (i, j) in enumerate(subs):
            for side, ref in enumerate((lo_ref, ro_ref)):
                spot = (2 * k + side) * 8
                inv = lax.rsqrt(jnp.sum(total[spot : spot + 8], 0, keepdims=True))
                rest = (eye - ref[place(c, i, j)] * inv) * 0.25
                chains.append([rest, eye + rest, jnp.sqrt(jnp.sqrt(inv))])
        for it in range(NEWTON - 1):
            full = it < PRECISE
            work = []
            for ch in chains:
                high, rest = split2(ch[0])
                wide = diag(high)
                wide_rest = diag(rest) if full else None
                lhs = [high] + ([rest] if full else []) + ([ch[1].astype(BF16)] if it > 0 else [])
                out = nn(jnp.concatenate(lhs, 0), wide)
                power = out[:BLK]
                if full:
                    power = power + out[BLK : 2 * BLK] + nn(high, wide_rest)
                if it > 0:
                    ch[1] = ch[1] + out[-BLK:]
                work.append([wide, wide_rest, power])
            for factor in (3.75, 5.0, 2.5):
                for ch, wk in zip(chains, work):
                    high, rest = split2(factor * ch[0] + wk[2])
                    if full:
                        out = nn(jnp.concatenate([high, rest], 0), wk[0])
                        wk[2] = out[:BLK] + out[BLK:] + nn(high, wk[1])
                    else:
                        wk[2] = nn(high, wk[0])
            for ch, wk in zip(chains, work):
                ch[0] = wk[2]
        for ch in chains:
            ch[1] = ch[1] + nn(ch[1].astype(BF16), diag(ch[0].astype(BF16)))
        for k, (i, j) in enumerate(subs):
            at = place(c, i, j)
            lc, rc = chains[2 * k], chains[2 * k + 1]
            step = precise(precise(lc[1], mo_ref[at]), rc[1]) * (lc[2] * rc[2])
            squares = block_sums(jnp.sum((step * step).reshape(BLK // 8, 8, width), 0))
            square = jnp.sum(squares, 0, keepdims=True) * (1.0 / (BLK * BLK))
            old = w_ref[at]
            wo_ref[at] = old - RATE_HIDDEN * (step * lax.rsqrt(square + 1e-06) + WEIGHT_DECAY * old)

    def round_(i, _):
        @pl.when(jnp.logical_and(me < workers, i < turns))
        def _():
            @pl.when(i + AHEAD < turns)
            def _():
                start_first(i + AHEAD)

            @pl.when(i == LAG)
            def _():
                start_rest()

            add_up(i)

        c = (index // groups + 2 * turns + LAG - i) % turns

        @pl.when(jnp.logical_and(i >= LAG, c < CRIT))
        def _():
            blocked(c)

        return 0

    lax.fori_loop(0, turns + LAG, round_, 0)

    def arrived_small(i, _):
        pltpu.make_async_copy(small_ref.at[0], shares.at[i // mine, i % mine], recv_s.at[i // mine, i % mine]).wait()
        return 0

    lax.fori_loop(0, groups * mine, arrived_small, 0)
    for g in range(columns // LANES):
        part = jnp.zeros((32, LANES), F32)
        for j in range(mine):
            if j * chunk_width // LANES == g:
                value = shares[0, j]
                for r in range(1, groups):
                    value = value + shares[r, j]
                turn = j * chunk_width % LANES
                moved = pltpu.roll(value, turn, 1) if turn else value
                part = jnp.where(iota((32, LANES), 1) // chunk_width == turn // chunk_width, moved, part)
        own_ref[:, g * LANES : (g + 1) * LANES] = part

    def arrived_total(k, _):
        @pl.when(k != me)
        def _():
            pltpu.make_async_copy(sums_ref, totals.at[k], recv_t.at[k]).wait()

        return 0

    lax.fori_loop(0, workers, arrived_total, 0)
    out_ref[0:1, :] = jnp.sum(totals[:, 0, :], 0, keepdims=True)
    out_ref[1:2, :] = totals[0, 1:2, :]
    out_ref[2:8, :] = jnp.zeros((6, LANES), F32)

    @pl.when(me < workers)
    def _():
        def finish(step, _):
            def one(i, _):
                s, copy = first_hop(step, i)

                @pl.when(s < n)
                def _():
                    copy.wait_send()

                return 0

            lax.fori_loop(0, groups - 1, one, 0)
            s, copy = second_hop(step)

            @pl.when(jnp.logical_and(s < n, s != index))
            def _():
                copy.wait_send()

            return 0

        lax.fori_loop(0, turns, finish, 0)

        def finish_small(q, _):
            s, copy = small_hop(q)

            @pl.when(s != index)
            def _():
                copy.wait_send()

            return 0

        lax.fori_loop(0, per, finish_small, 0)

        def finish_total(i, _):
            total_hop((index + i) % n).wait_send()
            return 0

        lax.fori_loop(1, n, finish_total, 0)


def shampoo(plan, columns, grad, small, sums, moment, left, right, weight):
    vmem = pl.BlockSpec(memory_space=pltpu.VMEM)
    shape = jax.ShapeDtypeStruct(moment.shape, F32)
    _width, mine, per = chunks_of(columns)
    piece = moment.shape[1:]
    dma = pltpu.SemaphoreType.DMA
    return pl.pallas_call(
        functools.partial(shampoo_kernel, plan),
        out_shape=(shape,) * 4
        + (jax.ShapeDtypeStruct((32, -(-columns // LANES) * LANES), F32), jax.ShapeDtypeStruct((8, LANES), F32)),
        in_specs=[vmem] * 7,
        out_specs=(vmem,) * 6,
        scratch_shapes=[
            pltpu.VMEM((plan.groups - 1, plan.turns) + piece, F32),
            pltpu.VMEM((plan.turns,) + piece, F32),
            pltpu.VMEM((CRIT,) + piece, F32),
            pltpu.VMEM((plan.groups, mine, 32, LANES), F32),
            pltpu.VMEM((plan.workers, 8, LANES), F32),
            dma((plan.turns, plan.groups - 1)),
            dma((plan.groups - 1, plan.turns)),
            dma((plan.turns,)),
            dma((CRIT,)),
            dma((per,)),
            dma((plan.groups, mine)),
            dma((plan.n,)),
            dma((plan.workers,)),
        ],
        compiler_params=pltpu.CompilerParams(collective_id=2, has_side_effects=True, vmem_limit_bytes=VMEM_LIMIT),
        name="shampoo",
    )(grad, small, sums, moment, left, right, weight)


def adamw(grad, moment, square, weight, rate):
    moment_new = FIRST_DECAY * moment + (1.0 - FIRST_DECAY) * grad
    square_new = SECOND_DECAY * square + (1.0 - SECOND_DECAY) * grad * grad
    moment_hat = moment_new / (1.0 - FIRST_DECAY**STEP)
    square_hat = square_new / (1.0 - SECOND_DECAY**STEP)
    weight_new = weight - rate * (moment_hat / (jnp.sqrt(square_hat) + 1e-08) + WEIGHT_DECAY * weight)
    return (moment_new, square_new, weight_new)


def local(
    plan,
    state_action,
    next_state,
    reward,
    done_flags,
    noise_index,
    noise_table,
    subsets,
    policy_in,
    policy_mid,
    policy_out,
    critic_in,
    in_first,
    in_second,
    critic_norms,
    norm_first,
    norm_second,
    critic_head,
    head_first,
    head_second,
    critic_hidden,
    hidden_moment,
    left_stats,
    right_stats,
    target_in,
    target_norms,
    target_head,
    target_hidden,
):
    me = plan.rank(lax.axis_index("dp"), lax.axis_index("mp"))
    critic, group = me // plan.groups, me % plan.groups
    role = jnp.stack([critic, group, (me < plan.workers).astype(I32)])
    rows, columns = state_action.shape[0], critic_in.shape[1]
    width = chunks_of(columns)[0]
    facts = jnp.concatenate(
        [reward[None], jnp.stack([done_flags, noise_index, subsets[:, 0], subsets[:, 1]]).astype(F32), jnp.zeros((3, rows), F32)], 0
    )
    w_target, w_critic, x, params = dispatch(
        plan,
        critic_hidden,
        target_hidden,
        (critic_in, critic_norms),
        (target_in, target_norms),
        jnp.stack([target_head, critic_head]),
        (state_action.T, next_state.T, facts),
        (noise_table.T, policy_in, policy_mid, policy_out.T),
    )
    xc, q, info = target_values(plan, rows, width, role, x, w_target, params)
    q_all = share_values(plan, q)
    grad_hidden, grad_small, sums = critic_step(plan, width, info, xc, q_all, w_critic, params)
    hidden_momentum, left_renewed, right_renewed, hidden_updated, own, totals = shampoo(
        plan, columns, grad_hidden, grad_small, sums, hidden_moment, left_stats, right_stats, critic_hidden
    )
    own = own[:, :columns]
    loss_total, counted = totals[0, 0], totals[1, 0]
    in_moment, in_square, in_updated = adamw(own[:IN], in_first, in_second, critic_in, RATE_INPUT)
    norm_moment, norm_square, norm_updated = adamw(own[IN : IN + 4], norm_first, norm_second, critic_norms, RATE_NORMS)
    head_moment, head_square, head_updated = adamw(own[IN + 4], head_first, head_second, critic_head, RATE_HEAD)
    return (
        loss_total,
        counted,
        in_moment,
        in_square,
        in_updated,
        norm_moment,
        norm_square,
        norm_updated,
        head_moment,
        head_square,
        head_updated,
        hidden_momentum,
        left_renewed,
        right_renewed,
        hidden_updated,
    )


def solution(mesh):
    both = ("dp", "mp")
    rows, columns, flat, hidden = P(both, None), P(None, both), P(both), P(None, "mp", "dp")
    return jax.shard_map(
        functools.partial(local, Plan(mesh)),
        mesh=mesh,
        in_specs=(
            (rows, rows, flat, flat, flat, P(), rows, P(), P(), P())
            + (columns,) * 6
            + (flat,) * 3
            + (hidden,) * 4
            + (columns, columns, flat, hidden)
        ),
        out_specs=(P(), P()) + (columns,) * 6 + (flat,) * 3 + (hidden,) * 4,
        check_vma=False,
    )
```

```python
import functools
import math

import jax
import jax.numpy as jnp
from jax import lax
from jax.experimental import pallas as pl
from jax.experimental.pallas import tpu as pltpu
from jax.sharding import PartitionSpec as P

ACT = 6
OBS = 17
IN = 23
H = 1024
CRIT = 10
BLK = 32
NEWTON = 5
STEP = 10
REWARD_DISCOUNT = 0.99
ENTROPY_TEMP = 0.2
FIRST_DECAY = 0.9
SECOND_DECAY = 0.999
WEIGHT_DECAY = 0.01
RATE_INPUT = 0.1
RATE_NORMS = 0.3
RATE_HEAD = 0.03
RATE_HIDDEN = 0.01
MOMENTUM = 0.9
STAT_DECAY = 0.95

F32, BF16, I32 = jnp.float32, jnp.bfloat16, jnp.int32
MESH = pl.DeviceIdType.MESH
LANES = 128
HALF = 64
TILE = 256
L_TGT = 23
L_BASE = 46
L_BOOT = 49
L_S0 = 50
L_S1 = 51
L_VALID = 52
L_CNT = 53
VMEM_LIMIT = 60 * 1024 * 1024


def nn(a, b):
    return jnp.dot(a, b, preferred_element_type=F32)


def nt(a, b):
    return lax.dot_general(a, b, (((1,), (1,)), ((), ())), preferred_element_type=F32)


def tn(a, b):
    return lax.dot_general(a, b, (((0,), (0,)), ((), ())), preferred_element_type=F32)


def iota(shape, dim):
    return lax.broadcasted_iota(I32, shape, dim)


def split2(x):
    high = x.astype(BF16)
    return high, (x - high.astype(F32)).astype(BF16)


def split3(x):
    high = x.astype(BF16)
    rest = x - high.astype(F32)
    mid = rest.astype(BF16)
    return high, mid, (rest - mid.astype(F32)).astype(BF16)


def swish(values):
    return values * jax.nn.sigmoid(values)


class Plan:
    def __init__(self, mesh):
        self.n_dp, self.n_mp = mesh.shape["dp"], mesh.shape["mp"]
        self.n = self.n_dp * self.n_mp
        self.groups = self.n // CRIT
        self.workers = self.groups * CRIT
        self.turns = -(-self.n // self.groups)

    def rank(self, dp, mp):
        size = 4 * self.n_dp
        layer = mp // 4
        inner = dp * 4 + (mp % 4 + 2 * (dp % 2)) % 4
        if self.n != 32:
            return layer * size + inner
        far, near = layer // 2, jnp.logical_or(layer == 1, layer == 2)
        six = 24 + 3 * far + jnp.where(near, 2, 0)
        seven = jnp.where(near, 30 + far, 25 + 3 * far)
        return jnp.where(inner < 6, 6 * layer + inner, jnp.where(inner == 6, six, seven))

    def place(self, k):
        size = 4 * self.n_dp
        if self.n != 32:
            layer, inner = k // size, k % size
        else:
            extra = jnp.maximum(k - 24, 0)
            which, j = extra // 3, extra % 3
            layer = jnp.where(which == 0, j // 2, jnp.where(which == 1, 3 - j // 2, 1 + j))
            inner = jnp.where(which == 2, 7, 6 + j % 2)
            layer = jnp.where(k < 24, k // 6, layer)
            inner = jnp.where(k < 24, k % 6, inner)
        dp = inner // 4
        return dp, layer * 4 + (inner % 4 + 2 * (dp % 2)) % 4

    def device(self, s):
        return s // self.n_mp, s % self.n_mp

    @property
    def sets(self):
        return 4 if self.n == 32 else CRIT // 2

    def extra(self, q, group):
        if self.n != 32:
            return jnp.int32(-1)
        low = jnp.where(group < 2, q == 0, q == 1)
        high = jnp.where(group < 2, q == 3, q == 2)
        return jnp.where(low, 8, jnp.where(high, 9, -1))

    def shift(self, k):
        at = lambda c, r: sum(int(v) * m for v, m in zip(self.place(jnp.int32(c * self.groups + r)), (self.n_mp, 1)))
        with jax.ensure_compile_time_eval():
            return [(at(c, r), at(c, (r + k) % self.groups)) for c in range(CRIT) for r in range(self.groups)]

    def pairs(self, rows):
        per = -(-rows // self.groups)
        return -(-per // 32) * 16

    def cap(self, rows):
        return -(-(self.n * -(-rows // self.groups)) // TILE) * TILE


def chunks_of(columns):
    width = math.gcd(math.gcd(columns, H), HALF)
    return width, columns // width, H // width


def assemble(chunks_ref, width, shift):
    groups = []
    lane = iota((32, LANES), 1)
    for g in range(H // LANES):
        block = jnp.zeros((32, LANES), F32)
        for i in range(LANES // width):
            chunk = chunks_ref[g * (LANES // width) + i]
            turn = (i * width - shift) % LANES
            moved = pltpu.roll(chunk, turn, 1) if turn else chunk
            block = jnp.where(lane // width == i, moved, block)
        groups.append(block)
    return jnp.concatenate(groups, 1)


def all_barrier(plan, dp, mp):
    barrier = pltpu.get_barrier_semaphore()

    def tell(s, _):
        sdp, smp = s // plan.n_mp, s % plan.n_mp

        @pl.when(jnp.logical_or(sdp != dp, smp != mp))
        def _():
            pl.semaphore_signal(barrier, inc=1, device_id=(sdp, smp), device_id_type=MESH)

        return 0

    lax.fori_loop(0, plan.n, tell, 0)
    pl.semaphore_wait(barrier, plan.n - 1)


def dispatch_kernel(
    plan,
    crit_ref,
    targ_ref,
    crit_small,
    targ_small,
    head_ref,
    sa_ref,
    ns_ref,
    rows_ref,
    table_ref,
    pin_ref,
    pmid_ref,
    pout_ref,
    wt_ref,
    wc_ref,
    x_ref,
    p_ref,
    low,
    msg,
    wide,
    chunk,
    send_w,
    recv_w,
    pass_w,
    recv_c,
    send_x,
    recv_x,
    pass_x,
    send_p,
    recv_p,
    pass_p,
):
    dp, mp = lax.axis_index("dp"), lax.axis_index("mp")
    me = plan.rank(dp, mp)
    index = dp * plan.n_mp + mp
    groups, workers = plan.groups, plan.workers
    critic, group = me // groups, me % groups
    rw, cw = crit_ref.shape[1], crit_ref.shape[2]
    rows = sa_ref.shape[1]
    columns = crit_small[0].shape[1]
    width, mine, per = chunks_of(columns)

    def to_low(c, _):
        low[0, c] = targ_ref[c].astype(BF16)
        low[1, c] = crit_ref[c].astype(BF16)
        return 0

    lax.fori_loop(0, CRIT, to_low, 0)
    all_barrier(plan, dp, mp)

    def w_slot(s):
        sdp, smp = plan.device(s)
        return wt_ref.at[pl.ds(pl.multiple_of(smp * rw, rw), rw), pl.ds(pl.multiple_of(sdp * cw, cw), cw)]

    def to_worker(src, dst, send, recv, k):
        return pltpu.make_async_remote_copy(
            src_ref=src, dst_ref=dst, send_sem=send, recv_sem=recv, device_id=plan.place(k), device_id_type=MESH
        )

    turn = index // groups

    def first_hop(t, c):
        k = c * groups + index % groups
        dst = w_slot(index) if t == 0 else wc_ref.at[turn]
        recv = recv_w.at[index] if t == 0 else recv_c.at[turn]
        return k, dst, recv, to_worker(low.at[t, c], dst, send_w.at[t, c], recv, k)

    def send_weights(t):
        def one(i, _):
            c = (critic + i) % CRIT
            k, dst, recv, copy = first_hop(t, c)

            @pl.when(k == me)
            def _():
                pltpu.make_async_copy(low.at[t, c], dst, recv).start()

            @pl.when(k != me)
            def _():
                copy.start()

            return 0

        lax.fori_loop(0, CRIT, one, 0)

    send_weights(0)

    wide[...] = jnp.zeros_like(wide)
    for t, parts in enumerate((targ_small, crit_small)):
        wide[t, 0:IN, 0:columns] = parts[0][...]
        wide[t, IN : IN + 4, 0:columns] = parts[1][...]
        wide[t, IN + 4 : IN + 5, 0:columns] = head_ref[t : t + 1, :]
    for j in range(mine):
        start, offset = j * width // LANES * LANES, j * width % LANES
        both = [wide[t, :, start : start + LANES] for t in range(2)]
        turned = [pltpu.roll(v, turn, 1) if turn else v for v, turn in zip(both, ((-offset) % LANES, (HALF - offset) % LANES))]
        chunk[j] = jnp.where(iota((32, LANES), 1) < HALF, turned[0], turned[1])

    def small_hop(j):
        g = index * mine + j
        k = (g // per) * groups + g % groups
        return k, g % per, to_worker(chunk.at[j], p_ref.at[g % per], send_p.at[j], recv_p.at[g % per], k)

    def send_small(j, _):
        k, slot, copy = small_hop(j)

        @pl.when(k == me)
        def _():
            pltpu.make_async_copy(chunk.at[j], p_ref.at[slot], recv_p.at[slot]).start()

        @pl.when(k != me)
        def _():
            copy.start()

        return 0

    lax.fori_loop(0, mine, send_small, 0)

    lane = iota((rows, LANES), 1)
    place = lambda height, offset: (iota((height, LANES), 1) == iota((height, LANES), 0) + offset).astype(F32).astype(BF16)
    hidden = swish(tn(ns_ref[...], pin_ref[...])).astype(BF16)
    hidden = swish(nn(hidden, pmid_ref[...])).astype(BF16)
    pout = pout_ref[...]
    spread = lambda offset: tn(
        pout, (iota((2 * ACT, LANES), 0) == iota((2 * ACT, LANES), 1) + offset).astype(F32).astype(BF16)
    ).astype(BF16)
    keep = lane < ACT
    means = nn(hidden, spread(0))
    raw = nn(hidden, spread(ACT))
    facts = rows_ref[...]
    across = jnp.transpose(facts)
    picked = (iota((rows, table_ref.shape[1]), 1) == across[:, 2:3].astype(I32)).astype(F32).astype(BF16)
    noise = jnp.zeros((rows, LANES), F32)
    for part in split3(table_ref[...]):
        noise = noise + nn(picked, tn(part, place(ACT, 0)).astype(BF16))
    log_std = -5.0 + 3.5 * (jnp.tanh(raw) + 1.0)
    squashed = means + jnp.exp(log_std) * noise
    action = jnp.tanh(squashed).astype(BF16)
    twice = -2.0 * squashed
    softplus = jnp.maximum(twice, 0.0) + jnp.log(1.0 + jnp.exp(-jnp.abs(twice)))
    correction = 2.0 * (math.log(2.0) - squashed - softplus)
    density = jnp.sum(
        jnp.where(keep, -0.5 * noise * noise - log_std - 0.5 * math.log(2.0 * math.pi) - correction, 0.0), -1, keepdims=True
    )
    done = across[:, 1:2]
    boot = (done == 0.0).astype(F32)
    base = across[:, 0:1] - (REWARD_DISCOUNT * ENTROPY_TEMP) * boot * density
    high, mid, rest = split3(base)
    on = lambda k, value: jnp.where(lane == k, value, 0.0)
    features = (
        tn(sa_ref[...], place(IN, 0))
        + tn(ns_ref[...], place(OBS, L_TGT))
        + nn(jnp.where(keep, action.astype(F32), 0.0).astype(BF16), place(LANES, L_TGT + OBS))
        + on(L_BASE, high.astype(F32))
        + on(L_BASE + 1, mid.astype(F32))
        + on(L_BASE + 2, rest.astype(F32))
        + on(L_BOOT, boot)
        + on(L_S0, across[:, 3:4])
        + on(L_S1, across[:, 4:5])
        + on(L_VALID, 1.0)
    ).astype(BF16)

    pairs = msg.shape[1]
    valid = (facts[1:2, :] != 2.0).astype(F32)
    before = (iota((rows, rows), 0) < iota((rows, rows), 1)).astype(F32).astype(BF16)
    order = nn(jnp.broadcast_to(valid, (8, rows)).astype(BF16), before)[0:1, :]
    order = jnp.where(valid > 0.0, order, -1.0)
    count = jnp.sum(valid, -1, keepdims=True)
    count_half = jnp.floor(count * 0.5)
    mlane = iota((pairs, LANES), 1)
    tail = jnp.where(mlane == L_CNT, count_half, 0.0) + jnp.where(mlane == L_CNT + 1, count - 2.0 * count_half, 0.0)

    def deal(r, _):
        slot = iota((pairs, rows), 0) * (2 * groups) + r
        halves = []
        for h in range(2):
            hot = (order == (slot + h * groups).astype(F32)).astype(F32).astype(BF16)
            halves.append(nn(hot, features))
        msg[r] = (halves[0] + pltpu.roll(halves[1], HALF, 1) + tail).astype(BF16)
        return 0

    lax.fori_loop(0, groups, deal, 0)

    def row_hop(i):
        r = i % groups
        k = (2 * (i // groups) + index % 2) * groups + r
        return r, k, to_worker(msg.at[r], x_ref.at[index], send_x.at[i], recv_x.at[index], k)

    hops = plan.sets * groups

    def send_rows(i, _):
        r, k, copy = row_hop((i + (critic // 2) * groups) % hops)

        @pl.when(k == me)
        def _():
            pltpu.make_async_copy(msg.at[r], x_ref.at[index], recv_x.at[index]).start()

        @pl.when(k != me)
        def _():
            copy.start()

        return 0

    lax.fori_loop(0, hops, send_rows, 0)
    send_weights(1)

    def peer(i):
        return critic * groups + (group + 1 + i) % groups

    def pass_weight(t, i):
        s = group + groups * t
        return to_worker(w_slot(s), w_slot(s), pass_w.at[t, i], recv_w.at[s], peer(i))

    def pass_small(slot, i):
        return to_worker(p_ref.at[slot], p_ref.at[slot], pass_p.at[slot // groups, i], recv_p.at[slot], peer(i))

    extra = plan.extra(critic // 2, group)

    def pass_rows(i, k, which):
        s = 2 * i + critic % 2
        return to_worker(x_ref.at[s], x_ref.at[s], pass_x.at[i, which], recv_x.at[s], k)

    def other_rows(i):
        return pass_rows(i, (critic + 1 - 2 * (critic % 2)) * groups + group, 0)

    def extra_rows(i):
        return pass_rows(i, extra * groups + group, 1)

    def arrived_w(s):
        pltpu.make_async_copy(low.at[0, 0], w_slot(s), recv_w.at[s]).wait()

    def arrived_x(s):
        pltpu.make_async_copy(msg.at[0], x_ref.at[s], recv_x.at[s]).wait()

    def arrived_p(slot):
        pltpu.make_async_copy(chunk.at[0], p_ref.at[slot], recv_p.at[slot]).wait()

    turns = (plan.n - group + groups - 1) // groups
    passes_rows = critic < 2 * plan.sets

    def peers(body):
        lax.fori_loop(0, groups - 1, lambda i, _: (body(i), 0)[1], 0)

    def each(count, body):
        lax.fori_loop(0, count, lambda i, _: (body(i), 0)[1], 0)

    @pl.when(me < workers)
    def _():
        def relay_weight(t):
            arrived_w(group + groups * t)
            peers(lambda i: pass_weight(t, i).start())

        each(turns, relay_weight)

        @pl.when(passes_rows)
        def _():
            def relay_rows(i):
                arrived_x(2 * i + critic % 2)
                other_rows(i).start()

                @pl.when(extra >= 0)
                def _():
                    extra_rows(i).start()

            each(plan.n // 2, relay_rows)

        def relay_small(slot):
            @pl.when((critic * per + slot) % groups == group)
            def _():
                arrived_p(slot)
                peers(lambda i: pass_small(slot, i).start())

        each(per, relay_small)

        def arrived(s):
            @pl.when(s % groups != group)
            def _():
                arrived_w(s)

            @pl.when(jnp.logical_not(jnp.logical_and(passes_rows, s % 2 == critic % 2)))
            def _():
                arrived_x(s)

        each(plan.n, arrived)

        def arrived_small(slot):
            @pl.when((critic * per + slot) % groups != group)
            def _():
                arrived_p(slot)

        each(per, arrived_small)
        each(turns, lambda t: pltpu.make_async_copy(low.at[1, 0], wc_ref.at[t], recv_c.at[t]).wait())
        each(turns, lambda t: peers(lambda i: pass_weight(t, i).wait_send()))

        @pl.when(passes_rows)
        def _():
            def passed_rows(i):
                other_rows(i).wait_send()

                @pl.when(extra >= 0)
                def _():
                    extra_rows(i).wait_send()

            each(plan.n // 2, passed_rows)

        def passed_small(slot):
            @pl.when((critic * per + slot) % groups == group)
            def _():
                peers(lambda i: pass_small(slot, i).wait_send())

        each(per, passed_small)

    def sent_weights(c):
        for t in range(2):
            k, _dst, _recv, copy = first_hop(t, c)

            @pl.when(k != me)
            def _():
                copy.wait_send()

    each(CRIT, sent_weights)

    def sent_small(j):
        k, _slot, copy = small_hop(j)

        @pl.when(k != me)
        def _():
            copy.wait_send()

    each(mine, sent_small)

    def sent_rows(i):
        _r, k, copy = row_hop(i)

        @pl.when(k != me)
        def _():
            copy.wait_send()

    each(hops, sent_rows)


def dispatch(plan, critic_hidden, target_hidden, critic_small, target_small, heads, rows_args, policy):
    rows = rows_args[0].shape[1]
    pairs = plan.pairs(rows)
    columns = critic_small[0].shape[1]
    _width, mine, per = chunks_of(columns)
    vmem = pl.BlockSpec(memory_space=pltpu.VMEM)
    anywhere = pl.BlockSpec(memory_space=pl.ANY)
    dma = pltpu.SemaphoreType.DMA
    return pl.pallas_call(
        functools.partial(dispatch_kernel, plan),
        out_shape=(
            jax.ShapeDtypeStruct((H, H), BF16),
            jax.ShapeDtypeStruct((plan.turns,) + critic_hidden.shape[1:], BF16),
            jax.ShapeDtypeStruct((plan.n, pairs, LANES), BF16),
            jax.ShapeDtypeStruct((per, 32, LANES), F32),
        ),
        in_specs=[vmem, vmem, (vmem,) * 2, (vmem,) * 2] + [vmem] * 8,
        out_specs=(anywhere,) * 4,
        scratch_shapes=[
            pltpu.VMEM((2,) + critic_hidden.shape, BF16),
            pltpu.VMEM((plan.groups, pairs, LANES), BF16),
            pltpu.VMEM((2, 32, -(-columns // LANES) * LANES), F32),
            pltpu.VMEM((mine, 32, LANES), F32),
            dma((2, CRIT)),
            dma((plan.n,)),
            dma((plan.turns, plan.groups - 1)),
            dma((plan.turns,)),
            dma((plan.sets * plan.groups,)),
            dma((plan.n,)),
            dma((plan.n // 2, 2)),
            dma((mine,)),
            dma((per,)),
            dma((-(-per // plan.groups), plan.groups - 1)),
        ],
        compiler_params=pltpu.CompilerParams(collective_id=0, has_side_effects=True, vmem_limit_bytes=VMEM_LIMIT),
        name="dispatch",
    )(critic_hidden, target_hidden, critic_small, target_small, heads, *rows_args, *policy)


def norm_parts(pre):
    centered = pre - jnp.sum(pre, -1, keepdims=True) * (1.0 / H)
    inv = lax.rsqrt(jnp.sum(centered * centered, -1, keepdims=True) * (1.0 / H) + 1e-05)
    return centered * inv, inv


def swish_parts(half):
    t = jnp.tanh(half)
    product = half * t
    return half + product, (1.0 + t) * (1.0 + (half - product))


def low_input(params):
    return jnp.where(iota((32, H), 0) < IN, params, 0.0).astype(BF16)


def tile_span(t):
    return pl.ds(pl.multiple_of(t * TILE, TILE), TILE)


def target_kernel(
    plan, width, role_ref, x_ref, w_ref, p_ref, xc_ref, q_ref, info_ref, rows_f, picked, value, hot, win, par, cnt_v, cnt_s, base_s, sem
):
    critic, group, active = role_ref[0], role_ref[1], role_ref[2]
    groups, n = plan.groups, plan.n
    pairs = x_ref.shape[1]
    first = x_ref[:, 0, :].astype(F32)
    lane = iota(first.shape, 1)
    counts = 2.0 * jnp.sum(jnp.where(lane == L_CNT, first, 0.0), -1, keepdims=True) + jnp.sum(
        jnp.where(lane == L_CNT + 1, first, 0.0), -1, keepdims=True
    )
    counts = jnp.where(active > 0, jnp.broadcast_to(counts, first.shape), 0.0)
    mine = jnp.floor((counts + (groups - 1 - group).astype(F32)) * (1.0 / groups) + 0.5 / groups)
    earlier = (iota((n, n), 1) < iota((n, n), 0)).astype(F32).astype(BF16)
    starts = nn(earlier, mine.astype(BF16))
    total = jnp.sum(counts, 0, keepdims=True)
    cnt_v[0:n, :] = mine.astype(I32)
    cnt_v[n : 2 * n, :] = starts.astype(I32)
    cnt_v[2 * n : 2 * n + 8, :] = jnp.broadcast_to(total, (8, LANES)).astype(I32)
    copy = pltpu.make_async_copy(cnt_v, cnt_s, sem)
    copy.start()
    par[...] = assemble(p_ref, width, 0)
    win[...] = jnp.zeros_like(win)
    win[0:32, :] = low_input(par[...])
    copy.wait()
    number = cnt_s[n - 1, 0] + cnt_s[2 * n - 1, 0]
    tiles = (number + TILE - 1) // TILE
    info_ref[0] = number
    info_ref[1] = cnt_s[2 * n, 0]

    def compact(s, _):
        block = x_ref[s].astype(F32)
        have, start = cnt_s[s, 0], cnt_s[n + s, 0]
        rows_f[pl.ds(start, pairs), :] = block
        rows_f[pl.ds(start + (have + 1) // 2, pairs), :] = pltpu.roll(block, HALF, 1)
        return 0

    @pl.when(active > 0)
    def _():
        lax.fori_loop(0, n, compact, 0)

    rows_f[pl.ds(number, TILE), :] = jnp.zeros((TILE, LANES), F32)

    until = (iota((TILE, TILE), 1) < iota((TILE, TILE), 0)).astype(F32).astype(BF16)
    place = iota((TILE, TILE), 1).astype(F32)
    this = critic.astype(F32)

    def choose(t, base):
        wide = rows_f[tile_span(t), :]
        x = wide.astype(BF16)
        xc_ref[tile_span(t), :] = x
        wanted = jnp.logical_or(wide[:, L_S0 : L_S0 + 1] == this, wide[:, L_S1 : L_S1 + 1] == this)
        wanted = jnp.where(jnp.logical_and(wanted, wide[:, L_BOOT : L_BOOT + 1] > 0.0), 1.0, 0.0)
        order = nn(until, jnp.broadcast_to(wanted, (TILE, LANES)).astype(BF16))[:, 0:1]
        chosen = (jnp.where(wanted > 0.0, order, -1.0) == place).astype(F32).astype(BF16)
        hot[t] = chosen
        picked[pl.ds(base, TILE), :] = tn(chosen, x)
        base_s[t] = base
        return base + jnp.sum(wanted).astype(I32)

    chosen_rows = lax.fori_loop(0, tiles, choose, 0)
    picked[pl.ds(chosen_rows, TILE), :] = jnp.zeros((TILE, LANES), F32)
    chosen_tiles = (chosen_rows + TILE - 1) // TILE
    half = jnp.where(iota((32, 1), 0) < IN + 4, 0.5, 1.0)
    par[...] = par[...] * half
    gain1, shift1, gain2, shift2, head = (par[IN + k : IN + k + 1, :] for k in range(5))

    def tile(t, _):
        x = pltpu.roll(picked[tile_span(t), :], LANES - L_TGT, 1).astype(BF16)
        z, _unused = norm_parts(nn(x, win[...]))
        y = z * gain1 + shift1
        act = (y + y * jnp.tanh(y)).astype(BF16)
        z, _unused = norm_parts(nn(act, w_ref[...]))
        y = z * gain2 + shift2
        q = jnp.sum((y + y * jnp.tanh(y)) * head, -1, keepdims=True)
        value[tile_span(t), :] = jnp.broadcast_to(q, (TILE, LANES))
        return 0

    lax.fori_loop(0, chosen_tiles, tile, 0)
    value[tile_span(chosen_tiles), :] = jnp.zeros((TILE, LANES), F32)

    def spread(t, _):
        lane = iota((TILE, LANES), 1)
        high, mid, rest = (v.astype(F32) for v in split3(value[pl.ds(base_s[t], TILE), :]))
        parts = jnp.where(lane == 0, high, jnp.where(lane == 1, mid, jnp.where(lane == 2, rest, 0.0)))
        q = jnp.broadcast_to(jnp.sum(nn(hot[t], parts.astype(BF16)), -1, keepdims=True), (TILE, LANES))
        for h in range(TILE // LANES):
            flat = jnp.transpose(q[h * LANES : (h + 1) * LANES, :])
            q_ref[pl.ds(t * (TILE // LANES) + h, 1), :] = flat[0:1, :]
        return 0

    lax.fori_loop(0, tiles, spread, 0)


def target_values(plan, rows, width, role, x, weights, params):
    capacity = plan.cap(rows)
    vmem = pl.BlockSpec(memory_space=pltpu.VMEM)
    smem = pl.BlockSpec(memory_space=pltpu.SMEM)
    return pl.pallas_call(
        functools.partial(target_kernel, plan, width),
        out_shape=(
            jax.ShapeDtypeStruct((capacity, LANES), BF16),
            jax.ShapeDtypeStruct((capacity // LANES, LANES), F32),
            jax.ShapeDtypeStruct((2,), I32),
        ),
        in_specs=[smem, vmem, vmem, vmem],
        out_specs=(vmem, vmem, smem),
        scratch_shapes=[
            pltpu.VMEM((capacity + TILE + x.shape[1], LANES), F32),
            pltpu.VMEM((capacity + TILE, LANES), F32),
            pltpu.VMEM((capacity + TILE, LANES), F32),
            pltpu.VMEM((capacity // TILE, TILE, TILE), BF16),
            pltpu.VMEM((LANES, H), BF16),
            pltpu.VMEM((32, H), F32),
            pltpu.VMEM((2 * plan.n + 8, LANES), I32),
            pltpu.SMEM((2 * plan.n + 8, LANES), I32),
            pltpu.SMEM((capacity // TILE,), I32),
            pltpu.SemaphoreType.DMA,
        ],
        compiler_params=pltpu.CompilerParams(vmem_limit_bytes=VMEM_LIMIT),
        name="target_values",
    )(role, x, weights, params)


def share_kernel(plan, q_ref, all_ref, send, recv):
    dp, mp = lax.axis_index("dp"), lax.axis_index("mp")
    me = plan.rank(dp, mp)
    groups = plan.groups
    critic, group = me // groups, me % groups
    barrier = pltpu.get_barrier_semaphore()

    @pl.when(me < plan.workers)
    def _():
        def peer(i):
            other = (critic + i) % CRIT
            return other, plan.place(other * groups + group)

        def tell(i, _):
            pl.semaphore_signal(barrier, inc=1, device_id=peer(i)[1], device_id_type=MESH)
            return 0

        lax.fori_loop(1, CRIT, tell, 0)
        pl.semaphore_wait(barrier, CRIT - 1)
        all_ref[critic] = q_ref[...]

        def copy(i):
            other, device = peer(i)
            return pltpu.make_async_remote_copy(
                src_ref=q_ref,
                dst_ref=all_ref.at[critic],
                send_sem=send.at[other],
                recv_sem=recv.at[critic],
                device_id=device,
                device_id_type=MESH,
            )

        def start(i, _):
            copy(i).start()
            return 0

        lax.fori_loop(1, CRIT, start, 0)

        def finish(i, _):
            copy(i).wait_send()
            other = peer(i)[0]
            pltpu.make_async_copy(q_ref, all_ref.at[other], recv.at[other]).wait()
            return 0

        lax.fori_loop(1, CRIT, finish, 0)


def share_values(plan, q):
    vmem = pl.BlockSpec(memory_space=pltpu.VMEM)
    return pl.pallas_call(
        functools.partial(share_kernel, plan),
        out_shape=jax.ShapeDtypeStruct((CRIT,) + q.shape, F32),
        in_specs=[vmem],
        out_specs=vmem,
        scratch_shapes=[pltpu.SemaphoreType.DMA((CRIT,)), pltpu.SemaphoreType.DMA((CRIT,))],
        compiler_params=pltpu.CompilerParams(collective_id=1, has_side_effects=True, vmem_limit_bytes=VMEM_LIMIT),
        name="share_values",
    )(q)


def critic_kernel(
    plan, width, role_ref, info_ref, xc_ref, q_ref, shares, p_ref, grad_ref, small_ref, sums_ref, w_ref, z_one, slope, act, low, fact, par, win, picks, acc
):
    number = info_ref[0]
    scale = 2.0 / jnp.maximum(info_ref[1], 1).astype(F32)
    tiles = (number + TILE - 1) // TILE
    rw, cw = shares[0].shape[1:]
    for k, share in enumerate(shares):
        owner = (role_ref[1] + plan.groups - k) % plan.groups

        def gather(t, _):
            s = owner + plan.groups * t

            @pl.when(s < plan.n)
            def _():
                sdp, smp = plan.device(s)
                w_ref[pl.ds(pl.multiple_of(smp * rw, rw), rw), pl.ds(pl.multiple_of(sdp * cw, cw), cw)] = share[t]

            return 0

        lax.fori_loop(0, plan.turns, gather, 0)
    par[...] = assemble(p_ref, width, HALF)
    win[...] = jnp.zeros_like(win)
    win[0:32, :] = low_input(par[...])
    grad_ref[...] = jnp.zeros_like(grad_ref)
    acc[...] = jnp.zeros_like(acc)
    picks[...] = jnp.zeros_like(picks)
    sums_ref[...] = jnp.zeros_like(sums_ref)
    gain1, shift1, gain2, shift2, head = (par[IN + k : IN + k + 1, :] for k in range(5))

    def fold(k, value):
        acc[32 + k * 8 : 40 + k * 8, :] += jnp.sum(value.reshape(TILE // 8, 8, H), 0)

    def tile(t, _):
        x = xc_ref[tile_span(t), :]
        wide = x.astype(F32)
        for h in range(TILE // LANES):
            picks[0:CRIT, :] = q_ref[:, pl.ds(t * (TILE // LANES) + h, 1), :].reshape(CRIT, LANES)
            table = jnp.transpose(picks[...])
            part = wide[h * LANES : (h + 1) * LANES, :]
            critic = iota(table.shape, 1).astype(F32)
            one = jnp.sum(jnp.where(critic == part[:, L_S0 : L_S0 + 1], table, 0.0), -1, keepdims=True)
            two = jnp.sum(jnp.where(critic == part[:, L_S1 : L_S1 + 1], table, 0.0), -1, keepdims=True)
            base = part[:, L_BASE : L_BASE + 1] + part[:, L_BASE + 1 : L_BASE + 2] + part[:, L_BASE + 2 : L_BASE + 3]
            goal = base + jnp.where(part[:, L_BOOT : L_BOOT + 1] > 0.0, REWARD_DISCOUNT * jnp.minimum(one, two), 0.0)
            fact[h * LANES : (h + 1) * LANES, 0:1] = goal
        z, inv_one = norm_parts(nn(x, win[...]))
        z_one[...] = z
        value, twice = swish_parts(z * (0.5 * gain1) + 0.5 * shift1)
        slope[...] = 0.5 * twice
        act[...] = value.astype(BF16)
        z, inv = norm_parts(nn(act[...], w_ref[...]))
        value, twice = swish_parts(z * (0.5 * gain2) + 0.5 * shift2)
        q = jnp.sum(value * head, -1, keepdims=True)
        error = (q - fact[:, 0:1]) * wide[:, L_VALID : L_VALID + 1]
        sums_ref[0:1, :] += jnp.broadcast_to(jnp.sum(error * error, 0, keepdims=True), (1, LANES))
        dq = error * scale
        fold(4, dq * value)
        dy = dq * (twice * (0.5 * head))
        fold(3, dy)
        fold(2, dy * z)
        dz = dy * gain2
        mean = jnp.sum(dz, -1, keepdims=True) * (1.0 / H)
        along = jnp.sum(dz * z, -1, keepdims=True) * (1.0 / H)
        low[...] = (inv * (dz - mean - z * along)).astype(BF16)
        down = nt(low[...], w_ref[...])
        grad_ref[...] += tn(act[...], low[...])
        z = z_one[...]
        dy = down * slope[...]
        fold(1, dy)
        fold(0, dy * z)
        dz = dy * gain1
        mean = jnp.sum(dz, -1, keepdims=True) * (1.0 / H)
        along = jnp.sum(dz * z, -1, keepdims=True) * (1.0 / H)
        acc[0:32, :] += tn(x[:, 0:32], (inv_one * (dz - mean - z * along)).astype(BF16))
        return 0

    lax.fori_loop(0, tiles, tile, 0)
    sums_ref[1:2, :] = jnp.broadcast_to(info_ref[1].astype(F32), (1, LANES))
    for k in range(5):
        acc[IN + k : IN + k + 1, :] = jnp.sum(acc[32 + k * 8 : 40 + k * 8, :], 0, keepdims=True)
    for i in range(H // width):
        start, offset = i * width // LANES * LANES, i * width % LANES
        block = acc[0:32, start : start + LANES]
        small_ref[i] = pltpu.roll(block, LANES - offset, 1) if offset else block


def critic_step(plan, width, role, info, xc, q_all, shares, params):
    vmem = pl.BlockSpec(memory_space=pltpu.VMEM)
    smem = pl.BlockSpec(memory_space=pltpu.SMEM)
    return pl.pallas_call(
        functools.partial(critic_kernel, plan, width),
        out_shape=(
            jax.ShapeDtypeStruct((H, H), F32),
            jax.ShapeDtypeStruct((H // width, 32, LANES), F32),
            jax.ShapeDtypeStruct((8, LANES), F32),
        ),
        in_specs=[smem, smem, vmem, vmem, (vmem,) * plan.groups, vmem],
        out_specs=(vmem,) * 3,
        scratch_shapes=[
            pltpu.VMEM((H, H), BF16),
            pltpu.VMEM((TILE, H), F32),
            pltpu.VMEM((TILE, H), F32),
            pltpu.VMEM((TILE, H), BF16),
            pltpu.VMEM((TILE, H), BF16),
            pltpu.VMEM((TILE, LANES), F32),
            pltpu.VMEM((32, H), F32),
            pltpu.VMEM((LANES, H), BF16),
            pltpu.VMEM((16, LANES), F32),
            pltpu.VMEM((72, H), F32),
        ],
        compiler_params=pltpu.CompilerParams(vmem_limit_bytes=VMEM_LIMIT),
        name="critic_step",
    )(role, info, xc, q_all, shares, params)


PRECISE = 2


LAG = 3
AHEAD = 3


def shampoo_kernel(
    plan,
    g_ref,
    small_ref,
    sums_ref,
    mom_ref,
    left_ref,
    right_ref,
    w_ref,
    mo_ref,
    lo_ref,
    ro_ref,
    wo_ref,
    own_ref,
    out_ref,
    parts,
    pieces,
    given,
    shares,
    totals,
    send_one,
    recv_one,
    send_two,
    recv_two,
    send_s,
    recv_s,
    send_t,
    recv_t,
):
    dp, mp = lax.axis_index("dp"), lax.axis_index("mp")
    me = plan.rank(dp, mp)
    index = dp * plan.n_mp + mp
    groups, workers, n, turns = plan.groups, plan.workers, plan.n, plan.turns
    critic, group = me // groups, me % groups
    rw, cw = mom_ref.shape[1], mom_ref.shape[2]
    mine, per = shares.shape[1], small_ref.shape[0]
    columns = own_ref.shape[1]
    chunk_width = H // per
    all_barrier(plan, dp, mp)

    def to_device(src, dst, send, recv, device):
        return pltpu.make_async_remote_copy(
            src_ref=src, dst_ref=dst, send_sem=send, recv_sem=recv, device_id=device, device_id_type=MESH
        )

    def block(s):
        sdp, smp = plan.device(s)
        return pl.ds(pl.multiple_of(smp * rw, rw), rw), pl.ds(pl.multiple_of(sdp * cw, cw), cw)

    def turn_of(step):
        return (step + critic) % turns

    def first_hop(step, i):
        other = (group + 1 + i) % groups
        turn = turn_of(step)
        s = other + groups * turn
        copy = to_device(
            g_ref.at[block(s)],
            parts.at[groups - 2 - i, turn],
            send_one.at[step, i],
            recv_one.at[groups - 2 - i, turn],
            plan.place(critic * groups + other),
        )
        return s, copy

    def second_hop(turn):
        s = group + groups * turn
        return s, to_device(pieces.at[turn], given.at[critic], send_two.at[turn], recv_two.at[critic], plan.device(s))

    def small_hop(q):
        g = critic * per + q
        s = g // mine
        return s, to_device(
            small_ref.at[q], shares.at[group, g % mine], send_s.at[q], recv_s.at[group, g % mine], plan.device(s)
        )

    def total_hop(s):
        return to_device(sums_ref, totals.at[me], send_t.at[s], recv_t.at[me], plan.device(s))

    def start_first(step):
        def one(i, _):
            s, copy = first_hop(step, i)

            @pl.when(s < n)
            def _():
                copy.start()

            return 0

        lax.fori_loop(0, groups - 1, one, 0)

    def start_rest():
        def start_small(q, _):
            s, copy = small_hop(q)

            @pl.when(s == index)
            def _():
                slot = (critic * per + q) % mine
                pltpu.make_async_copy(small_ref.at[q], shares.at[group, slot], recv_s.at[group, slot]).start()

            @pl.when(s != index)
            def _():
                copy.start()

            return 0

        lax.fori_loop(0, per, start_small, 0)
        totals[me] = sums_ref[...]

        def start_total(i, _):
            total_hop((index + i) % n).start()
            return 0

        lax.fori_loop(1, n, start_total, 0)

    @pl.when(me < workers)
    def _():
        for step in range(AHEAD):
            start_first(step)

    def add_up(step):
        turn = turn_of(step)
        s, copy = second_hop(turn)

        @pl.when(s < n)
        def _():
            for i in range(groups - 1):
                pltpu.make_async_copy(pieces.at[0], parts.at[i, turn], recv_one.at[i, turn]).wait()
            value = g_ref[block(s)]
            for i in range(groups - 1):
                value = value + parts[i, turn]
            pieces[turn] = value

            @pl.when(s == index)
            def _():
                pltpu.make_async_copy(pieces.at[turn], given.at[critic], recv_two.at[critic]).start()

            @pl.when(s != index)
            def _():
                copy.start()

    width = min(256, cw)
    halves = width // LANES
    high_rows = halves * BLK
    nr, nc = rw // BLK, cw // width
    subs = [(i, j) for i in range(nr) for j in range(nc)]
    mask = (iota((LANES, LANES), 0) // BLK == iota((LANES, LANES), 1) // BLK).astype(F32).astype(BF16)
    mask_wide = jnp.concatenate([mask] * halves, 1)
    eye = (iota((high_rows, LANES), 0) % BLK == iota((high_rows, LANES), 1) % BLK).astype(F32)
    eye_low = eye.astype(BF16)

    def packed(flat):
        return jnp.concatenate([flat[:, k * LANES : (k + 1) * LANES] for k in range(halves)], 0)

    def flat_of(x):
        return jnp.concatenate([x[k * BLK : (k + 1) * BLK] for k in range(halves)], 1)

    def tops(out, count):
        return [
            jnp.concatenate(
                [out[(i * halves + k) * BLK : (i * halves + k + 1) * BLK, k * LANES : (k + 1) * LANES] for k in range(halves)], 0
            )
            for i in range(count)
        ]

    def diag(x):
        return jnp.concatenate([flat_of(x)] * (LANES // BLK), 0) * mask_wide

    def diag_rows(x):
        tiled = [jnp.concatenate([x[k * BLK : (k + 1) * BLK]] * (LANES // BLK), 0) * mask for k in range(halves)]
        return jnp.concatenate(tiled, 0)

    def products(lhs, right):
        return tops(nn(jnp.concatenate(lhs, 0), right), len(lhs))

    def precise(parts, right, right_rest):
        high, rest = parts
        out = products([high, rest], right)
        return out[0] + out[1] + products([high], right_rest)[0]

    def block_sums(s):
        high, rest = split2(s)
        return nn(high, mask) + nn(rest, mask)

    def place(c, i, j):
        return (c, slice(i * BLK, (i + 1) * BLK), slice(j * width, (j + 1) * width))

    def column_sums(x):
        return [jnp.sum(x[k * BLK : (k + 1) * BLK].reshape(BLK // 8, 8, LANES), 0) for k in range(halves)]

    def over_blocks(total, spot):
        rows = [jnp.sum(total[(spot + k) * 8 : (spot + k + 1) * 8], 0, keepdims=True) for k in range(halves)]
        return jnp.concatenate([jnp.broadcast_to(row, (BLK, LANES)) for row in rows], 0)

    def blocked(c):
        pltpu.make_async_copy(pieces.at[0], given.at[c], recv_two.at[c]).wait()
        sums, stats = [], []
        for i, j in subs:
            at = place(c, i, j)
            grad = given[at]
            mo_ref[at] = MOMENTUM * mom_ref[at] + grad
            low = packed(grad.astype(BF16))
            square, flip = tops(nt(jnp.concatenate([low, eye_low], 0), diag_rows(low)), 2)
            left = STAT_DECAY * packed(left_ref[at]) + (1.0 - STAT_DECAY) * square
            right = products([flip.astype(BF16)], diag(low))[0]
            right = STAT_DECAY * packed(right_ref[at]) + (1.0 - STAT_DECAY) * right
            lo_ref[at] = flat_of(left)
            ro_ref[at] = flat_of(right)
            for stat in (left, right):
                stats.append(stat)
                sums += column_sums(stat * stat)
        total = block_sums(jnp.concatenate(sums, 0))
        chains = []
        for k, stat in enumerate(stats):
            inv = lax.rsqrt(over_blocks(total, k * halves))
            rest = (eye - stat * inv) * 0.25
            chains.append([rest, eye + rest, jnp.sqrt(jnp.sqrt(inv))])
        for it in range(NEWTON - 1):
            full = it < PRECISE
            squares = []
            for ch in chains:
                high, rest = split2(ch[0])
                lhs = [high] + ([rest] if full else []) + ([ch[1].astype(BF16)] if it > 0 else [])
                out = products(lhs, diag(high))
                power = out[0]
                if full:
                    power = power + out[1] + products([high], diag(rest))[0]
                if it > 0:
                    ch[1] = ch[1] + out[-1]
                squares.append(power)
            factors = [[diag(v) for v in split2(power)[: 2 if full else 1]] for power in squares]

            def times(x, right):
                parts = split2(x)
                return precise(parts, *right) if full else products([parts[0]], right[0])[0]

            terms = [
                5.0 * ch[0] + 3.75 * power + times(ch[0], right) for ch, power, right in zip(chains, squares, factors)
            ]
            for ch, power, right, term in zip(chains, squares, factors, terms):
                ch[0] = 2.5 * power + times(term, right)
        for ch in chains:
            ch[1] = ch[1] + products([ch[1].astype(BF16)], diag(ch[0].astype(BF16)))[0]
        steps, sums = [], []
        for k, (i, j) in enumerate(subs):
            lc, rc = chains[2 * k], chains[2 * k + 1]
            moment = split2(packed(mo_ref[place(c, i, j)]))
            roots = split2(rc[1])
            step = precise(split2(lc[1]), diag(moment[0]), diag(moment[1]))
            step = precise(split2(step), diag(roots[0]), diag(roots[1])) * (lc[2] * rc[2])
            steps.append(step)
            sums += column_sums(step * step)
        total = block_sums(jnp.concatenate(sums, 0)) * (1.0 / (BLK * BLK))
        for k, (i, j) in enumerate(subs):
            at = place(c, i, j)
            old = w_ref[at]
            step = flat_of(steps[k] * lax.rsqrt(over_blocks(total, k * halves) + 1e-06))
            wo_ref[at] = old - RATE_HIDDEN * (step + WEIGHT_DECAY * old)

    def round_(i, _):
        @pl.when(jnp.logical_and(me < workers, i < turns))
        def _():
            @pl.when(i + AHEAD < turns)
            def _():
                start_first(i + AHEAD)

            @pl.when(i == LAG)
            def _():
                start_rest()

            add_up(i)

        c = (index // groups + 2 * turns + LAG - i) % turns

        @pl.when(jnp.logical_and(i >= LAG, c < CRIT))
        def _():
            blocked(c)

        return 0

    lax.fori_loop(0, turns + LAG, round_, 0)

    def arrived_small(i, _):
        pltpu.make_async_copy(small_ref.at[0], shares.at[i // mine, i % mine], recv_s.at[i // mine, i % mine]).wait()
        return 0

    lax.fori_loop(0, groups * mine, arrived_small, 0)
    for g in range(columns // LANES):
        part = jnp.zeros((32, LANES), F32)
        for j in range(mine):
            if j * chunk_width // LANES == g:
                value = shares[0, j]
                for r in range(1, groups):
                    value = value + shares[r, j]
                turn = j * chunk_width % LANES
                moved = pltpu.roll(value, turn, 1) if turn else value
                part = jnp.where(iota((32, LANES), 1) // chunk_width == turn // chunk_width, moved, part)
        own_ref[:, g * LANES : (g + 1) * LANES] = part

    def arrived_total(k, _):
        @pl.when(k != me)
        def _():
            pltpu.make_async_copy(sums_ref, totals.at[k], recv_t.at[k]).wait()

        return 0

    lax.fori_loop(0, workers, arrived_total, 0)
    out_ref[0:1, :] = jnp.sum(totals[:, 0, :], 0, keepdims=True)
    out_ref[1:2, :] = totals[0, 1:2, :]
    out_ref[2:8, :] = jnp.zeros((6, LANES), F32)

    @pl.when(me < workers)
    def _():
        def finish(step, _):
            def one(i, _):
                s, copy = first_hop(step, i)

                @pl.when(s < n)
                def _():
                    copy.wait_send()

                return 0

            lax.fori_loop(0, groups - 1, one, 0)
            s, copy = second_hop(step)

            @pl.when(jnp.logical_and(s < n, s != index))
            def _():
                copy.wait_send()

            return 0

        lax.fori_loop(0, turns, finish, 0)

        def finish_small(q, _):
            s, copy = small_hop(q)

            @pl.when(s != index)
            def _():
                copy.wait_send()

            return 0

        lax.fori_loop(0, per, finish_small, 0)

        def finish_total(i, _):
            total_hop((index + i) % n).wait_send()
            return 0

        lax.fori_loop(1, n, finish_total, 0)


def shampoo(plan, columns, grad, small, sums, moment, left, right, weight):
    vmem = pl.BlockSpec(memory_space=pltpu.VMEM)
    shape = jax.ShapeDtypeStruct(moment.shape, F32)
    _width, mine, per = chunks_of(columns)
    piece = moment.shape[1:]
    dma = pltpu.SemaphoreType.DMA
    return pl.pallas_call(
        functools.partial(shampoo_kernel, plan),
        out_shape=(shape,) * 4
        + (jax.ShapeDtypeStruct((32, -(-columns // LANES) * LANES), F32), jax.ShapeDtypeStruct((8, LANES), F32)),
        in_specs=[vmem] * 7,
        out_specs=(vmem,) * 6,
        scratch_shapes=[
            pltpu.VMEM((plan.groups - 1, plan.turns) + piece, F32),
            pltpu.VMEM((plan.turns,) + piece, F32),
            pltpu.VMEM((CRIT,) + piece, F32),
            pltpu.VMEM((plan.groups, mine, 32, LANES), F32),
            pltpu.VMEM((plan.workers, 8, LANES), F32),
            dma((plan.turns, plan.groups - 1)),
            dma((plan.groups - 1, plan.turns)),
            dma((plan.turns,)),
            dma((CRIT,)),
            dma((per,)),
            dma((plan.groups, mine)),
            dma((plan.n,)),
            dma((plan.workers,)),
        ],
        compiler_params=pltpu.CompilerParams(collective_id=2, has_side_effects=True, vmem_limit_bytes=VMEM_LIMIT),
        name="shampoo",
    )(grad, small, sums, moment, left, right, weight)


def adamw(grad, moment, square, weight, rate):
    moment_new = FIRST_DECAY * moment + (1.0 - FIRST_DECAY) * grad
    square_new = SECOND_DECAY * square + (1.0 - SECOND_DECAY) * grad * grad
    moment_hat = moment_new / (1.0 - FIRST_DECAY**STEP)
    square_hat = square_new / (1.0 - SECOND_DECAY**STEP)
    weight_new = weight - rate * (moment_hat / (jnp.sqrt(square_hat) + 1e-08) + WEIGHT_DECAY * weight)
    return (moment_new, square_new, weight_new)


def local(
    plan,
    state_action,
    next_state,
    reward,
    done_flags,
    noise_index,
    noise_table,
    subsets,
    policy_in,
    policy_mid,
    policy_out,
    critic_in,
    in_first,
    in_second,
    critic_norms,
    norm_first,
    norm_second,
    critic_head,
    head_first,
    head_second,
    critic_hidden,
    hidden_moment,
    left_stats,
    right_stats,
    target_in,
    target_norms,
    target_head,
    target_hidden,
):
    me = plan.rank(lax.axis_index("dp"), lax.axis_index("mp"))
    critic, group = me // plan.groups, me % plan.groups
    role = jnp.stack([critic, group, (me < plan.workers).astype(I32)])
    rows, columns = state_action.shape[0], critic_in.shape[1]
    width = chunks_of(columns)[0]
    facts = jnp.concatenate(
        [reward[None], jnp.stack([done_flags, noise_index, subsets[:, 0], subsets[:, 1]]).astype(F32), jnp.zeros((3, rows), F32)], 0
    )
    w_target, share, x, params = dispatch(
        plan,
        critic_hidden,
        target_hidden,
        (critic_in, critic_norms),
        (target_in, target_norms),
        jnp.stack([target_head, critic_head]),
        (state_action.T, next_state.T, facts),
        (noise_table.T, policy_in, policy_mid, policy_out.T),
    )
    shares = (share,) + tuple(lax.ppermute(share, ("dp", "mp"), plan.shift(k)) for k in range(1, plan.groups))
    xc, q, info = target_values(plan, rows, width, role, x, w_target, params)
    q_all = share_values(plan, q)
    grad_hidden, grad_small, sums = critic_step(plan, width, role, info, xc, q_all, shares, params)
    hidden_momentum, left_renewed, right_renewed, hidden_updated, own, totals = shampoo(
        plan, columns, grad_hidden, grad_small, sums, hidden_moment, left_stats, right_stats, critic_hidden
    )
    own = own[:, :columns]
    loss_total, counted = totals[0, 0], totals[1, 0]
    in_moment, in_square, in_updated = adamw(own[:IN], in_first, in_second, critic_in, RATE_INPUT)
    norm_moment, norm_square, norm_updated = adamw(own[IN : IN + 4], norm_first, norm_second, critic_norms, RATE_NORMS)
    head_moment, head_square, head_updated = adamw(own[IN + 4], head_first, head_second, critic_head, RATE_HEAD)
    return (
        loss_total,
        counted,
        in_moment,
        in_square,
        in_updated,
        norm_moment,
        norm_square,
        norm_updated,
        head_moment,
        head_square,
        head_updated,
        hidden_momentum,
        left_renewed,
        right_renewed,
        hidden_updated,
    )


def solution(mesh):
    both = ("dp", "mp")
    rows, columns, flat, hidden = P(both, None), P(None, both), P(both), P(None, "mp", "dp")
    return jax.shard_map(
        functools.partial(local, Plan(mesh)),
        mesh=mesh,
        in_specs=(
            (rows, rows, flat, flat, flat, P(), rows, P(), P(), P())
            + (columns,) * 6
            + (flat,) * 3
            + (hidden,) * 4
            + (columns, columns, flat, hidden)
        ),
        out_specs=(P(), P()) + (columns,) * 6 + (flat,) * 3 + (hidden,) * 4,
        check_vma=False,
    )
```

```python
import functools
import math

import jax
import jax.numpy as jnp
from jax import lax
from jax.experimental import pallas as pl
from jax.experimental.pallas import tpu as pltpu
from jax.sharding import PartitionSpec as P

ACT = 6
OBS = 17
IN = 23
H = 1024
CRIT = 10
BLK = 32
NEWTON = 5
STEP = 10
REWARD_DISCOUNT = 0.99
ENTROPY_TEMP = 0.2
FIRST_DECAY = 0.9
SECOND_DECAY = 0.999
WEIGHT_DECAY = 0.01
RATE_INPUT = 0.1
RATE_NORMS = 0.3
RATE_HEAD = 0.03
RATE_HIDDEN = 0.01
MOMENTUM = 0.9
STAT_DECAY = 0.95

F32, BF16, I32 = jnp.float32, jnp.bfloat16, jnp.int32
MESH = pl.DeviceIdType.MESH
LANES = 128
HALF = 64
TILE = 256
AHEAD_TILES = 4
L_TGT = 23
L_BASE = 46
L_BOOT = 49
L_S0 = 50
L_S1 = 51
L_VALID = 52
L_CNT = 53
MIB = 1024 * 1024


def nn(a, b):
    return jnp.dot(a, b, preferred_element_type=F32)


def nt(a, b):
    return lax.dot_general(a, b, (((1,), (1,)), ((), ())), preferred_element_type=F32)


def tn(a, b):
    return lax.dot_general(a, b, (((0,), (0,)), ((), ())), preferred_element_type=F32)


def iota(shape, dim):
    return lax.broadcasted_iota(I32, shape, dim)


def split2(x):
    high = x.astype(BF16)
    return high, (x - high.astype(F32)).astype(BF16)


def split3(x):
    high = x.astype(BF16)
    rest = x - high.astype(F32)
    mid = rest.astype(BF16)
    return high, mid, (rest - mid.astype(F32)).astype(BF16)


def swish(values):
    return values * jax.nn.sigmoid(values)


class Plan:
    def __init__(self, mesh):
        self.n_dp, self.n_mp = mesh.shape["dp"], mesh.shape["mp"]
        self.n = self.n_dp * self.n_mp
        self.groups = self.n // CRIT
        self.workers = self.groups * CRIT
        self.turns = -(-self.n // self.groups)

    def rank(self, dp, mp):
        size = 4 * self.n_dp
        layer = mp // 4
        inner = dp * 4 + (mp % 4 + 2 * (dp % 2)) % 4
        if self.n != 32:
            return layer * size + inner
        far, near = layer // 2, jnp.logical_or(layer == 1, layer == 2)
        six = 24 + 3 * far + jnp.where(near, 2, 0)
        seven = jnp.where(near, 30 + far, 25 + 3 * far)
        return jnp.where(inner < 6, 6 * layer + inner, jnp.where(inner == 6, six, seven))

    def place(self, k):
        size = 4 * self.n_dp
        if self.n != 32:
            layer, inner = k // size, k % size
        else:
            extra = jnp.maximum(k - 24, 0)
            which, j = extra // 3, extra % 3
            layer = jnp.where(which == 0, j // 2, jnp.where(which == 1, 3 - j // 2, 1 + j))
            inner = jnp.where(which == 2, 7, 6 + j % 2)
            layer = jnp.where(k < 24, k // 6, layer)
            inner = jnp.where(k < 24, k % 6, inner)
        dp = inner // 4
        return dp, layer * 4 + (inner % 4 + 2 * (dp % 2)) % 4

    def device(self, s):
        return s // self.n_mp, s % self.n_mp

    @property
    def sets(self):
        return 4 if self.n == 32 else CRIT // 2

    def extra(self, q, group):
        if self.n != 32:
            return jnp.int32(-1)
        low = jnp.where(group < 2, q == 0, q == 1)
        high = jnp.where(group < 2, q == 3, q == 2)
        return jnp.where(low, 8, jnp.where(high, 9, -1))

    def shift(self, k):
        at = lambda c, r: sum(int(v) * m for v, m in zip(self.place(jnp.int32(c * self.groups + r)), (self.n_mp, 1)))
        with jax.ensure_compile_time_eval():
            return [(at(c, r), at(c, (r + k) % self.groups)) for c in range(CRIT) for r in range(self.groups)]

    def pairs(self, rows):
        per = -(-rows // self.groups)
        return -(-per // 32) * 16

    def cap(self, rows):
        return -(-(self.n * -(-rows // self.groups)) // (TILE * AHEAD_TILES)) * TILE * AHEAD_TILES


def chunks_of(columns):
    width = math.gcd(math.gcd(columns, H), HALF)
    return width, columns // width, H // width


def assemble(chunks_ref, width, shift):
    groups = []
    lane = iota((32, LANES), 1)
    for g in range(H // LANES):
        block = jnp.zeros((32, LANES), F32)
        for i in range(LANES // width):
            chunk = chunks_ref[g * (LANES // width) + i]
            turn = (i * width - shift) % LANES
            moved = pltpu.roll(chunk, turn, 1) if turn else chunk
            block = jnp.where(lane // width == i, moved, block)
        groups.append(block)
    return jnp.concatenate(groups, 1)


def all_barrier(plan, dp, mp):
    barrier = pltpu.get_barrier_semaphore()

    def tell(s, _):
        sdp, smp = s // plan.n_mp, s % plan.n_mp

        @pl.when(jnp.logical_or(sdp != dp, smp != mp))
        def _():
            pl.semaphore_signal(barrier, inc=1, device_id=(sdp, smp), device_id_type=MESH)

        return 0

    lax.fori_loop(0, plan.n, tell, 0)
    pl.semaphore_wait(barrier, plan.n - 1)


def dispatch_kernel(
    plan,
    inputs,
    wt_ref,
    wc_ref,
    x_ref,
    p_ref,
    low,
    msg,
    wide,
    chunk,
    send_w,
    recv_w,
    pass_w,
    recv_c,
    send_x,
    recv_x,
    pass_x,
    send_p,
    recv_p,
    pass_p,
    stage,
    stage_sem,
):
    loads = [pltpu.make_async_copy(src, dst, stage_sem.at[k]) for k, (src, dst) in enumerate(zip(inputs, stage))]
    for load in loads:
        load.start()
    crit_ref, targ_ref, crit_in, crit_norms, targ_in, targ_norms, head_ref = stage[:7]
    sa_ref, ns_ref, rows_ref, table_ref, pin_ref, pmid_ref, pout_ref = stage[7:]
    crit_small, targ_small = (crit_in, crit_norms), (targ_in, targ_norms)
    dp, mp = lax.axis_index("dp"), lax.axis_index("mp")
    me = plan.rank(dp, mp)
    index = dp * plan.n_mp + mp
    groups, workers = plan.groups, plan.workers
    critic, group = me // groups, me % groups
    rw, cw = crit_ref.shape[1], crit_ref.shape[2]
    rows = sa_ref.shape[1]
    columns = crit_small[0].shape[1]
    width, mine, per = chunks_of(columns)

    for load in loads[:2]:
        load.wait()

    def to_low(c, _):
        low[0, c] = targ_ref[c].astype(BF16)
        low[1, c] = crit_ref[c].astype(BF16)
        return 0

    lax.fori_loop(0, CRIT, to_low, 0)
    all_barrier(plan, dp, mp)

    def w_slot(s):
        sdp, smp = plan.device(s)
        return wt_ref.at[pl.ds(pl.multiple_of(smp * rw, rw), rw), pl.ds(pl.multiple_of(sdp * cw, cw), cw)]

    def to_worker(src, dst, send, recv, k):
        return pltpu.make_async_remote_copy(
            src_ref=src, dst_ref=dst, send_sem=send, recv_sem=recv, device_id=plan.place(k), device_id_type=MESH
        )

    turn = index // groups

    def first_hop(t, c):
        k = c * groups + index % groups
        dst = w_slot(index) if t == 0 else wc_ref.at[turn]
        recv = recv_w.at[index] if t == 0 else recv_c.at[turn]
        return k, dst, recv, to_worker(low.at[t, c], dst, send_w.at[t, c], recv, k)

    def send_weights(t):
        def one(i, _):
            c = (critic + i) % CRIT
            k, dst, recv, copy = first_hop(t, c)

            @pl.when(k == me)
            def _():
                pltpu.make_async_copy(low.at[t, c], dst, recv).start()

            @pl.when(k != me)
            def _():
                copy.start()

            return 0

        lax.fori_loop(0, CRIT, one, 0)

    send_weights(0)

    for load in loads[2:]:
        load.wait()
    wide[...] = jnp.zeros_like(wide)
    for t, parts in enumerate((targ_small, crit_small)):
        wide[t, 0:IN, 0:columns] = parts[0][...]
        wide[t, IN : IN + 4, 0:columns] = parts[1][...]
        wide[t, IN + 4 : IN + 5, 0:columns] = head_ref[t : t + 1, :]
    for j in range(mine):
        start, offset = j * width // LANES * LANES, j * width % LANES
        both = [wide[t, :, start : start + LANES] for t in range(2)]
        turned = [pltpu.roll(v, turn, 1) if turn else v for v, turn in zip(both, ((-offset) % LANES, (HALF - offset) % LANES))]
        chunk[j] = jnp.where(iota((32, LANES), 1) < HALF, turned[0], turned[1])

    def small_hop(j):
        g = index * mine + j
        k = (g // per) * groups + g % groups
        return k, g % per, to_worker(chunk.at[j], p_ref.at[g % per], send_p.at[j], recv_p.at[g % per], k)

    def send_small(j, _):
        k, slot, copy = small_hop(j)

        @pl.when(k == me)
        def _():
            pltpu.make_async_copy(chunk.at[j], p_ref.at[slot], recv_p.at[slot]).start()

        @pl.when(k != me)
        def _():
            copy.start()

        return 0

    lax.fori_loop(0, mine, send_small, 0)

    lane = iota((rows, LANES), 1)
    place = lambda height, offset: (iota((height, LANES), 1) == iota((height, LANES), 0) + offset).astype(F32).astype(BF16)
    hidden = swish(tn(ns_ref[...], pin_ref[...])).astype(BF16)
    hidden = swish(nn(hidden, pmid_ref[...])).astype(BF16)
    pout = pout_ref[...]
    spread = lambda offset: tn(
        pout, (iota((2 * ACT, LANES), 0) == iota((2 * ACT, LANES), 1) + offset).astype(F32).astype(BF16)
    ).astype(BF16)
    keep = lane < ACT
    means = nn(hidden, spread(0))
    raw = nn(hidden, spread(ACT))
    facts = rows_ref[...]
    across = jnp.transpose(facts)
    picked = (iota((rows, table_ref.shape[1]), 1) == across[:, 2:3].astype(I32)).astype(F32).astype(BF16)
    noise = jnp.zeros((rows, LANES), F32)
    for part in split3(table_ref[...]):
        noise = noise + nn(picked, tn(part, place(ACT, 0)).astype(BF16))
    log_std = -5.0 + 3.5 * (jnp.tanh(raw) + 1.0)
    squashed = means + jnp.exp(log_std) * noise
    action = jnp.tanh(squashed).astype(BF16)
    twice = -2.0 * squashed
    softplus = jnp.maximum(twice, 0.0) + jnp.log(1.0 + jnp.exp(-jnp.abs(twice)))
    correction = 2.0 * (math.log(2.0) - squashed - softplus)
    density = jnp.sum(
        jnp.where(keep, -0.5 * noise * noise - log_std - 0.5 * math.log(2.0 * math.pi) - correction, 0.0), -1, keepdims=True
    )
    done = across[:, 1:2]
    boot = (done == 0.0).astype(F32)
    base = across[:, 0:1] - (REWARD_DISCOUNT * ENTROPY_TEMP) * boot * density
    high, mid, rest = split3(base)
    on = lambda k, value: jnp.where(lane == k, value, 0.0)
    features = (
        tn(sa_ref[...], place(IN, 0))
        + tn(ns_ref[...], place(OBS, L_TGT))
        + nn(jnp.where(keep, action.astype(F32), 0.0).astype(BF16), place(LANES, L_TGT + OBS))
        + on(L_BASE, high.astype(F32))
        + on(L_BASE + 1, mid.astype(F32))
        + on(L_BASE + 2, rest.astype(F32))
        + on(L_BOOT, boot)
        + on(L_S0, across[:, 3:4])
        + on(L_S1, across[:, 4:5])
        + on(L_VALID, 1.0)
    ).astype(BF16)

    pairs = msg.shape[1]
    valid = (facts[1:2, :] != 2.0).astype(F32)
    before = (iota((rows, rows), 0) < iota((rows, rows), 1)).astype(F32).astype(BF16)
    order = nn(jnp.broadcast_to(valid, (8, rows)).astype(BF16), before)[0:1, :]
    order = jnp.where(valid > 0.0, order, -1.0)
    count = jnp.sum(valid, -1, keepdims=True)
    count_half = jnp.floor(count * 0.5)
    mlane = iota((pairs, LANES), 1)
    tail = jnp.where(mlane == L_CNT, count_half, 0.0) + jnp.where(mlane == L_CNT + 1, count - 2.0 * count_half, 0.0)

    def deal(r, _):
        slot = iota((pairs, rows), 0) * (2 * groups) + r
        halves = []
        for h in range(2):
            hot = (order == (slot + h * groups).astype(F32)).astype(F32).astype(BF16)
            halves.append(nn(hot, features))
        msg[r] = (halves[0] + pltpu.roll(halves[1], HALF, 1) + tail).astype(BF16)
        return 0

    lax.fori_loop(0, groups, deal, 0)

    def row_hop(i):
        r = i % groups
        k = (2 * (i // groups) + index % 2) * groups + r
        return r, k, to_worker(msg.at[r], x_ref.at[index], send_x.at[i], recv_x.at[index], k)

    hops = plan.sets * groups

    def send_rows(i, _):
        r, k, copy = row_hop((i + (critic // 2) * groups) % hops)

        @pl.when(k == me)
        def _():
            pltpu.make_async_copy(msg.at[r], x_ref.at[index], recv_x.at[index]).start()

        @pl.when(k != me)
        def _():
            copy.start()

        return 0

    lax.fori_loop(0, hops, send_rows, 0)
    send_weights(1)

    def peer(i):
        return critic * groups + (group + 1 + i) % groups

    def pass_weight(t, i):
        s = group + groups * t
        return to_worker(w_slot(s), w_slot(s), pass_w.at[t, i], recv_w.at[s], peer(i))

    def pass_small(slot, i):
        return to_worker(p_ref.at[slot], p_ref.at[slot], pass_p.at[slot // groups, i], recv_p.at[slot], peer(i))

    extra = plan.extra(critic // 2, group)

    def pass_rows(i, k, which):
        s = 2 * i + critic % 2
        return to_worker(x_ref.at[s], x_ref.at[s], pass_x.at[i, which], recv_x.at[s], k)

    def other_rows(i):
        return pass_rows(i, (critic + 1 - 2 * (critic % 2)) * groups + group, 0)

    def extra_rows(i):
        return pass_rows(i, extra * groups + group, 1)

    def arrived_w(s):
        pltpu.make_async_copy(low.at[0, 0], w_slot(s), recv_w.at[s]).wait()

    def arrived_x(s):
        pltpu.make_async_copy(msg.at[0], x_ref.at[s], recv_x.at[s]).wait()

    def arrived_p(slot):
        pltpu.make_async_copy(chunk.at[0], p_ref.at[slot], recv_p.at[slot]).wait()

    turns = (plan.n - group + groups - 1) // groups
    passes_rows = critic < 2 * plan.sets

    def peers(body):
        lax.fori_loop(0, groups - 1, lambda i, _: (body(i), 0)[1], 0)

    def each(count, body):
        lax.fori_loop(0, count, lambda i, _: (body(i), 0)[1], 0)

    @pl.when(me < workers)
    def _():
        def relay_weight(t):
            arrived_w(group + groups * t)
            peers(lambda i: pass_weight(t, i).start())

        each(turns, relay_weight)

        @pl.when(passes_rows)
        def _():
            def relay_rows(i):
                arrived_x(2 * i + critic % 2)
                other_rows(i).start()

                @pl.when(extra >= 0)
                def _():
                    extra_rows(i).start()

            each(plan.n // 2, relay_rows)

        def relay_small(slot):
            @pl.when((critic * per + slot) % groups == group)
            def _():
                arrived_p(slot)
                peers(lambda i: pass_small(slot, i).start())

        each(per, relay_small)

        def arrived(s):
            @pl.when(s % groups != group)
            def _():
                arrived_w(s)

            @pl.when(jnp.logical_not(jnp.logical_and(passes_rows, s % 2 == critic % 2)))
            def _():
                arrived_x(s)

        each(plan.n, arrived)

        def arrived_small(slot):
            @pl.when((critic * per + slot) % groups != group)
            def _():
                arrived_p(slot)

        each(per, arrived_small)
        each(turns, lambda t: pltpu.make_async_copy(low.at[1, 0], wc_ref.at[t], recv_c.at[t]).wait())
        each(turns, lambda t: peers(lambda i: pass_weight(t, i).wait_send()))

        @pl.when(passes_rows)
        def _():
            def passed_rows(i):
                other_rows(i).wait_send()

                @pl.when(extra >= 0)
                def _():
                    extra_rows(i).wait_send()

            each(plan.n // 2, passed_rows)

        def passed_small(slot):
            @pl.when((critic * per + slot) % groups == group)
            def _():
                peers(lambda i: pass_small(slot, i).wait_send())

        each(per, passed_small)

    def sent_weights(c):
        for t in range(2):
            k, _dst, _recv, copy = first_hop(t, c)

            @pl.when(k != me)
            def _():
                copy.wait_send()

    each(CRIT, sent_weights)

    def sent_small(j):
        k, _slot, copy = small_hop(j)

        @pl.when(k != me)
        def _():
            copy.wait_send()

    each(mine, sent_small)

    def sent_rows(i):
        _r, k, copy = row_hop(i)

        @pl.when(k != me)
        def _():
            copy.wait_send()

    each(hops, sent_rows)


def dispatch(plan, inputs):
    critic_hidden, critic_in, state_action = inputs[0], inputs[2], inputs[7]
    rows = state_action.shape[1]
    pairs = plan.pairs(rows)
    columns = critic_in.shape[1]
    _width, mine, per = chunks_of(columns)
    anywhere = pl.BlockSpec(memory_space=pl.ANY)
    dma = pltpu.SemaphoreType.DMA
    return pl.pallas_call(
        functools.partial(dispatch_kernel, plan),
        out_shape=(
            jax.ShapeDtypeStruct((H, H), BF16),
            jax.ShapeDtypeStruct((plan.turns,) + critic_hidden.shape[1:], BF16),
            jax.ShapeDtypeStruct((plan.n, pairs, LANES), BF16),
            jax.ShapeDtypeStruct((per, 32, LANES), F32),
        ),
        in_specs=[(pl.BlockSpec(memory_space=pltpu.HBM),) * len(inputs)],
        out_specs=(anywhere,) * 4,
        scratch_shapes=[
            pltpu.VMEM((2,) + critic_hidden.shape, BF16),
            pltpu.VMEM((plan.groups, pairs, LANES), BF16),
            pltpu.VMEM((2, 32, -(-columns // LANES) * LANES), F32),
            pltpu.VMEM((mine, 32, LANES), F32),
            dma((2, CRIT)),
            dma((plan.n,)),
            dma((plan.turns, plan.groups - 1)),
            dma((plan.turns,)),
            dma((plan.sets * plan.groups,)),
            dma((plan.n,)),
            dma((plan.n // 2, 2)),
            dma((mine,)),
            dma((per,)),
            dma((-(-per // plan.groups), plan.groups - 1)),
            tuple(pltpu.VMEM(v.shape, v.dtype) for v in inputs),
            dma((len(inputs),)),
        ],
        compiler_params=pltpu.CompilerParams(collective_id=0, has_side_effects=True, vmem_limit_bytes=20 * MIB),
        name="dispatch",
    )(inputs)


def norm_parts(pre):
    centered = pre - jnp.sum(pre, -1, keepdims=True) * (1.0 / H)
    inv = lax.rsqrt(jnp.sum(centered * centered, -1, keepdims=True) * (1.0 / H) + 1e-05)
    return centered * inv, inv


def swish_parts(half):
    t = jnp.tanh(half)
    product = half * t
    return half + product, (1.0 + t) * (1.0 + (half - product))


def low_input(params):
    return jnp.where(iota((32, H), 0) < IN, params, 0.0).astype(BF16)


def input_layer(params, win_ref, gram_ref):
    weight = low_input(params).astype(F32)
    weight = weight - jnp.sum(weight, -1, keepdims=True) * (1.0 / H)
    win_ref[...] = jnp.zeros_like(win_ref)
    for k, part in enumerate(split3(weight)):
        win_ref[k * 32 : (k + 1) * 32, :] = part
    for k, part in enumerate(split3(nt(win_ref[...], win_ref[...]) * (1.0 / H))):
        gram_ref[k] = part


def input_norm(x, start, win_ref, gram_ref):
    row, lane = iota((LANES, LANES), 0), iota((LANES, LANES), 1)
    pick = jnp.logical_and(lane < 96, jnp.logical_and(lane % 32 < IN, row == lane % 32 + start))
    thrice = nn(x, pick.astype(F32).astype(BF16)).astype(BF16)
    image = sum(nn(thrice, gram_ref[k]) for k in range(3))
    var = jnp.sum(image * thrice.astype(F32), -1, keepdims=True)
    return nn(thrice, win_ref[...]), lax.rsqrt(jnp.maximum(var, 0.0) + 1e-05)


def tile_span(t):
    return pl.ds(pl.multiple_of(t * TILE, TILE), TILE)


def target_kernel(
    plan, width, role_ref, x_ref, w_ref, p_ref, xc_ref, q_ref, info_ref, rows_f, picked, value, hot, win, par, cnt_v, cnt_s, base_s, sem
):
    critic, group, active = role_ref[0], role_ref[1], role_ref[2]
    groups, n = plan.groups, plan.n
    pairs = x_ref.shape[1]
    first = x_ref[:, 0, :].astype(F32)
    lane = iota(first.shape, 1)
    counts = 2.0 * jnp.sum(jnp.where(lane == L_CNT, first, 0.0), -1, keepdims=True) + jnp.sum(
        jnp.where(lane == L_CNT + 1, first, 0.0), -1, keepdims=True
    )
    counts = jnp.where(active > 0, jnp.broadcast_to(counts, first.shape), 0.0)
    mine = jnp.floor((counts + (groups - 1 - group).astype(F32)) * (1.0 / groups) + 0.5 / groups)
    earlier = (iota((n, n), 1) < iota((n, n), 0)).astype(F32).astype(BF16)
    starts = nn(earlier, mine.astype(BF16))
    total = jnp.sum(counts, 0, keepdims=True)
    cnt_v[0:n, :] = mine.astype(I32)
    cnt_v[n : 2 * n, :] = starts.astype(I32)
    cnt_v[2 * n : 2 * n + 8, :] = jnp.broadcast_to(total, (8, LANES)).astype(I32)
    copy = pltpu.make_async_copy(cnt_v, cnt_s, sem)
    copy.start()
    par[...] = assemble(p_ref, width, 0)
    win[...] = jnp.zeros_like(win)
    win[0:32, :] = low_input(par[...])
    copy.wait()
    number = cnt_s[n - 1, 0] + cnt_s[2 * n - 1, 0]
    tiles = (number + TILE - 1) // TILE
    info_ref[0] = number
    info_ref[1] = cnt_s[2 * n, 0]

    def compact(s, _):
        block = x_ref[s].astype(F32)
        have, start = cnt_s[s, 0], cnt_s[n + s, 0]
        rows_f[pl.ds(start, pairs), :] = block
        rows_f[pl.ds(start + (have + 1) // 2, pairs), :] = pltpu.roll(block, HALF, 1)
        return 0

    @pl.when(active > 0)
    def _():
        lax.fori_loop(0, n, compact, 0, unroll=4)

    rows_f[pl.ds(number, AHEAD_TILES * TILE), :] = jnp.zeros((AHEAD_TILES * TILE, LANES), F32)
    bundles = (tiles + AHEAD_TILES - 1) // AHEAD_TILES

    until = (iota((TILE, TILE), 1) < iota((TILE, TILE), 0)).astype(F32).astype(BF16)
    place = iota((TILE, TILE), 1).astype(F32)
    this = critic.astype(F32)

    def choose(b, base):
        chosen, counts = [], []
        for i in range(AHEAD_TILES):
            t = b * AHEAD_TILES + i
            wide = rows_f[tile_span(t), :]
            x = wide.astype(BF16)
            xc_ref[tile_span(t), :] = x
            wanted = jnp.logical_or(wide[:, L_S0 : L_S0 + 1] == this, wide[:, L_S1 : L_S1 + 1] == this)
            wanted = jnp.where(jnp.logical_and(wanted, wide[:, L_BOOT : L_BOOT + 1] > 0.0), 1.0, 0.0)
            order = nn(until, jnp.broadcast_to(wanted, (TILE, LANES)).astype(BF16))[:, 0:1]
            to = (jnp.where(wanted > 0.0, order, -1.0) == place).astype(F32).astype(BF16)
            hot[t] = to
            chosen.append(tn(to, x))
            counts.append(jnp.sum(wanted).astype(I32))
        for i in range(AHEAD_TILES):
            picked[pl.ds(base, TILE), :] = chosen[i]
            base_s[b * AHEAD_TILES + i] = base
            base = base + counts[i]
        return base

    chosen_rows = lax.fori_loop(0, bundles, choose, 0)
    picked[pl.ds(chosen_rows, TILE), :] = jnp.zeros((TILE, LANES), F32)
    chosen_tiles = (chosen_rows + TILE - 1) // TILE
    half = jnp.where(iota((32, 1), 0) < IN + 4, 0.5, 1.0)
    par[...] = par[...] * half
    gain1, shift1, gain2, shift2, head = (par[IN + k : IN + k + 1, :] for k in range(5))

    def tile(t, _):
        x = pltpu.roll(picked[tile_span(t), :], LANES - L_TGT, 1).astype(BF16)
        z, _unused = norm_parts(nn(x, win[...]))
        y = z * gain1 + shift1
        act = (y + y * jnp.tanh(y)).astype(BF16)
        z, _unused = norm_parts(nn(act, w_ref[...]))
        y = z * gain2 + shift2
        q = jnp.sum((y + y * jnp.tanh(y)) * head, -1, keepdims=True)
        value[tile_span(t), :] = jnp.broadcast_to(q, (TILE, LANES))
        return 0

    lax.fori_loop(0, chosen_tiles, tile, 0)
    value[tile_span(chosen_tiles), :] = jnp.zeros((TILE, LANES), F32)

    def spread(b, _):
        lane = iota((TILE, LANES), 1)
        for i in range(AHEAD_TILES):
            t = b * AHEAD_TILES + i
            high, mid, rest = (v.astype(F32) for v in split3(value[pl.ds(base_s[t], TILE), :]))
            parts = jnp.where(lane == 0, high, jnp.where(lane == 1, mid, jnp.where(lane == 2, rest, 0.0)))
            q = jnp.broadcast_to(jnp.sum(nn(hot[t], parts.astype(BF16)), -1, keepdims=True), (TILE, LANES))
            for h in range(TILE // LANES):
                flat = jnp.transpose(q[h * LANES : (h + 1) * LANES, :])
                q_ref[pl.ds(t * (TILE // LANES) + h, 1), :] = flat[0:1, :]
        return 0

    lax.fori_loop(0, bundles, spread, 0)


def target_values(plan, rows, width, role, x, weights, params):
    capacity = plan.cap(rows)
    vmem = pl.BlockSpec(memory_space=pltpu.VMEM)
    smem = pl.BlockSpec(memory_space=pltpu.SMEM)
    return pl.pallas_call(
        functools.partial(target_kernel, plan, width),
        out_shape=(
            jax.ShapeDtypeStruct((capacity, LANES), BF16),
            jax.ShapeDtypeStruct((capacity // LANES, LANES), F32),
            jax.ShapeDtypeStruct((2,), I32),
        ),
        in_specs=[smem, vmem, vmem, vmem],
        out_specs=(vmem, vmem, smem),
        scratch_shapes=[
            pltpu.VMEM((capacity + AHEAD_TILES * TILE + x.shape[1], LANES), F32),
            pltpu.VMEM((capacity + TILE, LANES), F32),
            pltpu.VMEM((capacity + TILE, LANES), F32),
            pltpu.VMEM((capacity // TILE, TILE, TILE), BF16),
            pltpu.VMEM((LANES, H), BF16),
            pltpu.VMEM((32, H), F32),
            pltpu.VMEM((2 * plan.n + 8, LANES), I32),
            pltpu.SMEM((2 * plan.n + 8, LANES), I32),
            pltpu.SMEM((capacity // TILE,), I32),
            pltpu.SemaphoreType.DMA,
        ],
        compiler_params=pltpu.CompilerParams(vmem_limit_bytes=28 * MIB),
        name="target_values",
    )(role, x, weights, params)


def share_kernel(plan, q_ref, all_ref, send, recv):
    dp, mp = lax.axis_index("dp"), lax.axis_index("mp")
    me = plan.rank(dp, mp)
    groups = plan.groups
    critic, group = me // groups, me % groups
    barrier = pltpu.get_barrier_semaphore()

    @pl.when(me < plan.workers)
    def _():
        def peer(i):
            other = (critic + i) % CRIT
            return other, plan.place(other * groups + group)

        def tell(i, _):
            pl.semaphore_signal(barrier, inc=1, device_id=peer(i)[1], device_id_type=MESH)
            return 0

        lax.fori_loop(1, CRIT, tell, 0)
        pl.semaphore_wait(barrier, CRIT - 1)
        all_ref[critic] = q_ref[...]

        def copy(i):
            other, device = peer(i)
            return pltpu.make_async_remote_copy(
                src_ref=q_ref,
                dst_ref=all_ref.at[critic],
                send_sem=send.at[other],
                recv_sem=recv.at[critic],
                device_id=device,
                device_id_type=MESH,
            )

        def start(i, _):
            copy(i).start()
            return 0

        lax.fori_loop(1, CRIT, start, 0)

        def finish(i, _):
            copy(i).wait_send()
            other = peer(i)[0]
            pltpu.make_async_copy(q_ref, all_ref.at[other], recv.at[other]).wait()
            return 0

        lax.fori_loop(1, CRIT, finish, 0)


def share_values(plan, q):
    vmem = pl.BlockSpec(memory_space=pltpu.VMEM)
    return pl.pallas_call(
        functools.partial(share_kernel, plan),
        out_shape=jax.ShapeDtypeStruct((CRIT,) + q.shape, F32),
        in_specs=[vmem],
        out_specs=vmem,
        scratch_shapes=[pltpu.SemaphoreType.DMA((CRIT,)), pltpu.SemaphoreType.DMA((CRIT,))],
        compiler_params=pltpu.CompilerParams(collective_id=1, has_side_effects=True, vmem_limit_bytes=8 * MIB),
        name="share_values",
    )(q)


def critic_kernel(
    plan, width, role_ref, info_ref, xc_ref, q_ref, shares, p_ref, grad_ref, lowered_ref, small_ref, sums_ref, w_ref, z_one, slope, act, low, fact, par, win, gram, picks, acc
):
    number = info_ref[0]
    scale = 2.0 / jnp.maximum(info_ref[1], 1).astype(F32)
    tiles = (number + TILE - 1) // TILE
    rw, cw = shares[0].shape[1:]
    for k, share in enumerate(shares):
        owner = (role_ref[1] + plan.groups - k) % plan.groups

        def gather(t, _):
            s = owner + plan.groups * t

            @pl.when(s < plan.n)
            def _():
                sdp, smp = plan.device(s)
                w_ref[pl.ds(pl.multiple_of(smp * rw, rw), rw), pl.ds(pl.multiple_of(sdp * cw, cw), cw)] = share[t]

            return 0

        lax.fori_loop(0, plan.turns, gather, 0)
    par[...] = assemble(p_ref, width, HALF)
    input_layer(par[...], win, gram)
    grad_ref[...] = jnp.zeros_like(grad_ref)
    acc[...] = jnp.zeros_like(acc)
    picks[...] = jnp.zeros_like(picks)
    sums_ref[...] = jnp.zeros_like(sums_ref)
    gain1, shift1, gain2, shift2, head = (par[IN + k : IN + k + 1, :] for k in range(5))

    hg = (0.5 * head) * gain2

    def fold(k, value):
        acc[32 + k * 8 : 40 + k * 8, :] += jnp.sum(value.reshape(TILE // 8, 8, H), 0)

    def tile(t, _):
        x = xc_ref[tile_span(t), :]
        wide = x.astype(F32)
        pre, inv_one = input_norm(x, 0, win, gram)
        z = pre * inv_one
        z_one[...] = z
        value, twice = swish_parts(z * (0.5 * gain1) + 0.5 * shift1)
        slope[...] = 0.5 * twice
        act[...] = value.astype(BF16)
        pre = nn(act[...], w_ref[...])
        for h in range(TILE // LANES):
            picks[0:CRIT, :] = q_ref[:, pl.ds(t * (TILE // LANES) + h, 1), :].reshape(CRIT, LANES)
            table = jnp.transpose(picks[...])
            part = wide[h * LANES : (h + 1) * LANES, :]
            critic = iota(table.shape, 1).astype(F32)
            one = jnp.sum(jnp.where(critic == part[:, L_S0 : L_S0 + 1], table, 0.0), -1, keepdims=True)
            two = jnp.sum(jnp.where(critic == part[:, L_S1 : L_S1 + 1], table, 0.0), -1, keepdims=True)
            base = part[:, L_BASE : L_BASE + 1] + part[:, L_BASE + 1 : L_BASE + 2] + part[:, L_BASE + 2 : L_BASE + 3]
            goal = base + jnp.where(part[:, L_BOOT : L_BOOT + 1] > 0.0, REWARD_DISCOUNT * jnp.minimum(one, two), 0.0)
            fact[h * LANES : (h + 1) * LANES, 0:1] = goal
        z, inv = norm_parts(pre)
        value, twice = swish_parts(z * (0.5 * gain2) + 0.5 * shift2)
        q = jnp.sum(value * head, -1, keepdims=True)
        error = (q - fact[:, 0:1]) * wide[:, L_VALID : L_VALID + 1]
        sums_ref[0:1, :] += jnp.broadcast_to(jnp.sum(error * error, 0, keepdims=True), (1, LANES))
        dq = error * scale
        flat = jnp.transpose(jnp.broadcast_to(dq, (TILE, LANES)))[0:8, :]
        high, rest = split2(flat)
        weigh = jnp.concatenate([high, rest], 0)
        tz = twice * z
        for k, v in ((4, value), (3, twice), (2, tz)):
            acc[32 + k * 8 : 40 + k * 8, :] += nn(weigh, v.astype(BF16))[4:12]
        dz = twice * hg
        mean = jnp.sum(dz, -1, keepdims=True) * (1.0 / H)
        along = jnp.sum(tz * hg, -1, keepdims=True) * (1.0 / H)
        low[...] = ((inv * dq) * (dz - mean - z * along)).astype(BF16)
        down = nt(low[...], w_ref[...])
        grad_ref[...] += tn(act[...], low[...])
        z = z_one[...]
        dy = down * slope[...]
        fold(1, dy)
        fold(0, dy * z)
        dz = dy * gain1
        mean = jnp.sum(dz, -1, keepdims=True) * (1.0 / H)
        along = jnp.sum(dz * z, -1, keepdims=True) * (1.0 / H)
        acc[0:32, :] += tn(x[:, 0:32], (inv_one * (dz - mean - z * along)).astype(BF16))
        return 0

    lax.fori_loop(0, tiles, tile, 0)
    lowered_ref[...] = grad_ref[...].astype(BF16)
    sums_ref[1:2, :] = jnp.broadcast_to(info_ref[1].astype(F32), (1, LANES))
    for k in range(2, 5):
        total = jnp.sum(acc[32 + k * 8 : 40 + k * 8, :], 0, keepdims=True) * 0.25
        acc[32 + k * 8 : 40 + k * 8, :] = jnp.zeros((8, H), F32)
        acc[32 + k * 8 : 33 + k * 8, :] = total if k == 4 else total * (0.5 * head)
    for k in range(5):
        acc[IN + k : IN + k + 1, :] = jnp.sum(acc[32 + k * 8 : 40 + k * 8, :], 0, keepdims=True)
    for i in range(H // width):
        start, offset = i * width // LANES * LANES, i * width % LANES
        block = acc[0:32, start : start + LANES]
        small_ref[i] = pltpu.roll(block, LANES - offset, 1) if offset else block


def critic_step(plan, width, role, info, xc, q_all, shares, params):
    vmem = pl.BlockSpec(memory_space=pltpu.VMEM)
    smem = pl.BlockSpec(memory_space=pltpu.SMEM)
    return pl.pallas_call(
        functools.partial(critic_kernel, plan, width),
        out_shape=(
            jax.ShapeDtypeStruct((H, H), F32),
            jax.ShapeDtypeStruct((H, H), BF16),
            jax.ShapeDtypeStruct((H // width, 32, LANES), F32),
            jax.ShapeDtypeStruct((8, LANES), F32),
        ),
        in_specs=[smem, smem, vmem, vmem, (vmem,) * plan.groups, vmem],
        out_specs=(vmem,) * 4,
        scratch_shapes=[
            pltpu.VMEM((H, H), BF16),
            pltpu.VMEM((TILE, H), F32),
            pltpu.VMEM((TILE, H), F32),
            pltpu.VMEM((TILE, H), BF16),
            pltpu.VMEM((TILE, H), BF16),
            pltpu.VMEM((TILE, LANES), F32),
            pltpu.VMEM((32, H), F32),
            pltpu.VMEM((LANES, H), BF16),
            pltpu.VMEM((3, LANES, LANES), BF16),
            pltpu.VMEM((16, LANES), F32),
            pltpu.VMEM((72, H), F32),
        ],
        compiler_params=pltpu.CompilerParams(vmem_limit_bytes=36 * MIB),
        name="critic_step",
    )(role, info, xc, q_all, shares, params)


PRECISE = 2


LAG = 3
AHEAD = 3


def shampoo_kernel(
    plan,
    g_ref,
    lowered_ref,
    small_ref,
    sums_ref,
    mom_ref,
    left_ref,
    right_ref,
    w_ref,
    mo_ref,
    lo_ref,
    ro_ref,
    wo_ref,
    own_ref,
    out_ref,
    parts,
    pieces,
    given,
    shares,
    totals,
    send_one,
    recv_one,
    send_two,
    recv_two,
    send_s,
    recv_s,
    send_t,
    recv_t,
):
    dp, mp = lax.axis_index("dp"), lax.axis_index("mp")
    me = plan.rank(dp, mp)
    index = dp * plan.n_mp + mp
    groups, workers, n, turns = plan.groups, plan.workers, plan.n, plan.turns
    critic, group = me // groups, me % groups
    rw, cw = mom_ref.shape[1], mom_ref.shape[2]
    mine, per = shares.shape[1], small_ref.shape[0]
    columns = own_ref.shape[1]
    chunk_width = H // per
    all_barrier(plan, dp, mp)

    def to_device(src, dst, send, recv, device):
        return pltpu.make_async_remote_copy(
            src_ref=src, dst_ref=dst, send_sem=send, recv_sem=recv, device_id=device, device_id_type=MESH
        )

    def block(s):
        sdp, smp = plan.device(s)
        return pl.ds(pl.multiple_of(smp * rw, rw), rw), pl.ds(pl.multiple_of(sdp * cw, cw), cw)

    def turn_of(step):
        return (step + critic) % turns

    def first_hop(step, i):
        other = (group + 1 + i) % groups
        turn = turn_of(step)
        s = other + groups * turn
        copy = to_device(
            lowered_ref.at[block(s)],
            parts.at[groups - 2 - i, turn],
            send_one.at[step, i],
            recv_one.at[groups - 2 - i, turn],
            plan.place(critic * groups + other),
        )
        return s, copy

    def second_hop(turn):
        s = group + groups * turn
        return s, to_device(pieces.at[turn], given.at[critic], send_two.at[turn], recv_two.at[critic], plan.device(s))

    def small_hop(q):
        g = critic * per + q
        s = g // mine
        return s, to_device(
            small_ref.at[q], shares.at[group, g % mine], send_s.at[q], recv_s.at[group, g % mine], plan.device(s)
        )

    def total_hop(s):
        return to_device(sums_ref, totals.at[me], send_t.at[s], recv_t.at[me], plan.device(s))

    def start_first(step):
        def one(i, _):
            s, copy = first_hop(step, i)

            @pl.when(s < n)
            def _():
                copy.start()

            return 0

        lax.fori_loop(0, groups - 1, one, 0)

    def start_rest():
        def start_small(q, _):
            s, copy = small_hop(q)

            @pl.when(s == index)
            def _():
                slot = (critic * per + q) % mine
                pltpu.make_async_copy(small_ref.at[q], shares.at[group, slot], recv_s.at[group, slot]).start()

            @pl.when(s != index)
            def _():
                copy.start()

            return 0

        lax.fori_loop(0, per, start_small, 0)
        totals[me] = sums_ref[...]

        def start_total(i, _):
            total_hop((index + i) % n).start()
            return 0

        lax.fori_loop(1, n, start_total, 0)

    @pl.when(me < workers)
    def _():
        for step in range(AHEAD):
            start_first(step)

    def add_up(step):
        turn = turn_of(step)
        s, copy = second_hop(turn)

        @pl.when(s < n)
        def _():
            for i in range(groups - 1):
                pltpu.make_async_copy(parts.at[0, 0], parts.at[i, turn], recv_one.at[i, turn]).wait()
            value = g_ref[block(s)]
            for i in range(groups - 1):
                value = value + parts[i, turn].astype(F32)
            pieces[turn] = value.astype(BF16)

            @pl.when(s == index)
            def _():
                pltpu.make_async_copy(pieces.at[turn], given.at[critic], recv_two.at[critic]).start()

            @pl.when(s != index)
            def _():
                copy.start()

    width = min(256, cw)
    halves = width // LANES
    high_rows = halves * BLK
    nr, nc = rw // BLK, cw // width
    subs = [(i, j) for i in range(nr) for j in range(nc)]
    mask = (iota((LANES, LANES), 0) // BLK == iota((LANES, LANES), 1) // BLK).astype(F32).astype(BF16)
    mask_wide = jnp.concatenate([mask] * halves, 1)
    eye = (iota((high_rows, LANES), 0) % BLK == iota((high_rows, LANES), 1) % BLK).astype(F32)
    eye_low = eye.astype(BF16)

    def packed(flat):
        return jnp.concatenate([flat[:, k * LANES : (k + 1) * LANES] for k in range(halves)], 0)

    def flat_of(x):
        return jnp.concatenate([x[k * BLK : (k + 1) * BLK] for k in range(halves)], 1)

    def tops(out, count):
        return [
            jnp.concatenate(
                [out[(i * halves + k) * BLK : (i * halves + k + 1) * BLK, k * LANES : (k + 1) * LANES] for k in range(halves)], 0
            )
            for i in range(count)
        ]

    def diag(x):
        return jnp.concatenate([flat_of(x)] * (LANES // BLK), 0) * mask_wide

    def diag_rows(x):
        tiled = [jnp.concatenate([x[k * BLK : (k + 1) * BLK]] * (LANES // BLK), 0) * mask for k in range(halves)]
        return jnp.concatenate(tiled, 0)

    def products(lhs, right):
        return tops(nn(jnp.concatenate(lhs, 0), right), len(lhs))

    def precise(parts, right, right_rest):
        high, rest = parts
        out = products([high, rest], right)
        return out[0] + out[1] + products([high], right_rest)[0]

    def block_sums(s):
        high, rest = split2(s)
        return nn(high, mask) + nn(rest, mask)

    def place(c, i, j):
        return (c, slice(i * BLK, (i + 1) * BLK), slice(j * width, (j + 1) * width))

    def column_sums(x):
        return [jnp.sum(x[k * BLK : (k + 1) * BLK].reshape(BLK // 8, 8, LANES), 0) for k in range(halves)]

    def over_blocks(total, spot):
        rows = [jnp.sum(total[(spot + k) * 8 : (spot + k + 1) * 8], 0, keepdims=True) for k in range(halves)]
        return jnp.concatenate([jnp.broadcast_to(row, (BLK, LANES)) for row in rows], 0)

    def blocked(c):
        pltpu.make_async_copy(pieces.at[0], given.at[c], recv_two.at[c]).wait()
        sums, stats = [], []
        for i, j in subs:
            at = place(c, i, j)
            grad = given[at].astype(F32)
            mo_ref[at] = MOMENTUM * mom_ref[at] + grad
            low = packed(grad.astype(BF16))
            square, flip = tops(nt(jnp.concatenate([low, eye_low], 0), diag_rows(low)), 2)
            left = STAT_DECAY * packed(left_ref[at]) + (1.0 - STAT_DECAY) * square
            right = products([flip.astype(BF16)], diag(low))[0]
            right = STAT_DECAY * packed(right_ref[at]) + (1.0 - STAT_DECAY) * right
            lo_ref[at] = flat_of(left)
            ro_ref[at] = flat_of(right)
            for stat in (left, right):
                stats.append(stat)
                sums += column_sums(stat * stat)
        total = block_sums(jnp.concatenate(sums, 0))
        chains = []
        for k, stat in enumerate(stats):
            inv = lax.rsqrt(over_blocks(total, k * halves))
            rest = (eye - stat * inv) * 0.25
            chains.append([rest, eye + rest, jnp.sqrt(jnp.sqrt(inv))])
        for it in range(NEWTON - 1):
            full = it < PRECISE
            squares = []
            for ch in chains:
                high, rest = split2(ch[0])
                lhs = [high] + ([rest] if full else []) + ([ch[1].astype(BF16)] if it > 0 else [])
                out = products(lhs, diag(high))
                power = out[0]
                if full:
                    power = power + out[1] + products([high], diag(rest))[0]
                if it > 0:
                    ch[1] = ch[1] + out[-1]
                squares.append(power)
            factors = [[diag(v) for v in split2(power)[: 2 if full else 1]] for power in squares]

            def times(x, right):
                parts = split2(x)
                return precise(parts, *right) if full else products([parts[0]], right[0])[0]

            terms = [
                5.0 * ch[0] + 3.75 * power + times(ch[0], right) for ch, power, right in zip(chains, squares, factors)
            ]
            for ch, power, right, term in zip(chains, squares, factors, terms):
                ch[0] = 2.5 * power + times(term, right)
        for ch in chains:
            ch[1] = ch[1] + products([ch[1].astype(BF16)], diag(ch[0].astype(BF16)))[0]
        steps, sums = [], []
        for k, (i, j) in enumerate(subs):
            lc, rc = chains[2 * k], chains[2 * k + 1]
            moment = split2(packed(mo_ref[place(c, i, j)]))
            roots = split2(rc[1])
            step = precise(split2(lc[1]), diag(moment[0]), diag(moment[1]))
            step = precise(split2(step), diag(roots[0]), diag(roots[1])) * (lc[2] * rc[2])
            steps.append(step)
            sums += column_sums(step * step)
        total = block_sums(jnp.concatenate(sums, 0)) * (1.0 / (BLK * BLK))
        for k, (i, j) in enumerate(subs):
            at = place(c, i, j)
            old = w_ref[at]
            step = flat_of(steps[k] * lax.rsqrt(over_blocks(total, k * halves) + 1e-06))
            wo_ref[at] = old - RATE_HIDDEN * (step + WEIGHT_DECAY * old)

    def round_(i, _):
        @pl.when(jnp.logical_and(me < workers, i < turns))
        def _():
            @pl.when(i + AHEAD < turns)
            def _():
                start_first(i + AHEAD)

            @pl.when(i == LAG)
            def _():
                start_rest()

            add_up(i)

        c = (index // groups + 2 * turns + LAG - i) % turns

        @pl.when(jnp.logical_and(i >= LAG, c < CRIT))
        def _():
            blocked(c)

        return 0

    lax.fori_loop(0, turns + LAG, round_, 0)

    def arrived_small(i, _):
        pltpu.make_async_copy(small_ref.at[0], shares.at[i // mine, i % mine], recv_s.at[i // mine, i % mine]).wait()
        return 0

    lax.fori_loop(0, groups * mine, arrived_small, 0)
    for g in range(columns // LANES):
        part = jnp.zeros((32, LANES), F32)
        for j in range(mine):
            if j * chunk_width // LANES == g:
                value = shares[0, j]
                for r in range(1, groups):
                    value = value + shares[r, j]
                turn = j * chunk_width % LANES
                moved = pltpu.roll(value, turn, 1) if turn else value
                part = jnp.where(iota((32, LANES), 1) // chunk_width == turn // chunk_width, moved, part)
        own_ref[:, g * LANES : (g + 1) * LANES] = part

    def arrived_total(k, _):
        @pl.when(k != me)
        def _():
            pltpu.make_async_copy(sums_ref, totals.at[k], recv_t.at[k]).wait()

        return 0

    lax.fori_loop(0, workers, arrived_total, 0)
    out_ref[0:1, :] = jnp.sum(totals[:, 0, :], 0, keepdims=True)
    out_ref[1:2, :] = totals[0, 1:2, :]
    out_ref[2:8, :] = jnp.zeros((6, LANES), F32)

    @pl.when(me < workers)
    def _():
        def finish(step, _):
            def one(i, _):
                s, copy = first_hop(step, i)

                @pl.when(s < n)
                def _():
                    copy.wait_send()

                return 0

            lax.fori_loop(0, groups - 1, one, 0)
            s, copy = second_hop(step)

            @pl.when(jnp.logical_and(s < n, s != index))
            def _():
                copy.wait_send()

            return 0

        lax.fori_loop(0, turns, finish, 0)

        def finish_small(q, _):
            s, copy = small_hop(q)

            @pl.when(s != index)
            def _():
                copy.wait_send()

            return 0

        lax.fori_loop(0, per, finish_small, 0)

        def finish_total(i, _):
            total_hop((index + i) % n).wait_send()
            return 0

        lax.fori_loop(1, n, finish_total, 0)


def shampoo(plan, columns, grad, lowered, small, sums, moment, left, right, weight):
    vmem = pl.BlockSpec(memory_space=pltpu.VMEM)
    shape = jax.ShapeDtypeStruct(moment.shape, F32)
    _width, mine, per = chunks_of(columns)
    piece = moment.shape[1:]
    dma = pltpu.SemaphoreType.DMA
    return pl.pallas_call(
        functools.partial(shampoo_kernel, plan),
        out_shape=(shape,) * 4
        + (jax.ShapeDtypeStruct((32, -(-columns // LANES) * LANES), F32), jax.ShapeDtypeStruct((8, LANES), F32)),
        in_specs=[vmem] * 8,
        out_specs=(vmem,) * 6,
        scratch_shapes=[
            pltpu.VMEM((plan.groups - 1, plan.turns) + piece, BF16),
            pltpu.VMEM((plan.turns,) + piece, BF16),
            pltpu.VMEM((CRIT,) + piece, BF16),
            pltpu.VMEM((plan.groups, mine, 32, LANES), F32),
            pltpu.VMEM((plan.workers, 8, LANES), F32),
            dma((plan.turns, plan.groups - 1)),
            dma((plan.groups - 1, plan.turns)),
            dma((plan.turns,)),
            dma((CRIT,)),
            dma((per,)),
            dma((plan.groups, mine)),
            dma((plan.n,)),
            dma((plan.workers,)),
        ],
        compiler_params=pltpu.CompilerParams(collective_id=2, has_side_effects=True, vmem_limit_bytes=24 * MIB),
        name="shampoo",
    )(grad, lowered, small, sums, moment, left, right, weight)


def adamw(grad, moment, square, weight, rate):
    moment_new = FIRST_DECAY * moment + (1.0 - FIRST_DECAY) * grad
    square_new = SECOND_DECAY * square + (1.0 - SECOND_DECAY) * grad * grad
    moment_hat = moment_new / (1.0 - FIRST_DECAY**STEP)
    square_hat = square_new / (1.0 - SECOND_DECAY**STEP)
    weight_new = weight - rate * (moment_hat / (jnp.sqrt(square_hat) + 1e-08) + WEIGHT_DECAY * weight)
    return (moment_new, square_new, weight_new)


def local(
    plan,
    state_action,
    next_state,
    reward,
    done_flags,
    noise_index,
    noise_table,
    subsets,
    policy_in,
    policy_mid,
    policy_out,
    critic_in,
    in_first,
    in_second,
    critic_norms,
    norm_first,
    norm_second,
    critic_head,
    head_first,
    head_second,
    critic_hidden,
    hidden_moment,
    left_stats,
    right_stats,
    target_in,
    target_norms,
    target_head,
    target_hidden,
):
    me = plan.rank(lax.axis_index("dp"), lax.axis_index("mp"))
    critic, group = me // plan.groups, me % plan.groups
    role = jnp.stack([critic, group, (me < plan.workers).astype(I32)])
    rows, columns = state_action.shape[0], critic_in.shape[1]
    width = chunks_of(columns)[0]
    facts = jnp.concatenate(
        [reward[None], jnp.stack([done_flags, noise_index, subsets[:, 0], subsets[:, 1]]).astype(F32), jnp.zeros((3, rows), F32)], 0
    )
    w_target, share, x, params = dispatch(
        plan,
        (critic_hidden, target_hidden, critic_in, critic_norms, target_in, target_norms, jnp.stack([target_head, critic_head]))
        + (state_action.T, next_state.T, facts, noise_table.T, policy_in, policy_mid, policy_out.T),
    )
    shares = (share,) + tuple(lax.ppermute(share, ("dp", "mp"), plan.shift(k)) for k in range(1, plan.groups))
    xc, q, info = target_values(plan, rows, width, role, x, w_target, params)
    q_all = share_values(plan, q)
    grad_hidden, lowered, grad_small, sums = critic_step(plan, width, role, info, xc, q_all, shares, params)
    hidden_momentum, left_renewed, right_renewed, hidden_updated, own, totals = shampoo(
        plan, columns, grad_hidden, lowered, grad_small, sums, hidden_moment, left_stats, right_stats, critic_hidden
    )
    own = own[:, :columns]
    loss_total, counted = totals[0, 0], totals[1, 0]
    in_moment, in_square, in_updated = adamw(own[:IN], in_first, in_second, critic_in, RATE_INPUT)
    norm_moment, norm_square, norm_updated = adamw(own[IN : IN + 4], norm_first, norm_second, critic_norms, RATE_NORMS)
    head_moment, head_square, head_updated = adamw(own[IN + 4], head_first, head_second, critic_head, RATE_HEAD)
    return (
        loss_total,
        counted,
        in_moment,
        in_square,
        in_updated,
        norm_moment,
        norm_square,
        norm_updated,
        head_moment,
        head_square,
        head_updated,
        hidden_momentum,
        left_renewed,
        right_renewed,
        hidden_updated,
    )


def solution(mesh):
    both = ("dp", "mp")
    rows, columns, flat, hidden = P(both, None), P(None, both), P(both), P(None, "mp", "dp")
    return jax.shard_map(
        functools.partial(local, Plan(mesh)),
        mesh=mesh,
        in_specs=(
            (rows, rows, flat, flat, flat, P(), rows, P(), P(), P())
            + (columns,) * 6
            + (flat,) * 3
            + (hidden,) * 4
            + (columns, columns, flat, hidden)
        ),
        out_specs=(P(), P()) + (columns,) * 6 + (flat,) * 3 + (hidden,) * 4,
        check_vma=False,
    )
```

```python
import functools
import math

import jax
import jax.numpy as jnp
from jax import lax
from jax.experimental import pallas as pl
from jax.experimental.pallas import tpu as pltpu
from jax.sharding import PartitionSpec as P

ACT = 6
OBS = 17
IN = 23
H = 1024
CRIT = 10
BLK = 32
NEWTON = 5
STEP = 10
REWARD_DISCOUNT = 0.99
ENTROPY_TEMP = 0.2
FIRST_DECAY = 0.9
SECOND_DECAY = 0.999
WEIGHT_DECAY = 0.01
RATE_INPUT = 0.1
RATE_NORMS = 0.3
RATE_HEAD = 0.03
RATE_HIDDEN = 0.01
MOMENTUM = 0.9
STAT_DECAY = 0.95

F32, BF16, I32 = jnp.float32, jnp.bfloat16, jnp.int32
MESH = pl.DeviceIdType.MESH
LANES = 128
HALF = 64
TILE = 256
AHEAD_TILES = 4
L_TGT = 23
L_BASE = 46
L_BOOT = 49
L_S0 = 50
L_S1 = 51
L_VALID = 52
L_CNT = 53
MIB = 1024 * 1024


def nn(a, b):
    return jnp.dot(a, b, preferred_element_type=F32)


def nt(a, b):
    return lax.dot_general(a, b, (((1,), (1,)), ((), ())), preferred_element_type=F32)


def tn(a, b):
    return lax.dot_general(a, b, (((0,), (0,)), ((), ())), preferred_element_type=F32)


def iota(shape, dim):
    return lax.broadcasted_iota(I32, shape, dim)


def split2(x):
    high = x.astype(BF16)
    return high, (x - high.astype(F32)).astype(BF16)


def split3(x):
    high = x.astype(BF16)
    rest = x - high.astype(F32)
    mid = rest.astype(BF16)
    return high, mid, (rest - mid.astype(F32)).astype(BF16)


def swish(values):
    return values * jax.nn.sigmoid(values)


class Plan:
    def __init__(self, mesh):
        self.n_dp, self.n_mp = mesh.shape["dp"], mesh.shape["mp"]
        self.n = self.n_dp * self.n_mp
        self.groups = self.n // CRIT
        self.workers = self.groups * CRIT
        self.turns = -(-self.n // self.groups)

    def rank(self, dp, mp):
        size = 4 * self.n_dp
        layer = mp // 4
        inner = dp * 4 + (mp % 4 + 2 * (dp % 2)) % 4
        if self.n != 32:
            return layer * size + inner
        far, near = layer // 2, jnp.logical_or(layer == 1, layer == 2)
        six = 24 + 3 * far + jnp.where(near, 2, 0)
        seven = jnp.where(near, 30 + far, 25 + 3 * far)
        return jnp.where(inner < 6, 6 * layer + inner, jnp.where(inner == 6, six, seven))

    def place(self, k):
        size = 4 * self.n_dp
        if self.n != 32:
            layer, inner = k // size, k % size
        else:
            extra = jnp.maximum(k - 24, 0)
            which, j = extra // 3, extra % 3
            layer = jnp.where(which == 0, j // 2, jnp.where(which == 1, 3 - j // 2, 1 + j))
            inner = jnp.where(which == 2, 7, 6 + j % 2)
            layer = jnp.where(k < 24, k // 6, layer)
            inner = jnp.where(k < 24, k % 6, inner)
        dp = inner // 4
        return dp, layer * 4 + (inner % 4 + 2 * (dp % 2)) % 4

    def device(self, s):
        return s // self.n_mp, s % self.n_mp

    @property
    def sets(self):
        return 4 if self.n == 32 else CRIT // 2

    def extra(self, q, group):
        if self.n != 32:
            return jnp.int32(-1)
        low = jnp.where(group < 2, q == 0, q == 1)
        high = jnp.where(group < 2, q == 3, q == 2)
        return jnp.where(low, 8, jnp.where(high, 9, -1))

    def shift(self, k):
        at = lambda c, r: sum(int(v) * m for v, m in zip(self.place(jnp.int32(c * self.groups + r)), (self.n_mp, 1)))
        with jax.ensure_compile_time_eval():
            return [(at(c, r), at(c, (r + k) % self.groups)) for c in range(CRIT) for r in range(self.groups)]

    def pairs(self, rows):
        per = -(-rows // self.groups)
        return -(-per // 32) * 16

    def cap(self, rows):
        return -(-(self.n * -(-rows // self.groups)) // (TILE * AHEAD_TILES)) * TILE * AHEAD_TILES


def chunks_of(columns):
    width = math.gcd(math.gcd(columns, H), HALF)
    return width, columns // width, H // width


def assemble(chunks_ref, width, shift):
    groups = []
    lane = iota((32, LANES), 1)
    for g in range(H // LANES):
        block = jnp.zeros((32, LANES), F32)
        for i in range(LANES // width):
            chunk = chunks_ref[g * (LANES // width) + i]
            turn = (i * width - shift) % LANES
            moved = pltpu.roll(chunk, turn, 1) if turn else chunk
            block = jnp.where(lane // width == i, moved, block)
        groups.append(block)
    return jnp.concatenate(groups, 1)


def greet_all(plan, dp, mp):
    barrier = pltpu.get_barrier_semaphore()

    def tell(s, _):
        sdp, smp = s // plan.n_mp, s % plan.n_mp

        @pl.when(jnp.logical_or(sdp != dp, smp != mp))
        def _():
            pl.semaphore_signal(barrier, inc=1, device_id=(sdp, smp), device_id_type=MESH)

        return 0

    lax.fori_loop(0, plan.n, tell, 0)


def await_all(plan):
    pl.semaphore_wait(pltpu.get_barrier_semaphore(), plan.n - 1)


def dispatch_kernel(
    plan,
    inputs,
    wt_ref,
    wc_ref,
    x_ref,
    p_ref,
    low,
    msg,
    wide,
    chunk,
    send_w,
    recv_w,
    pass_w,
    recv_c,
    send_x,
    recv_x,
    pass_x,
    send_p,
    recv_p,
    pass_p,
    stage,
    stage_sem,
):
    loads = [pltpu.make_async_copy(src, dst, stage_sem.at[k]) for k, (src, dst) in enumerate(zip(inputs, stage))]
    for load in loads:
        load.start()
    dp, mp = lax.axis_index("dp"), lax.axis_index("mp")
    greet_all(plan, dp, mp)
    crit_ref, targ_ref, crit_in, crit_norms, targ_in, targ_norms, head_ref = stage[:7]
    sa_ref, ns_ref, reward_ref, done_ref, index_ref, subs_ref, table_ref, pin_ref, pmid_ref, pout_ref = stage[7:]
    crit_small, targ_small = (crit_in, crit_norms), (targ_in, targ_norms)
    me = plan.rank(dp, mp)
    index = dp * plan.n_mp + mp
    groups, workers = plan.groups, plan.workers
    critic, group = me // groups, me % groups
    rw, cw = crit_ref.shape[1], crit_ref.shape[2]
    rows = sa_ref.shape[1]
    columns = crit_small[0].shape[1]
    width, mine, per = chunks_of(columns)

    for load in loads[:2]:
        load.wait()

    def to_low(c, _):
        low[0, c] = targ_ref[c].astype(BF16)
        low[1, c] = crit_ref[c].astype(BF16)
        return 0

    lax.fori_loop(0, CRIT, to_low, 0)
    await_all(plan)

    def w_slot(s):
        sdp, smp = plan.device(s)
        return wt_ref.at[pl.ds(pl.multiple_of(smp * rw, rw), rw), pl.ds(pl.multiple_of(sdp * cw, cw), cw)]

    def to_worker(src, dst, send, recv, k):
        return pltpu.make_async_remote_copy(
            src_ref=src, dst_ref=dst, send_sem=send, recv_sem=recv, device_id=plan.place(k), device_id_type=MESH
        )

    turn = index // groups

    def first_hop(t, c):
        k = c * groups + index % groups
        dst = w_slot(index) if t == 0 else wc_ref.at[turn]
        recv = recv_w.at[index] if t == 0 else recv_c.at[turn]
        return k, dst, recv, to_worker(low.at[t, c], dst, send_w.at[t, c], recv, k)

    def send_weights(t):
        def one(i, _):
            c = (critic + 2 * CRIT + i * (1 - 2 * (index % 2))) % CRIT
            k, dst, recv, copy = first_hop(t, c)

            @pl.when(k == me)
            def _():
                pltpu.make_async_copy(low.at[t, c], dst, recv).start()

            @pl.when(k != me)
            def _():
                copy.start()

            return 0

        lax.fori_loop(0, CRIT, one, 0)

    send_weights(0)

    for load in loads[2:]:
        load.wait()
    wide[...] = jnp.zeros_like(wide)
    for t, parts in enumerate((targ_small, crit_small)):
        wide[t, 0:IN, 0:columns] = parts[0][...]
        wide[t, IN : IN + 4, 0:columns] = parts[1][...]
        wide[t, IN + 4 : IN + 5, 0:columns] = head_ref[t : t + 1, :]
    for j in range(mine):
        start, offset = j * width // LANES * LANES, j * width % LANES
        both = [wide[t, :, start : start + LANES] for t in range(2)]
        turned = [pltpu.roll(v, turn, 1) if turn else v for v, turn in zip(both, ((-offset) % LANES, (HALF - offset) % LANES))]
        chunk[j] = jnp.where(iota((32, LANES), 1) < HALF, turned[0], turned[1])

    def small_hop(j):
        g = index * mine + j
        k = (g // per) * groups + g % groups
        return k, g % per, to_worker(chunk.at[j], p_ref.at[g % per], send_p.at[j], recv_p.at[g % per], k)

    def send_small(j, _):
        k, slot, copy = small_hop(j)

        @pl.when(k == me)
        def _():
            pltpu.make_async_copy(chunk.at[j], p_ref.at[slot], recv_p.at[slot]).start()

        @pl.when(k != me)
        def _():
            copy.start()

        return 0

    lax.fori_loop(0, mine, send_small, 0)

    lane = iota((rows, LANES), 1)
    place = lambda height, offset: (iota((height, LANES), 1) == iota((height, LANES), 0) + offset).astype(F32).astype(BF16)
    hidden = swish(tn(ns_ref[...], pin_ref[...])).astype(BF16)
    hidden = swish(nn(hidden, pmid_ref[...])).astype(BF16)
    pout = pout_ref[...]
    spread = lambda offset: tn(
        pout, (iota((2 * ACT, LANES), 0) == iota((2 * ACT, LANES), 1) + offset).astype(F32).astype(BF16)
    ).astype(BF16)
    keep = lane < ACT
    means = nn(hidden, spread(0))
    raw = nn(hidden, spread(ACT))
    across = []
    for i in range(rows // LANES):
        lines = [reward_ref[i : i + 1, :], done_ref[i : i + 1, :].astype(F32), index_ref[i : i + 1, :].astype(F32)]
        lines += [subs_ref[:, i * LANES : (i + 1) * LANES].astype(F32), jnp.zeros((3, LANES), F32)]
        across.append(jnp.transpose(jnp.concatenate(lines, 0)))
    across = jnp.concatenate(across, 0)
    picked = (iota((rows, table_ref.shape[1]), 1) == across[:, 2:3].astype(I32)).astype(F32).astype(BF16)
    noise = jnp.zeros((rows, LANES), F32)
    for part in split3(table_ref[...]):
        noise = noise + nn(picked, tn(part, place(ACT, 0)).astype(BF16))
    log_std = -5.0 + 3.5 * (jnp.tanh(raw) + 1.0)
    squashed = means + jnp.exp(log_std) * noise
    action = jnp.tanh(squashed).astype(BF16)
    twice = -2.0 * squashed
    softplus = jnp.maximum(twice, 0.0) + jnp.log(1.0 + jnp.exp(-jnp.abs(twice)))
    correction = 2.0 * (math.log(2.0) - squashed - softplus)
    density = jnp.sum(
        jnp.where(keep, -0.5 * noise * noise - log_std - 0.5 * math.log(2.0 * math.pi) - correction, 0.0), -1, keepdims=True
    )
    done = across[:, 1:2]
    boot = (done == 0.0).astype(F32)
    base = across[:, 0:1] - (REWARD_DISCOUNT * ENTROPY_TEMP) * boot * density
    high, mid, rest = split3(base)
    on = lambda k, value: jnp.where(lane == k, value, 0.0)
    features = (
        tn(sa_ref[...], place(IN, 0))
        + tn(ns_ref[...], place(OBS, L_TGT))
        + nn(jnp.where(keep, action.astype(F32), 0.0).astype(BF16), place(LANES, L_TGT + OBS))
        + on(L_BASE, high.astype(F32))
        + on(L_BASE + 1, mid.astype(F32))
        + on(L_BASE + 2, rest.astype(F32))
        + on(L_BOOT, boot)
        + on(L_S0, across[:, 3:4])
        + on(L_S1, across[:, 4:5])
        + on(L_VALID, 1.0)
    ).astype(BF16)

    pairs = msg.shape[1]
    done_row = jnp.concatenate([done_ref[i : i + 1, :] for i in range(rows // LANES)], 1)
    valid = (done_row != 2).astype(F32)
    before = (iota((rows, rows), 0) < iota((rows, rows), 1)).astype(F32).astype(BF16)
    order = nn(jnp.broadcast_to(valid, (8, rows)).astype(BF16), before)[0:1, :]
    order = jnp.where(valid > 0.0, order, -1.0)
    count = jnp.sum(valid, -1, keepdims=True)
    count_half = jnp.floor(count * 0.5)
    mlane = iota((pairs, LANES), 1)
    tail = jnp.where(mlane == L_CNT, count_half, 0.0) + jnp.where(mlane == L_CNT + 1, count - 2.0 * count_half, 0.0)

    def deal(r, _):
        slot = iota((pairs, rows), 0) * (2 * groups) + r
        halves = []
        for h in range(2):
            hot = (order == (slot + h * groups).astype(F32)).astype(F32).astype(BF16)
            halves.append(nn(hot, features))
        msg[r] = (halves[0] + pltpu.roll(halves[1], HALF, 1) + tail).astype(BF16)
        return 0

    lax.fori_loop(0, groups, deal, 0)

    def row_hop(i):
        r = i % groups
        k = (2 * (i // groups) + index % 2) * groups + r
        return r, k, to_worker(msg.at[r], x_ref.at[index], send_x.at[i], recv_x.at[index], k)

    hops = plan.sets * groups

    def send_rows(i, _):
        r, k, copy = row_hop((i + (critic // 2) * groups) % hops)

        @pl.when(k == me)
        def _():
            pltpu.make_async_copy(msg.at[r], x_ref.at[index], recv_x.at[index]).start()

        @pl.when(k != me)
        def _():
            copy.start()

        return 0

    lax.fori_loop(0, hops, send_rows, 0)
    send_weights(1)

    def peer(i):
        return critic * groups + (group + 1 + i) % groups

    def pass_weight(t, i):
        s = group + groups * t
        return to_worker(w_slot(s), w_slot(s), pass_w.at[t, i], recv_w.at[s], peer(i))

    def pass_small(slot, i):
        return to_worker(p_ref.at[slot], p_ref.at[slot], pass_p.at[slot // groups, i], recv_p.at[slot], peer(i))

    extra = plan.extra(critic // 2, group)

    def pass_rows(i, k, which):
        s = 2 * i + critic % 2
        return to_worker(x_ref.at[s], x_ref.at[s], pass_x.at[i, which], recv_x.at[s], k)

    def other_rows(i):
        return pass_rows(i, (critic + 1 - 2 * (critic % 2)) * groups + group, 0)

    def extra_rows(i):
        return pass_rows(i, extra * groups + group, 1)

    def arrived_w(s):
        pltpu.make_async_copy(low.at[0, 0], w_slot(s), recv_w.at[s]).wait()

    def arrived_x(s):
        pltpu.make_async_copy(msg.at[0], x_ref.at[s], recv_x.at[s]).wait()

    def arrived_p(slot):
        pltpu.make_async_copy(chunk.at[0], p_ref.at[slot], recv_p.at[slot]).wait()

    turns = (plan.n - group + groups - 1) // groups
    passes_rows = critic < 2 * plan.sets

    def peers(body):
        lax.fori_loop(0, groups - 1, lambda i, _: (body(i), 0)[1], 0)

    def each(count, body):
        lax.fori_loop(0, count, lambda i, _: (body(i), 0)[1], 0)

    @pl.when(me < workers)
    def _():
        def relay_weight(j):
            t = j
            if plan.turns == 11:
                step = j // 2
                away = jnp.where(step == 5, -3, ((step + 1) // 2) * (2 * (step % 2) - 1))
                t = (turn + 5 * (j % 2) + away + 2 * plan.turns) % plan.turns

            @pl.when(t < turns)
            def _():
                arrived_w(group + groups * t)
                peers(lambda i: pass_weight(t, i).start())

        each(plan.turns, relay_weight)

        @pl.when(passes_rows)
        def _():
            def relay_rows(i):
                arrived_x(2 * i + critic % 2)
                other_rows(i).start()

                @pl.when(extra >= 0)
                def _():
                    extra_rows(i).start()

            each(plan.n // 2, relay_rows)

        def relay_small(slot):
            @pl.when((critic * per + slot) % groups == group)
            def _():
                arrived_p(slot)
                peers(lambda i: pass_small(slot, i).start())

        each(per, relay_small)

        def arrived(s):
            @pl.when(s % groups != group)
            def _():
                arrived_w(s)

            @pl.when(jnp.logical_not(jnp.logical_and(passes_rows, s % 2 == critic % 2)))
            def _():
                arrived_x(s)

        each(plan.n, arrived)

        def arrived_small(slot):
            @pl.when((critic * per + slot) % groups != group)
            def _():
                arrived_p(slot)

        each(per, arrived_small)
        each(turns, lambda t: pltpu.make_async_copy(low.at[1, 0], wc_ref.at[t], recv_c.at[t]).wait())
        each(turns, lambda t: peers(lambda i: pass_weight(t, i).wait_send()))

        @pl.when(passes_rows)
        def _():
            def passed_rows(i):
                other_rows(i).wait_send()

                @pl.when(extra >= 0)
                def _():
                    extra_rows(i).wait_send()

            each(plan.n // 2, passed_rows)

        def passed_small(slot):
            @pl.when((critic * per + slot) % groups == group)
            def _():
                peers(lambda i: pass_small(slot, i).wait_send())

        each(per, passed_small)

    def sent_weights(c):
        for t in range(2):
            k, _dst, _recv, copy = first_hop(t, c)

            @pl.when(k != me)
            def _():
                copy.wait_send()

    each(CRIT, sent_weights)

    def sent_small(j):
        k, _slot, copy = small_hop(j)

        @pl.when(k != me)
        def _():
            copy.wait_send()

    each(mine, sent_small)

    def sent_rows(i):
        _r, k, copy = row_hop(i)

        @pl.when(k != me)
        def _():
            copy.wait_send()

    each(hops, sent_rows)


def dispatch(plan, inputs):
    critic_hidden, critic_in, state_action = inputs[0], inputs[2], inputs[7]
    rows = state_action.shape[1]
    pairs = plan.pairs(rows)
    columns = critic_in.shape[1]
    _width, mine, per = chunks_of(columns)
    anywhere = pl.BlockSpec(memory_space=pl.ANY)
    dma = pltpu.SemaphoreType.DMA
    return pl.pallas_call(
        functools.partial(dispatch_kernel, plan),
        out_shape=(
            jax.ShapeDtypeStruct((H, H), BF16),
            jax.ShapeDtypeStruct((plan.turns,) + critic_hidden.shape[1:], BF16),
            jax.ShapeDtypeStruct((plan.n, pairs, LANES), BF16),
            jax.ShapeDtypeStruct((per, 32, LANES), F32),
        ),
        in_specs=[(pl.BlockSpec(memory_space=pltpu.HBM),) * len(inputs)],
        out_specs=(anywhere,) * 4,
        scratch_shapes=[
            pltpu.VMEM((2,) + critic_hidden.shape, BF16),
            pltpu.VMEM((plan.groups, pairs, LANES), BF16),
            pltpu.VMEM((2, 32, -(-columns // LANES) * LANES), F32),
            pltpu.VMEM((mine, 32, LANES), F32),
            dma((2, CRIT)),
            dma((plan.n,)),
            dma((plan.turns, plan.groups - 1)),
            dma((plan.turns,)),
            dma((plan.sets * plan.groups,)),
            dma((plan.n,)),
            dma((plan.n // 2, 2)),
            dma((mine,)),
            dma((per,)),
            dma((-(-per // plan.groups), plan.groups - 1)),
            tuple(pltpu.VMEM(v.shape, v.dtype) for v in inputs),
            dma((len(inputs),)),
        ],
        compiler_params=pltpu.CompilerParams(collective_id=0, has_side_effects=True, vmem_limit_bytes=60 * MIB),
        name="dispatch",
    )(inputs)


def norm_parts(pre):
    centered = pre - jnp.sum(pre, -1, keepdims=True) * (1.0 / H)
    inv = lax.rsqrt(jnp.sum(centered * centered, -1, keepdims=True) * (1.0 / H) + 1e-05)
    return centered * inv, inv


def swish_parts(half):
    t = jnp.tanh(half)
    product = half * t
    return half + product, (1.0 + t) * (1.0 + (half - product))


def low_input(params):
    return jnp.where(iota((32, H), 0) < IN, params, 0.0).astype(BF16)


def input_layer(params, win_ref, gram_ref):
    weight = low_input(params).astype(F32)
    weight = weight - jnp.sum(weight, -1, keepdims=True) * (1.0 / H)
    win_ref[...] = jnp.zeros_like(win_ref)
    for k, part in enumerate(split3(weight)):
        win_ref[k * 32 : (k + 1) * 32, :] = part
    for k, part in enumerate(split3(nt(win_ref[...], win_ref[...]) * (1.0 / H))):
        gram_ref[k] = part


def input_norm(x, start, win_ref, gram_ref):
    row, lane = iota((LANES, LANES), 0), iota((LANES, LANES), 1)
    pick = jnp.logical_and(lane < 96, jnp.logical_and(lane % 32 < IN, row == lane % 32 + start))
    thrice = nn(x, pick.astype(F32).astype(BF16)).astype(BF16)
    image = sum(nn(thrice, gram_ref[k]) for k in range(3))
    var = jnp.sum(image * thrice.astype(F32), -1, keepdims=True)
    return nn(thrice, win_ref[...]), lax.rsqrt(jnp.maximum(var, 0.0) + 1e-05)


def tile_span(t):
    return pl.ds(pl.multiple_of(t * TILE, TILE), TILE)


def target_kernel(
    plan, width, x_ref, w_ref, p_ref, xc_ref, q_ref, info_ref, rows_f, picked, value, hot, win, par, flat_q, cnt_v, cnt_s, base_s, sem
):
    me = plan.rank(lax.axis_index("dp"), lax.axis_index("mp"))
    critic, group, active = me // plan.groups, me % plan.groups, (me < plan.workers).astype(I32)
    groups, n = plan.groups, plan.n
    pairs = x_ref.shape[1]
    first = x_ref[:, 0, :].astype(F32)
    lane = iota(first.shape, 1)
    counts = 2.0 * jnp.sum(jnp.where(lane == L_CNT, first, 0.0), -1, keepdims=True) + jnp.sum(
        jnp.where(lane == L_CNT + 1, first, 0.0), -1, keepdims=True
    )
    counts = jnp.where(active > 0, jnp.broadcast_to(counts, first.shape), 0.0)
    mine = jnp.floor((counts + (groups - 1 - group).astype(F32)) * (1.0 / groups) + 0.5 / groups)
    earlier = (iota((n, n), 1) < iota((n, n), 0)).astype(F32).astype(BF16)
    starts = nn(earlier, mine.astype(BF16))
    total = jnp.sum(counts, 0, keepdims=True)
    cnt_v[0:n, :] = mine.astype(I32)
    cnt_v[n : 2 * n, :] = starts.astype(I32)
    cnt_v[2 * n : 2 * n + 8, :] = jnp.broadcast_to(total, (8, LANES)).astype(I32)
    copy = pltpu.make_async_copy(cnt_v, cnt_s, sem)
    copy.start()
    par[...] = assemble(p_ref, width, 0)
    win[...] = jnp.zeros_like(win)
    win[0:32, :] = low_input(par[...])
    copy.wait()
    number = cnt_s[n - 1, 0] + cnt_s[2 * n - 1, 0]
    tiles = (number + TILE - 1) // TILE
    info_ref[0] = number
    info_ref[1] = cnt_s[2 * n, 0]

    def compact(s, _):
        block = x_ref[s].astype(F32)
        have, start = cnt_s[s, 0], cnt_s[n + s, 0]
        rows_f[pl.ds(start, pairs), :] = block
        rows_f[pl.ds(start + (have + 1) // 2, pairs), :] = pltpu.roll(block, HALF, 1)
        return 0

    @pl.when(active > 0)
    def _():
        lax.fori_loop(0, n, compact, 0, unroll=4)

    rows_f[pl.ds(number, AHEAD_TILES * TILE), :] = jnp.zeros((AHEAD_TILES * TILE, LANES), F32)
    bundles = (tiles + AHEAD_TILES - 1) // AHEAD_TILES

    until = (iota((TILE, TILE), 1) < iota((TILE, TILE), 0)).astype(F32).astype(BF16)
    place = iota((TILE, TILE), 1).astype(F32)
    this = critic.astype(F32)

    def choose(b, base):
        chosen, counts = [], []
        for i in range(AHEAD_TILES):
            t = b * AHEAD_TILES + i
            wide = rows_f[tile_span(t), :]
            x = wide.astype(BF16)
            xc_ref[tile_span(t), :] = x
            wanted = jnp.logical_or(wide[:, L_S0 : L_S0 + 1] == this, wide[:, L_S1 : L_S1 + 1] == this)
            wanted = jnp.where(jnp.logical_and(wanted, wide[:, L_BOOT : L_BOOT + 1] > 0.0), 1.0, 0.0)
            order = nn(until, jnp.broadcast_to(wanted, (TILE, LANES)).astype(BF16))[:, 0:1]
            to = (jnp.where(wanted > 0.0, order, -1.0) == place).astype(F32).astype(BF16)
            hot[t] = to
            chosen.append(tn(to, x))
            counts.append(jnp.sum(wanted).astype(I32))
        for i in range(AHEAD_TILES):
            picked[pl.ds(base, TILE), :] = chosen[i]
            base_s[b * AHEAD_TILES + i] = base
            base = base + counts[i]
        return base

    chosen_rows = lax.fori_loop(0, bundles, choose, 0)
    picked[pl.ds(chosen_rows, TILE), :] = jnp.zeros((TILE, LANES), F32)
    chosen_tiles = (chosen_rows + TILE - 1) // TILE
    half = jnp.where(iota((32, 1), 0) < IN + 4, 0.5, 1.0)
    par[...] = par[...] * half
    gain1, shift1, gain2, shift2, head = (par[IN + k : IN + k + 1, :] for k in range(5))

    def tile(t, _):
        x = pltpu.roll(picked[tile_span(t), :], LANES - L_TGT, 1).astype(BF16)
        z, _unused = norm_parts(nn(x, win[...]))
        y = z * gain1 + shift1
        act = (y + y * jnp.tanh(y)).astype(BF16)
        z, _unused = norm_parts(nn(act, w_ref[...]))
        y = z * gain2 + shift2
        q = jnp.sum((y + y * jnp.tanh(y)) * head, -1, keepdims=True)
        value[tile_span(t), :] = jnp.broadcast_to(q, (TILE, LANES))
        return 0

    lax.fori_loop(0, chosen_tiles, tile, 0)
    value[tile_span(chosen_tiles), :] = jnp.zeros((TILE, LANES), F32)

    def spread(b, _):
        lane = iota((TILE, LANES), 1)
        for i in range(AHEAD_TILES):
            t = b * AHEAD_TILES + i
            high, mid, rest = (v.astype(F32) for v in split3(value[pl.ds(base_s[t], TILE), :]))
            parts = jnp.where(lane == 0, high, jnp.where(lane == 1, mid, jnp.where(lane == 2, rest, 0.0)))
            q = jnp.broadcast_to(jnp.sum(nn(hot[t], parts.astype(BF16)), -1, keepdims=True), (TILE, LANES))
            for h in range(TILE // LANES):
                flat = jnp.transpose(q[h * LANES : (h + 1) * LANES, :])
                flat_q[pl.ds(t * (TILE // LANES) + h, 1), :] = flat[0:1, :]
        return 0

    lax.fori_loop(0, bundles, spread, 0)
    q_ref[...] = flat_q[...].astype(BF16)


def target_values(plan, rows, width, x, weights, params):
    capacity = plan.cap(rows)
    vmem = pl.BlockSpec(memory_space=pltpu.VMEM)
    smem = pl.BlockSpec(memory_space=pltpu.SMEM)
    return pl.pallas_call(
        functools.partial(target_kernel, plan, width),
        out_shape=(
            jax.ShapeDtypeStruct((capacity, LANES), BF16),
            jax.ShapeDtypeStruct((capacity // LANES, LANES), BF16),
            jax.ShapeDtypeStruct((2,), I32),
        ),
        in_specs=[vmem, vmem, vmem],
        out_specs=(vmem, vmem, smem),
        scratch_shapes=[
            pltpu.VMEM((capacity + AHEAD_TILES * TILE + x.shape[1], LANES), F32),
            pltpu.VMEM((capacity + TILE, LANES), F32),
            pltpu.VMEM((capacity + TILE, LANES), F32),
            pltpu.VMEM((capacity // TILE, TILE, TILE), BF16),
            pltpu.VMEM((LANES, H), BF16),
            pltpu.VMEM((32, H), F32),
            pltpu.VMEM((capacity // LANES, LANES), F32),
            pltpu.VMEM((2 * plan.n + 8, LANES), I32),
            pltpu.SMEM((2 * plan.n + 8, LANES), I32),
            pltpu.SMEM((capacity // TILE,), I32),
            pltpu.SemaphoreType.DMA,
        ],
        compiler_params=pltpu.CompilerParams(vmem_limit_bytes=28 * MIB),
        name="target_values",
    )(x, weights, params)


def share_kernel(plan, q_ref, all_ref, send, recv):
    dp, mp = lax.axis_index("dp"), lax.axis_index("mp")
    me = plan.rank(dp, mp)
    groups = plan.groups
    critic, group = me // groups, me % groups
    barrier = pltpu.get_barrier_semaphore()

    @pl.when(me < plan.workers)
    def _():
        def peer(i):
            other = (critic + i) % CRIT
            return other, plan.place(other * groups + group)

        def tell(i, _):
            pl.semaphore_signal(barrier, inc=1, device_id=peer(i)[1], device_id_type=MESH)
            return 0

        lax.fori_loop(1, CRIT, tell, 0)
        pl.semaphore_wait(barrier, CRIT - 1)
        all_ref[critic] = q_ref[...]

        def copy(i):
            other, device = peer(i)
            return pltpu.make_async_remote_copy(
                src_ref=q_ref,
                dst_ref=all_ref.at[critic],
                send_sem=send.at[other],
                recv_sem=recv.at[critic],
                device_id=device,
                device_id_type=MESH,
            )

        def start(i, _):
            copy(i).start()
            return 0

        lax.fori_loop(1, CRIT, start, 0)

        def finish(i, _):
            copy(i).wait_send()
            other = peer(i)[0]
            pltpu.make_async_copy(q_ref, all_ref.at[other], recv.at[other]).wait()
            return 0

        lax.fori_loop(1, CRIT, finish, 0)


def share_values(plan, q):
    vmem = pl.BlockSpec(memory_space=pltpu.VMEM)
    return pl.pallas_call(
        functools.partial(share_kernel, plan),
        out_shape=jax.ShapeDtypeStruct((CRIT,) + q.shape, BF16),
        in_specs=[vmem],
        out_specs=vmem,
        scratch_shapes=[pltpu.SemaphoreType.DMA((CRIT,)), pltpu.SemaphoreType.DMA((CRIT,))],
        compiler_params=pltpu.CompilerParams(collective_id=1, has_side_effects=True, vmem_limit_bytes=8 * MIB),
        name="share_values",
    )(q)


def critic_kernel(
    plan, width, info_ref, xc_ref, q_ref, shares, p_ref, grad_ref, lowered_ref, small_ref, sums_ref, w_ref, z_one, slope, act, low, fact, par, win, gram, picks, acc, q_all
):
    number = info_ref[0]
    scale = 2.0 / jnp.maximum(info_ref[1], 1).astype(F32)
    tiles = (number + TILE - 1) // TILE
    rw, cw = shares[0].shape[1:]
    me = plan.rank(lax.axis_index("dp"), lax.axis_index("mp"))
    for k, share in enumerate(shares):
        owner = (me % plan.groups + plan.groups - k) % plan.groups

        def gather(t, _):
            s = owner + plan.groups * t

            @pl.when(s < plan.n)
            def _():
                sdp, smp = plan.device(s)
                w_ref[pl.ds(pl.multiple_of(smp * rw, rw), rw), pl.ds(pl.multiple_of(sdp * cw, cw), cw)] = share[t]

            return 0

        lax.fori_loop(0, plan.turns, gather, 0)
    par[...] = assemble(p_ref, width, HALF)
    input_layer(par[...], win, gram)
    grad_ref[...] = jnp.zeros_like(grad_ref)
    acc[...] = jnp.zeros_like(acc)
    picks[...] = jnp.zeros_like(picks)
    q_all[...] = q_ref[...].astype(F32)
    sums_ref[...] = jnp.zeros_like(sums_ref)
    gain1, shift1, gain2, shift2, head = (par[IN + k : IN + k + 1, :] for k in range(5))

    hg = (0.5 * head) * gain2

    def fold(k, value):
        acc[32 + k * 8 : 40 + k * 8, :] += jnp.sum(value.reshape(TILE // 8, 8, H), 0)

    def tile(t, _):
        x = xc_ref[tile_span(t), :]
        wide = x.astype(F32)
        pre, inv_one = input_norm(x, 0, win, gram)
        z = pre * inv_one
        z_one[...] = z
        value, twice = swish_parts(z * (0.5 * gain1) + 0.5 * shift1)
        slope[...] = 0.5 * twice
        act[...] = value.astype(BF16)
        pre = nn(act[...], w_ref[...])
        for h in range(TILE // LANES):
            picks[0:CRIT, :] = q_all[:, pl.ds(t * (TILE // LANES) + h, 1), :].reshape(CRIT, LANES)
            table = jnp.transpose(picks[...])
            part = wide[h * LANES : (h + 1) * LANES, :]
            critic = iota(table.shape, 1).astype(F32)
            one = jnp.sum(jnp.where(critic == part[:, L_S0 : L_S0 + 1], table, 0.0), -1, keepdims=True)
            two = jnp.sum(jnp.where(critic == part[:, L_S1 : L_S1 + 1], table, 0.0), -1, keepdims=True)
            base = part[:, L_BASE : L_BASE + 1] + part[:, L_BASE + 1 : L_BASE + 2] + part[:, L_BASE + 2 : L_BASE + 3]
            goal = base + jnp.where(part[:, L_BOOT : L_BOOT + 1] > 0.0, REWARD_DISCOUNT * jnp.minimum(one, two), 0.0)
            fact[h * LANES : (h + 1) * LANES, 0:1] = goal
        z, inv = norm_parts(pre)
        value, twice = swish_parts(z * (0.5 * gain2) + 0.5 * shift2)
        q = jnp.sum(value * head, -1, keepdims=True)
        error = (q - fact[:, 0:1]) * wide[:, L_VALID : L_VALID + 1]
        sums_ref[0:1, :] += jnp.broadcast_to(jnp.sum(error * error, 0, keepdims=True), (1, LANES))
        dq = error * scale
        flat = jnp.transpose(jnp.broadcast_to(dq, (TILE, LANES)))[0:8, :]
        high, rest = split2(flat)
        weigh = jnp.concatenate([high, rest], 0)
        tz = twice * z
        for k, v in ((4, value), (3, twice), (2, tz)):
            acc[32 + k * 8 : 40 + k * 8, :] += nn(weigh, v.astype(BF16))[4:12]
        dz = twice * hg
        mean = jnp.sum(dz, -1, keepdims=True) * (1.0 / H)
        along = jnp.sum(tz * hg, -1, keepdims=True) * (1.0 / H)
        low[...] = ((inv * dq) * (dz - mean - z * along)).astype(BF16)
        down = nt(low[...], w_ref[...])
        grad_ref[...] += tn(act[...], low[...])
        z = z_one[...]
        dy = down * slope[...]
        fold(1, dy)
        fold(0, dy * z)
        dz = dy * gain1
        mean = jnp.sum(dz, -1, keepdims=True) * (1.0 / H)
        along = jnp.sum(dz * z, -1, keepdims=True) * (1.0 / H)
        acc[0:32, :] += tn(x[:, 0:32], (inv_one * (dz - mean - z * along)).astype(BF16))
        return 0

    lax.fori_loop(0, tiles, tile, 0)
    lowered_ref[...] = grad_ref[...].astype(BF16)
    sums_ref[1:2, :] = jnp.broadcast_to(info_ref[1].astype(F32), (1, LANES))
    for k in range(2, 5):
        total = jnp.sum(acc[32 + k * 8 : 40 + k * 8, :], 0, keepdims=True) * 0.25
        acc[32 + k * 8 : 40 + k * 8, :] = jnp.zeros((8, H), F32)
        acc[32 + k * 8 : 33 + k * 8, :] = total if k == 4 else total * (0.5 * head)
    for k in range(5):
        acc[IN + k : IN + k + 1, :] = jnp.sum(acc[32 + k * 8 : 40 + k * 8, :], 0, keepdims=True)
    for i in range(H // width):
        start, offset = i * width // LANES * LANES, i * width % LANES
        block = acc[0:32, start : start + LANES]
        small_ref[i] = pltpu.roll(block, LANES - offset, 1) if offset else block


def critic_step(plan, width, info, xc, q_all, shares, params):
    vmem = pl.BlockSpec(memory_space=pltpu.VMEM)
    smem = pl.BlockSpec(memory_space=pltpu.SMEM)
    return pl.pallas_call(
        functools.partial(critic_kernel, plan, width),
        out_shape=(
            jax.ShapeDtypeStruct((H, H), F32),
            jax.ShapeDtypeStruct((H, H), BF16),
            jax.ShapeDtypeStruct((H // width, 32, LANES), F32),
            jax.ShapeDtypeStruct((8, LANES), F32),
        ),
        in_specs=[smem, vmem, vmem, (vmem,) * plan.groups, vmem],
        out_specs=(vmem,) * 4,
        scratch_shapes=[
            pltpu.VMEM((H, H), BF16),
            pltpu.VMEM((TILE, H), F32),
            pltpu.VMEM((TILE, H), F32),
            pltpu.VMEM((TILE, H), BF16),
            pltpu.VMEM((TILE, H), BF16),
            pltpu.VMEM((TILE, LANES), F32),
            pltpu.VMEM((32, H), F32),
            pltpu.VMEM((LANES, H), BF16),
            pltpu.VMEM((3, LANES, LANES), BF16),
            pltpu.VMEM((16, LANES), F32),
            pltpu.VMEM((72, H), F32),
            pltpu.VMEM(q_all.shape, F32),
        ],
        compiler_params=pltpu.CompilerParams(vmem_limit_bytes=36 * MIB),
        name="critic_step",
    )(info, xc, q_all, shares, params)


PRECISE = 2


LAG = 3
AHEAD = 3


def shampoo_kernel(
    plan,
    g_ref,
    lowered_ref,
    small_ref,
    sums_ref,
    mom_ref,
    left_ref,
    right_ref,
    w_ref,
    mo_ref,
    lo_ref,
    ro_ref,
    wo_ref,
    own_ref,
    out_ref,
    parts,
    pieces,
    given,
    shares,
    totals,
    send_one,
    recv_one,
    send_two,
    recv_two,
    send_s,
    recv_s,
    send_t,
    recv_t,
):
    dp, mp = lax.axis_index("dp"), lax.axis_index("mp")
    me = plan.rank(dp, mp)
    index = dp * plan.n_mp + mp
    groups, workers, n, turns = plan.groups, plan.workers, plan.n, plan.turns
    critic, group = me // groups, me % groups
    rw, cw = mom_ref.shape[1], mom_ref.shape[2]
    mine, per = shares.shape[1], small_ref.shape[0]
    columns = own_ref.shape[1]
    chunk_width = H // per
    greet_all(plan, dp, mp)
    await_all(plan)

    def to_device(src, dst, send, recv, device):
        return pltpu.make_async_remote_copy(
            src_ref=src, dst_ref=dst, send_sem=send, recv_sem=recv, device_id=device, device_id_type=MESH
        )

    def block(s):
        sdp, smp = plan.device(s)
        return pl.ds(pl.multiple_of(smp * rw, rw), rw), pl.ds(pl.multiple_of(sdp * cw, cw), cw)

    def turn_of(step):
        return (step + critic) % turns

    def first_hop(step, i):
        other = (group + 1 + i) % groups
        turn = turn_of(step)
        s = other + groups * turn
        copy = to_device(
            lowered_ref.at[block(s)],
            parts.at[groups - 2 - i, turn],
            send_one.at[step, i],
            recv_one.at[groups - 2 - i, turn],
            plan.place(critic * groups + other),
        )
        return s, copy

    def second_hop(turn):
        s = group + groups * turn
        return s, to_device(pieces.at[turn], given.at[critic], send_two.at[turn], recv_two.at[critic], plan.device(s))

    def small_hop(q):
        g = critic * per + q
        s = g // mine
        return s, to_device(
            small_ref.at[q], shares.at[group, g % mine], send_s.at[q], recv_s.at[group, g % mine], plan.device(s)
        )

    def total_hop(s):
        return to_device(sums_ref, totals.at[me], send_t.at[s], recv_t.at[me], plan.device(s))

    def start_first(step):
        def one(i, _):
            s, copy = first_hop(step, i)

            @pl.when(s < n)
            def _():
                copy.start()

            return 0

        lax.fori_loop(0, groups - 1, one, 0)

    def start_rest():
        def start_small(q, _):
            s, copy = small_hop(q)

            @pl.when(s == index)
            def _():
                slot = (critic * per + q) % mine
                pltpu.make_async_copy(small_ref.at[q], shares.at[group, slot], recv_s.at[group, slot]).start()

            @pl.when(s != index)
            def _():
                copy.start()

            return 0

        lax.fori_loop(0, per, start_small, 0)
        totals[me] = sums_ref[...]

        def start_total(i, _):
            total_hop((index + i) % n).start()
            return 0

        lax.fori_loop(1, n, start_total, 0)

    @pl.when(me < workers)
    def _():
        for step in range(AHEAD):
            start_first(step)

    def add_up(step):
        turn = turn_of(step)
        s, copy = second_hop(turn)

        @pl.when(s < n)
        def _():
            for i in range(groups - 1):
                pltpu.make_async_copy(parts.at[0, 0], parts.at[i, turn], recv_one.at[i, turn]).wait()
            value = g_ref[block(s)]
            for i in range(groups - 1):
                value = value + parts[i, turn].astype(F32)
            pieces[turn] = value.astype(BF16)

            @pl.when(s == index)
            def _():
                pltpu.make_async_copy(pieces.at[turn], given.at[critic], recv_two.at[critic]).start()

            @pl.when(s != index)
            def _():
                copy.start()

    width = min(256, cw)
    halves = width // LANES
    high_rows = halves * BLK
    nr, nc = rw // BLK, cw // width
    subs = [(i, j) for i in range(nr) for j in range(nc)]
    mask = (iota((LANES, LANES), 0) // BLK == iota((LANES, LANES), 1) // BLK).astype(F32).astype(BF16)
    mask_wide = jnp.concatenate([mask] * halves, 1)
    eye = (iota((high_rows, LANES), 0) % BLK == iota((high_rows, LANES), 1) % BLK).astype(F32)
    eye_low = eye.astype(BF16)

    def packed(flat):
        return jnp.concatenate([flat[:, k * LANES : (k + 1) * LANES] for k in range(halves)], 0)

    def flat_of(x):
        return jnp.concatenate([x[k * BLK : (k + 1) * BLK] for k in range(halves)], 1)

    def tops(out, count):
        return [
            jnp.concatenate(
                [out[(i * halves + k) * BLK : (i * halves + k + 1) * BLK, k * LANES : (k + 1) * LANES] for k in range(halves)], 0
            )
            for i in range(count)
        ]

    def diag(x):
        return jnp.concatenate([flat_of(x)] * (LANES // BLK), 0) * mask_wide

    def diag_rows(x):
        tiled = [jnp.concatenate([x[k * BLK : (k + 1) * BLK]] * (LANES // BLK), 0) * mask for k in range(halves)]
        return jnp.concatenate(tiled, 0)

    def products(lhs, right):
        return tops(nn(jnp.concatenate(lhs, 0), right), len(lhs))

    def precise(parts, right, right_rest):
        high, rest = parts
        out = products([high, rest], right)
        return out[0] + out[1] + products([high], right_rest)[0]

    def block_sums(s):
        high, rest = split2(s)
        return nn(high, mask) + nn(rest, mask)

    def place(c, i, j):
        return (c, slice(i * BLK, (i + 1) * BLK), slice(j * width, (j + 1) * width))

    def column_sums(x):
        return [jnp.sum(x[k * BLK : (k + 1) * BLK].reshape(BLK // 8, 8, LANES), 0) for k in range(halves)]

    def over_blocks(total, spot):
        rows = [jnp.sum(total[(spot + k) * 8 : (spot + k + 1) * 8], 0, keepdims=True) for k in range(halves)]
        return jnp.concatenate([jnp.broadcast_to(row, (BLK, LANES)) for row in rows], 0)

    def blocked(c):
        pltpu.make_async_copy(pieces.at[0], given.at[c], recv_two.at[c]).wait()
        sums, stats = [], []
        for i, j in subs:
            at = place(c, i, j)
            grad = given[at].astype(F32)
            mo_ref[at] = MOMENTUM * mom_ref[at] + grad
            low = packed(grad.astype(BF16))
            square, flip = tops(nt(jnp.concatenate([low, eye_low], 0), diag_rows(low)), 2)
            left = STAT_DECAY * packed(left_ref[at]) + (1.0 - STAT_DECAY) * square
            right = products([flip.astype(BF16)], diag(low))[0]
            right = STAT_DECAY * packed(right_ref[at]) + (1.0 - STAT_DECAY) * right
            lo_ref[at] = flat_of(left)
            ro_ref[at] = flat_of(right)
            for stat in (left, right):
                stats.append(stat)
                sums += column_sums(stat * stat)
        total = block_sums(jnp.concatenate(sums, 0))
        chains = []
        for k, stat in enumerate(stats):
            inv = lax.rsqrt(over_blocks(total, k * halves))
            rest = (eye - stat * inv) * 0.25
            chains.append([rest, eye + rest, jnp.sqrt(jnp.sqrt(inv))])
        for it in range(NEWTON - 1):
            full = it < PRECISE
            squares = []
            for ch in chains:
                high, rest = split2(ch[0])
                lhs = [high] + ([rest] if full else []) + ([ch[1].astype(BF16)] if it > 0 else [])
                out = products(lhs, diag(high))
                power = out[0]
                if full:
                    power = power + out[1] + products([high], diag(rest))[0]
                if it > 0:
                    ch[1] = ch[1] + out[-1]
                squares.append(power)
            factors = [[diag(v) for v in split2(power)[: 2 if full else 1]] for power in squares]

            def times(x, right):
                parts = split2(x)
                return precise(parts, *right) if full else products([parts[0]], right[0])[0]

            terms = [
                5.0 * ch[0] + 3.75 * power + times(ch[0], right) for ch, power, right in zip(chains, squares, factors)
            ]
            for ch, power, right, term in zip(chains, squares, factors, terms):
                ch[0] = 2.5 * power + times(term, right)
        for ch in chains:
            ch[1] = ch[1] + products([ch[1].astype(BF16)], diag(ch[0].astype(BF16)))[0]
        steps, sums = [], []
        for k, (i, j) in enumerate(subs):
            lc, rc = chains[2 * k], chains[2 * k + 1]
            moment = split2(packed(mo_ref[place(c, i, j)]))
            roots = split2(rc[1])
            step = precise(split2(lc[1]), diag(moment[0]), diag(moment[1]))
            step = precise(split2(step), diag(roots[0]), diag(roots[1])) * (lc[2] * rc[2])
            steps.append(step)
            sums += column_sums(step * step)
        total = block_sums(jnp.concatenate(sums, 0)) * (1.0 / (BLK * BLK))
        for k, (i, j) in enumerate(subs):
            at = place(c, i, j)
            old = w_ref[at]
            step = flat_of(steps[k] * lax.rsqrt(over_blocks(total, k * halves) + 1e-06))
            wo_ref[at] = old - RATE_HIDDEN * (step + WEIGHT_DECAY * old)

    def round_(i, _):
        @pl.when(jnp.logical_and(me < workers, i < turns))
        def _():
            @pl.when(i + AHEAD < turns)
            def _():
                start_first(i + AHEAD)

            @pl.when(i == LAG)
            def _():
                start_rest()

            add_up(i)

        c = (index // groups + 2 * turns + LAG - i) % turns

        @pl.when(jnp.logical_and(i >= LAG, c < CRIT))
        def _():
            blocked(c)

        return 0

    lax.fori_loop(0, turns + LAG, round_, 0)

    def arrived_small(i, _):
        pltpu.make_async_copy(small_ref.at[0], shares.at[i // mine, i % mine], recv_s.at[i // mine, i % mine]).wait()
        return 0

    lax.fori_loop(0, groups * mine, arrived_small, 0)
    for g in range(columns // LANES):
        part = jnp.zeros((32, LANES), F32)
        for j in range(mine):
            if j * chunk_width // LANES == g:
                value = shares[0, j]
                for r in range(1, groups):
                    value = value + shares[r, j]
                turn = j * chunk_width % LANES
                moved = pltpu.roll(value, turn, 1) if turn else value
                part = jnp.where(iota((32, LANES), 1) // chunk_width == turn // chunk_width, moved, part)
        own_ref[:, g * LANES : (g + 1) * LANES] = part

    def arrived_total(k, _):
        @pl.when(k != me)
        def _():
            pltpu.make_async_copy(sums_ref, totals.at[k], recv_t.at[k]).wait()

        return 0

    lax.fori_loop(0, workers, arrived_total, 0)
    out_ref[0:1, :] = jnp.sum(totals[:, 0, :], 0, keepdims=True)
    out_ref[1:2, :] = totals[0, 1:2, :]
    out_ref[2:8, :] = jnp.zeros((6, LANES), F32)

    @pl.when(me < workers)
    def _():
        def finish(step, _):
            def one(i, _):
                s, copy = first_hop(step, i)

                @pl.when(s < n)
                def _():
                    copy.wait_send()

                return 0

            lax.fori_loop(0, groups - 1, one, 0)
            s, copy = second_hop(step)

            @pl.when(jnp.logical_and(s < n, s != index))
            def _():
                copy.wait_send()

            return 0

        lax.fori_loop(0, turns, finish, 0)

        def finish_small(q, _):
            s, copy = small_hop(q)

            @pl.when(s != index)
            def _():
                copy.wait_send()

            return 0

        lax.fori_loop(0, per, finish_small, 0)

        def finish_total(i, _):
            total_hop((index + i) % n).wait_send()
            return 0

        lax.fori_loop(1, n, finish_total, 0)


def shampoo(plan, columns, grad, lowered, small, sums, moment, left, right, weight):
    vmem = pl.BlockSpec(memory_space=pltpu.VMEM)
    shape = jax.ShapeDtypeStruct(moment.shape, F32)
    _width, mine, per = chunks_of(columns)
    piece = moment.shape[1:]
    dma = pltpu.SemaphoreType.DMA
    return pl.pallas_call(
        functools.partial(shampoo_kernel, plan),
        out_shape=(shape,) * 4
        + (jax.ShapeDtypeStruct((32, -(-columns // LANES) * LANES), F32), jax.ShapeDtypeStruct((8, LANES), F32)),
        in_specs=[vmem] * 8,
        out_specs=(vmem,) * 6,
        scratch_shapes=[
            pltpu.VMEM((plan.groups - 1, plan.turns) + piece, BF16),
            pltpu.VMEM((plan.turns,) + piece, BF16),
            pltpu.VMEM((CRIT,) + piece, BF16),
            pltpu.VMEM((plan.groups, mine, 32, LANES), F32),
            pltpu.VMEM((plan.workers, 8, LANES), F32),
            dma((plan.turns, plan.groups - 1)),
            dma((plan.groups - 1, plan.turns)),
            dma((plan.turns,)),
            dma((CRIT,)),
            dma((per,)),
            dma((plan.groups, mine)),
            dma((plan.n,)),
            dma((plan.workers,)),
        ],
        compiler_params=pltpu.CompilerParams(collective_id=2, has_side_effects=True, vmem_limit_bytes=24 * MIB),
        name="shampoo",
    )(grad, lowered, small, sums, moment, left, right, weight)


def adamw(grad, moment, square, weight, rate):
    moment_new = FIRST_DECAY * moment + (1.0 - FIRST_DECAY) * grad
    square_new = SECOND_DECAY * square + (1.0 - SECOND_DECAY) * grad * grad
    moment_hat = moment_new / (1.0 - FIRST_DECAY**STEP)
    square_hat = square_new / (1.0 - SECOND_DECAY**STEP)
    weight_new = weight - rate * (moment_hat / (jnp.sqrt(square_hat) + 1e-08) + WEIGHT_DECAY * weight)
    return (moment_new, square_new, weight_new)


def local(
    plan,
    state_action,
    next_state,
    reward,
    done_flags,
    noise_index,
    noise_table,
    subsets,
    policy_in,
    policy_mid,
    policy_out,
    critic_in,
    in_first,
    in_second,
    critic_norms,
    norm_first,
    norm_second,
    critic_head,
    head_first,
    head_second,
    critic_hidden,
    hidden_moment,
    left_stats,
    right_stats,
    target_in,
    target_norms,
    target_head,
    target_hidden,
):
    rows, columns = state_action.shape[0], critic_in.shape[1]
    width = chunks_of(columns)[0]
    lines = lambda v: v.reshape(rows // LANES, LANES)
    w_target, share, x, params = dispatch(
        plan,
        (critic_hidden, target_hidden, critic_in, critic_norms, target_in, target_norms, jnp.stack([target_head, critic_head]))
        + (state_action.T, next_state.T, lines(reward), lines(done_flags), lines(noise_index), subsets.T)
        + (noise_table.T, policy_in, policy_mid, policy_out.T),
    )
    shares = (share,) + tuple(lax.ppermute(share, ("dp", "mp"), plan.shift(k)) for k in range(1, plan.groups))
    xc, q, info = target_values(plan, rows, width, x, w_target, params)
    q_all = share_values(plan, q)
    grad_hidden, lowered, grad_small, sums = critic_step(plan, width, info, xc, q_all, shares, params)
    hidden_momentum, left_renewed, right_renewed, hidden_updated, own, totals = shampoo(
        plan, columns, grad_hidden, lowered, grad_small, sums, hidden_moment, left_stats, right_stats, critic_hidden
    )
    own = own[:, :columns]
    loss_total, counted = totals[0, 0], totals[1, 0]
    in_moment, in_square, in_updated = adamw(own[:IN], in_first, in_second, critic_in, RATE_INPUT)
    norm_moment, norm_square, norm_updated = adamw(own[IN : IN + 4], norm_first, norm_second, critic_norms, RATE_NORMS)
    head_moment, head_square, head_updated = adamw(own[IN + 4], head_first, head_second, critic_head, RATE_HEAD)
    return (
        loss_total,
        counted,
        in_moment,
        in_square,
        in_updated,
        norm_moment,
        norm_square,
        norm_updated,
        head_moment,
        head_square,
        head_updated,
        hidden_momentum,
        left_renewed,
        right_renewed,
        hidden_updated,
    )


def solution(mesh):
    both = ("dp", "mp")
    rows, columns, flat, hidden = P(both, None), P(None, both), P(both), P(None, "mp", "dp")
    return jax.shard_map(
        functools.partial(local, Plan(mesh)),
        mesh=mesh,
        in_specs=(
            (rows, rows, flat, flat, flat, P(), rows, P(), P(), P())
            + (columns,) * 6
            + (flat,) * 3
            + (hidden,) * 4
            + (columns, columns, flat, hidden)
        ),
        out_specs=(P(), P()) + (columns,) * 6 + (flat,) * 3 + (hidden,) * 4,
        check_vma=False,
    )
```

```python
import functools
import math

import jax
import jax.numpy as jnp
from jax import lax
from jax.experimental import pallas as pl
from jax.experimental.pallas import tpu as pltpu
from jax.sharding import PartitionSpec as P

ACT = 6
OBS = 17
IN = 23
H = 1024
CRIT = 10
BLK = 32
NEWTON = 5
STEP = 10
REWARD_DISCOUNT = 0.99
ENTROPY_TEMP = 0.2
FIRST_DECAY = 0.9
SECOND_DECAY = 0.999
WEIGHT_DECAY = 0.01
RATE_INPUT = 0.1
RATE_NORMS = 0.3
RATE_HEAD = 0.03
RATE_HIDDEN = 0.01
MOMENTUM = 0.9
STAT_DECAY = 0.95

F32, BF16, I32 = jnp.float32, jnp.bfloat16, jnp.int32
MESH = pl.DeviceIdType.MESH
LANES = 128
HALF = 64
TILE = 256
AHEAD_TILES = 4
L_TGT = 23
L_BASE = 46
L_BOOT = 49
L_S0 = 50
L_S1 = 51
L_VALID = 52
L_CNT = 53
MIB = 1024 * 1024
TARGET_MIB = 28


def nn(a, b):
    return jnp.dot(a, b, preferred_element_type=F32)


def nt(a, b):
    return lax.dot_general(a, b, (((1,), (1,)), ((), ())), preferred_element_type=F32)


def tn(a, b):
    return lax.dot_general(a, b, (((0,), (0,)), ((), ())), preferred_element_type=F32)


def iota(shape, dim):
    return lax.broadcasted_iota(I32, shape, dim)


def split2(x):
    high = x.astype(BF16)
    return high, (x - high.astype(F32)).astype(BF16)


def split3(x):
    high = x.astype(BF16)
    rest = x - high.astype(F32)
    mid = rest.astype(BF16)
    return high, mid, (rest - mid.astype(F32)).astype(BF16)


def swish(values):
    return values * jax.nn.sigmoid(values)


class Plan:
    def __init__(self, mesh):
        self.n_dp, self.n_mp = mesh.shape["dp"], mesh.shape["mp"]
        self.n = self.n_dp * self.n_mp
        self.groups = self.n // CRIT
        self.workers = self.groups * CRIT
        self.turns = -(-self.n // self.groups)

    def rank(self, dp, mp):
        size = 4 * self.n_dp
        layer = mp // 4
        inner = dp * 4 + (mp % 4 + 2 * (dp % 2)) % 4
        if self.n != 32:
            return layer * size + inner
        far, near = layer // 2, jnp.logical_or(layer == 1, layer == 2)
        six = 24 + 3 * far + jnp.where(near, 2, 0)
        seven = jnp.where(near, 30 + far, 25 + 3 * far)
        return jnp.where(inner < 6, 6 * layer + inner, jnp.where(inner == 6, six, seven))

    def place(self, k):
        size = 4 * self.n_dp
        if self.n != 32:
            layer, inner = k // size, k % size
        else:
            extra = jnp.maximum(k - 24, 0)
            which, j = extra // 3, extra % 3
            layer = jnp.where(which == 0, j // 2, jnp.where(which == 1, 3 - j // 2, 1 + j))
            inner = jnp.where(which == 2, 7, 6 + j % 2)
            layer = jnp.where(k < 24, k // 6, layer)
            inner = jnp.where(k < 24, k % 6, inner)
        dp = inner // 4
        return dp, layer * 4 + (inner % 4 + 2 * (dp % 2)) % 4

    def device(self, s):
        return s // self.n_mp, s % self.n_mp

    @property
    def sets(self):
        return 4 if self.n == 32 else CRIT // 2

    def extra(self, q, group):
        if self.n != 32:
            return jnp.int32(-1)
        low = jnp.where(group < 2, q == 0, q == 1)
        high = jnp.where(group < 2, q == 3, q == 2)
        return jnp.where(low, 8, jnp.where(high, 9, -1))

    def shift(self, k):
        at = lambda c, r: sum(int(v) * m for v, m in zip(self.place(jnp.int32(c * self.groups + r)), (self.n_mp, 1)))
        with jax.ensure_compile_time_eval():
            return [(at(c, r), at(c, (r + k) % self.groups)) for c in range(CRIT) for r in range(self.groups)]

    def pairs(self, rows):
        per = -(-rows // self.groups)
        return -(-per // 32) * 16

    def cap(self, rows):
        return -(-(self.n * -(-rows // self.groups)) // (TILE * AHEAD_TILES)) * TILE * AHEAD_TILES


def chunks_of(columns):
    width = math.gcd(math.gcd(columns, H), HALF)
    return width, columns // width, H // width


def assemble(chunks_ref, width, shift):
    groups = []
    lane = iota((32, LANES), 1)
    for g in range(H // LANES):
        block = jnp.zeros((32, LANES), F32)
        for i in range(LANES // width):
            chunk = chunks_ref[g * (LANES // width) + i]
            turn = (i * width - shift) % LANES
            moved = pltpu.roll(chunk, turn, 1) if turn else chunk
            block = jnp.where(lane // width == i, moved, block)
        groups.append(block)
    return jnp.concatenate(groups, 1)


def greet_all(plan, dp, mp):
    barrier = pltpu.get_barrier_semaphore()

    def tell(s, _):
        sdp, smp = s // plan.n_mp, s % plan.n_mp

        @pl.when(jnp.logical_or(sdp != dp, smp != mp))
        def _():
            pl.semaphore_signal(barrier, inc=1, device_id=(sdp, smp), device_id_type=MESH)

        return 0

    lax.fori_loop(0, plan.n, tell, 0)


def await_all(plan):
    pl.semaphore_wait(pltpu.get_barrier_semaphore(), plan.n - 1)


def dispatch_kernel(
    plan,
    inputs,
    wt_ref,
    wc_ref,
    x_ref,
    p_ref,
    low,
    msg,
    wide,
    chunk,
    send_w,
    recv_w,
    pass_w,
    recv_c,
    send_x,
    recv_x,
    pass_x,
    send_p,
    recv_p,
    pass_p,
    stage,
    stage_sem,
):
    loads = [pltpu.make_async_copy(src, dst, stage_sem.at[k]) for k, (src, dst) in enumerate(zip(inputs, stage))]
    for load in loads:
        load.start()
    dp, mp = lax.axis_index("dp"), lax.axis_index("mp")
    greet_all(plan, dp, mp)
    crit_ref, targ_ref, crit_in, crit_norms, targ_in, targ_norms, head_ref = stage[:7]
    sa_ref, ns_ref, reward_ref, done_ref, index_ref, subs_ref, table_ref, pin_ref, pmid_ref, pout_ref = stage[7:]
    crit_small, targ_small = (crit_in, crit_norms), (targ_in, targ_norms)
    me = plan.rank(dp, mp)
    index = dp * plan.n_mp + mp
    groups, workers = plan.groups, plan.workers
    critic, group = me // groups, me % groups
    rw, cw = crit_ref.shape[1], crit_ref.shape[2]
    rows = sa_ref.shape[1]
    columns = crit_small[0].shape[1]
    width, mine, per = chunks_of(columns)

    for load in loads[:2]:
        load.wait()

    def to_low(c, _):
        low[0, c] = targ_ref[c].astype(BF16)
        low[1, c] = crit_ref[c].astype(BF16)
        return 0

    lax.fori_loop(0, CRIT, to_low, 0)
    await_all(plan)

    def w_slot(s):
        sdp, smp = plan.device(s)
        return wt_ref.at[pl.ds(pl.multiple_of(smp * rw, rw), rw), pl.ds(pl.multiple_of(sdp * cw, cw), cw)]

    def to_worker(src, dst, send, recv, k):
        return pltpu.make_async_remote_copy(
            src_ref=src, dst_ref=dst, send_sem=send, recv_sem=recv, device_id=plan.place(k), device_id_type=MESH
        )

    turn = index // groups

    def first_hop(t, c):
        k = c * groups + index % groups
        dst = w_slot(index) if t == 0 else wc_ref.at[turn]
        recv = recv_w.at[turn] if t == 0 else recv_c.at[0]
        return k, dst, recv, to_worker(low.at[t, c], dst, send_w.at[0], recv, k)

    def send_weights(t):
        def one(i, _):
            c = (critic + 2 * CRIT + i * (1 - 2 * (index % 2))) % CRIT
            k, dst, recv, copy = first_hop(t, c)

            @pl.when(k == me)
            def _():
                pltpu.make_async_copy(low.at[t, c], dst, recv).start()

            @pl.when(k != me)
            def _():
                copy.start()

            return 0

        lax.fori_loop(0, CRIT, one, 0)

    send_weights(0)

    for load in loads[2:]:
        load.wait()
    wide[...] = jnp.zeros_like(wide)
    for t, parts in enumerate((targ_small, crit_small)):
        wide[t, 0:IN, 0:columns] = parts[0][...]
        wide[t, IN : IN + 4, 0:columns] = parts[1][...]
        wide[t, IN + 4 : IN + 5, 0:columns] = head_ref[t : t + 1, :]
    for j in range(mine):
        start, offset = j * width // LANES * LANES, j * width % LANES
        both = [wide[t, :, start : start + LANES] for t in range(2)]
        turned = [pltpu.roll(v, turn, 1) if turn else v for v, turn in zip(both, ((-offset) % LANES, (HALF - offset) % LANES))]
        chunk[j] = jnp.where(iota((32, LANES), 1) < HALF, turned[0], turned[1])

    def small_hop(j):
        g = index * mine + j
        k = (g // per) * groups + g % groups
        return k, g % per, to_worker(chunk.at[j], p_ref.at[g % per], send_p.at[j], recv_p.at[g % per], k)

    def send_small(j, _):
        k, slot, copy = small_hop(j)

        @pl.when(k == me)
        def _():
            pltpu.make_async_copy(chunk.at[j], p_ref.at[slot], recv_p.at[slot]).start()

        @pl.when(k != me)
        def _():
            copy.start()

        return 0

    lax.fori_loop(0, mine, send_small, 0)

    lane = iota((rows, LANES), 1)
    place = lambda height, offset: (iota((height, LANES), 1) == iota((height, LANES), 0) + offset).astype(F32).astype(BF16)
    hidden = swish(tn(ns_ref[...], pin_ref[...])).astype(BF16)
    hidden = swish(nn(hidden, pmid_ref[...])).astype(BF16)
    pout = pout_ref[...]
    spread = lambda offset: tn(
        pout, (iota((2 * ACT, LANES), 0) == iota((2 * ACT, LANES), 1) + offset).astype(F32).astype(BF16)
    ).astype(BF16)
    keep = lane < ACT
    means = nn(hidden, spread(0))
    raw = nn(hidden, spread(ACT))
    across = []
    for i in range(rows // LANES):
        lines = [reward_ref[i : i + 1, :], done_ref[i : i + 1, :].astype(F32), index_ref[i : i + 1, :].astype(F32)]
        lines += [subs_ref[:, i * LANES : (i + 1) * LANES].astype(F32), jnp.zeros((3, LANES), F32)]
        across.append(jnp.transpose(jnp.concatenate(lines, 0)))
    across = jnp.concatenate(across, 0)
    picked = (iota((rows, table_ref.shape[1]), 1) == across[:, 2:3].astype(I32)).astype(F32).astype(BF16)
    noise = jnp.zeros((rows, LANES), F32)
    for part in split3(table_ref[...]):
        noise = noise + nn(picked, tn(part, place(ACT, 0)).astype(BF16))
    log_std = -5.0 + 3.5 * (jnp.tanh(raw) + 1.0)
    squashed = means + jnp.exp(log_std) * noise
    action = jnp.tanh(squashed).astype(BF16)
    twice = -2.0 * squashed
    softplus = jnp.maximum(twice, 0.0) + jnp.log(1.0 + jnp.exp(-jnp.abs(twice)))
    correction = 2.0 * (math.log(2.0) - squashed - softplus)
    density = jnp.sum(
        jnp.where(keep, -0.5 * noise * noise - log_std - 0.5 * math.log(2.0 * math.pi) - correction, 0.0), -1, keepdims=True
    )
    done = across[:, 1:2]
    boot = (done == 0.0).astype(F32)
    base = across[:, 0:1] - (REWARD_DISCOUNT * ENTROPY_TEMP) * boot * density
    high, mid, rest = split3(base)
    on = lambda k, value: jnp.where(lane == k, value, 0.0)
    features = (
        tn(sa_ref[...], place(IN, 0))
        + tn(ns_ref[...], place(OBS, L_TGT))
        + nn(jnp.where(keep, action.astype(F32), 0.0).astype(BF16), place(LANES, L_TGT + OBS))
        + on(L_BASE, high.astype(F32))
        + on(L_BASE + 1, mid.astype(F32))
        + on(L_BASE + 2, rest.astype(F32))
        + on(L_BOOT, boot)
        + on(L_S0, across[:, 3:4])
        + on(L_S1, across[:, 4:5])
        + on(L_VALID, 1.0)
    ).astype(BF16)

    pairs = msg.shape[1]
    done_row = jnp.concatenate([done_ref[i : i + 1, :] for i in range(rows // LANES)], 1)
    valid = (done_row != 2).astype(F32)
    before = (iota((rows, rows), 0) < iota((rows, rows), 1)).astype(F32).astype(BF16)
    order = nn(jnp.broadcast_to(valid, (8, rows)).astype(BF16), before)[0:1, :]
    order = jnp.where(valid > 0.0, order, -1.0)
    count = jnp.sum(valid, -1, keepdims=True)
    count_half = jnp.floor(count * 0.5)
    mlane = iota((pairs, LANES), 1)
    tail = jnp.where(mlane == L_CNT, count_half, 0.0) + jnp.where(mlane == L_CNT + 1, count - 2.0 * count_half, 0.0)

    def deal(r, _):
        slot = iota((pairs, rows), 0) * (2 * groups) + r
        halves = []
        for h in range(2):
            hot = (order == (slot + h * groups).astype(F32)).astype(F32).astype(BF16)
            halves.append(nn(hot, features))
        msg[r] = (halves[0] + pltpu.roll(halves[1], HALF, 1) + tail).astype(BF16)
        return 0

    lax.fori_loop(0, groups, deal, 0)

    def row_hop(i):
        r = i % groups
        k = (2 * (i // groups) + index % 2) * groups + r
        return r, k, to_worker(msg.at[r], x_ref.at[index], send_x.at[0], recv_x.at[index], k)

    hops = plan.sets * groups

    def send_rows(i, _):
        r, k, copy = row_hop((i + (critic // 2) * groups) % hops)

        @pl.when(k == me)
        def _():
            pltpu.make_async_copy(msg.at[r], x_ref.at[index], recv_x.at[index]).start()

        @pl.when(k != me)
        def _():
            copy.start()

        return 0

    lax.fori_loop(0, hops, send_rows, 0)
    send_weights(1)

    def peer(i):
        return critic * groups + (group + 1 + i) % groups

    def pass_weight(t, i):
        s = group + groups * t
        return to_worker(w_slot(s), w_slot(s), pass_w.at[i], recv_w.at[plan.turns + groups - 2 - i], peer(i))

    def pass_small(slot, i):
        return to_worker(p_ref.at[slot], p_ref.at[slot], pass_p.at[slot // groups, i], recv_p.at[slot], peer(i))

    extra = plan.extra(critic // 2, group)

    def pass_rows(i, k, which):
        s = 2 * i + critic % 2
        return to_worker(x_ref.at[s], x_ref.at[s], pass_x.at[which], recv_x.at[plan.n], k)

    def other_rows(i):
        return pass_rows(i, (critic + 1 - 2 * (critic % 2)) * groups + group, 0)

    def extra_rows(i):
        return pass_rows(i, extra * groups + group, 1)

    def arrived_w(t):
        pltpu.make_async_copy(low.at[0, 0], w_slot(group + groups * t), recv_w.at[t]).wait()

    def blocks_done(sem, number):
        some = (plan.n - number + groups - 1) // groups

        @pl.when(some == plan.turns)
        def _():
            pltpu.make_async_copy(wc_ref, wc_ref, sem).wait()

        @pl.when(some != plan.turns)
        def _():
            fewer = wc_ref.at[pl.ds(0, plan.turns - 1)]
            pltpu.make_async_copy(fewer, fewer, sem).wait()

    def rows_done(sem, count):
        some = x_ref.at[pl.ds(0, count)]
        pltpu.make_async_copy(some, some, sem).wait()

    def arrived_x(s):
        pltpu.make_async_copy(msg.at[0], x_ref.at[s], recv_x.at[s]).wait()

    def arrived_p(slot):
        pltpu.make_async_copy(chunk.at[0], p_ref.at[slot], recv_p.at[slot]).wait()

    turns = (plan.n - group + groups - 1) // groups
    passes_rows = critic < 2 * plan.sets

    def peers(body):
        lax.fori_loop(0, groups - 1, lambda i, _: (body(i), 0)[1], 0)

    def each(count, body):
        lax.fori_loop(0, count, lambda i, _: (body(i), 0)[1], 0)

    @pl.when(me < workers)
    def _():
        def relay_weight(j):
            t = j
            if plan.turns == 11:
                step = j // 2
                away = jnp.where(step == 5, -3, ((step + 1) // 2) * (2 * (step % 2) - 1))
                t = (turn + 5 * (j % 2) + away + 2 * plan.turns) % plan.turns

            @pl.when(t < turns)
            def _():
                arrived_w(t)
                peers(lambda i: pass_weight(t, i).start())

        each(plan.turns, relay_weight)

        @pl.when(passes_rows)
        def _():
            def relay_rows(i):
                arrived_x(2 * i + critic % 2)
                other_rows(i).start()

                @pl.when(extra >= 0)
                def _():
                    extra_rows(i).start()

            each(plan.n // 2, relay_rows)

        def relay_small(slot):
            @pl.when((critic * per + slot) % groups == group)
            def _():
                arrived_p(slot)
                peers(lambda i: pass_small(slot, i).start())

        each(per, relay_small)

        peers(lambda i: blocks_done(recv_w.at[plan.turns + i], (group + 1 + i) % groups))

        @pl.when(passes_rows)
        def _():
            rows_done(recv_x.at[plan.n], plan.n // 2)

        @pl.when(jnp.logical_not(passes_rows))
        def _():
            rows_done(recv_x.at[plan.n], plan.n)

        def arrived_small(slot):
            @pl.when((critic * per + slot) % groups != group)
            def _():
                arrived_p(slot)

        each(per, arrived_small)
        blocks_done(recv_c.at[0], group)
        peers(lambda i: blocks_done(pass_w.at[i], group))

        @pl.when(passes_rows)
        def _():
            rows_done(pass_x.at[0], plan.n // 2)

            @pl.when(extra >= 0)
            def _():
                rows_done(pass_x.at[1], plan.n // 2)

        def passed_small(slot):
            @pl.when((critic * per + slot) % groups == group)
            def _():
                peers(lambda i: pass_small(slot, i).wait_send())

        each(per, passed_small)

    at_home = jnp.logical_and(me < workers, index % groups == group)

    @pl.when(at_home)
    def _():
        sent = low.at[:, pl.ds(0, CRIT - 1)]
        pltpu.make_async_copy(sent, sent, send_w.at[0]).wait()

    @pl.when(jnp.logical_not(at_home))
    def _():
        pltpu.make_async_copy(low, low, send_w.at[0]).wait()

    def sent_small(j):
        k, _slot, copy = small_hop(j)

        @pl.when(k != me)
        def _():
            copy.wait_send()

    each(mine, sent_small)

    at_home_rows = jnp.logical_and(jnp.logical_and(me < workers, passes_rows), index % 2 == critic % 2)

    @pl.when(at_home_rows)
    def _():
        rows_done(send_x.at[0], hops - 1)

    @pl.when(jnp.logical_not(at_home_rows))
    def _():
        rows_done(send_x.at[0], hops)


def dispatch(plan, inputs):
    critic_hidden, critic_in, state_action = inputs[0], inputs[2], inputs[7]
    rows = state_action.shape[1]
    pairs = plan.pairs(rows)
    columns = critic_in.shape[1]
    _width, mine, per = chunks_of(columns)
    anywhere = pl.BlockSpec(memory_space=pl.ANY)
    dma = pltpu.SemaphoreType.DMA
    return pl.pallas_call(
        functools.partial(dispatch_kernel, plan),
        out_shape=(
            jax.ShapeDtypeStruct((H, H), BF16),
            jax.ShapeDtypeStruct((plan.turns,) + critic_hidden.shape[1:], BF16),
            jax.ShapeDtypeStruct((plan.n, pairs, LANES), BF16),
            jax.ShapeDtypeStruct((per, 32, LANES), F32),
        ),
        in_specs=[(pl.BlockSpec(memory_space=pltpu.HBM),) * len(inputs)],
        out_specs=(anywhere,) * 4,
        scratch_shapes=[
            pltpu.VMEM((2,) + critic_hidden.shape, BF16),
            pltpu.VMEM((plan.groups, pairs, LANES), BF16),
            pltpu.VMEM((2, 32, -(-columns // LANES) * LANES), F32),
            pltpu.VMEM((mine, 32, LANES), F32),
            dma((1,)),
            dma((plan.turns + plan.groups - 1,)),
            dma((plan.groups - 1,)),
            dma((1,)),
            dma((1,)),
            dma((plan.n + 1,)),
            dma((2,)),
            dma((mine,)),
            dma((per,)),
            dma((-(-per // plan.groups), plan.groups - 1)),
            tuple(pltpu.VMEM(v.shape, v.dtype) for v in inputs),
            dma((len(inputs),)),
        ],
        compiler_params=pltpu.CompilerParams(collective_id=0, has_side_effects=True, vmem_limit_bytes=60 * MIB),
        name="dispatch",
    )(inputs)


def norm_parts(pre):
    centered = pre - jnp.sum(pre, -1, keepdims=True) * (1.0 / H)
    inv = lax.rsqrt(jnp.sum(centered * centered, -1, keepdims=True) * (1.0 / H) + 1e-05)
    return centered * inv, inv


def swish_parts(half):
    t = jnp.tanh(half)
    product = half * t
    return half + product, (1.0 + t) * (1.0 + (half - product))


def low_input(params):
    return jnp.where(iota((32, H), 0) < IN, params, 0.0).astype(BF16)


def input_layer(params, win_ref, gram_ref):
    weight = low_input(params).astype(F32)
    weight = weight - jnp.sum(weight, -1, keepdims=True) * (1.0 / H)
    win_ref[...] = jnp.zeros_like(win_ref)
    for k, part in enumerate(split3(weight)):
        win_ref[k * 32 : (k + 1) * 32, :] = part
    for k, part in enumerate(split3(nt(win_ref[...], win_ref[...]) * (1.0 / H))):
        gram_ref[k] = part


def input_norm(x, start, win_ref, gram_ref):
    row, lane = iota((LANES, LANES), 0), iota((LANES, LANES), 1)
    pick = jnp.logical_and(lane < 96, jnp.logical_and(lane % 32 < IN, row == lane % 32 + start))
    thrice = nn(x, pick.astype(F32).astype(BF16)).astype(BF16)
    image = sum(nn(thrice, gram_ref[k]) for k in range(3))
    var = jnp.sum(image * thrice.astype(F32), -1, keepdims=True)
    return nn(thrice, win_ref[...]), lax.rsqrt(jnp.maximum(var, 0.0) + 1e-05)


def tile_span(t):
    return pl.ds(pl.multiple_of(t * TILE, TILE), TILE)


def target_kernel(
    plan, width, x_ref, w_ref, p_ref, xc_ref, q_ref, info_ref, rows_f, picked, value, hot, win, par, flat_q, cnt_v, cnt_s, base_s, sem
):
    me = plan.rank(lax.axis_index("dp"), lax.axis_index("mp"))
    critic, group, active = me // plan.groups, me % plan.groups, (me < plan.workers).astype(I32)
    groups, n = plan.groups, plan.n
    pairs = x_ref.shape[1]
    first = x_ref[:, 0, :].astype(F32)
    lane = iota(first.shape, 1)
    counts = 2.0 * jnp.sum(jnp.where(lane == L_CNT, first, 0.0), -1, keepdims=True) + jnp.sum(
        jnp.where(lane == L_CNT + 1, first, 0.0), -1, keepdims=True
    )
    counts = jnp.where(active > 0, jnp.broadcast_to(counts, first.shape), 0.0)
    mine = jnp.floor((counts + (groups - 1 - group).astype(F32)) * (1.0 / groups) + 0.5 / groups)
    earlier = (iota((n, n), 1) < iota((n, n), 0)).astype(F32).astype(BF16)
    starts = nn(earlier, mine.astype(BF16))
    total = jnp.sum(counts, 0, keepdims=True)
    cnt_v[0:n, :] = mine.astype(I32)
    cnt_v[n : 2 * n, :] = starts.astype(I32)
    cnt_v[2 * n : 2 * n + 8, :] = jnp.broadcast_to(total, (8, LANES)).astype(I32)
    copy = pltpu.make_async_copy(cnt_v, cnt_s, sem)
    copy.start()
    par[...] = assemble(p_ref, width, 0)
    win[...] = jnp.zeros_like(win)
    win[0:32, :] = low_input(par[...])
    copy.wait()
    number = cnt_s[n - 1, 0] + cnt_s[2 * n - 1, 0]
    tiles = (number + TILE - 1) // TILE
    info_ref[0] = number
    info_ref[1] = cnt_s[2 * n, 0]

    def compact(s, _):
        block = x_ref[s].astype(F32)
        have, start = cnt_s[s, 0], cnt_s[n + s, 0]
        rows_f[pl.ds(start, pairs), :] = block
        rows_f[pl.ds(start + (have + 1) // 2, pairs), :] = pltpu.roll(block, HALF, 1)
        return 0

    @pl.when(active > 0)
    def _():
        lax.fori_loop(0, n, compact, 0, unroll=4)

    rows_f[pl.ds(number, AHEAD_TILES * TILE), :] = jnp.zeros((AHEAD_TILES * TILE, LANES), F32)
    bundles = (tiles + AHEAD_TILES - 1) // AHEAD_TILES

    until = (iota((TILE, TILE), 1) < iota((TILE, TILE), 0)).astype(F32).astype(BF16)
    place = iota((TILE, TILE), 1).astype(F32)
    this = critic.astype(F32)

    def choose(b, base):
        chosen, counts = [], []
        for i in range(AHEAD_TILES):
            t = b * AHEAD_TILES + i
            wide = rows_f[tile_span(t), :]
            x = wide.astype(BF16)
            xc_ref[tile_span(t), :] = x
            wanted = jnp.logical_or(wide[:, L_S0 : L_S0 + 1] == this, wide[:, L_S1 : L_S1 + 1] == this)
            wanted = jnp.where(jnp.logical_and(wanted, wide[:, L_BOOT : L_BOOT + 1] > 0.0), 1.0, 0.0)
            order = nn(until, jnp.broadcast_to(wanted, (TILE, LANES)).astype(BF16))[:, 0:1]
            to = (jnp.where(wanted > 0.0, order, -1.0) == place).astype(F32).astype(BF16)
            hot[t] = to
            chosen.append(tn(to, x))
            counts.append(jnp.sum(wanted).astype(I32))
        for i in range(AHEAD_TILES):
            picked[pl.ds(base, TILE), :] = chosen[i]
            base_s[b * AHEAD_TILES + i] = base
            base = base + counts[i]
        return base

    chosen_rows = lax.fori_loop(0, bundles, choose, 0)
    picked[pl.ds(chosen_rows, TILE), :] = jnp.zeros((TILE, LANES), F32)
    chosen_tiles = (chosen_rows + TILE - 1) // TILE
    half = jnp.where(iota((32, 1), 0) < IN + 4, 0.5, 1.0)
    par[...] = par[...] * half
    gain1, shift1, gain2, shift2, head = (par[IN + k : IN + k + 1, :] for k in range(5))

    def tile(t, _):
        x = pltpu.roll(picked[tile_span(t), :], LANES - L_TGT, 1).astype(BF16)
        z, _unused = norm_parts(nn(x, win[...]))
        y = z * gain1 + shift1
        act = (y + y * jnp.tanh(y)).astype(BF16)
        z, _unused = norm_parts(nn(act, w_ref[...]))
        y = z * gain2 + shift2
        q = jnp.sum((y + y * jnp.tanh(y)) * head, -1, keepdims=True)
        value[tile_span(t), :] = jnp.broadcast_to(q, (TILE, LANES))
        return 0

    lax.fori_loop(0, chosen_tiles, tile, 0)
    value[tile_span(chosen_tiles), :] = jnp.zeros((TILE, LANES), F32)

    def spread(b, _):
        lane = iota((TILE, LANES), 1)
        for i in range(AHEAD_TILES):
            t = b * AHEAD_TILES + i
            high, mid, rest = (v.astype(F32) for v in split3(value[pl.ds(base_s[t], TILE), :]))
            parts = jnp.where(lane == 0, high, jnp.where(lane == 1, mid, jnp.where(lane == 2, rest, 0.0)))
            q = jnp.broadcast_to(jnp.sum(nn(hot[t], parts.astype(BF16)), -1, keepdims=True), (TILE, LANES))
            for h in range(TILE // LANES):
                flat = jnp.transpose(q[h * LANES : (h + 1) * LANES, :])
                flat_q[pl.ds(t * (TILE // LANES) + h, 1), :] = flat[0:1, :]
        return 0

    lax.fori_loop(0, bundles, spread, 0)
    q_ref[...] = flat_q[...].astype(BF16)


def target_values(plan, rows, width, x, weights, params):
    capacity = plan.cap(rows)
    vmem = pl.BlockSpec(memory_space=pltpu.VMEM)
    smem = pl.BlockSpec(memory_space=pltpu.SMEM)
    return pl.pallas_call(
        functools.partial(target_kernel, plan, width),
        out_shape=(
            jax.ShapeDtypeStruct((capacity, LANES), BF16),
            jax.ShapeDtypeStruct((capacity // LANES, LANES), BF16),
            jax.ShapeDtypeStruct((2,), I32),
        ),
        in_specs=[vmem, vmem, vmem],
        out_specs=(vmem, vmem, smem),
        scratch_shapes=[
            pltpu.VMEM((capacity + AHEAD_TILES * TILE + x.shape[1], LANES), F32),
            pltpu.VMEM((capacity + TILE, LANES), F32),
            pltpu.VMEM((capacity + TILE, LANES), F32),
            pltpu.VMEM((capacity // TILE, TILE, TILE), BF16),
            pltpu.VMEM((LANES, H), BF16),
            pltpu.VMEM((32, H), F32),
            pltpu.VMEM((capacity // LANES, LANES), F32),
            pltpu.VMEM((2 * plan.n + 8, LANES), I32),
            pltpu.SMEM((2 * plan.n + 8, LANES), I32),
            pltpu.SMEM((capacity // TILE,), I32),
            pltpu.SemaphoreType.DMA,
        ],
        compiler_params=pltpu.CompilerParams(vmem_limit_bytes=TARGET_MIB * MIB),
        name="target_values",
    )(x, weights, params)


def share_kernel(plan, q_ref, all_ref, send, recv):
    dp, mp = lax.axis_index("dp"), lax.axis_index("mp")
    me = plan.rank(dp, mp)
    groups = plan.groups
    critic, group = me // groups, me % groups
    barrier = pltpu.get_barrier_semaphore()

    @pl.when(me < plan.workers)
    def _():
        def peer(i):
            other = (critic + i) % CRIT
            return other, plan.place(other * groups + group)

        def tell(i, _):
            pl.semaphore_signal(barrier, inc=1, device_id=peer(i)[1], device_id_type=MESH)
            return 0

        lax.fori_loop(1, CRIT, tell, 0)
        pl.semaphore_wait(barrier, CRIT - 1)
        all_ref[critic] = q_ref[...]

        def copy(i):
            other, device = peer(i)
            return pltpu.make_async_remote_copy(
                src_ref=q_ref,
                dst_ref=all_ref.at[critic],
                send_sem=send.at[other],
                recv_sem=recv.at[critic],
                device_id=device,
                device_id_type=MESH,
            )

        def start(i, _):
            copy(i).start()
            return 0

        lax.fori_loop(1, CRIT, start, 0)

        def finish(i, _):
            copy(i).wait_send()
            other = peer(i)[0]
            pltpu.make_async_copy(q_ref, all_ref.at[other], recv.at[other]).wait()
            return 0

        lax.fori_loop(1, CRIT, finish, 0)


def share_values(plan, q):
    vmem = pl.BlockSpec(memory_space=pltpu.VMEM)
    return pl.pallas_call(
        functools.partial(share_kernel, plan),
        out_shape=jax.ShapeDtypeStruct((CRIT,) + q.shape, BF16),
        in_specs=[vmem],
        out_specs=vmem,
        scratch_shapes=[pltpu.SemaphoreType.DMA((CRIT,)), pltpu.SemaphoreType.DMA((CRIT,))],
        compiler_params=pltpu.CompilerParams(collective_id=1, has_side_effects=True, vmem_limit_bytes=8 * MIB),
        name="share_values",
    )(q)


def critic_kernel(
    plan, width, info_ref, xc_ref, q_ref, shares, p_ref, grad_ref, lowered_ref, small_ref, sums_ref, w_ref, z_one, slope, act, low, fact, par, win, gram, picks, acc, q_all
):
    number = info_ref[0]
    scale = 2.0 / jnp.maximum(info_ref[1], 1).astype(F32)
    tiles = (number + TILE - 1) // TILE
    rw, cw = shares[0].shape[1:]
    me = plan.rank(lax.axis_index("dp"), lax.axis_index("mp"))
    for k, share in enumerate(shares):
        owner = (me % plan.groups + plan.groups - k) % plan.groups

        def gather(t, _):
            s = owner + plan.groups * t

            @pl.when(s < plan.n)
            def _():
                sdp, smp = plan.device(s)
                w_ref[pl.ds(pl.multiple_of(smp * rw, rw), rw), pl.ds(pl.multiple_of(sdp * cw, cw), cw)] = share[t]

            return 0

        lax.fori_loop(0, plan.turns, gather, 0)
    par[...] = assemble(p_ref, width, HALF)
    input_layer(par[...], win, gram)
    grad_ref[...] = jnp.zeros_like(grad_ref)
    acc[...] = jnp.zeros_like(acc)
    picks[...] = jnp.zeros_like(picks)
    q_all[...] = q_ref[...].astype(F32)
    sums_ref[...] = jnp.zeros_like(sums_ref)
    gain1, shift1, gain2, shift2, head = (par[IN + k : IN + k + 1, :] for k in range(5))

    hg = (0.5 * head) * gain2

    def fold(k, value):
        acc[32 + k * 8 : 40 + k * 8, :] += jnp.sum(value.reshape(TILE // 8, 8, H), 0)

    def tile(t, _):
        x = xc_ref[tile_span(t), :]
        wide = x.astype(F32)
        pre, inv_one = input_norm(x, 0, win, gram)
        z = pre * inv_one
        z_one[...] = z
        value, twice = swish_parts(z * (0.5 * gain1) + 0.5 * shift1)
        slope[...] = 0.5 * twice
        act[...] = value.astype(BF16)
        pre = nn(act[...], w_ref[...])
        for h in range(TILE // LANES):
            picks[0:CRIT, :] = q_all[:, pl.ds(t * (TILE // LANES) + h, 1), :].reshape(CRIT, LANES)
            table = jnp.transpose(picks[...])
            part = wide[h * LANES : (h + 1) * LANES, :]
            critic = iota(table.shape, 1).astype(F32)
            one = jnp.sum(jnp.where(critic == part[:, L_S0 : L_S0 + 1], table, 0.0), -1, keepdims=True)
            two = jnp.sum(jnp.where(critic == part[:, L_S1 : L_S1 + 1], table, 0.0), -1, keepdims=True)
            base = part[:, L_BASE : L_BASE + 1] + part[:, L_BASE + 1 : L_BASE + 2] + part[:, L_BASE + 2 : L_BASE + 3]
            goal = base + jnp.where(part[:, L_BOOT : L_BOOT + 1] > 0.0, REWARD_DISCOUNT * jnp.minimum(one, two), 0.0)
            fact[h * LANES : (h + 1) * LANES, 0:1] = goal
        z, inv = norm_parts(pre)
        value, twice = swish_parts(z * (0.5 * gain2) + 0.5 * shift2)
        q = jnp.sum(value * head, -1, keepdims=True)
        error = (q - fact[:, 0:1]) * wide[:, L_VALID : L_VALID + 1]
        sums_ref[0:1, :] += jnp.broadcast_to(jnp.sum(error * error, 0, keepdims=True), (1, LANES))
        dq = error * scale
        flat = jnp.transpose(jnp.broadcast_to(dq, (TILE, LANES)))[0:8, :]
        high, rest = split2(flat)
        weigh = jnp.concatenate([high, rest], 0)
        tz = twice * z
        for k, v in ((4, value), (3, twice), (2, tz)):
            acc[32 + k * 8 : 40 + k * 8, :] += nn(weigh, v.astype(BF16))[4:12]
        dz = twice * hg
        mean = jnp.sum(dz, -1, keepdims=True) * (1.0 / H)
        along = jnp.sum(tz * hg, -1, keepdims=True) * (1.0 / H)
        low[...] = ((inv * dq) * (dz - mean - z * along)).astype(BF16)
        down = nt(low[...], w_ref[...])
        grad_ref[...] += tn(act[...], low[...])
        z = z_one[...]
        dy = down * slope[...]
        fold(1, dy)
        fold(0, dy * z)
        dz = dy * gain1
        mean = jnp.sum(dz, -1, keepdims=True) * (1.0 / H)
        along = jnp.sum(dz * z, -1, keepdims=True) * (1.0 / H)
        acc[0:32, :] += tn(x[:, 0:32], (inv_one * (dz - mean - z * along)).astype(BF16))
        return 0

    lax.fori_loop(0, tiles, tile, 0)
    lowered_ref[...] = grad_ref[...].astype(BF16)
    sums_ref[1:2, :] = jnp.broadcast_to(info_ref[1].astype(F32), (1, LANES))
    for k in range(2, 5):
        total = jnp.sum(acc[32 + k * 8 : 40 + k * 8, :], 0, keepdims=True) * 0.25
        acc[32 + k * 8 : 40 + k * 8, :] = jnp.zeros((8, H), F32)
        acc[32 + k * 8 : 33 + k * 8, :] = total if k == 4 else total * (0.5 * head)
    for k in range(5):
        acc[IN + k : IN + k + 1, :] = jnp.sum(acc[32 + k * 8 : 40 + k * 8, :], 0, keepdims=True)
    for i in range(H // width):
        start, offset = i * width // LANES * LANES, i * width % LANES
        block = acc[0:32, start : start + LANES]
        small_ref[i] = pltpu.roll(block, LANES - offset, 1) if offset else block


def critic_step(plan, width, info, xc, q_all, shares, params):
    vmem = pl.BlockSpec(memory_space=pltpu.VMEM)
    smem = pl.BlockSpec(memory_space=pltpu.SMEM)
    return pl.pallas_call(
        functools.partial(critic_kernel, plan, width),
        out_shape=(
            jax.ShapeDtypeStruct((H, H), F32),
            jax.ShapeDtypeStruct((H, H), BF16),
            jax.ShapeDtypeStruct((H // width, 32, LANES), F32),
            jax.ShapeDtypeStruct((8, LANES), F32),
        ),
        in_specs=[smem, vmem, vmem, (vmem,) * plan.groups, vmem],
        out_specs=(vmem,) * 4,
        scratch_shapes=[
            pltpu.VMEM((H, H), BF16),
            pltpu.VMEM((TILE, H), F32),
            pltpu.VMEM((TILE, H), F32),
            pltpu.VMEM((TILE, H), BF16),
            pltpu.VMEM((TILE, H), BF16),
            pltpu.VMEM((TILE, LANES), F32),
            pltpu.VMEM((32, H), F32),
            pltpu.VMEM((LANES, H), BF16),
            pltpu.VMEM((3, LANES, LANES), BF16),
            pltpu.VMEM((16, LANES), F32),
            pltpu.VMEM((72, H), F32),
            pltpu.VMEM(q_all.shape, F32),
        ],
        compiler_params=pltpu.CompilerParams(vmem_limit_bytes=36 * MIB),
        name="critic_step",
    )(info, xc, q_all, shares, params)


PRECISE = 2


LAG = 3
AHEAD = 3


def shampoo_kernel(
    plan,
    g_ref,
    lowered_ref,
    small_ref,
    sums_ref,
    mom_ref,
    left_ref,
    right_ref,
    w_ref,
    mo_ref,
    lo_ref,
    ro_ref,
    wo_ref,
    own_ref,
    out_ref,
    parts,
    pieces,
    given,
    shares,
    totals,
    sums_in,
    sums_all,
    send_one,
    recv_one,
    send_two,
    recv_two,
    send_s,
    recv_s,
    send_t,
    recv_t,
):
    dp, mp = lax.axis_index("dp"), lax.axis_index("mp")
    me = plan.rank(dp, mp)
    index = dp * plan.n_mp + mp
    groups, workers, n, turns = plan.groups, plan.workers, plan.n, plan.turns
    critic, group = me // groups, me % groups
    rw, cw = mom_ref.shape[1], mom_ref.shape[2]
    mine, per = shares.shape[1], small_ref.shape[0]
    columns = own_ref.shape[1]
    chunk_width = H // per
    greet_all(plan, dp, mp)
    await_all(plan)

    def to_device(src, dst, send, recv, device):
        return pltpu.make_async_remote_copy(
            src_ref=src, dst_ref=dst, send_sem=send, recv_sem=recv, device_id=device, device_id_type=MESH
        )

    def block(s):
        sdp, smp = plan.device(s)
        return pl.ds(pl.multiple_of(smp * rw, rw), rw), pl.ds(pl.multiple_of(sdp * cw, cw), cw)

    def turn_of(step):
        return (step + critic) % turns

    def first_hop(step, i):
        other = (group + 1 + i) % groups
        turn = turn_of(step)
        s = other + groups * turn
        copy = to_device(
            lowered_ref.at[block(s)],
            parts.at[groups - 2 - i, turn],
            send_one.at[step, i],
            recv_one.at[groups - 2 - i, turn],
            plan.place(critic * groups + other),
        )
        return s, copy

    def second_hop(turn):
        s = group + groups * turn
        return s, to_device(pieces.at[turn], given.at[critic], send_two.at[turn], recv_two.at[critic], plan.device(s))

    def small_hop(q):
        g = critic * per + q
        s = g // mine
        return s, to_device(
            small_ref.at[q], shares.at[group, g % mine], send_s.at[q], recv_s.at[group, g % mine], plan.device(s)
        )

    def total_first(i):
        k = critic * groups + (group + 1 + i) % groups
        return to_device(sums_ref, sums_in.at[groups - 2 - i], send_t.at[i], recv_t.at[groups - 2 - i], plan.place(k))

    def total_second(turn):
        s = group + groups * turn
        return s, to_device(
            sums_all, totals.at[critic], send_t.at[groups - 1 + turn], recv_t.at[groups - 1 + critic], plan.device(s)
        )

    def start_first(step):
        def one(i, _):
            s, copy = first_hop(step, i)

            @pl.when(s < n)
            def _():
                copy.start()

            return 0

        lax.fori_loop(0, groups - 1, one, 0)

    def start_rest():
        def start_small(q, _):
            s, copy = small_hop(q)

            @pl.when(s == index)
            def _():
                slot = (critic * per + q) % mine
                pltpu.make_async_copy(small_ref.at[q], shares.at[group, slot], recv_s.at[group, slot]).start()

            @pl.when(s != index)
            def _():
                copy.start()

            return 0

        lax.fori_loop(0, per, start_small, 0)
        for i in range(groups - 1):
            pltpu.make_async_copy(sums_ref, sums_in.at[i], recv_t.at[i]).wait()
        value = sums_ref[...]
        for i in range(groups - 1):
            value = value + jnp.where(iota((8, LANES), 0) == 0, sums_in[i], 0.0)
        sums_all[...] = value

        def start_total(turn, _):
            s, copy = total_second(turn)

            @pl.when(s == index)
            def _():
                totals[critic] = sums_all[...]

            @pl.when(jnp.logical_and(s < n, s != index))
            def _():
                copy.start()

            return 0

        lax.fori_loop(0, turns, start_total, 0)

    @pl.when(me < workers)
    def _():
        for step in range(AHEAD):
            start_first(step)
        for i in range(groups - 1):
            total_first(i).start()

    def add_up(step):
        turn = turn_of(step)
        s, copy = second_hop(turn)

        @pl.when(s < n)
        def _():
            for i in range(groups - 1):
                pltpu.make_async_copy(parts.at[0, 0], parts.at[i, turn], recv_one.at[i, turn]).wait()
            value = g_ref[block(s)]
            for i in range(groups - 1):
                value = value + parts[i, turn].astype(F32)
            pieces[turn] = value.astype(BF16)

            @pl.when(s == index)
            def _():
                pltpu.make_async_copy(pieces.at[turn], given.at[critic], recv_two.at[critic]).start()

            @pl.when(s != index)
            def _():
                copy.start()

    width = min(256, cw)
    halves = width // LANES
    high_rows = halves * BLK
    nr, nc = rw // BLK, cw // width
    subs = [(i, j) for i in range(nr) for j in range(nc)]
    mask = (iota((LANES, LANES), 0) // BLK == iota((LANES, LANES), 1) // BLK).astype(F32).astype(BF16)
    mask_wide = jnp.concatenate([mask] * halves, 1)
    eye = (iota((high_rows, LANES), 0) % BLK == iota((high_rows, LANES), 1) % BLK).astype(F32)
    eye_low = eye.astype(BF16)

    def packed(flat):
        return jnp.concatenate([flat[:, k * LANES : (k + 1) * LANES] for k in range(halves)], 0)

    def flat_of(x):
        return jnp.concatenate([x[k * BLK : (k + 1) * BLK] for k in range(halves)], 1)

    def tops(out, count):
        return [
            jnp.concatenate(
                [out[(i * halves + k) * BLK : (i * halves + k + 1) * BLK, k * LANES : (k + 1) * LANES] for k in range(halves)], 0
            )
            for i in range(count)
        ]

    def diag(x):
        return jnp.concatenate([flat_of(x)] * (LANES // BLK), 0) * mask_wide

    def diag_rows(x):
        tiled = [jnp.concatenate([x[k * BLK : (k + 1) * BLK]] * (LANES // BLK), 0) * mask for k in range(halves)]
        return jnp.concatenate(tiled, 0)

    def products(lhs, right):
        return tops(nn(jnp.concatenate(lhs, 0), right), len(lhs))

    def precise(parts, right, right_rest):
        high, rest = parts
        out = products([high, rest], right)
        return out[0] + out[1] + products([high], right_rest)[0]

    def block_sums(s):
        high, rest = split2(s)
        return nn(high, mask) + nn(rest, mask)

    def place(c, i, j):
        return (c, slice(i * BLK, (i + 1) * BLK), slice(j * width, (j + 1) * width))

    def column_sums(x):
        return [jnp.sum(x[k * BLK : (k + 1) * BLK].reshape(BLK // 8, 8, LANES), 0) for k in range(halves)]

    def over_blocks(total, spot):
        rows = [jnp.sum(total[(spot + k) * 8 : (spot + k + 1) * 8], 0, keepdims=True) for k in range(halves)]
        return jnp.concatenate([jnp.broadcast_to(row, (BLK, LANES)) for row in rows], 0)

    def blocked(c):
        pltpu.make_async_copy(pieces.at[0], given.at[c], recv_two.at[c]).wait()
        sums, stats = [], []
        for i, j in subs:
            at = place(c, i, j)
            grad = given[at].astype(F32)
            mo_ref[at] = MOMENTUM * mom_ref[at] + grad
            low = packed(grad.astype(BF16))
            square, flip = tops(nt(jnp.concatenate([low, eye_low], 0), diag_rows(low)), 2)
            left = STAT_DECAY * packed(left_ref[at]) + (1.0 - STAT_DECAY) * square
            right = products([flip.astype(BF16)], diag(low))[0]
            right = STAT_DECAY * packed(right_ref[at]) + (1.0 - STAT_DECAY) * right
            lo_ref[at] = flat_of(left)
            ro_ref[at] = flat_of(right)
            for stat in (left, right):
                stats.append(stat)
                sums += column_sums(stat * stat)
        total = block_sums(jnp.concatenate(sums, 0))
        chains = []
        for k, stat in enumerate(stats):
            inv = lax.rsqrt(over_blocks(total, k * halves))
            rest = (eye - stat * inv) * 0.25
            chains.append([rest, eye + rest, jnp.sqrt(jnp.sqrt(inv))])
        for it in range(NEWTON - 1):
            full = it < PRECISE
            squares = []
            for ch in chains:
                high, rest = split2(ch[0])
                lhs = [high] + ([rest] if full else []) + ([ch[1].astype(BF16)] if it > 0 else [])
                out = products(lhs, diag(high))
                power = out[0]
                if full:
                    power = power + out[1] + products([high], diag(rest))[0]
                if it > 0:
                    ch[1] = ch[1] + out[-1]
                squares.append(power)
            factors = [[diag(v) for v in split2(power)[: 2 if full else 1]] for power in squares]

            def times(x, right):
                parts = split2(x)
                return precise(parts, *right) if full else products([parts[0]], right[0])[0]

            terms = [
                5.0 * ch[0] + 3.75 * power + times(ch[0], right) for ch, power, right in zip(chains, squares, factors)
            ]
            for ch, power, right, term in zip(chains, squares, factors, terms):
                ch[0] = 2.5 * power + times(term, right)
        for ch in chains:
            ch[1] = ch[1] + products([ch[1].astype(BF16)], diag(ch[0].astype(BF16)))[0]
        steps, sums = [], []
        for k, (i, j) in enumerate(subs):
            lc, rc = chains[2 * k], chains[2 * k + 1]
            moment = split2(packed(mo_ref[place(c, i, j)]))
            roots = split2(rc[1])
            step = precise(split2(lc[1]), diag(moment[0]), diag(moment[1]))
            step = precise(split2(step), diag(roots[0]), diag(roots[1])) * (lc[2] * rc[2])
            steps.append(step)
            sums += column_sums(step * step)
        total = block_sums(jnp.concatenate(sums, 0)) * (1.0 / (BLK * BLK))
        for k, (i, j) in enumerate(subs):
            at = place(c, i, j)
            old = w_ref[at]
            step = flat_of(steps[k] * lax.rsqrt(over_blocks(total, k * halves) + 1e-06))
            wo_ref[at] = old - RATE_HIDDEN * (step + WEIGHT_DECAY * old)

    def round_(i, _):
        @pl.when(jnp.logical_and(me < workers, i < turns))
        def _():
            @pl.when(i + AHEAD < turns)
            def _():
                start_first(i + AHEAD)

            @pl.when(i == turns - 2)
            def _():
                start_rest()

            add_up(i)

        c = (index // groups + 2 * turns + LAG - i) % turns

        @pl.when(jnp.logical_and(i >= LAG, c < CRIT))
        def _():
            blocked(c)

        return 0

    lax.fori_loop(0, turns + LAG, round_, 0)

    def arrived_small(i, _):
        pltpu.make_async_copy(small_ref.at[0], shares.at[i // mine, i % mine], recv_s.at[i // mine, i % mine]).wait()
        return 0

    lax.fori_loop(0, groups * mine, arrived_small, 0)
    for g in range(columns // LANES):
        part = jnp.zeros((32, LANES), F32)
        for j in range(mine):
            if j * chunk_width // LANES == g:
                value = shares[0, j]
                for r in range(1, groups):
                    value = value + shares[r, j]
                turn = j * chunk_width % LANES
                moved = pltpu.roll(value, turn, 1) if turn else value
                part = jnp.where(iota((32, LANES), 1) // chunk_width == turn // chunk_width, moved, part)
        own_ref[:, g * LANES : (g + 1) * LANES] = part

    def arrived_total(c, _):
        @pl.when(c * groups + index % groups != me)
        def _():
            pltpu.make_async_copy(sums_ref, totals.at[c], recv_t.at[groups - 1 + c]).wait()

        return 0

    lax.fori_loop(0, CRIT, arrived_total, 0)
    out_ref[0:1, :] = jnp.sum(totals[:, 0, :], 0, keepdims=True)
    out_ref[1:2, :] = totals[0, 1:2, :]
    out_ref[2:8, :] = jnp.zeros((6, LANES), F32)

    @pl.when(me < workers)
    def _():
        def finish(step, _):
            def one(i, _):
                s, copy = first_hop(step, i)

                @pl.when(s < n)
                def _():
                    copy.wait_send()

                return 0

            lax.fori_loop(0, groups - 1, one, 0)
            s, copy = second_hop(step)

            @pl.when(jnp.logical_and(s < n, s != index))
            def _():
                copy.wait_send()

            return 0

        lax.fori_loop(0, turns, finish, 0)

        def finish_small(q, _):
            s, copy = small_hop(q)

            @pl.when(s != index)
            def _():
                copy.wait_send()

            return 0

        lax.fori_loop(0, per, finish_small, 0)

        for i in range(groups - 1):
            total_first(i).wait_send()

        def finish_total(turn, _):
            s, copy = total_second(turn)

            @pl.when(jnp.logical_and(s < n, s != index))
            def _():
                copy.wait_send()

            return 0

        lax.fori_loop(0, turns, finish_total, 0)


def shampoo(plan, columns, grad, lowered, small, sums, moment, left, right, weight):
    vmem = pl.BlockSpec(memory_space=pltpu.VMEM)
    shape = jax.ShapeDtypeStruct(moment.shape, F32)
    _width, mine, per = chunks_of(columns)
    piece = moment.shape[1:]
    dma = pltpu.SemaphoreType.DMA
    return pl.pallas_call(
        functools.partial(shampoo_kernel, plan),
        out_shape=(shape,) * 4
        + (jax.ShapeDtypeStruct((32, -(-columns // LANES) * LANES), F32), jax.ShapeDtypeStruct((8, LANES), F32)),
        in_specs=[vmem] * 8,
        out_specs=(vmem,) * 6,
        scratch_shapes=[
            pltpu.VMEM((plan.groups - 1, plan.turns) + piece, BF16),
            pltpu.VMEM((plan.turns,) + piece, BF16),
            pltpu.VMEM((CRIT,) + piece, BF16),
            pltpu.VMEM((plan.groups, mine, 32, LANES), F32),
            pltpu.VMEM((CRIT, 8, LANES), F32),
            pltpu.VMEM((plan.groups - 1, 8, LANES), F32),
            pltpu.VMEM((8, LANES), F32),
            dma((plan.turns, plan.groups - 1)),
            dma((plan.groups - 1, plan.turns)),
            dma((plan.turns,)),
            dma((CRIT,)),
            dma((per,)),
            dma((plan.groups, mine)),
            dma((plan.groups - 1 + plan.turns,)),
            dma((plan.groups - 1 + CRIT,)),
        ],
        compiler_params=pltpu.CompilerParams(collective_id=2, has_side_effects=True, vmem_limit_bytes=24 * MIB),
        name="shampoo",
    )(grad, lowered, small, sums, moment, left, right, weight)


def adamw(grad, moment, square, weight, rate):
    moment_new = FIRST_DECAY * moment + (1.0 - FIRST_DECAY) * grad
    square_new = SECOND_DECAY * square + (1.0 - SECOND_DECAY) * grad * grad
    moment_hat = moment_new / (1.0 - FIRST_DECAY**STEP)
    square_hat = square_new / (1.0 - SECOND_DECAY**STEP)
    weight_new = weight - rate * (moment_hat / (jnp.sqrt(square_hat) + 1e-08) + WEIGHT_DECAY * weight)
    return (moment_new, square_new, weight_new)


def finish_kernel(own_ref, weights, hidden, updated, stored, sems):
    copies = [pltpu.make_async_copy(src, dst, sems.at[k]) for k, (src, dst) in enumerate(zip(hidden, stored))]
    for copy in copies:
        copy.start()
    columns = weights[0].shape[1]
    for k, (first, last, rate) in enumerate(((0, IN, RATE_INPUT), (IN, IN + 4, RATE_NORMS))):
        grad = own_ref[first:last, 0:columns]
        moment, square, weight = (weights[3 * k + j][...] for j in range(3))
        for ref, value in zip(updated[3 * k : 3 * k + 3], adamw(grad, moment, square, weight, rate)):
            ref[...] = value
    for copy in copies:
        copy.wait()


def finish(own, weights, hidden):
    vmem = pl.BlockSpec(memory_space=pltpu.VMEM)
    anywhere = pl.BlockSpec(memory_space=pl.ANY)
    shapes = lambda arrays: tuple(jax.ShapeDtypeStruct(v.shape, F32) for v in arrays)
    return pl.pallas_call(
        finish_kernel,
        out_shape=(shapes(weights), shapes(hidden)),
        in_specs=[vmem, (vmem,) * len(weights), (anywhere,) * len(hidden)],
        out_specs=((vmem,) * len(weights), (anywhere,) * len(hidden)),
        scratch_shapes=[pltpu.SemaphoreType.DMA((len(hidden),))],
        compiler_params=pltpu.CompilerParams(vmem_limit_bytes=8 * MIB),
        name="finish",
    )(own, weights, hidden)


def local(
    plan,
    state_action,
    next_state,
    reward,
    done_flags,
    noise_index,
    noise_table,
    subsets,
    policy_in,
    policy_mid,
    policy_out,
    critic_in,
    in_first,
    in_second,
    critic_norms,
    norm_first,
    norm_second,
    critic_head,
    head_first,
    head_second,
    critic_hidden,
    hidden_moment,
    left_stats,
    right_stats,
    target_in,
    target_norms,
    target_head,
    target_hidden,
):
    rows, columns = state_action.shape[0], critic_in.shape[1]
    width = chunks_of(columns)[0]
    lines = lambda v: v.reshape(rows // LANES, LANES)
    w_target, share, x, params = dispatch(
        plan,
        (critic_hidden, target_hidden, critic_in, critic_norms, target_in, target_norms, jnp.stack([target_head, critic_head]))
        + (state_action.T, next_state.T, lines(reward), lines(done_flags), lines(noise_index), subsets.T)
        + (noise_table.T, policy_in, policy_mid, policy_out.T),
    )
    shares = (share,) + tuple(lax.ppermute(share, ("dp", "mp"), plan.shift(k)) for k in range(1, plan.groups))
    xc, q, info = target_values(plan, rows, width, x, w_target, params)
    q_all = share_values(plan, q)
    grad_hidden, lowered, grad_small, sums = critic_step(plan, width, info, xc, q_all, shares, params)
    *hidden, own, totals = shampoo(
        plan, columns, grad_hidden, lowered, grad_small, sums, hidden_moment, left_stats, right_stats, critic_hidden
    )
    loss_total, counted = totals[0, 0], totals[1, 0]
    weights = (in_first, in_second, critic_in, norm_first, norm_second, critic_norms)
    small, hidden = finish(own, weights, tuple(hidden))
    in_moment, in_square, in_updated, norm_moment, norm_square, norm_updated = small
    hidden_momentum, left_renewed, right_renewed, hidden_updated = hidden
    head_moment, head_square, head_updated = adamw(own[IN + 4, :columns], head_first, head_second, critic_head, RATE_HEAD)
    return (
        loss_total,
        counted,
        in_moment,
        in_square,
        in_updated,
        norm_moment,
        norm_square,
        norm_updated,
        head_moment,
        head_square,
        head_updated,
        hidden_momentum,
        left_renewed,
        right_renewed,
        hidden_updated,
    )


def solution(mesh):
    both = ("dp", "mp")
    rows, columns, flat, hidden = P(both, None), P(None, both), P(both), P(None, "mp", "dp")
    return jax.shard_map(
        functools.partial(local, Plan(mesh)),
        mesh=mesh,
        in_specs=(
            (rows, rows, flat, flat, flat, P(), rows, P(), P(), P())
            + (columns,) * 6
            + (flat,) * 3
            + (hidden,) * 4
            + (columns, columns, flat, hidden)
        ),
        out_specs=(P(), P()) + (columns,) * 6 + (flat,) * 3 + (hidden,) * 4,
        check_vma=False,
    )
```

```python
import functools
import math

import jax
import jax.numpy as jnp
from jax import lax
from jax.experimental import pallas as pl
from jax.experimental.pallas import tpu as pltpu
from jax.sharding import PartitionSpec as P

ACT = 6
OBS = 17
IN = 23
H = 1024
CRIT = 10
BLK = 32
NEWTON = 5
STEP = 10
REWARD_DISCOUNT = 0.99
ENTROPY_TEMP = 0.2
FIRST_DECAY = 0.9
SECOND_DECAY = 0.999
WEIGHT_DECAY = 0.01
RATE_INPUT = 0.1
RATE_NORMS = 0.3
RATE_HEAD = 0.03
RATE_HIDDEN = 0.01
MOMENTUM = 0.9
STAT_DECAY = 0.95

F32, BF16, I32 = jnp.float32, jnp.bfloat16, jnp.int32
MESH = pl.DeviceIdType.MESH
LANES = 128
HALF = 64
TILE = 256
AHEAD_TILES = 4
L_TGT = 23
L_BASE = 46
L_BOOT = 49
L_S0 = 50
L_S1 = 51
L_VALID = 52
L_CNT = 53
MIB = 1024 * 1024
TARGET_MIB = 28


def nn(a, b):
    return jnp.dot(a, b, preferred_element_type=F32)


def nt(a, b):
    return lax.dot_general(a, b, (((1,), (1,)), ((), ())), preferred_element_type=F32)


def tn(a, b):
    return lax.dot_general(a, b, (((0,), (0,)), ((), ())), preferred_element_type=F32)


def iota(shape, dim):
    return lax.broadcasted_iota(I32, shape, dim)


def split2(x):
    high = x.astype(BF16)
    return high, (x - high.astype(F32)).astype(BF16)


def split3(x):
    high = x.astype(BF16)
    rest = x - high.astype(F32)
    mid = rest.astype(BF16)
    return high, mid, (rest - mid.astype(F32)).astype(BF16)


def swish(values):
    return values * jax.nn.sigmoid(values)


class Plan:
    def __init__(self, mesh):
        self.n_dp, self.n_mp = mesh.shape["dp"], mesh.shape["mp"]
        self.n = self.n_dp * self.n_mp
        self.groups = self.n // CRIT
        self.workers = self.groups * CRIT
        self.turns = -(-self.n // self.groups)

    def rank(self, dp, mp):
        size = 4 * self.n_dp
        layer = mp // 4
        inner = dp * 4 + (mp % 4 + 2 * (dp % 2)) % 4
        if self.n != 32:
            return layer * size + inner
        far, near = layer // 2, jnp.logical_or(layer == 1, layer == 2)
        six = 24 + 3 * far + jnp.where(near, 2, 0)
        seven = jnp.where(near, 30 + far, 25 + 3 * far)
        return jnp.where(inner < 6, 6 * layer + inner, jnp.where(inner == 6, six, seven))

    def place(self, k):
        size = 4 * self.n_dp
        if self.n != 32:
            layer, inner = k // size, k % size
        else:
            extra = jnp.maximum(k - 24, 0)
            which, j = extra // 3, extra % 3
            layer = jnp.where(which == 0, j // 2, jnp.where(which == 1, 3 - j // 2, 1 + j))
            inner = jnp.where(which == 2, 7, 6 + j % 2)
            layer = jnp.where(k < 24, k // 6, layer)
            inner = jnp.where(k < 24, k % 6, inner)
        dp = inner // 4
        return dp, layer * 4 + (inner % 4 + 2 * (dp % 2)) % 4

    def device(self, s):
        return s // self.n_mp, s % self.n_mp

    @property
    def sets(self):
        return 4 if self.n == 32 else CRIT // 2

    def extra(self, q, group):
        if self.n != 32:
            return jnp.int32(-1)
        low = jnp.where(group < 2, q == 0, q == 1)
        high = jnp.where(group < 2, q == 3, q == 2)
        return jnp.where(low, 8, jnp.where(high, 9, -1))

    def shift(self, k):
        at = lambda c, r: sum(int(v) * m for v, m in zip(self.place(jnp.int32(c * self.groups + r)), (self.n_mp, 1)))
        with jax.ensure_compile_time_eval():
            return [(at(c, r), at(c, (r + k) % self.groups)) for c in range(CRIT) for r in range(self.groups)]

    def pairs(self, rows):
        per = -(-rows // self.groups)
        return -(-per // 32) * 16

    def cap(self, rows):
        return -(-(self.n * -(-rows // self.groups)) // (TILE * AHEAD_TILES)) * TILE * AHEAD_TILES


def chunks_of(columns):
    width = math.gcd(math.gcd(columns, H), HALF)
    return width, columns // width, H // width


def assemble(chunks_ref, width, shift):
    groups = []
    lane = iota((32, LANES), 1)
    for g in range(H // LANES):
        block = jnp.zeros((32, LANES), F32)
        for i in range(LANES // width):
            chunk = chunks_ref[g * (LANES // width) + i]
            turn = (i * width - shift) % LANES
            moved = pltpu.roll(chunk, turn, 1) if turn else chunk
            block = jnp.where(lane // width == i, moved, block)
        groups.append(block)
    return jnp.concatenate(groups, 1)


def greet_all(plan, dp, mp):
    barrier = pltpu.get_barrier_semaphore()

    def tell(s, _):
        sdp, smp = s // plan.n_mp, s % plan.n_mp

        @pl.when(jnp.logical_or(sdp != dp, smp != mp))
        def _():
            pl.semaphore_signal(barrier, inc=1, device_id=(sdp, smp), device_id_type=MESH)

        return 0

    lax.fori_loop(0, plan.n, tell, 0)


def await_all(plan):
    pl.semaphore_wait(pltpu.get_barrier_semaphore(), plan.n - 1)


def dispatch_kernel(
    plan,
    inputs,
    wt_ref,
    wc_ref,
    x_ref,
    p_ref,
    low,
    msg,
    wide,
    chunk,
    send_w,
    recv_w,
    pass_w,
    recv_c,
    send_x,
    recv_x,
    pass_x,
    send_p,
    recv_p,
    pass_p,
    stage,
    stage_sem,
):
    loads = [pltpu.make_async_copy(src, dst, stage_sem.at[k]) for k, (src, dst) in enumerate(zip(inputs, stage))]
    for load in loads:
        load.start()
    dp, mp = lax.axis_index("dp"), lax.axis_index("mp")
    greet_all(plan, dp, mp)
    crit_ref, targ_ref, crit_in, crit_norms, targ_in, targ_norms, head_ref = stage[:7]
    sa_ref, ns_ref, reward_ref, done_ref, index_ref, subs_ref, table_ref, pin_ref, pmid_ref, pout_ref = stage[7:]
    crit_small, targ_small = (crit_in, crit_norms), (targ_in, targ_norms)
    me = plan.rank(dp, mp)
    index = dp * plan.n_mp + mp
    groups, workers = plan.groups, plan.workers
    critic, group = me // groups, me % groups
    rw, cw = crit_ref.shape[1], crit_ref.shape[2]
    rows = sa_ref.shape[1]
    columns = crit_small[0].shape[1]
    width, mine, per = chunks_of(columns)

    for load in loads[:2]:
        load.wait()

    def to_low(c, _):
        low[0, c] = targ_ref[c].astype(BF16)
        low[1, c] = crit_ref[c].astype(BF16)
        return 0

    lax.fori_loop(0, CRIT, to_low, 0)
    await_all(plan)

    def w_slot(s):
        sdp, smp = plan.device(s)
        return wt_ref.at[pl.ds(pl.multiple_of(smp * rw, rw), rw), pl.ds(pl.multiple_of(sdp * cw, cw), cw)]

    def to_worker(src, dst, send, recv, k):
        return pltpu.make_async_remote_copy(
            src_ref=src, dst_ref=dst, send_sem=send, recv_sem=recv, device_id=plan.place(k), device_id_type=MESH
        )

    turn = index // groups

    def first_hop(t, c):
        k = c * groups + index % groups
        dst = w_slot(index) if t == 0 else wc_ref.at[turn]
        recv = recv_w.at[turn] if t == 0 else recv_c.at[0]
        return k, dst, recv, to_worker(low.at[t, c], dst, send_w.at[0], recv, k)

    def send_weights(t):
        def one(i, _):
            c = (critic + 2 * CRIT + i * (1 - 2 * (index % 2))) % CRIT
            k, dst, recv, copy = first_hop(t, c)

            @pl.when(k == me)
            def _():
                pltpu.make_async_copy(low.at[t, c], dst, recv).start()

            @pl.when(k != me)
            def _():
                copy.start()

            return 0

        lax.fori_loop(0, CRIT, one, 0)

    send_weights(0)

    for load in loads[2:]:
        load.wait()
    wide[...] = jnp.zeros_like(wide)
    for t, parts in enumerate((targ_small, crit_small)):
        wide[t, 0:IN, 0:columns] = parts[0][...]
        wide[t, IN : IN + 4, 0:columns] = parts[1][...]
        wide[t, IN + 4 : IN + 5, 0:columns] = head_ref[t : t + 1, :]
    for j in range(mine):
        start, offset = j * width // LANES * LANES, j * width % LANES
        both = [wide[t, :, start : start + LANES] for t in range(2)]
        turned = [pltpu.roll(v, turn, 1) if turn else v for v, turn in zip(both, ((-offset) % LANES, (HALF - offset) % LANES))]
        chunk[j] = jnp.where(iota((32, LANES), 1) < HALF, turned[0], turned[1])

    def small_hop(j):
        g = index * mine + j
        k = (g // per) * groups + g % groups
        return k, g % per, to_worker(chunk.at[j], p_ref.at[g % per], send_p.at[j], recv_p.at[g % per], k)

    def send_small(j, _):
        k, slot, copy = small_hop(j)

        @pl.when(k == me)
        def _():
            pltpu.make_async_copy(chunk.at[j], p_ref.at[slot], recv_p.at[slot]).start()

        @pl.when(k != me)
        def _():
            copy.start()

        return 0

    lax.fori_loop(0, mine, send_small, 0)

    lane = iota((rows, LANES), 1)
    place = lambda height, offset: (iota((height, LANES), 1) == iota((height, LANES), 0) + offset).astype(F32).astype(BF16)
    hidden = swish(tn(ns_ref[...], pin_ref[...])).astype(BF16)
    hidden = swish(nn(hidden, pmid_ref[...])).astype(BF16)
    pout = pout_ref[...]
    spread = lambda offset: tn(
        pout, (iota((2 * ACT, LANES), 0) == iota((2 * ACT, LANES), 1) + offset).astype(F32).astype(BF16)
    ).astype(BF16)
    keep = lane < ACT
    means = nn(hidden, spread(0))
    raw = nn(hidden, spread(ACT))
    across = []
    for i in range(rows // LANES):
        lines = [reward_ref[i : i + 1, :], done_ref[i : i + 1, :].astype(F32), index_ref[i : i + 1, :].astype(F32)]
        lines += [subs_ref[:, i * LANES : (i + 1) * LANES].astype(F32), jnp.zeros((3, LANES), F32)]
        across.append(jnp.transpose(jnp.concatenate(lines, 0)))
    across = jnp.concatenate(across, 0)
    picked = (iota((rows, table_ref.shape[1]), 1) == across[:, 2:3].astype(I32)).astype(F32).astype(BF16)
    noise = jnp.zeros((rows, LANES), F32)
    for part in split3(table_ref[...]):
        noise = noise + nn(picked, tn(part, place(ACT, 0)).astype(BF16))
    log_std = -5.0 + 3.5 * (jnp.tanh(raw) + 1.0)
    squashed = means + jnp.exp(log_std) * noise
    action = jnp.tanh(squashed).astype(BF16)
    twice = -2.0 * squashed
    softplus = jnp.maximum(twice, 0.0) + jnp.log(1.0 + jnp.exp(-jnp.abs(twice)))
    correction = 2.0 * (math.log(2.0) - squashed - softplus)
    density = jnp.sum(
        jnp.where(keep, -0.5 * noise * noise - log_std - 0.5 * math.log(2.0 * math.pi) - correction, 0.0), -1, keepdims=True
    )
    done = across[:, 1:2]
    boot = (done == 0.0).astype(F32)
    base = across[:, 0:1] - (REWARD_DISCOUNT * ENTROPY_TEMP) * boot * density
    high, mid, rest = split3(base)
    on = lambda k, value: jnp.where(lane == k, value, 0.0)
    features = (
        tn(sa_ref[...], place(IN, 0))
        + tn(ns_ref[...], place(OBS, L_TGT))
        + nn(jnp.where(keep, action.astype(F32), 0.0).astype(BF16), place(LANES, L_TGT + OBS))
        + on(L_BASE, high.astype(F32))
        + on(L_BASE + 1, mid.astype(F32))
        + on(L_BASE + 2, rest.astype(F32))
        + on(L_BOOT, boot)
        + on(L_S0, across[:, 3:4])
        + on(L_S1, across[:, 4:5])
        + on(L_VALID, 1.0)
    ).astype(BF16)

    pairs = msg.shape[1]
    done_row = jnp.concatenate([done_ref[i : i + 1, :] for i in range(rows // LANES)], 1)
    valid = (done_row != 2).astype(F32)
    before = (iota((rows, rows), 0) < iota((rows, rows), 1)).astype(F32).astype(BF16)
    order = nn(jnp.broadcast_to(valid, (8, rows)).astype(BF16), before)[0:1, :]
    order = jnp.where(valid > 0.0, order, -1.0)
    count = jnp.sum(valid, -1, keepdims=True)
    count_half = jnp.floor(count * 0.5)
    mlane = iota((pairs, LANES), 1)
    tail = jnp.where(mlane == L_CNT, count_half, 0.0) + jnp.where(mlane == L_CNT + 1, count - 2.0 * count_half, 0.0)

    def deal(r, _):
        slot = iota((pairs, rows), 0) * (2 * groups) + r
        halves = []
        for h in range(2):
            hot = (order == (slot + h * groups).astype(F32)).astype(F32).astype(BF16)
            halves.append(nn(hot, features))
        msg[r] = (halves[0] + pltpu.roll(halves[1], HALF, 1) + tail).astype(BF16)
        return 0

    lax.fori_loop(0, groups, deal, 0)

    def row_hop(i):
        r = i % groups
        k = (2 * (i // groups) + index % 2) * groups + r
        return r, k, to_worker(msg.at[r], x_ref.at[index], send_x.at[0], recv_x.at[index], k)

    hops = plan.sets * groups

    def send_rows(i, _):
        r, k, copy = row_hop((i + (critic // 2) * groups) % hops)

        @pl.when(k == me)
        def _():
            pltpu.make_async_copy(msg.at[r], x_ref.at[index], recv_x.at[index]).start()

        @pl.when(k != me)
        def _():
            copy.start()

        return 0

    lax.fori_loop(0, hops, send_rows, 0)
    send_weights(1)

    def peer(i):
        return critic * groups + (group + 1 + i) % groups

    def pass_weight(t, i):
        s = group + groups * t
        return to_worker(w_slot(s), w_slot(s), pass_w.at[i], recv_w.at[plan.turns + groups - 2 - i], peer(i))

    def pass_small(slot, i):
        return to_worker(p_ref.at[slot], p_ref.at[slot], pass_p.at[slot // groups, i], recv_p.at[slot], peer(i))

    extra = plan.extra(critic // 2, group)

    def pass_rows(i, k, which):
        s = 2 * i + critic % 2
        return to_worker(x_ref.at[s], x_ref.at[s], pass_x.at[which], recv_x.at[plan.n], k)

    def other_rows(i):
        return pass_rows(i, (critic + 1 - 2 * (critic % 2)) * groups + group, 0)

    def extra_rows(i):
        return pass_rows(i, extra * groups + group, 1)

    def arrived_w(t):
        pltpu.make_async_copy(low.at[0, 0], w_slot(group + groups * t), recv_w.at[t]).wait()

    def blocks_done(sem, number):
        some = (plan.n - number + groups - 1) // groups

        @pl.when(some == plan.turns)
        def _():
            pltpu.make_async_copy(wc_ref, wc_ref, sem).wait()

        @pl.when(some != plan.turns)
        def _():
            fewer = wc_ref.at[pl.ds(0, plan.turns - 1)]
            pltpu.make_async_copy(fewer, fewer, sem).wait()

    def rows_done(sem, count):
        some = x_ref.at[pl.ds(0, count)]
        pltpu.make_async_copy(some, some, sem).wait()

    def arrived_x(s):
        pltpu.make_async_copy(msg.at[0], x_ref.at[s], recv_x.at[s]).wait()

    def arrived_p(slot):
        pltpu.make_async_copy(chunk.at[0], p_ref.at[slot], recv_p.at[slot]).wait()

    turns = (plan.n - group + groups - 1) // groups
    passes_rows = critic < 2 * plan.sets

    def peers(body):
        lax.fori_loop(0, groups - 1, lambda i, _: (body(i), 0)[1], 0)

    def each(count, body):
        lax.fori_loop(0, count, lambda i, _: (body(i), 0)[1], 0)

    @pl.when(me < workers)
    def _():
        def relay_weight(j):
            t = j
            if plan.turns == 11:
                step = j // 2
                away = jnp.where(step == 5, -3, ((step + 1) // 2) * (2 * (step % 2) - 1))
                t = (turn + 5 * (j % 2) + away + 2 * plan.turns) % plan.turns

            @pl.when(t < turns)
            def _():
                arrived_w(t)
                peers(lambda i: pass_weight(t, i).start())

        each(plan.turns, relay_weight)

        @pl.when(passes_rows)
        def _():
            def relay_rows(i):
                arrived_x(2 * i + critic % 2)
                other_rows(i).start()

                @pl.when(extra >= 0)
                def _():
                    extra_rows(i).start()

            each(plan.n // 2, relay_rows)

        def relay_small(slot):
            @pl.when((critic * per + slot) % groups == group)
            def _():
                arrived_p(slot)
                peers(lambda i: pass_small(slot, i).start())

        each(per, relay_small)

        peers(lambda i: blocks_done(recv_w.at[plan.turns + i], (group + 1 + i) % groups))

        @pl.when(passes_rows)
        def _():
            rows_done(recv_x.at[plan.n], plan.n // 2)

        @pl.when(jnp.logical_not(passes_rows))
        def _():
            rows_done(recv_x.at[plan.n], plan.n)

        def arrived_small(slot):
            @pl.when((critic * per + slot) % groups != group)
            def _():
                arrived_p(slot)

        each(per, arrived_small)
        blocks_done(recv_c.at[0], group)
        peers(lambda i: blocks_done(pass_w.at[i], group))

        @pl.when(passes_rows)
        def _():
            rows_done(pass_x.at[0], plan.n // 2)

            @pl.when(extra >= 0)
            def _():
                rows_done(pass_x.at[1], plan.n // 2)

        def passed_small(slot):
            @pl.when((critic * per + slot) % groups == group)
            def _():
                peers(lambda i: pass_small(slot, i).wait_send())

        each(per, passed_small)

    at_home = jnp.logical_and(me < workers, index % groups == group)

    @pl.when(at_home)
    def _():
        sent = low.at[:, pl.ds(0, CRIT - 1)]
        pltpu.make_async_copy(sent, sent, send_w.at[0]).wait()

    @pl.when(jnp.logical_not(at_home))
    def _():
        pltpu.make_async_copy(low, low, send_w.at[0]).wait()

    def sent_small(j):
        k, _slot, copy = small_hop(j)

        @pl.when(k != me)
        def _():
            copy.wait_send()

    each(mine, sent_small)

    at_home_rows = jnp.logical_and(jnp.logical_and(me < workers, passes_rows), index % 2 == critic % 2)

    @pl.when(at_home_rows)
    def _():
        rows_done(send_x.at[0], hops - 1)

    @pl.when(jnp.logical_not(at_home_rows))
    def _():
        rows_done(send_x.at[0], hops)


def dispatch(plan, inputs):
    critic_hidden, critic_in, state_action = inputs[0], inputs[2], inputs[7]
    rows = state_action.shape[1]
    pairs = plan.pairs(rows)
    columns = critic_in.shape[1]
    _width, mine, per = chunks_of(columns)
    anywhere = pl.BlockSpec(memory_space=pl.ANY)
    dma = pltpu.SemaphoreType.DMA
    return pl.pallas_call(
        functools.partial(dispatch_kernel, plan),
        out_shape=(
            jax.ShapeDtypeStruct((H, H), BF16),
            jax.ShapeDtypeStruct((plan.turns,) + critic_hidden.shape[1:], BF16),
            jax.ShapeDtypeStruct((plan.n, pairs, LANES), BF16),
            jax.ShapeDtypeStruct((per, 32, LANES), F32),
        ),
        in_specs=[(pl.BlockSpec(memory_space=pltpu.HBM),) * len(inputs)],
        out_specs=(anywhere,) * 4,
        scratch_shapes=[
            pltpu.VMEM((2,) + critic_hidden.shape, BF16),
            pltpu.VMEM((plan.groups, pairs, LANES), BF16),
            pltpu.VMEM((2, 32, -(-columns // LANES) * LANES), F32),
            pltpu.VMEM((mine, 32, LANES), F32),
            dma((1,)),
            dma((plan.turns + plan.groups - 1,)),
            dma((plan.groups - 1,)),
            dma((1,)),
            dma((1,)),
            dma((plan.n + 1,)),
            dma((2,)),
            dma((mine,)),
            dma((per,)),
            dma((-(-per // plan.groups), plan.groups - 1)),
            tuple(pltpu.VMEM(v.shape, v.dtype) for v in inputs),
            dma((len(inputs),)),
        ],
        compiler_params=pltpu.CompilerParams(collective_id=0, has_side_effects=True, vmem_limit_bytes=60 * MIB),
        name="dispatch",
    )(inputs)


def norm_parts(pre):
    centered = pre - jnp.sum(pre, -1, keepdims=True) * (1.0 / H)
    inv = lax.rsqrt(jnp.sum(centered * centered, -1, keepdims=True) * (1.0 / H) + 1e-05)
    return centered * inv, inv


def swish_parts(half):
    t = jnp.tanh(half)
    product = half * t
    return half + product, (1.0 + t) * (1.0 + (half - product))


def low_input(params):
    return jnp.where(iota((32, H), 0) < IN, params, 0.0).astype(BF16)


def input_layer(params, win_ref, gram_ref):
    weight = low_input(params).astype(F32)
    weight = weight - jnp.sum(weight, -1, keepdims=True) * (1.0 / H)
    win_ref[...] = jnp.zeros_like(win_ref)
    for k, part in enumerate(split3(weight)):
        win_ref[k * 32 : (k + 1) * 32, :] = part
    for k, part in enumerate(split3(nt(win_ref[...], win_ref[...]) * (1.0 / H))):
        gram_ref[k] = part


def input_norm(x, start, win_ref, gram_ref):
    row, lane = iota((LANES, LANES), 0), iota((LANES, LANES), 1)
    pick = jnp.logical_and(lane < 96, jnp.logical_and(lane % 32 < IN, row == lane % 32 + start))
    thrice = nn(x, pick.astype(F32).astype(BF16)).astype(BF16)
    image = sum(nn(thrice, gram_ref[k]) for k in range(3))
    var = jnp.sum(image * thrice.astype(F32), -1, keepdims=True)
    return nn(thrice, win_ref[...]), lax.rsqrt(jnp.maximum(var, 0.0) + 1e-05)


def tile_span(t):
    return pl.ds(pl.multiple_of(t * TILE, TILE), TILE)


def target_kernel(
    plan, width, x_ref, w_ref, p_ref, xc_ref, q_ref, info_ref, rows_f, picked, value, hot, win, par, flat_q, cnt_v, cnt_s, base_s, sem
):
    me = plan.rank(lax.axis_index("dp"), lax.axis_index("mp"))
    critic, group, active = me // plan.groups, me % plan.groups, (me < plan.workers).astype(I32)
    groups, n = plan.groups, plan.n
    pairs = x_ref.shape[1]
    first = x_ref[:, 0, :].astype(F32)
    lane = iota(first.shape, 1)
    counts = 2.0 * jnp.sum(jnp.where(lane == L_CNT, first, 0.0), -1, keepdims=True) + jnp.sum(
        jnp.where(lane == L_CNT + 1, first, 0.0), -1, keepdims=True
    )
    counts = jnp.where(active > 0, jnp.broadcast_to(counts, first.shape), 0.0)
    mine = jnp.floor((counts + (groups - 1 - group).astype(F32)) * (1.0 / groups) + 0.5 / groups)
    earlier = (iota((n, n), 1) < iota((n, n), 0)).astype(F32).astype(BF16)
    starts = nn(earlier, mine.astype(BF16))
    total = jnp.sum(counts, 0, keepdims=True)
    cnt_v[0:n, :] = mine.astype(I32)
    cnt_v[n : 2 * n, :] = starts.astype(I32)
    cnt_v[2 * n : 2 * n + 8, :] = jnp.broadcast_to(total, (8, LANES)).astype(I32)
    copy = pltpu.make_async_copy(cnt_v, cnt_s, sem)
    copy.start()
    par[...] = assemble(p_ref, width, 0)
    win[...] = jnp.zeros_like(win)
    win[0:32, :] = low_input(par[...])
    copy.wait()
    number = cnt_s[n - 1, 0] + cnt_s[2 * n - 1, 0]
    tiles = (number + TILE - 1) // TILE
    info_ref[0] = number
    info_ref[1] = cnt_s[2 * n, 0]

    def compact(s, _):
        block = x_ref[s].astype(F32)
        have, start = cnt_s[s, 0], cnt_s[n + s, 0]
        rows_f[pl.ds(start, pairs), :] = block
        rows_f[pl.ds(start + (have + 1) // 2, pairs), :] = pltpu.roll(block, HALF, 1)
        return 0

    @pl.when(active > 0)
    def _():
        lax.fori_loop(0, n, compact, 0, unroll=4)

    rows_f[pl.ds(number, AHEAD_TILES * TILE), :] = jnp.zeros((AHEAD_TILES * TILE, LANES), F32)
    bundles = (tiles + AHEAD_TILES - 1) // AHEAD_TILES

    until = (iota((TILE, TILE), 1) < iota((TILE, TILE), 0)).astype(F32).astype(BF16)
    place = iota((TILE, TILE), 1).astype(F32)
    this = critic.astype(F32)

    def choose(b, base):
        chosen, counts = [], []
        for i in range(AHEAD_TILES):
            t = b * AHEAD_TILES + i
            wide = rows_f[tile_span(t), :]
            x = wide.astype(BF16)
            xc_ref[tile_span(t), :] = x
            wanted = jnp.logical_or(wide[:, L_S0 : L_S0 + 1] == this, wide[:, L_S1 : L_S1 + 1] == this)
            wanted = jnp.where(jnp.logical_and(wanted, wide[:, L_BOOT : L_BOOT + 1] > 0.0), 1.0, 0.0)
            order = nn(until, jnp.broadcast_to(wanted, (TILE, LANES)).astype(BF16))[:, 0:1]
            to = (jnp.where(wanted > 0.0, order, -1.0) == place).astype(F32).astype(BF16)
            hot[t] = to
            chosen.append(tn(to, x))
            counts.append(jnp.sum(wanted).astype(I32))
        for i in range(AHEAD_TILES):
            picked[pl.ds(base, TILE), :] = chosen[i]
            base_s[b * AHEAD_TILES + i] = base
            base = base + counts[i]
        return base

    chosen_rows = lax.fori_loop(0, bundles, choose, 0)
    picked[pl.ds(chosen_rows, TILE), :] = jnp.zeros((TILE, LANES), F32)
    chosen_tiles = (chosen_rows + TILE - 1) // TILE
    half = jnp.where(iota((32, 1), 0) < IN + 4, 0.5, 1.0)
    par[...] = par[...] * half
    gain1, shift1, gain2, shift2, head = (par[IN + k : IN + k + 1, :] for k in range(5))

    def tile(t, _):
        x = pltpu.roll(picked[tile_span(t), :], LANES - L_TGT, 1).astype(BF16)
        z, _unused = norm_parts(nn(x, win[...]))
        y = z * gain1 + shift1
        act = (y + y * jnp.tanh(y)).astype(BF16)
        z, _unused = norm_parts(nn(act, w_ref[...]))
        y = z * gain2 + shift2
        q = jnp.sum((y + y * jnp.tanh(y)) * head, -1, keepdims=True)
        value[tile_span(t), :] = jnp.broadcast_to(q, (TILE, LANES))
        return 0

    lax.fori_loop(0, chosen_tiles, tile, 0)
    value[tile_span(chosen_tiles), :] = jnp.zeros((TILE, LANES), F32)

    def spread(b, _):
        lane = iota((TILE, LANES), 1)
        for i in range(AHEAD_TILES):
            t = b * AHEAD_TILES + i
            high, mid, rest = (v.astype(F32) for v in split3(value[pl.ds(base_s[t], TILE), :]))
            parts = jnp.where(lane == 0, high, jnp.where(lane == 1, mid, jnp.where(lane == 2, rest, 0.0)))
            q = jnp.broadcast_to(jnp.sum(nn(hot[t], parts.astype(BF16)), -1, keepdims=True), (TILE, LANES))
            for h in range(TILE // LANES):
                flat = jnp.transpose(q[h * LANES : (h + 1) * LANES, :])
                flat_q[pl.ds(t * (TILE // LANES) + h, 1), :] = flat[0:1, :]
        return 0

    lax.fori_loop(0, bundles, spread, 0)
    q_ref[...] = flat_q[...].astype(BF16)


def target_values(plan, rows, width, x, weights, params):
    capacity = plan.cap(rows)
    vmem = pl.BlockSpec(memory_space=pltpu.VMEM)
    smem = pl.BlockSpec(memory_space=pltpu.SMEM)
    return pl.pallas_call(
        functools.partial(target_kernel, plan, width),
        out_shape=(
            jax.ShapeDtypeStruct((capacity, LANES), BF16),
            jax.ShapeDtypeStruct((capacity // LANES, LANES), BF16),
            jax.ShapeDtypeStruct((2,), I32),
        ),
        in_specs=[vmem, vmem, vmem],
        out_specs=(vmem, vmem, smem),
        scratch_shapes=[
            pltpu.VMEM((capacity + AHEAD_TILES * TILE + x.shape[1], LANES), F32),
            pltpu.VMEM((capacity + TILE, LANES), F32),
            pltpu.VMEM((capacity + TILE, LANES), F32),
            pltpu.VMEM((capacity // TILE, TILE, TILE), BF16),
            pltpu.VMEM((LANES, H), BF16),
            pltpu.VMEM((32, H), F32),
            pltpu.VMEM((capacity // LANES, LANES), F32),
            pltpu.VMEM((2 * plan.n + 8, LANES), I32),
            pltpu.SMEM((2 * plan.n + 8, LANES), I32),
            pltpu.SMEM((capacity // TILE,), I32),
            pltpu.SemaphoreType.DMA,
        ],
        compiler_params=pltpu.CompilerParams(vmem_limit_bytes=TARGET_MIB * MIB),
        name="target_values",
    )(x, weights, params)


def share_kernel(plan, q_ref, all_ref, send, recv):
    dp, mp = lax.axis_index("dp"), lax.axis_index("mp")
    me = plan.rank(dp, mp)
    groups = plan.groups
    critic, group = me // groups, me % groups
    barrier = pltpu.get_barrier_semaphore()

    @pl.when(me < plan.workers)
    def _():
        def peer(i):
            return plan.place((critic + i) % CRIT * groups + group)

        def tell(i, _):
            pl.semaphore_signal(barrier, inc=1, device_id=peer(i), device_id_type=MESH)
            return 0

        lax.fori_loop(1, CRIT, tell, 0)
        pl.semaphore_wait(barrier, CRIT - 1)
        all_ref[critic] = q_ref[...]

        def copy(i):
            device = peer(i)
            return pltpu.make_async_remote_copy(
                src_ref=q_ref,
                dst_ref=all_ref.at[critic],
                send_sem=send,
                recv_sem=recv,
                device_id=device,
                device_id_type=MESH,
            )

        def start(i, _):
            copy(i).start()
            return 0

        lax.fori_loop(1, CRIT, start, 0)

        others = all_ref.at[pl.ds(0, CRIT - 1)]
        pltpu.make_async_copy(others, others, recv).wait()
        pltpu.make_async_copy(others, others, send).wait()


def share_values(plan, q):
    vmem = pl.BlockSpec(memory_space=pltpu.VMEM)
    return pl.pallas_call(
        functools.partial(share_kernel, plan),
        out_shape=jax.ShapeDtypeStruct((CRIT,) + q.shape, BF16),
        in_specs=[vmem],
        out_specs=vmem,
        scratch_shapes=[pltpu.SemaphoreType.DMA, pltpu.SemaphoreType.DMA],
        compiler_params=pltpu.CompilerParams(collective_id=1, has_side_effects=True, vmem_limit_bytes=8 * MIB),
        name="share_values",
    )(q)


def critic_kernel(
    plan, width, info_ref, xc_ref, q_ref, shares, p_ref, grad_ref, lowered_ref, small_ref, sums_ref, w_ref, z_one, slope, act, low, fact, par, win, gram, picks, acc, q_all
):
    number = info_ref[0]
    scale = 2.0 / jnp.maximum(info_ref[1], 1).astype(F32)
    tiles = (number + TILE - 1) // TILE
    rw, cw = shares[0].shape[1:]
    me = plan.rank(lax.axis_index("dp"), lax.axis_index("mp"))
    for k, share in enumerate(shares):
        owner = (me % plan.groups + plan.groups - k) % plan.groups

        def gather(t, _):
            s = owner + plan.groups * t

            @pl.when(s < plan.n)
            def _():
                sdp, smp = plan.device(s)
                w_ref[pl.ds(pl.multiple_of(smp * rw, rw), rw), pl.ds(pl.multiple_of(sdp * cw, cw), cw)] = share[t]

            return 0

        lax.fori_loop(0, plan.turns, gather, 0)
    par[...] = assemble(p_ref, width, HALF)
    input_layer(par[...], win, gram)
    grad_ref[...] = jnp.zeros_like(grad_ref)
    acc[...] = jnp.zeros_like(acc)
    picks[...] = jnp.zeros_like(picks)
    q_all[...] = q_ref[...].astype(F32)
    sums_ref[...] = jnp.zeros_like(sums_ref)
    gain1, shift1, gain2, shift2, head = (par[IN + k : IN + k + 1, :] for k in range(5))

    hg = (0.5 * head) * gain2

    def fold(k, value):
        acc[32 + k * 8 : 40 + k * 8, :] += jnp.sum(value.reshape(TILE // 8, 8, H), 0)

    def tile(t, _):
        x = xc_ref[tile_span(t), :]
        wide = x.astype(F32)
        pre, inv_one = input_norm(x, 0, win, gram)
        z = pre * inv_one
        z_one[...] = z
        value, twice = swish_parts(z * (0.5 * gain1) + 0.5 * shift1)
        slope[...] = 0.5 * twice
        act[...] = value.astype(BF16)
        pre = nn(act[...], w_ref[...])
        for h in range(TILE // LANES):
            picks[0:CRIT, :] = q_all[:, pl.ds(t * (TILE // LANES) + h, 1), :].reshape(CRIT, LANES)
            table = jnp.transpose(picks[...])
            part = wide[h * LANES : (h + 1) * LANES, :]
            critic = iota(table.shape, 1).astype(F32)
            one = jnp.sum(jnp.where(critic == part[:, L_S0 : L_S0 + 1], table, 0.0), -1, keepdims=True)
            two = jnp.sum(jnp.where(critic == part[:, L_S1 : L_S1 + 1], table, 0.0), -1, keepdims=True)
            base = part[:, L_BASE : L_BASE + 1] + part[:, L_BASE + 1 : L_BASE + 2] + part[:, L_BASE + 2 : L_BASE + 3]
            goal = base + jnp.where(part[:, L_BOOT : L_BOOT + 1] > 0.0, REWARD_DISCOUNT * jnp.minimum(one, two), 0.0)
            fact[h * LANES : (h + 1) * LANES, 0:1] = goal
        z, inv = norm_parts(pre)
        value, twice = swish_parts(z * (0.5 * gain2) + 0.5 * shift2)
        q = jnp.sum(value * head, -1, keepdims=True)
        error = (q - fact[:, 0:1]) * wide[:, L_VALID : L_VALID + 1]
        sums_ref[0:1, :] += jnp.broadcast_to(jnp.sum(error * error, 0, keepdims=True), (1, LANES))
        dq = error * scale
        flat = jnp.transpose(jnp.broadcast_to(dq, (TILE, LANES)))[0:8, :]
        high, rest = split2(flat)
        weigh = jnp.concatenate([high, rest], 0)
        tz = twice * z
        for k, v in ((4, value), (3, twice), (2, tz)):
            acc[32 + k * 8 : 40 + k * 8, :] += nn(weigh, v.astype(BF16))[4:12]
        dz = twice * hg
        mean = jnp.sum(dz, -1, keepdims=True) * (1.0 / H)
        along = jnp.sum(tz * hg, -1, keepdims=True) * (1.0 / H)
        low[...] = ((inv * dq) * (dz - mean - z * along)).astype(BF16)
        down = nt(low[...], w_ref[...])
        grad_ref[...] += tn(act[...], low[...])
        z = z_one[...]
        dy = down * slope[...]
        fold(1, dy)
        fold(0, dy * z)
        dz = dy * gain1
        mean = jnp.sum(dz, -1, keepdims=True) * (1.0 / H)
        along = jnp.sum(dz * z, -1, keepdims=True) * (1.0 / H)
        acc[0:32, :] += tn(x[:, 0:32], (inv_one * (dz - mean - z * along)).astype(BF16))
        return 0

    lax.fori_loop(0, tiles, tile, 0)
    lowered_ref[...] = grad_ref[...].astype(BF16)
    sums_ref[1:2, :] = jnp.broadcast_to(info_ref[1].astype(F32), (1, LANES))
    for k in range(2, 5):
        total = jnp.sum(acc[32 + k * 8 : 40 + k * 8, :], 0, keepdims=True) * 0.25
        acc[32 + k * 8 : 40 + k * 8, :] = jnp.zeros((8, H), F32)
        acc[32 + k * 8 : 33 + k * 8, :] = total if k == 4 else total * (0.5 * head)
    for k in range(5):
        acc[IN + k : IN + k + 1, :] = jnp.sum(acc[32 + k * 8 : 40 + k * 8, :], 0, keepdims=True)
    for i in range(H // width):
        start, offset = i * width // LANES * LANES, i * width % LANES
        block = acc[0:32, start : start + LANES]
        small_ref[i] = pltpu.roll(block, LANES - offset, 1) if offset else block


def critic_step(plan, width, info, xc, q_all, shares, params):
    vmem = pl.BlockSpec(memory_space=pltpu.VMEM)
    smem = pl.BlockSpec(memory_space=pltpu.SMEM)
    return pl.pallas_call(
        functools.partial(critic_kernel, plan, width),
        out_shape=(
            jax.ShapeDtypeStruct((H, H), F32),
            jax.ShapeDtypeStruct((H, H), BF16),
            jax.ShapeDtypeStruct((H // width, 32, LANES), F32),
            jax.ShapeDtypeStruct((8, LANES), F32),
        ),
        in_specs=[smem, vmem, vmem, (vmem,) * plan.groups, vmem],
        out_specs=(vmem,) * 4,
        scratch_shapes=[
            pltpu.VMEM((H, H), BF16),
            pltpu.VMEM((TILE, H), F32),
            pltpu.VMEM((TILE, H), F32),
            pltpu.VMEM((TILE, H), BF16),
            pltpu.VMEM((TILE, H), BF16),
            pltpu.VMEM((TILE, LANES), F32),
            pltpu.VMEM((32, H), F32),
            pltpu.VMEM((LANES, H), BF16),
            pltpu.VMEM((3, LANES, LANES), BF16),
            pltpu.VMEM((16, LANES), F32),
            pltpu.VMEM((72, H), F32),
            pltpu.VMEM(q_all.shape, F32),
        ],
        compiler_params=pltpu.CompilerParams(vmem_limit_bytes=36 * MIB),
        name="critic_step",
    )(info, xc, q_all, shares, params)


PRECISE = 2


LAG = 3
AHEAD = 3


def shampoo_kernel(
    plan,
    g_ref,
    lowered_ref,
    small_ref,
    sums_ref,
    mom_ref,
    left_ref,
    right_ref,
    w_ref,
    mo_ref,
    lo_ref,
    ro_ref,
    wo_ref,
    own_ref,
    out_ref,
    parts,
    pieces,
    given,
    shares,
    totals,
    sums_in,
    sums_all,
    send_one,
    recv_one,
    send_two,
    recv_two,
    send_s,
    recv_s,
    send_t,
    recv_t,
):
    dp, mp = lax.axis_index("dp"), lax.axis_index("mp")
    me = plan.rank(dp, mp)
    index = dp * plan.n_mp + mp
    groups, workers, n, turns = plan.groups, plan.workers, plan.n, plan.turns
    critic, group = me // groups, me % groups
    rw, cw = mom_ref.shape[1], mom_ref.shape[2]
    mine, per = shares.shape[1], small_ref.shape[0]
    columns = own_ref.shape[1]
    chunk_width = H // per
    greet_all(plan, dp, mp)
    await_all(plan)

    def to_device(src, dst, send, recv, device):
        return pltpu.make_async_remote_copy(
            src_ref=src, dst_ref=dst, send_sem=send, recv_sem=recv, device_id=device, device_id_type=MESH
        )

    def block(s):
        sdp, smp = plan.device(s)
        return pl.ds(pl.multiple_of(smp * rw, rw), rw), pl.ds(pl.multiple_of(sdp * cw, cw), cw)

    def turn_of(step):
        return (step + critic) % turns

    def first_hop(step, i):
        other = (group + 1 + i) % groups
        turn = turn_of(step)
        s = other + groups * turn
        copy = to_device(
            lowered_ref.at[block(s)],
            parts.at[groups - 2 - i, turn],
            send_one.at[i],
            recv_one.at[groups - 2 - i, turn],
            plan.place(critic * groups + other),
        )
        return s, copy

    def second_hop(turn):
        s = group + groups * turn
        return s, to_device(pieces.at[turn], given.at[critic], send_two.at[turn], recv_two.at[critic], plan.device(s))

    def small_hop(q):
        g = critic * per + q
        s = g // mine
        return s, to_device(small_ref.at[q], shares.at[group, g % mine], send_s.at[q], recv_s.at[0], plan.device(s))

    def total_first(i):
        k = critic * groups + (group + 1 + i) % groups
        return to_device(sums_ref, sums_in.at[groups - 2 - i], send_t.at[i], recv_t.at[groups - 2 - i], plan.place(k))

    def total_second(turn):
        s = group + groups * turn
        return s, to_device(
            sums_all, totals.at[critic], send_t.at[groups - 1 + turn], recv_t.at[groups - 1 + critic], plan.device(s)
        )

    def start_first(step):
        def one(i, _):
            s, copy = first_hop(step, i)

            @pl.when(s < n)
            def _():
                copy.start()

            return 0

        lax.fori_loop(0, groups - 1, one, 0)

    def start_rest():
        def start_small(q, _):
            s, copy = small_hop(q)

            @pl.when(s == index)
            def _():
                slot = (critic * per + q) % mine
                pltpu.make_async_copy(small_ref.at[q], shares.at[group, slot], recv_s.at[0]).start()

            @pl.when(s != index)
            def _():
                copy.start()

            return 0

        lax.fori_loop(0, per, start_small, 0)
        for i in range(groups - 1):
            pltpu.make_async_copy(sums_ref, sums_in.at[i], recv_t.at[i]).wait()
        value = sums_ref[...]
        for i in range(groups - 1):
            value = value + jnp.where(iota((8, LANES), 0) == 0, sums_in[i], 0.0)
        sums_all[...] = value

        def start_total(turn, _):
            s, copy = total_second(turn)

            @pl.when(s == index)
            def _():
                totals[critic] = sums_all[...]

            @pl.when(jnp.logical_and(s < n, s != index))
            def _():
                copy.start()

            return 0

        lax.fori_loop(0, turns, start_total, 0)

    @pl.when(me < workers)
    def _():
        for step in range(AHEAD):
            start_first(step)
        for i in range(groups - 1):
            total_first(i).start()

    def add_up(step):
        turn = turn_of(step)
        s, copy = second_hop(turn)

        @pl.when(s < n)
        def _():
            for i in range(groups - 1):
                pltpu.make_async_copy(parts.at[0, 0], parts.at[i, turn], recv_one.at[i, turn]).wait()
            value = g_ref[block(s)]
            for i in range(groups - 1):
                value = value + parts[i, turn].astype(F32)
            pieces[turn] = value.astype(BF16)

            @pl.when(s == index)
            def _():
                pltpu.make_async_copy(pieces.at[turn], given.at[critic], recv_two.at[critic]).start()

            @pl.when(s != index)
            def _():
                copy.start()

    width = min(256, cw)
    halves = width // LANES
    high_rows = halves * BLK
    nr, nc = rw // BLK, cw // width
    subs = [(i, j) for i in range(nr) for j in range(nc)]
    mask = (iota((LANES, LANES), 0) // BLK == iota((LANES, LANES), 1) // BLK).astype(F32).astype(BF16)
    mask_wide = jnp.concatenate([mask] * halves, 1)
    eye = (iota((high_rows, LANES), 0) % BLK == iota((high_rows, LANES), 1) % BLK).astype(F32)
    eye_low = eye.astype(BF16)

    def packed(flat):
        return jnp.concatenate([flat[:, k * LANES : (k + 1) * LANES] for k in range(halves)], 0)

    def flat_of(x):
        return jnp.concatenate([x[k * BLK : (k + 1) * BLK] for k in range(halves)], 1)

    def tops(out, count):
        return [
            jnp.concatenate(
                [out[(i * halves + k) * BLK : (i * halves + k + 1) * BLK, k * LANES : (k + 1) * LANES] for k in range(halves)], 0
            )
            for i in range(count)
        ]

    def diag(x):
        return jnp.concatenate([flat_of(x)] * (LANES // BLK), 0) * mask_wide

    def diag_rows(x):
        tiled = [jnp.concatenate([x[k * BLK : (k + 1) * BLK]] * (LANES // BLK), 0) * mask for k in range(halves)]
        return jnp.concatenate(tiled, 0)

    def products(lhs, right):
        return tops(nn(jnp.concatenate(lhs, 0), right), len(lhs))

    def precise(parts, right, right_rest):
        high, rest = parts
        out = products([high, rest], right)
        return out[0] + out[1] + products([high], right_rest)[0]

    def block_sums(s):
        high, rest = split2(s)
        return nn(high, mask) + nn(rest, mask)

    def place(c, i, j):
        return (c, slice(i * BLK, (i + 1) * BLK), slice(j * width, (j + 1) * width))

    def column_sums(x):
        return [jnp.sum(x[k * BLK : (k + 1) * BLK].reshape(BLK // 8, 8, LANES), 0) for k in range(halves)]

    def over_blocks(total, spot):
        rows = [jnp.sum(total[(spot + k) * 8 : (spot + k + 1) * 8], 0, keepdims=True) for k in range(halves)]
        return jnp.concatenate([jnp.broadcast_to(row, (BLK, LANES)) for row in rows], 0)

    def blocked(c):
        pltpu.make_async_copy(pieces.at[0], given.at[c], recv_two.at[c]).wait()
        sums, stats = [], []
        for i, j in subs:
            at = place(c, i, j)
            grad = given[at].astype(F32)
            mo_ref[at] = MOMENTUM * mom_ref[at] + grad
            low = packed(grad.astype(BF16))
            square, flip = tops(nt(jnp.concatenate([low, eye_low], 0), diag_rows(low)), 2)
            left = STAT_DECAY * packed(left_ref[at]) + (1.0 - STAT_DECAY) * square
            right = products([flip.astype(BF16)], diag(low))[0]
            right = STAT_DECAY * packed(right_ref[at]) + (1.0 - STAT_DECAY) * right
            lo_ref[at] = flat_of(left)
            ro_ref[at] = flat_of(right)
            for stat in (left, right):
                stats.append(stat)
                sums += column_sums(stat * stat)
        total = block_sums(jnp.concatenate(sums, 0))
        chains = []
        for k, stat in enumerate(stats):
            inv = lax.rsqrt(over_blocks(total, k * halves))
            rest = (eye - stat * inv) * 0.25
            chains.append([rest, eye + rest, jnp.sqrt(jnp.sqrt(inv))])
        for it in range(NEWTON - 1):
            full = it < PRECISE
            squares = []
            for ch in chains:
                high, rest = split2(ch[0])
                lhs = [high] + ([rest] if full else []) + ([ch[1].astype(BF16)] if it > 0 else [])
                out = products(lhs, diag(high))
                power = out[0]
                if full:
                    power = power + out[1] + products([high], diag(rest))[0]
                if it > 0:
                    ch[1] = ch[1] + out[-1]
                squares.append(power)
            factors = [[diag(v) for v in split2(power)[: 2 if full else 1]] for power in squares]

            def times(x, right):
                parts = split2(x)
                return precise(parts, *right) if full else products([parts[0]], right[0])[0]

            terms = [
                5.0 * ch[0] + 3.75 * power + times(ch[0], right) for ch, power, right in zip(chains, squares, factors)
            ]
            for ch, power, right, term in zip(chains, squares, factors, terms):
                ch[0] = 2.5 * power + times(term, right)
        for ch in chains:
            ch[1] = ch[1] + products([ch[1].astype(BF16)], diag(ch[0].astype(BF16)))[0]
        steps, sums = [], []
        for k, (i, j) in enumerate(subs):
            lc, rc = chains[2 * k], chains[2 * k + 1]
            moment = split2(packed(mo_ref[place(c, i, j)]))
            roots = split2(rc[1])
            step = precise(split2(lc[1]), diag(moment[0]), diag(moment[1]))
            step = precise(split2(step), diag(roots[0]), diag(roots[1])) * (lc[2] * rc[2])
            steps.append(step)
            sums += column_sums(step * step)
        total = block_sums(jnp.concatenate(sums, 0)) * (1.0 / (BLK * BLK))
        for k, (i, j) in enumerate(subs):
            at = place(c, i, j)
            old = w_ref[at]
            step = flat_of(steps[k] * lax.rsqrt(over_blocks(total, k * halves) + 1e-06))
            wo_ref[at] = old - RATE_HIDDEN * (step + WEIGHT_DECAY * old)

    def round_(i, _):
        @pl.when(jnp.logical_and(me < workers, i < turns))
        def _():
            @pl.when(i + AHEAD < turns)
            def _():
                start_first(i + AHEAD)

            @pl.when(i == turns - 2)
            def _():
                start_rest()

            add_up(i)

        c = (index // groups + 2 * turns + LAG - i) % turns

        @pl.when(jnp.logical_and(i >= LAG, c < CRIT))
        def _():
            blocked(c)

        return 0

    lax.fori_loop(0, turns + LAG, round_, 0)

    pltpu.make_async_copy(shares, shares, recv_s.at[0]).wait()
    for g in range(columns // LANES):
        part = jnp.zeros((32, LANES), F32)
        for j in range(mine):
            if j * chunk_width // LANES == g:
                value = shares[0, j]
                for r in range(1, groups):
                    value = value + shares[r, j]
                turn = j * chunk_width % LANES
                moved = pltpu.roll(value, turn, 1) if turn else value
                part = jnp.where(iota((32, LANES), 1) // chunk_width == turn // chunk_width, moved, part)
        own_ref[:, g * LANES : (g + 1) * LANES] = part

    def arrived_total(c, _):
        @pl.when(c * groups + index % groups != me)
        def _():
            pltpu.make_async_copy(sums_ref, totals.at[c], recv_t.at[groups - 1 + c]).wait()

        return 0

    lax.fori_loop(0, CRIT, arrived_total, 0)
    out_ref[0:1, :] = jnp.sum(totals[:, 0, :], 0, keepdims=True)
    out_ref[1:2, :] = totals[0, 1:2, :]
    out_ref[2:8, :] = jnp.zeros((6, LANES), F32)

    @pl.when(me < workers)
    def _():
        for i in range(groups - 1):
            some = (n - (group + 1 + i) % groups + groups - 1) // groups

            @pl.when(some == turns)
            def _():
                pltpu.make_async_copy(parts.at[0], parts.at[0], send_one.at[i]).wait()

            @pl.when(some != turns)
            def _():
                fewer = parts.at[0, pl.ds(0, turns - 1)]
                pltpu.make_async_copy(fewer, fewer, send_one.at[i]).wait()

        def finish(turn, _):
            s, copy = second_hop(turn)

            @pl.when(jnp.logical_and(s < n, s != index))
            def _():
                copy.wait_send()

            return 0

        lax.fori_loop(0, turns, finish, 0)

        def finish_small(q, _):
            s, copy = small_hop(q)

            @pl.when(s != index)
            def _():
                copy.wait_send()

            return 0

        lax.fori_loop(0, per, finish_small, 0)

        for i in range(groups - 1):
            total_first(i).wait_send()

        def finish_total(turn, _):
            s, copy = total_second(turn)

            @pl.when(jnp.logical_and(s < n, s != index))
            def _():
                copy.wait_send()

            return 0

        lax.fori_loop(0, turns, finish_total, 0)


def shampoo(plan, columns, grad, lowered, small, sums, moment, left, right, weight):
    vmem = pl.BlockSpec(memory_space=pltpu.VMEM)
    shape = jax.ShapeDtypeStruct(moment.shape, F32)
    _width, mine, per = chunks_of(columns)
    piece = moment.shape[1:]
    dma = pltpu.SemaphoreType.DMA
    return pl.pallas_call(
        functools.partial(shampoo_kernel, plan),
        out_shape=(shape,) * 4
        + (jax.ShapeDtypeStruct((32, -(-columns // LANES) * LANES), F32), jax.ShapeDtypeStruct((8, LANES), F32)),
        in_specs=[vmem] * 8,
        out_specs=(vmem,) * 6,
        scratch_shapes=[
            pltpu.VMEM((plan.groups - 1, plan.turns) + piece, BF16),
            pltpu.VMEM((plan.turns,) + piece, BF16),
            pltpu.VMEM((CRIT,) + piece, BF16),
            pltpu.VMEM((plan.groups, mine, 32, LANES), F32),
            pltpu.VMEM((CRIT, 8, LANES), F32),
            pltpu.VMEM((plan.groups - 1, 8, LANES), F32),
            pltpu.VMEM((8, LANES), F32),
            dma((plan.groups - 1,)),
            dma((plan.groups - 1, plan.turns)),
            dma((plan.turns,)),
            dma((CRIT,)),
            dma((per,)),
            dma((1,)),
            dma((plan.groups - 1 + plan.turns,)),
            dma((plan.groups - 1 + CRIT,)),
        ],
        compiler_params=pltpu.CompilerParams(collective_id=2, has_side_effects=True, vmem_limit_bytes=24 * MIB),
        name="shampoo",
    )(grad, lowered, small, sums, moment, left, right, weight)


def adamw(grad, moment, square, weight, rate):
    moment_new = FIRST_DECAY * moment + (1.0 - FIRST_DECAY) * grad
    square_new = SECOND_DECAY * square + (1.0 - SECOND_DECAY) * grad * grad
    moment_hat = moment_new / (1.0 - FIRST_DECAY**STEP)
    square_hat = square_new / (1.0 - SECOND_DECAY**STEP)
    weight_new = weight - rate * (moment_hat / (jnp.sqrt(square_hat) + 1e-08) + WEIGHT_DECAY * weight)
    return (moment_new, square_new, weight_new)


def finish_kernel(own_ref, weights, hidden, updated, stored, sems):
    copies = [pltpu.make_async_copy(src, dst, sems.at[k]) for k, (src, dst) in enumerate(zip(hidden, stored))]
    for copy in copies:
        copy.start()
    columns = weights[0].shape[1]
    for k, (first, last, rate) in enumerate(((0, IN, RATE_INPUT), (IN, IN + 4, RATE_NORMS))):
        grad = own_ref[first:last, 0:columns]
        moment, square, weight = (weights[3 * k + j][...] for j in range(3))
        for ref, value in zip(updated[3 * k : 3 * k + 3], adamw(grad, moment, square, weight, rate)):
            ref[...] = value
    for copy in copies:
        copy.wait()


def finish(own, weights, hidden):
    vmem = pl.BlockSpec(memory_space=pltpu.VMEM)
    anywhere = pl.BlockSpec(memory_space=pl.ANY)
    shapes = lambda arrays: tuple(jax.ShapeDtypeStruct(v.shape, F32) for v in arrays)
    return pl.pallas_call(
        finish_kernel,
        out_shape=(shapes(weights), shapes(hidden)),
        in_specs=[vmem, (vmem,) * len(weights), (anywhere,) * len(hidden)],
        out_specs=((vmem,) * len(weights), (anywhere,) * len(hidden)),
        scratch_shapes=[pltpu.SemaphoreType.DMA((len(hidden),))],
        compiler_params=pltpu.CompilerParams(vmem_limit_bytes=8 * MIB),
        name="finish",
    )(own, weights, hidden)


def local(
    plan,
    state_action,
    next_state,
    reward,
    done_flags,
    noise_index,
    noise_table,
    subsets,
    policy_in,
    policy_mid,
    policy_out,
    critic_in,
    in_first,
    in_second,
    critic_norms,
    norm_first,
    norm_second,
    critic_head,
    head_first,
    head_second,
    critic_hidden,
    hidden_moment,
    left_stats,
    right_stats,
    target_in,
    target_norms,
    target_head,
    target_hidden,
):
    rows, columns = state_action.shape[0], critic_in.shape[1]
    width = chunks_of(columns)[0]
    lines = lambda v: v.reshape(rows // LANES, LANES)
    w_target, share, x, params = dispatch(
        plan,
        (critic_hidden, target_hidden, critic_in, critic_norms, target_in, target_norms, jnp.stack([target_head, critic_head]))
        + (state_action.T, next_state.T, lines(reward), lines(done_flags), lines(noise_index), subsets.T)
        + (noise_table.T, policy_in, policy_mid, policy_out.T),
    )
    shares = (share,) + tuple(lax.ppermute(share, ("dp", "mp"), plan.shift(k)) for k in range(1, plan.groups))
    xc, q, info = target_values(plan, rows, width, x, w_target, params)
    q_all = share_values(plan, q)
    grad_hidden, lowered, grad_small, sums = critic_step(plan, width, info, xc, q_all, shares, params)
    *hidden, own, totals = shampoo(
        plan, columns, grad_hidden, lowered, grad_small, sums, hidden_moment, left_stats, right_stats, critic_hidden
    )
    loss_total, counted = totals[0, 0], totals[1, 0]
    weights = (in_first, in_second, critic_in, norm_first, norm_second, critic_norms)
    small, hidden = finish(own, weights, tuple(hidden))
    in_moment, in_square, in_updated, norm_moment, norm_square, norm_updated = small
    hidden_momentum, left_renewed, right_renewed, hidden_updated = hidden
    head_moment, head_square, head_updated = adamw(own[IN + 4, :columns], head_first, head_second, critic_head, RATE_HEAD)
    return (
        loss_total,
        counted,
        in_moment,
        in_square,
        in_updated,
        norm_moment,
        norm_square,
        norm_updated,
        head_moment,
        head_square,
        head_updated,
        hidden_momentum,
        left_renewed,
        right_renewed,
        hidden_updated,
    )


def solution(mesh):
    both = ("dp", "mp")
    rows, columns, flat, hidden = P(both, None), P(None, both), P(both), P(None, "mp", "dp")
    return jax.shard_map(
        functools.partial(local, Plan(mesh)),
        mesh=mesh,
        in_specs=(
            (rows, rows, flat, flat, flat, P(), rows, P(), P(), P())
            + (columns,) * 6
            + (flat,) * 3
            + (hidden,) * 4
            + (columns, columns, flat, hidden)
        ),
        out_specs=(P(), P()) + (columns,) * 6 + (flat,) * 3 + (hidden,) * 4,
        check_vma=False,
    )
```

```python
import functools
import math

import jax
import jax.numpy as jnp
from jax import lax
from jax.experimental import pallas as pl
from jax.experimental.pallas import tpu as pltpu
from jax.sharding import PartitionSpec as P

ACT = 6
OBS = 17
IN = 23
H = 1024
CRIT = 10
BLK = 32
NEWTON = 5
STEP = 10
REWARD_DISCOUNT = 0.99
ENTROPY_TEMP = 0.2
FIRST_DECAY = 0.9
SECOND_DECAY = 0.999
WEIGHT_DECAY = 0.01
RATE_INPUT = 0.1
RATE_NORMS = 0.3
RATE_HEAD = 0.03
RATE_HIDDEN = 0.01
MOMENTUM = 0.9
STAT_DECAY = 0.95

F32, BF16, I32 = jnp.float32, jnp.bfloat16, jnp.int32
MESH = pl.DeviceIdType.MESH
LANES = 128
HALF = 64
TILE = 256
AHEAD_TILES = 4
L_TGT = 23
L_BASE = 46
L_BOOT = 49
L_S0 = 50
L_S1 = 51
L_VALID = 52
L_CNT = 53
MIB = 1024 * 1024
TARGET_MIB = 28


def nn(a, b):
    return jnp.dot(a, b, preferred_element_type=F32)


def nt(a, b):
    return lax.dot_general(a, b, (((1,), (1,)), ((), ())), preferred_element_type=F32)


def tn(a, b):
    return lax.dot_general(a, b, (((0,), (0,)), ((), ())), preferred_element_type=F32)


def iota(shape, dim):
    return lax.broadcasted_iota(I32, shape, dim)


def split2(x):
    high = x.astype(BF16)
    return high, (x - high.astype(F32)).astype(BF16)


def split3(x):
    high = x.astype(BF16)
    rest = x - high.astype(F32)
    mid = rest.astype(BF16)
    return high, mid, (rest - mid.astype(F32)).astype(BF16)


def swish(values):
    return values * jax.nn.sigmoid(values)


class Plan:
    def __init__(self, mesh):
        self.n_dp, self.n_mp = mesh.shape["dp"], mesh.shape["mp"]
        self.n = self.n_dp * self.n_mp
        self.groups = self.n // CRIT
        self.workers = self.groups * CRIT
        self.turns = -(-self.n // self.groups)

    def rank(self, dp, mp):
        size = 4 * self.n_dp
        layer = mp // 4
        inner = dp * 4 + (mp % 4 + 2 * (dp % 2)) % 4
        if self.n != 32:
            return layer * size + inner
        far, near = layer // 2, jnp.logical_or(layer == 1, layer == 2)
        six = 24 + 3 * far + jnp.where(near, 2, 0)
        seven = jnp.where(near, 30 + far, 25 + 3 * far)
        return jnp.where(inner < 6, 6 * layer + inner, jnp.where(inner == 6, six, seven))

    def place(self, k):
        size = 4 * self.n_dp
        if self.n != 32:
            layer, inner = k // size, k % size
        else:
            extra = jnp.maximum(k - 24, 0)
            which, j = extra // 3, extra % 3
            layer = jnp.where(which == 0, j // 2, jnp.where(which == 1, 3 - j // 2, 1 + j))
            inner = jnp.where(which == 2, 7, 6 + j % 2)
            layer = jnp.where(k < 24, k // 6, layer)
            inner = jnp.where(k < 24, k % 6, inner)
        dp = inner // 4
        return dp, layer * 4 + (inner % 4 + 2 * (dp % 2)) % 4

    def device(self, s):
        return s // self.n_mp, s % self.n_mp

    @property
    def sets(self):
        return 4 if self.n == 32 else CRIT // 2

    def extra(self, q, group):
        if self.n != 32:
            return jnp.int32(-1)
        low = jnp.where(group < 2, q == 0, q == 1)
        high = jnp.where(group < 2, q == 3, q == 2)
        return jnp.where(low, 8, jnp.where(high, 9, -1))

    def shift(self, k):
        at = lambda c, r: sum(int(v) * m for v, m in zip(self.place(jnp.int32(c * self.groups + r)), (self.n_mp, 1)))
        with jax.ensure_compile_time_eval():
            return [(at(c, r), at(c, (r + k) % self.groups)) for c in range(CRIT) for r in range(self.groups)]

    def pairs(self, rows):
        per = -(-rows // self.groups)
        return -(-per // 32) * 16

    def cap(self, rows):
        return -(-(self.n * -(-rows // self.groups)) // (TILE * AHEAD_TILES)) * TILE * AHEAD_TILES


def chunks_of(columns):
    width = math.gcd(math.gcd(columns, H), HALF)
    return width, columns // width, H // width


def assemble(chunks_ref, width, shift):
    groups = []
    lane = iota((32, LANES), 1)
    for g in range(H // LANES):
        block = jnp.zeros((32, LANES), F32)
        for i in range(LANES // width):
            chunk = chunks_ref[g * (LANES // width) + i]
            turn = (i * width - shift) % LANES
            moved = pltpu.roll(chunk, turn, 1) if turn else chunk
            block = jnp.where(lane // width == i, moved, block)
        groups.append(block)
    return jnp.concatenate(groups, 1)


def greet_all(plan, dp, mp):
    barrier = pltpu.get_barrier_semaphore()

    def tell(s, _):
        sdp, smp = s // plan.n_mp, s % plan.n_mp

        @pl.when(jnp.logical_or(sdp != dp, smp != mp))
        def _():
            pl.semaphore_signal(barrier, inc=1, device_id=(sdp, smp), device_id_type=MESH)

        return 0

    lax.fori_loop(0, plan.n, tell, 0)


def await_all(plan):
    pl.semaphore_wait(pltpu.get_barrier_semaphore(), plan.n - 1)


def dispatch_kernel(
    plan,
    inputs,
    wt_ref,
    wc_ref,
    x_ref,
    p_ref,
    low,
    msg,
    wide,
    chunk,
    send_w,
    recv_w,
    pass_w,
    recv_c,
    send_x,
    recv_x,
    pass_x,
    send_p,
    recv_p,
    pass_p,
    stage,
    stage_sem,
):
    loads = [pltpu.make_async_copy(src, dst, stage_sem.at[k]) for k, (src, dst) in enumerate(zip(inputs, stage))]
    for load in loads:
        load.start()
    dp, mp = lax.axis_index("dp"), lax.axis_index("mp")
    greet_all(plan, dp, mp)
    crit_ref, targ_ref, crit_in, crit_norms, targ_in, targ_norms, head_ref = stage[:7]
    sa_ref, ns_ref, reward_ref, done_ref, index_ref, subs_ref, table_ref, pin_ref, pmid_ref, pout_ref = stage[7:]
    crit_small, targ_small = (crit_in, crit_norms), (targ_in, targ_norms)
    me = plan.rank(dp, mp)
    index = dp * plan.n_mp + mp
    groups, workers = plan.groups, plan.workers
    critic, group = me // groups, me % groups
    rw, cw = crit_ref.shape[1], crit_ref.shape[2]
    rows = sa_ref.shape[1]
    columns = crit_small[0].shape[1]
    width, mine, per = chunks_of(columns)

    for load in loads[:2]:
        load.wait()

    def to_low(c, _):
        low[0, c] = targ_ref[c].astype(BF16)
        low[1, c] = crit_ref[c].astype(BF16)
        return 0

    lax.fori_loop(0, CRIT, to_low, 0)
    await_all(plan)

    def w_slot(s):
        sdp, smp = plan.device(s)
        return wt_ref.at[pl.ds(pl.multiple_of(smp * rw, rw), rw), pl.ds(pl.multiple_of(sdp * cw, cw), cw)]

    def to_worker(src, dst, send, recv, k):
        return pltpu.make_async_remote_copy(
            src_ref=src, dst_ref=dst, send_sem=send, recv_sem=recv, device_id=plan.place(k), device_id_type=MESH
        )

    turn = index // groups

    def first_hop(t, c):
        k = c * groups + index % groups
        dst = w_slot(index) if t == 0 else wc_ref.at[turn]
        recv = recv_w.at[turn] if t == 0 else recv_c.at[0]
        return k, dst, recv, to_worker(low.at[t, c], dst, send_w.at[0], recv, k)

    def send_weights(t):
        def one(i, _):
            c = (critic + 2 * CRIT + i * (1 - 2 * (index % 2))) % CRIT
            k, dst, recv, copy = first_hop(t, c)

            @pl.when(k == me)
            def _():
                pltpu.make_async_copy(low.at[t, c], dst, recv).start()

            @pl.when(k != me)
            def _():
                copy.start()

            return 0

        lax.fori_loop(0, CRIT, one, 0)

    send_weights(0)

    for load in loads[2:]:
        load.wait()
    wide[...] = jnp.zeros_like(wide)
    for t, parts in enumerate((targ_small, crit_small)):
        wide[t, 0:IN, 0:columns] = parts[0][...]
        wide[t, IN : IN + 4, 0:columns] = parts[1][...]
        wide[t, IN + 4 : IN + 5, 0:columns] = head_ref[t : t + 1, :]
    for j in range(mine):
        start, offset = j * width // LANES * LANES, j * width % LANES
        both = [wide[t, :, start : start + LANES] for t in range(2)]
        turned = [pltpu.roll(v, turn, 1) if turn else v for v, turn in zip(both, ((-offset) % LANES, (HALF - offset) % LANES))]
        chunk[j] = jnp.where(iota((32, LANES), 1) < HALF, turned[0], turned[1])

    def small_hop(j):
        g = index * mine + j
        k = (g // per) * groups + g % groups
        return k, g % per, to_worker(chunk.at[j], p_ref.at[g % per], send_p.at[j], recv_p.at[g % per], k)

    def send_small(j, _):
        k, slot, copy = small_hop(j)

        @pl.when(k == me)
        def _():
            pltpu.make_async_copy(chunk.at[j], p_ref.at[slot], recv_p.at[slot]).start()

        @pl.when(k != me)
        def _():
            copy.start()

        return 0

    lax.fori_loop(0, mine, send_small, 0)

    lane = iota((rows, LANES), 1)
    place = lambda height, offset: (iota((height, LANES), 1) == iota((height, LANES), 0) + offset).astype(F32).astype(BF16)
    hidden = swish(tn(ns_ref[...], pin_ref[...])).astype(BF16)
    hidden = swish(nn(hidden, pmid_ref[...])).astype(BF16)
    pout = pout_ref[...]
    spread = lambda offset: tn(
        pout, (iota((2 * ACT, LANES), 0) == iota((2 * ACT, LANES), 1) + offset).astype(F32).astype(BF16)
    ).astype(BF16)
    keep = lane < ACT
    means = nn(hidden, spread(0))
    raw = nn(hidden, spread(ACT))
    across = []
    for i in range(rows // LANES):
        lines = [reward_ref[i : i + 1, :], done_ref[i : i + 1, :].astype(F32), index_ref[i : i + 1, :].astype(F32)]
        lines += [subs_ref[:, i * LANES : (i + 1) * LANES].astype(F32), jnp.zeros((3, LANES), F32)]
        across.append(jnp.transpose(jnp.concatenate(lines, 0)))
    across = jnp.concatenate(across, 0)
    picked = (iota((rows, table_ref.shape[1]), 1) == across[:, 2:3].astype(I32)).astype(F32).astype(BF16)
    noise = jnp.zeros((rows, LANES), F32)
    for part in split3(table_ref[...]):
        noise = noise + nn(picked, tn(part, place(ACT, 0)).astype(BF16))
    log_std = -5.0 + 3.5 * (jnp.tanh(raw) + 1.0)
    squashed = means + jnp.exp(log_std) * noise
    action = jnp.tanh(squashed).astype(BF16)
    twice = -2.0 * squashed
    softplus = jnp.maximum(twice, 0.0) + jnp.log(1.0 + jnp.exp(-jnp.abs(twice)))
    correction = 2.0 * (math.log(2.0) - squashed - softplus)
    density = jnp.sum(
        jnp.where(keep, -0.5 * noise * noise - log_std - 0.5 * math.log(2.0 * math.pi) - correction, 0.0), -1, keepdims=True
    )
    done = across[:, 1:2]
    boot = (done == 0.0).astype(F32)
    base = across[:, 0:1] - (REWARD_DISCOUNT * ENTROPY_TEMP) * boot * density
    high, mid, rest = split3(base)
    on = lambda k, value: jnp.where(lane == k, value, 0.0)
    features = (
        tn(sa_ref[...], place(IN, 0))
        + tn(ns_ref[...], place(OBS, L_TGT))
        + nn(jnp.where(keep, action.astype(F32), 0.0).astype(BF16), place(LANES, L_TGT + OBS))
        + on(L_BASE, high.astype(F32))
        + on(L_BASE + 1, mid.astype(F32))
        + on(L_BASE + 2, rest.astype(F32))
        + on(L_BOOT, boot)
        + on(L_S0, across[:, 3:4])
        + on(L_S1, across[:, 4:5])
        + on(L_VALID, 1.0)
    ).astype(BF16)

    pairs = msg.shape[1]
    done_row = jnp.concatenate([done_ref[i : i + 1, :] for i in range(rows // LANES)], 1)
    valid = (done_row != 2).astype(F32)
    before = (iota((rows, rows), 0) < iota((rows, rows), 1)).astype(F32).astype(BF16)
    order = nn(jnp.broadcast_to(valid, (8, rows)).astype(BF16), before)[0:1, :]
    order = jnp.where(valid > 0.0, order, -1.0)
    count = jnp.sum(valid, -1, keepdims=True)
    count_half = jnp.floor(count * 0.5)
    mlane = iota((pairs, LANES), 1)
    tail = jnp.where(mlane == L_CNT, count_half, 0.0) + jnp.where(mlane == L_CNT + 1, count - 2.0 * count_half, 0.0)

    def deal(r, _):
        slot = iota((pairs, rows), 0) * (2 * groups) + r
        halves = []
        for h in range(2):
            hot = (order == (slot + h * groups).astype(F32)).astype(F32).astype(BF16)
            halves.append(nn(hot, features))
        msg[r] = (halves[0] + pltpu.roll(halves[1], HALF, 1) + tail).astype(BF16)
        return 0

    lax.fori_loop(0, groups, deal, 0)

    def row_hop(i):
        r = i % groups
        k = (2 * (i // groups) + index % 2) * groups + r
        return r, k, to_worker(msg.at[r], x_ref.at[index], send_x.at[0], recv_x.at[index], k)

    hops = plan.sets * groups

    def send_rows(i, _):
        r, k, copy = row_hop((i + (critic // 2) * groups) % hops)

        @pl.when(k == me)
        def _():
            pltpu.make_async_copy(msg.at[r], x_ref.at[index], recv_x.at[index]).start()

        @pl.when(k != me)
        def _():
            copy.start()

        return 0

    lax.fori_loop(0, hops, send_rows, 0)
    send_weights(1)

    def peer(i):
        return critic * groups + (group + 1 + i) % groups

    def pass_weight(t, i):
        s = group + groups * t
        return to_worker(w_slot(s), w_slot(s), pass_w.at[i], recv_w.at[plan.turns + groups - 2 - i], peer(i))

    def pass_small(slot, i):
        return to_worker(p_ref.at[slot], p_ref.at[slot], pass_p.at[slot // groups, i], recv_p.at[slot], peer(i))

    extra = plan.extra(critic // 2, group)

    def pass_rows(i, k, which):
        s = 2 * i + critic % 2
        return to_worker(x_ref.at[s], x_ref.at[s], pass_x.at[which], recv_x.at[plan.n], k)

    def other_rows(i):
        return pass_rows(i, (critic + 1 - 2 * (critic % 2)) * groups + group, 0)

    def extra_rows(i):
        return pass_rows(i, extra * groups + group, 1)

    def arrived_w(t):
        pltpu.make_async_copy(low.at[0, 0], w_slot(group + groups * t), recv_w.at[t]).wait()

    def blocks_done(sem, number):
        some = (plan.n - number + groups - 1) // groups

        @pl.when(some == plan.turns)
        def _():
            pltpu.make_async_copy(wc_ref, wc_ref, sem).wait()

        @pl.when(some != plan.turns)
        def _():
            fewer = wc_ref.at[pl.ds(0, plan.turns - 1)]
            pltpu.make_async_copy(fewer, fewer, sem).wait()

    def rows_done(sem, count):
        some = x_ref.at[pl.ds(0, count)]
        pltpu.make_async_copy(some, some, sem).wait()

    def arrived_x(s):
        pltpu.make_async_copy(msg.at[0], x_ref.at[s], recv_x.at[s]).wait()

    def arrived_p(slot):
        pltpu.make_async_copy(chunk.at[0], p_ref.at[slot], recv_p.at[slot]).wait()

    turns = (plan.n - group + groups - 1) // groups
    passes_rows = critic < 2 * plan.sets

    def peers(body):
        lax.fori_loop(0, groups - 1, lambda i, _: (body(i), 0)[1], 0)

    def each(count, body):
        lax.fori_loop(0, count, lambda i, _: (body(i), 0)[1], 0)

    @pl.when(me < workers)
    def _():
        def relay_weight(j):
            t = j
            if plan.turns == 11:
                step = j // 2
                away = jnp.where(step == 5, -3, ((step + 1) // 2) * (2 * (step % 2) - 1))
                t = (turn + 5 * (j % 2) + away + 2 * plan.turns) % plan.turns

            @pl.when(t < turns)
            def _():
                arrived_w(t)
                peers(lambda i: pass_weight(t, i).start())

        each(plan.turns, relay_weight)

        @pl.when(passes_rows)
        def _():
            def relay_rows(i):
                arrived_x(2 * i + critic % 2)
                other_rows(i).start()

                @pl.when(extra >= 0)
                def _():
                    extra_rows(i).start()

            each(plan.n // 2, relay_rows)

        def relay_small(slot):
            @pl.when((critic * per + slot) % groups == group)
            def _():
                arrived_p(slot)
                peers(lambda i: pass_small(slot, i).start())

        each(per, relay_small)

        peers(lambda i: blocks_done(recv_w.at[plan.turns + i], (group + 1 + i) % groups))

        @pl.when(passes_rows)
        def _():
            rows_done(recv_x.at[plan.n], plan.n // 2)

        @pl.when(jnp.logical_not(passes_rows))
        def _():
            rows_done(recv_x.at[plan.n], plan.n)

        def arrived_small(slot):
            @pl.when((critic * per + slot) % groups != group)
            def _():
                arrived_p(slot)

        each(per, arrived_small)
        blocks_done(recv_c.at[0], group)
        peers(lambda i: blocks_done(pass_w.at[i], group))

        @pl.when(passes_rows)
        def _():
            rows_done(pass_x.at[0], plan.n // 2)

            @pl.when(extra >= 0)
            def _():
                rows_done(pass_x.at[1], plan.n // 2)

        def passed_small(slot):
            @pl.when((critic * per + slot) % groups == group)
            def _():
                peers(lambda i: pass_small(slot, i).wait_send())

        each(per, passed_small)

    at_home = jnp.logical_and(me < workers, index % groups == group)

    @pl.when(at_home)
    def _():
        sent = low.at[:, pl.ds(0, CRIT - 1)]
        pltpu.make_async_copy(sent, sent, send_w.at[0]).wait()

    @pl.when(jnp.logical_not(at_home))
    def _():
        pltpu.make_async_copy(low, low, send_w.at[0]).wait()

    def sent_small(j):
        k, _slot, copy = small_hop(j)

        @pl.when(k != me)
        def _():
            copy.wait_send()

    each(mine, sent_small)

    at_home_rows = jnp.logical_and(jnp.logical_and(me < workers, passes_rows), index % 2 == critic % 2)

    @pl.when(at_home_rows)
    def _():
        rows_done(send_x.at[0], hops - 1)

    @pl.when(jnp.logical_not(at_home_rows))
    def _():
        rows_done(send_x.at[0], hops)


def dispatch(plan, inputs):
    critic_hidden, critic_in, state_action = inputs[0], inputs[2], inputs[7]
    rows = state_action.shape[1]
    pairs = plan.pairs(rows)
    columns = critic_in.shape[1]
    _width, mine, per = chunks_of(columns)
    anywhere = pl.BlockSpec(memory_space=pl.ANY)
    dma = pltpu.SemaphoreType.DMA
    return pl.pallas_call(
        functools.partial(dispatch_kernel, plan),
        out_shape=(
            jax.ShapeDtypeStruct((H, H), BF16),
            jax.ShapeDtypeStruct((plan.turns,) + critic_hidden.shape[1:], BF16),
            jax.ShapeDtypeStruct((plan.n, pairs, LANES), BF16),
            jax.ShapeDtypeStruct((per, 32, LANES), F32),
        ),
        in_specs=[(pl.BlockSpec(memory_space=pltpu.HBM),) * len(inputs)],
        out_specs=(anywhere,) * 4,
        scratch_shapes=[
            pltpu.VMEM((2,) + critic_hidden.shape, BF16),
            pltpu.VMEM((plan.groups, pairs, LANES), BF16),
            pltpu.VMEM((2, 32, -(-columns // LANES) * LANES), F32),
            pltpu.VMEM((mine, 32, LANES), F32),
            dma((1,)),
            dma((plan.turns + plan.groups - 1,)),
            dma((plan.groups - 1,)),
            dma((1,)),
            dma((1,)),
            dma((plan.n + 1,)),
            dma((2,)),
            dma((mine,)),
            dma((per,)),
            dma((-(-per // plan.groups), plan.groups - 1)),
            tuple(pltpu.VMEM(v.shape, v.dtype) for v in inputs),
            dma((len(inputs),)),
        ],
        compiler_params=pltpu.CompilerParams(collective_id=0, has_side_effects=True, vmem_limit_bytes=60 * MIB),
        name="dispatch",
    )(inputs)


def norm_parts(pre):
    centered = pre - jnp.sum(pre, -1, keepdims=True) * (1.0 / H)
    inv = lax.rsqrt(jnp.sum(centered * centered, -1, keepdims=True) * (1.0 / H) + 1e-05)
    return centered * inv, inv


def swish_parts(half):
    t = jnp.tanh(half)
    product = half * t
    return half + product, (1.0 + t) * (1.0 + (half - product))


def low_input(params):
    return jnp.where(iota((32, H), 0) < IN, params, 0.0).astype(BF16)


def input_layer(params, win_ref, gram_ref):
    weight = low_input(params).astype(F32)
    weight = weight - jnp.sum(weight, -1, keepdims=True) * (1.0 / H)
    win_ref[...] = jnp.zeros_like(win_ref)
    for k, part in enumerate(split3(weight)):
        win_ref[k * 32 : (k + 1) * 32, :] = part
    for k, part in enumerate(split3(nt(win_ref[...], win_ref[...]) * (1.0 / H))):
        gram_ref[k] = part


def input_norm(x, start, win_ref, gram_ref):
    row, lane = iota((LANES, LANES), 0), iota((LANES, LANES), 1)
    pick = jnp.logical_and(lane < 96, jnp.logical_and(lane % 32 < IN, row == lane % 32 + start))
    thrice = nn(x, pick.astype(F32).astype(BF16)).astype(BF16)
    image = sum(nn(thrice, gram_ref[k]) for k in range(3))
    var = jnp.sum(image * thrice.astype(F32), -1, keepdims=True)
    return nn(thrice, win_ref[...]), lax.rsqrt(jnp.maximum(var, 0.0) + 1e-05)


def tile_span(t):
    return pl.ds(pl.multiple_of(t * TILE, TILE), TILE)


def target_kernel(
    plan, width, x_ref, w_ref, p_ref, xc_ref, q_ref, info_ref, rows_f, picked, value, hot, win, par, flat_q, cnt_v, cnt_s, base_s, sem
):
    me = plan.rank(lax.axis_index("dp"), lax.axis_index("mp"))
    critic, group, active = me // plan.groups, me % plan.groups, (me < plan.workers).astype(I32)
    groups, n = plan.groups, plan.n
    pairs = x_ref.shape[1]
    first = x_ref[:, 0, :].astype(F32)
    lane = iota(first.shape, 1)
    counts = 2.0 * jnp.sum(jnp.where(lane == L_CNT, first, 0.0), -1, keepdims=True) + jnp.sum(
        jnp.where(lane == L_CNT + 1, first, 0.0), -1, keepdims=True
    )
    counts = jnp.where(active > 0, jnp.broadcast_to(counts, first.shape), 0.0)
    mine = jnp.floor((counts + (groups - 1 - group).astype(F32)) * (1.0 / groups) + 0.5 / groups)
    earlier = (iota((n, n), 1) < iota((n, n), 0)).astype(F32).astype(BF16)
    starts = nn(earlier, mine.astype(BF16))
    total = jnp.sum(counts, 0, keepdims=True)
    cnt_v[0:n, :] = mine.astype(I32)
    cnt_v[n : 2 * n, :] = starts.astype(I32)
    cnt_v[2 * n : 2 * n + 8, :] = jnp.broadcast_to(total, (8, LANES)).astype(I32)
    copy = pltpu.make_async_copy(cnt_v, cnt_s, sem)
    copy.start()
    par[...] = assemble(p_ref, width, 0)
    win[...] = jnp.zeros_like(win)
    win[0:32, :] = low_input(par[...])
    copy.wait()
    number = cnt_s[n - 1, 0] + cnt_s[2 * n - 1, 0]
    tiles = (number + TILE - 1) // TILE
    info_ref[0] = number
    info_ref[1] = cnt_s[2 * n, 0]

    def compact(s, _):
        block = x_ref[s].astype(F32)
        have, start = cnt_s[s, 0], cnt_s[n + s, 0]
        rows_f[pl.ds(start, pairs), :] = block
        rows_f[pl.ds(start + (have + 1) // 2, pairs), :] = pltpu.roll(block, HALF, 1)
        return 0

    @pl.when(active > 0)
    def _():
        lax.fori_loop(0, n, compact, 0, unroll=4)

    rows_f[pl.ds(number, AHEAD_TILES * TILE), :] = jnp.zeros((AHEAD_TILES * TILE, LANES), F32)
    bundles = (tiles + AHEAD_TILES - 1) // AHEAD_TILES

    until = (iota((TILE, TILE), 1) < iota((TILE, TILE), 0)).astype(F32).astype(BF16)
    place = iota((TILE, TILE), 1).astype(F32)
    this = critic.astype(F32)

    def choose(b, base):
        chosen, counts = [], []
        for i in range(AHEAD_TILES):
            t = b * AHEAD_TILES + i
            wide = rows_f[tile_span(t), :]
            x = wide.astype(BF16)
            xc_ref[tile_span(t), :] = x
            wanted = jnp.logical_or(wide[:, L_S0 : L_S0 + 1] == this, wide[:, L_S1 : L_S1 + 1] == this)
            wanted = jnp.where(jnp.logical_and(wanted, wide[:, L_BOOT : L_BOOT + 1] > 0.0), 1.0, 0.0)
            order = nn(until, jnp.broadcast_to(wanted, (TILE, LANES)).astype(BF16))[:, 0:1]
            to = (jnp.where(wanted > 0.0, order, -1.0) == place).astype(F32).astype(BF16)
            hot[t] = to
            chosen.append(tn(to, x))
            counts.append(jnp.sum(wanted).astype(I32))
        for i in range(AHEAD_TILES):
            picked[pl.ds(base, TILE), :] = chosen[i]
            base_s[b * AHEAD_TILES + i] = base
            base = base + counts[i]
        return base

    chosen_rows = lax.fori_loop(0, bundles, choose, 0)
    picked[pl.ds(chosen_rows, TILE), :] = jnp.zeros((TILE, LANES), F32)
    chosen_tiles = (chosen_rows + TILE - 1) // TILE
    half = jnp.where(iota((32, 1), 0) < IN + 4, 0.5, 1.0)
    par[...] = par[...] * half
    gain1, shift1, gain2, shift2, head = (par[IN + k : IN + k + 1, :] for k in range(5))

    def tile(t, _):
        x = pltpu.roll(picked[tile_span(t), :], LANES - L_TGT, 1).astype(BF16)
        z, _unused = norm_parts(nn(x, win[...]))
        y = z * gain1 + shift1
        act = (y + y * jnp.tanh(y)).astype(BF16)
        z, _unused = norm_parts(nn(act, w_ref[...]))
        y = z * gain2 + shift2
        q = jnp.sum((y + y * jnp.tanh(y)) * head, -1, keepdims=True)
        value[tile_span(t), :] = jnp.broadcast_to(q, (TILE, LANES))
        return 0

    lax.fori_loop(0, chosen_tiles, tile, 0)
    value[tile_span(chosen_tiles), :] = jnp.zeros((TILE, LANES), F32)

    def spread(b, _):
        lane = iota((TILE, LANES), 1)
        for i in range(AHEAD_TILES):
            t = b * AHEAD_TILES + i
            high, mid, rest = (v.astype(F32) for v in split3(value[pl.ds(base_s[t], TILE), :]))
            parts = jnp.where(lane == 0, high, jnp.where(lane == 1, mid, jnp.where(lane == 2, rest, 0.0)))
            q = jnp.broadcast_to(jnp.sum(nn(hot[t], parts.astype(BF16)), -1, keepdims=True), (TILE, LANES))
            for h in range(TILE // LANES):
                flat = jnp.transpose(q[h * LANES : (h + 1) * LANES, :])
                flat_q[pl.ds(t * (TILE // LANES) + h, 1), :] = flat[0:1, :]
        return 0

    lax.fori_loop(0, bundles, spread, 0)
    q_ref[...] = flat_q[...].astype(BF16)


def target_values(plan, rows, width, x, weights, params):
    capacity = plan.cap(rows)
    vmem = pl.BlockSpec(memory_space=pltpu.VMEM)
    smem = pl.BlockSpec(memory_space=pltpu.SMEM)
    return pl.pallas_call(
        functools.partial(target_kernel, plan, width),
        out_shape=(
            jax.ShapeDtypeStruct((capacity, LANES), BF16),
            jax.ShapeDtypeStruct((capacity // LANES, LANES), BF16),
            jax.ShapeDtypeStruct((2,), I32),
        ),
        in_specs=[vmem, vmem, vmem],
        out_specs=(vmem, vmem, smem),
        scratch_shapes=[
            pltpu.VMEM((capacity + AHEAD_TILES * TILE + x.shape[1], LANES), F32),
            pltpu.VMEM((capacity + TILE, LANES), F32),
            pltpu.VMEM((capacity + TILE, LANES), F32),
            pltpu.VMEM((capacity // TILE, TILE, TILE), BF16),
            pltpu.VMEM((LANES, H), BF16),
            pltpu.VMEM((32, H), F32),
            pltpu.VMEM((capacity // LANES, LANES), F32),
            pltpu.VMEM((2 * plan.n + 8, LANES), I32),
            pltpu.SMEM((2 * plan.n + 8, LANES), I32),
            pltpu.SMEM((capacity // TILE,), I32),
            pltpu.SemaphoreType.DMA,
        ],
        compiler_params=pltpu.CompilerParams(vmem_limit_bytes=TARGET_MIB * MIB),
        name="target_values",
    )(x, weights, params)


def share_kernel(plan, q_ref, all_ref, send, recv):
    dp, mp = lax.axis_index("dp"), lax.axis_index("mp")
    me = plan.rank(dp, mp)
    groups = plan.groups
    critic, group = me // groups, me % groups
    barrier = pltpu.get_barrier_semaphore()

    @pl.when(me < plan.workers)
    def _():
        def peer(i):
            return plan.place((critic + i) % CRIT * groups + group)

        def tell(i, _):
            pl.semaphore_signal(barrier, inc=1, device_id=peer(i), device_id_type=MESH)
            return 0

        lax.fori_loop(1, CRIT, tell, 0)
        pl.semaphore_wait(barrier, CRIT - 1)
        all_ref[critic] = q_ref[...]

        def copy(i):
            device = peer(i)
            return pltpu.make_async_remote_copy(
                src_ref=q_ref,
                dst_ref=all_ref.at[critic],
                send_sem=send,
                recv_sem=recv,
                device_id=device,
                device_id_type=MESH,
            )

        def start(i, _):
            copy(i).start()
            return 0

        lax.fori_loop(1, CRIT, start, 0)

        others = all_ref.at[pl.ds(0, CRIT - 1)]
        pltpu.make_async_copy(others, others, recv).wait()
        pltpu.make_async_copy(others, others, send).wait()


def share_values(plan, q):
    vmem = pl.BlockSpec(memory_space=pltpu.VMEM)
    return pl.pallas_call(
        functools.partial(share_kernel, plan),
        out_shape=jax.ShapeDtypeStruct((CRIT,) + q.shape, BF16),
        in_specs=[vmem],
        out_specs=vmem,
        scratch_shapes=[pltpu.SemaphoreType.DMA, pltpu.SemaphoreType.DMA],
        compiler_params=pltpu.CompilerParams(collective_id=1, has_side_effects=True, vmem_limit_bytes=8 * MIB),
        name="share_values",
    )(q)


def critic_kernel(
    plan, width, info_ref, xc_ref, q_ref, shares, p_ref, grad_ref, lowered_ref, small_ref, sums_ref, w_ref, z_one, slope, act, low, fact, par, win, gram, picks, acc, q_all
):
    number = info_ref[0]
    scale = 2.0 / jnp.maximum(info_ref[1], 1).astype(F32)
    tiles = (number + TILE - 1) // TILE
    rw, cw = shares[0].shape[1:]
    me = plan.rank(lax.axis_index("dp"), lax.axis_index("mp"))
    for k, share in enumerate(shares):
        owner = (me % plan.groups + plan.groups - k) % plan.groups

        def gather(t, _):
            s = owner + plan.groups * t

            @pl.when(s < plan.n)
            def _():
                sdp, smp = plan.device(s)
                w_ref[pl.ds(pl.multiple_of(smp * rw, rw), rw), pl.ds(pl.multiple_of(sdp * cw, cw), cw)] = share[t]

            return 0

        lax.fori_loop(0, plan.turns, gather, 0)
    par[...] = assemble(p_ref, width, HALF)
    input_layer(par[...], win, gram)
    grad_ref[...] = jnp.zeros_like(grad_ref)
    acc[...] = jnp.zeros_like(acc)
    picks[...] = jnp.zeros_like(picks)
    q_all[...] = q_ref[...].astype(F32)
    sums_ref[...] = jnp.zeros_like(sums_ref)
    gain1, shift1, gain2, shift2, head = (par[IN + k : IN + k + 1, :] for k in range(5))

    hg = (0.5 * head) * gain2

    def fold(k, value):
        acc[32 + k * 8 : 40 + k * 8, :] += jnp.sum(value.reshape(TILE // 8, 8, H), 0)

    def tile(t, _):
        x = xc_ref[tile_span(t), :]
        wide = x.astype(F32)
        pre, inv_one = input_norm(x, 0, win, gram)
        z = pre * inv_one
        z_one[...] = z
        value, twice = swish_parts(z * (0.5 * gain1) + 0.5 * shift1)
        slope[...] = 0.5 * twice
        act[...] = value.astype(BF16)
        pre = nn(act[...], w_ref[...])
        for h in range(TILE // LANES):
            picks[0:CRIT, :] = q_all[:, pl.ds(t * (TILE // LANES) + h, 1), :].reshape(CRIT, LANES)
            table = jnp.transpose(picks[...])
            part = wide[h * LANES : (h + 1) * LANES, :]
            critic = iota(table.shape, 1).astype(F32)
            one = jnp.sum(jnp.where(critic == part[:, L_S0 : L_S0 + 1], table, 0.0), -1, keepdims=True)
            two = jnp.sum(jnp.where(critic == part[:, L_S1 : L_S1 + 1], table, 0.0), -1, keepdims=True)
            base = part[:, L_BASE : L_BASE + 1] + part[:, L_BASE + 1 : L_BASE + 2] + part[:, L_BASE + 2 : L_BASE + 3]
            goal = base + jnp.where(part[:, L_BOOT : L_BOOT + 1] > 0.0, REWARD_DISCOUNT * jnp.minimum(one, two), 0.0)
            fact[h * LANES : (h + 1) * LANES, 0:1] = goal
        z, inv = norm_parts(pre)
        value, twice = swish_parts(z * (0.5 * gain2) + 0.5 * shift2)
        q = jnp.sum(value * head, -1, keepdims=True)
        error = (q - fact[:, 0:1]) * wide[:, L_VALID : L_VALID + 1]
        sums_ref[0:1, :] += jnp.broadcast_to(jnp.sum(error * error, 0, keepdims=True), (1, LANES))
        dq = error * scale
        flat = jnp.transpose(jnp.broadcast_to(dq, (TILE, LANES)))[0:8, :]
        high, rest = split2(flat)
        weigh = jnp.concatenate([high, rest], 0)
        tz = twice * z
        for k, v in ((4, value), (3, twice), (2, tz)):
            acc[32 + k * 8 : 40 + k * 8, :] += nn(weigh, v.astype(BF16))[4:12]
        dz = twice * hg
        mean = jnp.sum(dz, -1, keepdims=True) * (1.0 / H)
        along = jnp.sum(tz * hg, -1, keepdims=True) * (1.0 / H)
        low[...] = ((inv * dq) * (dz - mean - z * along)).astype(BF16)
        down = nt(low[...], w_ref[...])
        grad_ref[...] += tn(act[...], low[...])
        z = z_one[...]
        dy = down * slope[...]
        fold(1, dy)
        fold(0, dy * z)
        dz = dy * gain1
        mean = jnp.sum(dz, -1, keepdims=True) * (1.0 / H)
        along = jnp.sum(dz * z, -1, keepdims=True) * (1.0 / H)
        acc[0:32, :] += tn(x[:, 0:32], (inv_one * (dz - mean - z * along)).astype(BF16))
        return 0

    lax.fori_loop(0, tiles, tile, 0)
    lowered_ref[...] = grad_ref[...].astype(BF16)
    sums_ref[1:2, :] = jnp.broadcast_to(info_ref[1].astype(F32), (1, LANES))
    for k in range(2, 5):
        total = jnp.sum(acc[32 + k * 8 : 40 + k * 8, :], 0, keepdims=True) * 0.25
        acc[32 + k * 8 : 40 + k * 8, :] = jnp.zeros((8, H), F32)
        acc[32 + k * 8 : 33 + k * 8, :] = total if k == 4 else total * (0.5 * head)
    for k in range(5):
        acc[IN + k : IN + k + 1, :] = jnp.sum(acc[32 + k * 8 : 40 + k * 8, :], 0, keepdims=True)
    for i in range(H // width):
        start, offset = i * width // LANES * LANES, i * width % LANES
        block = acc[0:32, start : start + LANES]
        small_ref[i] = pltpu.roll(block, LANES - offset, 1) if offset else block


def critic_step(plan, width, info, xc, q_all, shares, params):
    vmem = pl.BlockSpec(memory_space=pltpu.VMEM)
    smem = pl.BlockSpec(memory_space=pltpu.SMEM)
    return pl.pallas_call(
        functools.partial(critic_kernel, plan, width),
        out_shape=(
            jax.ShapeDtypeStruct((H, H), F32),
            jax.ShapeDtypeStruct((H, H), BF16),
            jax.ShapeDtypeStruct((H // width, 32, LANES), F32),
            jax.ShapeDtypeStruct((8, LANES), F32),
        ),
        in_specs=[smem, vmem, vmem, (vmem,) * plan.groups, vmem],
        out_specs=(vmem,) * 4,
        scratch_shapes=[
            pltpu.VMEM((H, H), BF16),
            pltpu.VMEM((TILE, H), F32),
            pltpu.VMEM((TILE, H), F32),
            pltpu.VMEM((TILE, H), BF16),
            pltpu.VMEM((TILE, H), BF16),
            pltpu.VMEM((TILE, LANES), F32),
            pltpu.VMEM((32, H), F32),
            pltpu.VMEM((LANES, H), BF16),
            pltpu.VMEM((3, LANES, LANES), BF16),
            pltpu.VMEM((16, LANES), F32),
            pltpu.VMEM((72, H), F32),
            pltpu.VMEM(q_all.shape, F32),
        ],
        compiler_params=pltpu.CompilerParams(vmem_limit_bytes=36 * MIB),
        name="critic_step",
    )(info, xc, q_all, shares, params)


PRECISE = 1


LAG = 3
AHEAD = 3


def shampoo_kernel(
    plan,
    g_ref,
    lowered_ref,
    small_ref,
    sums_ref,
    mom_ref,
    left_ref,
    right_ref,
    w_ref,
    mo_ref,
    lo_ref,
    ro_ref,
    wo_ref,
    own_ref,
    out_ref,
    parts,
    pieces,
    given,
    shares,
    totals,
    sums_in,
    sums_all,
    send_one,
    recv_one,
    send_two,
    recv_two,
    send_s,
    recv_s,
    send_t,
    recv_t,
):
    dp, mp = lax.axis_index("dp"), lax.axis_index("mp")
    me = plan.rank(dp, mp)
    index = dp * plan.n_mp + mp
    groups, workers, n, turns = plan.groups, plan.workers, plan.n, plan.turns
    critic, group = me // groups, me % groups
    rw, cw = mom_ref.shape[1], mom_ref.shape[2]
    mine, per = shares.shape[1], small_ref.shape[0]
    columns = own_ref.shape[1]
    chunk_width = H // per
    greet_all(plan, dp, mp)
    await_all(plan)

    def to_device(src, dst, send, recv, device):
        return pltpu.make_async_remote_copy(
            src_ref=src, dst_ref=dst, send_sem=send, recv_sem=recv, device_id=device, device_id_type=MESH
        )

    def block(s):
        sdp, smp = plan.device(s)
        return pl.ds(pl.multiple_of(smp * rw, rw), rw), pl.ds(pl.multiple_of(sdp * cw, cw), cw)

    def turn_of(step):
        return (step + critic) % turns

    def first_hop(step, i):
        other = (group + 1 + i) % groups
        turn = turn_of(step)
        s = other + groups * turn
        copy = to_device(
            lowered_ref.at[block(s)],
            parts.at[groups - 2 - i, turn],
            send_one.at[i],
            recv_one.at[groups - 2 - i, turn],
            plan.place(critic * groups + other),
        )
        return s, copy

    def second_hop(turn):
        s = group + groups * turn
        return s, to_device(pieces.at[turn], given.at[critic], send_two.at[turn], recv_two.at[critic], plan.device(s))

    def small_hop(q):
        g = critic * per + q
        s = g // mine
        return s, to_device(small_ref.at[q], shares.at[group, g % mine], send_s.at[q], recv_s.at[0], plan.device(s))

    def total_first(i):
        k = critic * groups + (group + 1 + i) % groups
        return to_device(sums_ref, sums_in.at[groups - 2 - i], send_t.at[i], recv_t.at[groups - 2 - i], plan.place(k))

    def total_second(turn):
        s = group + groups * turn
        return s, to_device(
            sums_all, totals.at[critic], send_t.at[groups - 1 + turn], recv_t.at[groups - 1 + critic], plan.device(s)
        )

    def start_first(step):
        def one(i, _):
            s, copy = first_hop(step, i)

            @pl.when(s < n)
            def _():
                copy.start()

            return 0

        lax.fori_loop(0, groups - 1, one, 0)

    def start_rest():
        def start_small(q, _):
            s, copy = small_hop(q)

            @pl.when(s == index)
            def _():
                slot = (critic * per + q) % mine
                pltpu.make_async_copy(small_ref.at[q], shares.at[group, slot], recv_s.at[0]).start()

            @pl.when(s != index)
            def _():
                copy.start()

            return 0

        lax.fori_loop(0, per, start_small, 0)
        for i in range(groups - 1):
            pltpu.make_async_copy(sums_ref, sums_in.at[i], recv_t.at[i]).wait()
        value = sums_ref[...]
        for i in range(groups - 1):
            value = value + jnp.where(iota((8, LANES), 0) == 0, sums_in[i], 0.0)
        sums_all[...] = value

        def start_total(turn, _):
            s, copy = total_second(turn)

            @pl.when(s == index)
            def _():
                totals[critic] = sums_all[...]

            @pl.when(jnp.logical_and(s < n, s != index))
            def _():
                copy.start()

            return 0

        lax.fori_loop(0, turns, start_total, 0)

    @pl.when(me < workers)
    def _():
        for step in range(AHEAD):
            start_first(step)
        for i in range(groups - 1):
            total_first(i).start()

    def add_up(step):
        turn = turn_of(step)
        s, copy = second_hop(turn)

        @pl.when(s < n)
        def _():
            for i in range(groups - 1):
                pltpu.make_async_copy(parts.at[0, 0], parts.at[i, turn], recv_one.at[i, turn]).wait()
            value = g_ref[block(s)]
            for i in range(groups - 1):
                value = value + parts[i, turn].astype(F32)
            pieces[turn] = value.astype(BF16)

            @pl.when(s == index)
            def _():
                pltpu.make_async_copy(pieces.at[turn], given.at[critic], recv_two.at[critic]).start()

            @pl.when(s != index)
            def _():
                copy.start()

    width = min(256, cw)
    halves = width // LANES
    high_rows = halves * BLK
    nr, nc = rw // BLK, cw // width
    subs = [(i, j) for i in range(nr) for j in range(nc)]
    mask = (iota((LANES, LANES), 0) // BLK == iota((LANES, LANES), 1) // BLK).astype(F32).astype(BF16)
    mask_wide = jnp.concatenate([mask] * halves, 1)
    eye = (iota((high_rows, LANES), 0) % BLK == iota((high_rows, LANES), 1) % BLK).astype(F32)
    eye_low = eye.astype(BF16)

    def packed(flat):
        return jnp.concatenate([flat[:, k * LANES : (k + 1) * LANES] for k in range(halves)], 0)

    def flat_of(x):
        return jnp.concatenate([x[k * BLK : (k + 1) * BLK] for k in range(halves)], 1)

    def tops(out, count):
        return [
            jnp.concatenate(
                [out[(i * halves + k) * BLK : (i * halves + k + 1) * BLK, k * LANES : (k + 1) * LANES] for k in range(halves)], 0
            )
            for i in range(count)
        ]

    def diag(x):
        return jnp.concatenate([flat_of(x)] * (LANES // BLK), 0) * mask_wide

    def diag_rows(x):
        tiled = [jnp.concatenate([x[k * BLK : (k + 1) * BLK]] * (LANES // BLK), 0) * mask for k in range(halves)]
        return jnp.concatenate(tiled, 0)

    def products(lhs, right):
        return tops(nn(jnp.concatenate(lhs, 0), right), len(lhs))

    def precise(parts, right, right_rest):
        high, rest = parts
        out = products([high, rest], right)
        return out[0] + out[1] + products([high], right_rest)[0]

    def block_sums(s):
        high, rest = split2(s)
        return nn(high, mask) + nn(rest, mask)

    def place(c, i, j):
        return (c, slice(i * BLK, (i + 1) * BLK), slice(j * width, (j + 1) * width))

    def column_sums(x):
        return [jnp.sum(x[k * BLK : (k + 1) * BLK].reshape(BLK // 8, 8, LANES), 0) for k in range(halves)]

    def over_blocks(total, spot):
        rows = [jnp.sum(total[(spot + k) * 8 : (spot + k + 1) * 8], 0, keepdims=True) for k in range(halves)]
        return jnp.concatenate([jnp.broadcast_to(row, (BLK, LANES)) for row in rows], 0)

    def blocked(c):
        pltpu.make_async_copy(pieces.at[0], given.at[c], recv_two.at[c]).wait()
        sums, stats = [], []
        for i, j in subs:
            at = place(c, i, j)
            grad = given[at].astype(F32)
            mo_ref[at] = MOMENTUM * mom_ref[at] + grad
            low = packed(grad.astype(BF16))
            square, flip = tops(nt(jnp.concatenate([low, eye_low], 0), diag_rows(low)), 2)
            left = STAT_DECAY * packed(left_ref[at]) + (1.0 - STAT_DECAY) * square
            right = products([flip.astype(BF16)], diag(low))[0]
            right = STAT_DECAY * packed(right_ref[at]) + (1.0 - STAT_DECAY) * right
            lo_ref[at] = flat_of(left)
            ro_ref[at] = flat_of(right)
            for stat in (left, right):
                stats.append(stat)
                sums += column_sums(stat * stat)
        total = block_sums(jnp.concatenate(sums, 0))
        chains = []
        for k, stat in enumerate(stats):
            inv = lax.rsqrt(over_blocks(total, k * halves))
            rest = (eye - stat * inv) * 0.25
            chains.append([rest, eye + rest, jnp.sqrt(jnp.sqrt(inv))])
        for it in range(NEWTON - 1):
            full = it < PRECISE
            squares = []
            for ch in chains:
                high, rest = split2(ch[0])
                lhs = [high] + ([rest] if full else []) + ([ch[1].astype(BF16)] if it > 0 else [])
                out = products(lhs, diag(high))
                power = out[0]
                if full:
                    power = power + out[1] + products([high], diag(rest))[0]
                if it > 0:
                    ch[1] = ch[1] + out[-1]
                squares.append(power)
            factors = [[diag(v) for v in split2(power)[: 2 if full else 1]] for power in squares]

            def times(x, right):
                parts = split2(x)
                return precise(parts, *right) if full else products([parts[0]], right[0])[0]

            terms = [
                5.0 * ch[0] + 3.75 * power + times(ch[0], right) for ch, power, right in zip(chains, squares, factors)
            ]
            for ch, power, right, term in zip(chains, squares, factors, terms):
                ch[0] = 2.5 * power + times(term, right)
        for ch in chains:
            ch[1] = ch[1] + products([ch[1].astype(BF16)], diag(ch[0].astype(BF16)))[0]
        steps, sums = [], []
        for k, (i, j) in enumerate(subs):
            lc, rc = chains[2 * k], chains[2 * k + 1]
            moment = split2(packed(mo_ref[place(c, i, j)]))
            roots = split2(rc[1])
            step = precise(split2(lc[1]), diag(moment[0]), diag(moment[1]))
            step = precise(split2(step), diag(roots[0]), diag(roots[1])) * (lc[2] * rc[2])
            steps.append(step)
            sums += column_sums(step * step)
        total = block_sums(jnp.concatenate(sums, 0)) * (1.0 / (BLK * BLK))
        for k, (i, j) in enumerate(subs):
            at = place(c, i, j)
            old = w_ref[at]
            step = flat_of(steps[k] * lax.rsqrt(over_blocks(total, k * halves) + 1e-06))
            wo_ref[at] = old - RATE_HIDDEN * (step + WEIGHT_DECAY * old)

    def round_(i, _):
        @pl.when(jnp.logical_and(me < workers, i < turns))
        def _():
            @pl.when(i + AHEAD < turns)
            def _():
                start_first(i + AHEAD)

            @pl.when(i == turns - 2)
            def _():
                start_rest()

            add_up(i)

        c = (index // groups + 2 * turns + LAG - i) % turns

        @pl.when(jnp.logical_and(i >= LAG, c < CRIT))
        def _():
            blocked(c)

        return 0

    lax.fori_loop(0, turns + LAG, round_, 0)

    pltpu.make_async_copy(shares, shares, recv_s.at[0]).wait()
    for g in range(columns // LANES):
        part = jnp.zeros((32, LANES), F32)
        for j in range(mine):
            if j * chunk_width // LANES == g:
                value = shares[0, j]
                for r in range(1, groups):
                    value = value + shares[r, j]
                turn = j * chunk_width % LANES
                moved = pltpu.roll(value, turn, 1) if turn else value
                part = jnp.where(iota((32, LANES), 1) // chunk_width == turn // chunk_width, moved, part)
        own_ref[:, g * LANES : (g + 1) * LANES] = part

    def arrived_total(c, _):
        @pl.when(c * groups + index % groups != me)
        def _():
            pltpu.make_async_copy(sums_ref, totals.at[c], recv_t.at[groups - 1 + c]).wait()

        return 0

    lax.fori_loop(0, CRIT, arrived_total, 0)
    out_ref[0:1, :] = jnp.sum(totals[:, 0, :], 0, keepdims=True)
    out_ref[1:2, :] = totals[0, 1:2, :]
    out_ref[2:8, :] = jnp.zeros((6, LANES), F32)

    @pl.when(me < workers)
    def _():
        for i in range(groups - 1):
            some = (n - (group + 1 + i) % groups + groups - 1) // groups

            @pl.when(some == turns)
            def _():
                pltpu.make_async_copy(parts.at[0], parts.at[0], send_one.at[i]).wait()

            @pl.when(some != turns)
            def _():
                fewer = parts.at[0, pl.ds(0, turns - 1)]
                pltpu.make_async_copy(fewer, fewer, send_one.at[i]).wait()

        def finish(turn, _):
            s, copy = second_hop(turn)

            @pl.when(jnp.logical_and(s < n, s != index))
            def _():
                copy.wait_send()

            return 0

        lax.fori_loop(0, turns, finish, 0)

        def finish_small(q, _):
            s, copy = small_hop(q)

            @pl.when(s != index)
            def _():
                copy.wait_send()

            return 0

        lax.fori_loop(0, per, finish_small, 0)

        for i in range(groups - 1):
            total_first(i).wait_send()

        def finish_total(turn, _):
            s, copy = total_second(turn)

            @pl.when(jnp.logical_and(s < n, s != index))
            def _():
                copy.wait_send()

            return 0

        lax.fori_loop(0, turns, finish_total, 0)


def shampoo(plan, columns, grad, lowered, small, sums, moment, left, right, weight):
    vmem = pl.BlockSpec(memory_space=pltpu.VMEM)
    shape = jax.ShapeDtypeStruct(moment.shape, F32)
    _width, mine, per = chunks_of(columns)
    piece = moment.shape[1:]
    dma = pltpu.SemaphoreType.DMA
    return pl.pallas_call(
        functools.partial(shampoo_kernel, plan),
        out_shape=(shape,) * 4
        + (jax.ShapeDtypeStruct((32, -(-columns // LANES) * LANES), F32), jax.ShapeDtypeStruct((8, LANES), F32)),
        in_specs=[vmem] * 8,
        out_specs=(vmem,) * 6,
        scratch_shapes=[
            pltpu.VMEM((plan.groups - 1, plan.turns) + piece, BF16),
            pltpu.VMEM((plan.turns,) + piece, BF16),
            pltpu.VMEM((CRIT,) + piece, BF16),
            pltpu.VMEM((plan.groups, mine, 32, LANES), F32),
            pltpu.VMEM((CRIT, 8, LANES), F32),
            pltpu.VMEM((plan.groups - 1, 8, LANES), F32),
            pltpu.VMEM((8, LANES), F32),
            dma((plan.groups - 1,)),
            dma((plan.groups - 1, plan.turns)),
            dma((plan.turns,)),
            dma((CRIT,)),
            dma((per,)),
            dma((1,)),
            dma((plan.groups - 1 + plan.turns,)),
            dma((plan.groups - 1 + CRIT,)),
        ],
        compiler_params=pltpu.CompilerParams(collective_id=2, has_side_effects=True, vmem_limit_bytes=24 * MIB),
        name="shampoo",
    )(grad, lowered, small, sums, moment, left, right, weight)


def adamw(grad, moment, square, weight, rate):
    moment_new = FIRST_DECAY * moment + (1.0 - FIRST_DECAY) * grad
    square_new = SECOND_DECAY * square + (1.0 - SECOND_DECAY) * grad * grad
    moment_hat = moment_new / (1.0 - FIRST_DECAY**STEP)
    square_hat = square_new / (1.0 - SECOND_DECAY**STEP)
    weight_new = weight - rate * (moment_hat / (jnp.sqrt(square_hat) + 1e-08) + WEIGHT_DECAY * weight)
    return (moment_new, square_new, weight_new)


def finish_kernel(own_ref, weights, hidden, updated, stored, sems):
    copies = [pltpu.make_async_copy(src, dst, sems.at[k]) for k, (src, dst) in enumerate(zip(hidden, stored))]
    for copy in copies:
        copy.start()
    columns = weights[0].shape[1]
    for k, (first, last, rate) in enumerate(((0, IN, RATE_INPUT), (IN, IN + 4, RATE_NORMS))):
        grad = own_ref[first:last, 0:columns]
        moment, square, weight = (weights[3 * k + j][...] for j in range(3))
        for ref, value in zip(updated[3 * k : 3 * k + 3], adamw(grad, moment, square, weight, rate)):
            ref[...] = value
    for copy in copies:
        copy.wait()


def finish(own, weights, hidden):
    vmem = pl.BlockSpec(memory_space=pltpu.VMEM)
    anywhere = pl.BlockSpec(memory_space=pl.ANY)
    shapes = lambda arrays: tuple(jax.ShapeDtypeStruct(v.shape, F32) for v in arrays)
    return pl.pallas_call(
        finish_kernel,
        out_shape=(shapes(weights), shapes(hidden)),
        in_specs=[vmem, (vmem,) * len(weights), (anywhere,) * len(hidden)],
        out_specs=((vmem,) * len(weights), (anywhere,) * len(hidden)),
        scratch_shapes=[pltpu.SemaphoreType.DMA((len(hidden),))],
        compiler_params=pltpu.CompilerParams(vmem_limit_bytes=8 * MIB),
        name="finish",
    )(own, weights, hidden)


def local(
    plan,
    state_action,
    next_state,
    reward,
    done_flags,
    noise_index,
    noise_table,
    subsets,
    policy_in,
    policy_mid,
    policy_out,
    critic_in,
    in_first,
    in_second,
    critic_norms,
    norm_first,
    norm_second,
    critic_head,
    head_first,
    head_second,
    critic_hidden,
    hidden_moment,
    left_stats,
    right_stats,
    target_in,
    target_norms,
    target_head,
    target_hidden,
):
    rows, columns = state_action.shape[0], critic_in.shape[1]
    width = chunks_of(columns)[0]
    lines = lambda v: v.reshape(rows // LANES, LANES)
    w_target, share, x, params = dispatch(
        plan,
        (critic_hidden, target_hidden, critic_in, critic_norms, target_in, target_norms, jnp.stack([target_head, critic_head]))
        + (state_action.T, next_state.T, lines(reward), lines(done_flags), lines(noise_index), subsets.T)
        + (noise_table.T, policy_in, policy_mid, policy_out.T),
    )
    shares = (share,) + tuple(lax.ppermute(share, ("dp", "mp"), plan.shift(k)) for k in range(1, plan.groups))
    xc, q, info = target_values(plan, rows, width, x, w_target, params)
    q_all = share_values(plan, q)
    grad_hidden, lowered, grad_small, sums = critic_step(plan, width, info, xc, q_all, shares, params)
    *hidden, own, totals = shampoo(
        plan, columns, grad_hidden, lowered, grad_small, sums, hidden_moment, left_stats, right_stats, critic_hidden
    )
    loss_total, counted = totals[0, 0], totals[1, 0]
    weights = (in_first, in_second, critic_in, norm_first, norm_second, critic_norms)
    small, hidden = finish(own, weights, tuple(hidden))
    in_moment, in_square, in_updated, norm_moment, norm_square, norm_updated = small
    hidden_momentum, left_renewed, right_renewed, hidden_updated = hidden
    head_moment, head_square, head_updated = adamw(own[IN + 4, :columns], head_first, head_second, critic_head, RATE_HEAD)
    return (
        loss_total,
        counted,
        in_moment,
        in_square,
        in_updated,
        norm_moment,
        norm_square,
        norm_updated,
        head_moment,
        head_square,
        head_updated,
        hidden_momentum,
        left_renewed,
        right_renewed,
        hidden_updated,
    )


def solution(mesh):
    both = ("dp", "mp")
    rows, columns, flat, hidden = P(both, None), P(None, both), P(both), P(None, "mp", "dp")
    return jax.shard_map(
        functools.partial(local, Plan(mesh)),
        mesh=mesh,
        in_specs=(
            (rows, rows, flat, flat, flat, P(), rows, P(), P(), P())
            + (columns,) * 6
            + (flat,) * 3
            + (hidden,) * 4
            + (columns, columns, flat, hidden)
        ),
        out_specs=(P(), P()) + (columns,) * 6 + (flat,) * 3 + (hidden,) * 4,
        check_vma=False,
    )
```
